32 devices in a mesh: dp: 8 (over y, x, core), seq: 4 (over z).
Axes of the slice: x: 2, y: 2, z: 4, core: 2. Of those that a mesh axis runs over, the one named last changes fastest.
Arguments:
- tokens: bfloat16 [8, 1024, 1152], P('dp', 'seq'), may hold values from -6 to 6
- segment_ids: int32 [8, 1024], P('dp', 'seq'), may hold values from 0 to 2, as said below
- routes: int32 [8, 1024, 1], P('dp', 'seq'), may hold values from 0 to 3; in each aligned block of 256 rows (0 to 255, 256 to 511, ..., all dimensions but the last counted through in order) at most 128 rows name the same one
- cotangent: bfloat16 [8, 1024, 1152], P('dp', 'seq'), may hold values from -6 to 6
- small_params: bfloat16 [6912], P(('dp', 'seq'))
- w_in: bfloat16 [4608, 1152], P(('dp', 'seq')), may hold values from -0.1875 to 0.1875
- conv_w: bfloat16 [2304, 4], P(('dp', 'seq')), may hold values from -0.5 to 0.5
- conv_b: bfloat16 [2304], P(('dp', 'seq')), may hold values from -0.5 to 0.5
- w_x: bfloat16 [2304, 104], P(('dp', 'seq')), may hold values from -0.125 to 0.125
- w_dt: bfloat16 [2304, 72], P(('dp', 'seq')), may hold values from -0.75 to 0.75
- dt_bias: bfloat16 [2304], P(('dp', 'seq')), may hold values from -9 to -2
- a_log: bfloat16 [2304, 16], P(('dp', 'seq')), may hold values from 0 to 2.796875
- d_skip: bfloat16 [2304], P(('dp', 'seq')), may hold values from 0.5 to 1.5
- w_out: bfloat16 [2304, 1152], P(('dp', 'seq')), may hold values from -0.125 to 0.125
- w_up: bfloat16 [4, 1152, 3072], P(None, None, ('dp', 'seq')), may hold values from -0.1875 to 0.1875
- w_down: bfloat16 [4, 3072, 1152], P(None, ('dp', 'seq')), may hold values from -0.4375 to 0.4375
Outputs:
- mixed_out: bfloat16 [8, 1024, 1152], P('dp', 'seq')
- tokens_grad: bfloat16 [8, 1024, 1152], P('dp', 'seq')
- small_grad: float32 [6912], P(('dp', 'seq'))
- w_in_grad: float32 [4608, 1152], P(('dp', 'seq'))
- conv_w_grad: float32 [2304, 4], P(('dp', 'seq'))
- conv_b_grad: float32 [2304], P(('dp', 'seq'))
- w_x_grad: float32 [2304, 104], P(('dp', 'seq'))
- w_dt_grad: float32 [2304, 72], P(('dp', 'seq'))
- dt_bias_grad: float32 [2304], P(('dp', 'seq'))
- a_log_grad: float32 [2304, 16], P(('dp', 'seq'))
- d_skip_grad: float32 [2304], P(('dp', 'seq'))
- w_out_grad: float32 [2304, 1152], P(('dp', 'seq'))
- w_up_grad: float32 [4, 1152, 3072], P(None, None, ('dp', 'seq'))
- w_down_grad: float32 [4, 3072, 1152], P(None, ('dp', 'seq'))
The draws below stay inside these ranges and needn't reach their ends.
Inputs may be any that keep to these rules, and one draw needn't show every extreme that they name: `segment_ids`: along a row the ids start at 0, never fall and rise by one at a time. `routes`: no expert is named by more than 128 of the rows of one device.
All inputs are finite; a program needn't handle non-finite values.
Results may differ from the reference program's by a relative error of at most 0.012.
Values may be sent and summed in bfloat16 or wider, within the bound.
A program may use at most 448 MiB of HBM per device.

```python
import math
import jax
import jax.numpy as jnp
import numpy as np
from jax import lax

D = 1152
FF = 3072
N = 16
KC = 4
EXPERTS = 4
TOK_DEV = 256
DI = 2304
R = 72
CAP = 128
LEN = 1024
ROWS = 8


def draw_segment_ids(key, part):
    key = jax.random.fold_in(key, 11)
    first_key, second_key = jax.random.split(key)
    first_cut = jax.random.randint(first_key, (ROWS, 1), 1, TOK_DEV // 2 + 1)
    second_cut = jax.random.randint(second_key, (ROWS, 1), LEN - TOK_DEV // 2, LEN)
    position = jnp.arange(LEN, dtype=jnp.int32)[None, :]
    return (position >= first_cut).astype(jnp.int32) + (position >= second_cut).astype(jnp.int32)


def draw_small_params(key, part):
    key = jax.random.fold_in(key, 23)
    gain_key, route_key = jax.random.split(key)
    gains = 1.0 + 0.15 * jax.random.normal(gain_key, (2 * D,), jnp.float32)
    router_vals = 0.75 * jax.random.normal(route_key, (D * EXPERTS,), jnp.float32) / math.sqrt(D)
    return jnp.concatenate([gains, router_vals]).astype(jnp.bfloat16)


def level_of(rng, shape, shards, smallest, high):
    level = 1.0
    for dim, shards_of in shards:
        steps = jax.random.uniform(jax.random.fold_in(jax.random.fold_in(rng, 6), dim), (shards_of,), jnp.float32, smallest / len(shards), high / len(shards))
        level = level * jnp.repeat(jnp.exp(steps), shape[dim] // shards_of).reshape((-1,) + (1,) * (len(shape) - 1 - dim))
    return level


def routed_block(rng, own, number, rows, count, top, bound, lean):
    sequence = jax.random.permutation(rng, count)
    packed, usual = load_shares(count, rows * top, bound, lean, True), load_shares(count, rows * top, bound, lean, False)
    places = jnp.arange(count)

    def named(lengths, rotation):
        used = int((lengths > 0).sum())
        fixed = max(1, used // 4)
        passed = fixed + (places - fixed + rotation * (used - fixed)) % max(1, count - fixed)
        return jnp.zeros((count,), jnp.int32).at[sequence[jnp.where(places < fixed, places, passed)]].set(jnp.asarray(lengths, jnp.int32))

    lengths = jnp.where(number % 4 == 0, named(packed, number // 4), named(usual, number - number // 4 - 1))
    mixed = jax.random.permutation(jax.random.fold_in(own, 3), count)
    donor, sink = mixed[0:count // 2 * 2:2], mixed[1:count // 2 * 2:2]
    slack = jnp.minimum(lengths[donor] - 1, bound - lengths[sink]) // 2
    slack = jnp.where((donor == sequence[0]) | (sink == sequence[0]) | (lengths[sink] == 0), 0, jnp.maximum(slack, 0))
    passed = jax.random.randint(jax.random.fold_in(own, 4), (count // 2,), 0, 1 << 20) % (slack + 1)
    lengths = lengths.at[donor].add(-passed).at[sink].add(passed)
    members = jnp.searchsorted(jnp.cumsum(lengths), jnp.arange(rows * top), side="right").astype(jnp.int32)
    grid = members.reshape(top, rows).T
    grid = grid[jax.random.permutation(jax.random.fold_in(own, 1), rows)]
    rotation = jax.random.randint(jax.random.fold_in(own, 2), (rows, 1), 0, top)
    return jnp.take_along_axis(grid, (jnp.arange(top)[None, :] + rotation) % top, axis=1)


def load_shares(amount, total, reach, skew, full):
    portions = [(1 << 20) // math.isqrt(standing ** skew) + 1 for standing in range(1, amount + 1)]
    largest = reach if full else min(reach, max(-(-total // amount), total * portions[0] // sum(portions)))
    least = 1 if total - largest >= amount - 1 else 0
    counts, surplus = [largest] + [least] * (amount - 1), total - largest - least * (amount - 1)
    while surplus > 0:
        free = [i for i in range(1, amount) if counts[i] < largest] or [i for i in range(1, amount) if counts[i] < reach]
        mass, left = sum([portions[i] for i in free]), surplus
        for i in free:
            more = min(reach - counts[i], max(1, left * portions[i] // mass), surplus)
            counts[i] = counts[i] + more
            surplus = surplus - more
    return np.array(counts)


def centred(key, extent, deviation, most, shards=(), kind=jnp.bfloat16):
    loudness = level_of(key, extent, shards, -0.22, 0.18) if shards else 1.0
    entries = jax.random.normal(key, extent, jnp.float32) * deviation * loudness
    return jnp.minimum(jnp.maximum(entries, -most), most).astype(kind)


def setup_inputs(seed: int = 0) -> dict:
    key_of = jax.random.split(jax.random.key(seed), 17)
    tokens = centred(key_of[0], (ROWS, LEN, D), 1.0, 6.0, ((0, 8), (1, 4)))
    segment_ids = draw_segment_ids(jax.random.fold_in(key_of[16], 71), 0)
    routes_keys = jax.random.split(jax.random.fold_in(key_of[2], 1), ROWS * LEN // TOK_DEV)
    routes_turns = jax.random.permutation(jax.random.fold_in(key_of[2], 3), ROWS * LEN // TOK_DEV)
    routes = jax.vmap(lambda own, number: routed_block(jax.random.fold_in(key_of[2], 2), own, number, TOK_DEV, EXPERTS, 1, CAP, 1))(routes_keys, routes_turns).reshape((ROWS, LEN, 1))
    cotangent = centred(key_of[3], (ROWS, LEN, D), 1.0, 6.0, ((0, 8), (1, 4)))
    small_params = draw_small_params(jax.random.fold_in(key_of[16], 71), 0)
    w_in = centred(key_of[5], (2 * DI, D), D ** -0.5, 0.1875, ((0, 32),))
    conv_w = jnp.clip(jax.random.uniform(key_of[6], (DI, KC), jnp.float32, -0.5, 0.5) * level_of(key_of[6], (DI, KC), ((0, 32),), -0.4, 0.0), -0.5, 0.5).astype(jnp.bfloat16)
    conv_b = jnp.clip(jax.random.uniform(key_of[7], (DI,), jnp.float32, -0.5, 0.5) * level_of(key_of[7], (DI,), ((0, 32),), -0.4, 0.0), -0.5, 0.5).astype(jnp.bfloat16)
    w_x = centred(key_of[8], (DI, R + 2 * N), DI ** -0.5, 0.125, ((0, 32),))
    w_dt = centred(key_of[9], (DI, R), R ** -0.5, 0.75, ((0, 32),))
    dt_bias = jnp.clip(-9.0 + 7.0 * jax.random.uniform(key_of[10], (DI,), jnp.float32) ** level_of(key_of[10], (DI,), ((0, 32),), -0.2, 0.2), -9.0, -2.0).astype(jnp.bfloat16)
    a_log = jnp.clip(2.796875 * jax.random.uniform(key_of[11], (DI, N), jnp.float32) ** level_of(key_of[11], (DI, N), ((0, 32),), -0.2, 0.2), 0.0, 2.796875).astype(jnp.bfloat16)
    d_skip = jnp.clip(0.5 + 1.0 * jax.random.uniform(key_of[12], (DI,), jnp.float32) ** level_of(key_of[12], (DI,), ((0, 32),), -0.2, 0.2), 0.5, 1.5).astype(jnp.bfloat16)
    w_out = centred(key_of[13], (DI, D), DI ** -0.5, 0.125, ((0, 32),))
    w_up = centred(key_of[14], (EXPERTS, D, FF), D ** -0.5, 0.1875, ((2, 32),))
    w_down = centred(key_of[15], (EXPERTS, FF, D), (FF // 16) ** -0.5, 0.4375, ((1, 32),))
    return dict(tokens=tokens, segment_ids=segment_ids, routes=routes, cotangent=cotangent, small_params=small_params, w_in=w_in, conv_w=conv_w, conv_b=conv_b, w_x=w_x, w_dt=w_dt, dt_bias=dt_bias, a_log=a_log, d_skip=d_skip, w_out=w_out, w_up=w_up, w_down=w_down)


EPS = 1e-05

@jax.custom_vjp
def low(v):
    return lax.optimization_barrier(v.astype(jnp.bfloat16)).astype(jnp.float32)

@jax.custom_vjp
def low_back(v):
    return v

def low_keep(v):
    return (low(v), None)

def low_pass(kept, grad):
    return (grad,)

def back_keep(v):
    return (v, None)

def back_low(kept, grad):
    return (low(grad),)
low.defvjp(low_keep, low_pass)
low_back.defvjp(back_keep, back_low)

def matmul_hi(first_op, second_op):
    return jnp.dot(first_op, second_op, precision=lax.Precision.HIGHEST)

def rms_gain(value, gain):
    return value * lax.rsqrt(lax.optimization_barrier(jnp.mean(value * value, axis=-1, keepdims=True)) + EPS) * gain

def selective(steps_dt, values, b_rows, c_rows, keep_mask, decay_rates):
    length = steps_dt.shape[0]
    block_len = math.gcd(64, length)

    def advance(cur_state, step_item):
        dt_now, value_now, b_now, c_now, keep_now = step_item
        cur_state = jnp.exp(dt_now[:, None] * decay_rates) * keep_now * cur_state + (dt_now * value_now)[:, None] * b_now[None, :]
        return (cur_state, lax.optimization_barrier(jnp.sum(cur_state * c_now[None, :], axis=1)))

    def block_run(cur_state, step_items):
        return lax.scan(advance, cur_state, step_items)
    step_items = (steps_dt.reshape(-1, block_len, DI), values.reshape(-1, block_len, DI), b_rows.reshape(-1, block_len, N), c_rows.reshape(-1, block_len, N), keep_mask.reshape(-1, block_len))
    _, outputs = lax.scan(jax.checkpoint(block_run), jnp.zeros((DI, N), jnp.float32), step_items)
    return outputs.reshape(length, DI)

def mixer(row_vals, seg_ids, gain_one, w_in, conv_w, conv_b, w_x, w_dt, dt_bias, a_log, d_skip, w_out):
    length = row_vals.shape[0]
    normed = low(rms_gain(row_vals, gain_one))
    mixed_in = low_back(matmul_hi(normed, w_in.T))
    conv_in = low(mixed_in[:, :DI])
    z_vals = mixed_in[:, DI:]
    padded = jnp.concatenate([jnp.zeros((KC - 1, DI), jnp.float32), conv_in], axis=0)
    padded_ids = jnp.concatenate([jnp.full((KC - 1,), -1, jnp.int32), seg_ids], axis=0)
    conv_sum = conv_b
    for offset in range(KC):
        same_mask = (padded_ids[offset:offset + length] == seg_ids).astype(jnp.float32)
        conv_sum = conv_sum + conv_w[:, offset] * padded[offset:offset + length] * same_mask[:, None]
    values = jax.nn.silu(conv_sum)
    projected = low_back(matmul_hi(low(values), w_x))
    low_rank = low(projected[:, :R])
    b_rows = projected[:, R:R + N]
    c_rows = projected[:, R + N:]
    steps_dt = jax.nn.softplus(low_back(matmul_hi(low_rank, w_dt.T)) + dt_bias)
    keep_mask = (padded_ids[KC - 2:KC - 2 + length] == seg_ids).astype(jnp.float32)
    scanned = selective(steps_dt, values, b_rows, c_rows, keep_mask, -jnp.exp(a_log))
    gated = low((scanned + d_skip * values) * jax.nn.silu(z_vals))
    return low_back(matmul_hi(gated, w_out))

def experts(first_sum, route_ids, gain_two, router_mat, w_up, w_down):
    normed_two = low(rms_gain(first_sum, gain_two))
    logits = low_back(matmul_hi(normed_two, router_mat))
    onehot = (route_ids[:, None] == jnp.arange(EXPERTS)[None, :]).astype(jnp.float32)
    gate_prob = lax.optimization_barrier(jnp.sum(jax.nn.softmax(logits, axis=-1) * onehot, axis=-1, keepdims=True))
    hidden = low_back(jnp.einsum('td,edf->tef', normed_two, w_up, precision=lax.Precision.HIGHEST))
    activated = low(jax.nn.gelu(hidden, approximate=False))
    expert_all = jnp.einsum('tef,efd->ted', activated, w_down, precision=lax.Precision.HIGHEST)
    expert_out = low_back(lax.optimization_barrier(jnp.sum(expert_all * onehot[:, :, None], axis=1)))
    return first_sum + gate_prob * expert_out

def layer(row_vals, seg_ids, route_ids, params):
    small_vec, w_in, conv_w, conv_b, w_x, w_dt, dt_bias, a_log, d_skip, w_out, w_up, w_down = params
    gain_one = small_vec[:D]
    gain_two = small_vec[D:2 * D]
    router_mat = small_vec[2 * D:].reshape(D, EXPERTS)
    first_sum = row_vals + mixer(row_vals, seg_ids, gain_one, w_in, conv_w, conv_b, w_x, w_dt, dt_bias, a_log, d_skip, w_out)
    return experts(first_sum, route_ids, gain_two, router_mat, w_up, w_down)

def reference(tokens, segment_ids, routes, cotangent, small_params, w_in, conv_w, conv_b, w_x, w_dt, dt_bias, a_log, d_skip, w_out, w_up, w_down):
    params = tuple((weight.astype(jnp.float32) for weight in (small_params, w_in, conv_w, conv_b, w_x, w_dt, dt_bias, a_log, d_skip, w_out, w_up, w_down)))

    def row_step(totals, step_item):
        row_vals, seg_ids, route_ids, row_grad = step_item

        def row_layer(inputs, weights):
            return layer(inputs, seg_ids, route_ids[:, 0], weights)
        result, pull_back = jax.vjp(row_layer, row_vals.astype(jnp.float32), params)
        grad_row, grad_params = pull_back(row_grad.astype(jnp.float32))
        totals = jax.tree.map(jnp.add, totals, grad_params)
        return (totals, (result.astype(jnp.bfloat16), grad_row.astype(jnp.bfloat16)))
    zero_grads = jax.tree.map(jnp.zeros_like, params)
    totals, outputs = lax.scan(row_step, zero_grads, (tokens, segment_ids, routes, cotangent))
    return (outputs[0], outputs[1], totals[0], totals[1], totals[2], totals[3], totals[4], totals[5], totals[6], totals[7], totals[8], totals[9], totals[10], totals[11])
```

```python
import functools
import math

import jax
import jax.numpy as jnp
from jax import lax
from jax.experimental import pallas as pl
from jax.experimental.pallas import tpu as pltpu
from jax.sharding import PartitionSpec as P

F32, BF = jnp.float32, jnp.bfloat16
EPS = 1e-05
STEP = 16
VM = 56 * 1024 * 1024
MESH = pl.DeviceIdType.MESH
NT = (((1,), (1,)), ((), ()))
TN = (((0,), (0,)), ((), ()))


def rowb(block, i, n):
    return jnp.broadcast_to(block[i:i+1, :], (n, block.shape[1]))

def state_kernel(n, dte_ref, dtx_ref, rate_ref, b_ref, state_ref, carry_ref):
    rows, wide = dte_ref.shape
    tiles = wide // 128
    rates = [rate_ref[:, j*128:(j+1)*128] for j in range(tiles)]
    def block(k, carry):
        state, total = carry
        at = pl.multiple_of(k * STEP, STEP)
        dte = dte_ref[pl.ds(at, STEP), :]
        dtx = dtx_ref[pl.ds(at, STEP), :]
        state = list(state)
        for i in range(STEP):
            bs = b_ref[pl.ds((at + i) * n, n), :]
            for j in range(tiles):
                c = slice(j*128, (j+1)*128)
                decay = jnp.exp2(rowb(dte[:, c], i, n) * rates[j])
                state[j] = decay * state[j] + bs * rowb(dtx[:, c], i, n)
        return tuple(state), total + dte
    zero = tuple(jnp.zeros((n, 128), F32) for _ in range(tiles))
    state, total = lax.fori_loop(0, rows // STEP, block, (zero, jnp.zeros((STEP, wide), F32)))
    summed = jnp.sum(total, axis=0, keepdims=True)
    for j in range(tiles):
        c = slice(j*128, (j+1)*128)
        state_ref[:, c] = state[j]
        carry_ref[:, c] = jnp.exp2(jnp.broadcast_to(summed[:, c], (n, 128)) * rates[j])

def state_pass(dte, dtx, rates2, b_wide, wide):
    rows, chans = dte.shape
    n = rates2.shape[0]
    return pl.pallas_call(
        functools.partial(state_kernel, n),
        grid=(chans // wide,),
        in_specs=[pl.BlockSpec((rows, wide), lambda g: (0, g)),
                  pl.BlockSpec((rows, wide), lambda g: (0, g)),
                  pl.BlockSpec((n, wide), lambda g: (0, g)),
                  pl.BlockSpec(b_wide.shape, lambda g: (0, 0))],
        out_specs=[pl.BlockSpec((n, wide), lambda g: (0, g))] * 2,
        out_shape=[jax.ShapeDtypeStruct((n, chans), F32)] * 2,
        compiler_params=pltpu.CompilerParams(vmem_limit_bytes=VM),
        cost_estimate=pl.CostEstimate(flops=8*rows*chans*n, bytes_accessed=8*rows*chans, transcendentals=rows*chans*n),
    )(dte, dtx, rates2, b_wide)

def scan_kernel(n, dte_ref, dtx_ref, rate_ref, b_ref, cblk_ref, start_ref, y_ref, check_ref, hs):
    rows, wide = dte_ref.shape
    tiles = wide // 128
    rates = [rate_ref[:, j*128:(j+1)*128] for j in range(tiles)]
    def block(k, state):
        at = pl.multiple_of(k * STEP, STEP)
        dte = dte_ref[pl.ds(at, STEP), :]
        dtx = dtx_ref[pl.ds(at, STEP), :]
        state = list(state)
        kn = pl.multiple_of(k * n, n)
        for j in range(tiles):
            check_ref[pl.ds(kn, n), j*128:(j+1)*128] = state[j]
        for i in range(STEP):
            bs = b_ref[pl.ds((at + i) * n, n), :]
            for j in range(tiles):
                c = slice(j*128, (j+1)*128)
                decay = jnp.exp2(rowb(dte[:, c], i, n) * rates[j])
                state[j] = decay * state[j] + bs * rowb(dtx[:, c], i, n)
                hs[i*n:(i+1)*n, c] = state[j].astype(BF)
        y_ref[pl.ds(at, STEP), :] = jnp.dot(cblk_ref[pl.ds(at, STEP), :], hs[...], preferred_element_type=F32)
        return tuple(state)
    start = tuple(start_ref[:, j*128:(j+1)*128] for j in range(tiles))
    lax.fori_loop(0, rows // STEP, block, start)

def scan_pass(dte, dtx, rates2, b_wide, c_blk, start, wide):
    rows, chans = dte.shape
    n = rates2.shape[0]
    return pl.pallas_call(
        functools.partial(scan_kernel, n),
        grid=(chans // wide,),
        in_specs=[pl.BlockSpec((rows, wide), lambda g: (0, g)),
                  pl.BlockSpec((rows, wide), lambda g: (0, g)),
                  pl.BlockSpec((n, wide), lambda g: (0, g)),
                  pl.BlockSpec(b_wide.shape, lambda g: (0, 0)),
                  pl.BlockSpec(c_blk.shape, lambda g: (0, 0)),
                  pl.BlockSpec((n, wide), lambda g: (0, g))],
        out_specs=[pl.BlockSpec((rows, wide), lambda g: (0, g)),
                   pl.BlockSpec((rows // STEP * n, wide), lambda g: (0, g))],
        out_shape=[jax.ShapeDtypeStruct((rows, chans), F32),
                   jax.ShapeDtypeStruct((rows // STEP * n, chans), F32)],
        scratch_shapes=[pltpu.VMEM((STEP * n, wide), BF)],
        compiler_params=pltpu.CompilerParams(vmem_limit_bytes=VM),
        cost_estimate=pl.CostEstimate(flops=10*rows*chans*n, bytes_accessed=12*rows*chans, transcendentals=rows*chans*n),
    )(dte, dtx, rates2, b_wide, c_blk, start)

def back_state_kernel(n, dte_ref, gs_ref, rate_ref, c_ref, out_ref):
    rows, wide = dte_ref.shape
    tiles = wide // 128
    rates = [rate_ref[:, j*128:(j+1)*128] for j in range(tiles)]
    def block(k, state):
        at = pl.multiple_of(rows - STEP - k * STEP, STEP)
        dte = dte_ref[pl.ds(at, STEP), :]
        gs = gs_ref[pl.ds(at, STEP), :]
        state = list(state)
        for i in reversed(range(STEP)):
            cs = c_ref[pl.ds((at + i) * n, n), :]
            for j in range(tiles):
                c = slice(j*128, (j+1)*128)
                decay = jnp.exp2(rowb(dte[:, c], i, n) * rates[j])
                state[j] = decay * (state[j] + cs * rowb(gs[:, c], i, n))
        return tuple(state)
    zero = tuple(jnp.zeros((n, 128), F32) for _ in range(tiles))
    state = lax.fori_loop(0, rows // STEP, block, zero)
    for j in range(tiles):
        out_ref[:, j*128:(j+1)*128] = state[j]

def back_state_pass(dte, gs, rates2, c_wide, wide):
    rows, chans = dte.shape
    n = rates2.shape[0]
    return pl.pallas_call(
        functools.partial(back_state_kernel, n),
        grid=(chans // wide,),
        in_specs=[pl.BlockSpec((rows, wide), lambda g: (0, g)),
                  pl.BlockSpec((rows, wide), lambda g: (0, g)),
                  pl.BlockSpec((n, wide), lambda g: (0, g)),
                  pl.BlockSpec(c_wide.shape, lambda g: (0, 0))],
        out_specs=pl.BlockSpec((n, wide), lambda g: (0, g)),
        out_shape=jax.ShapeDtypeStruct((n, chans), F32),
        compiler_params=pltpu.CompilerParams(vmem_limit_bytes=VM),
        cost_estimate=pl.CostEstimate(flops=8*rows*chans*n, bytes_accessed=8*rows*chans, transcendentals=rows*chans*n),
    )(dte, gs, rates2, c_wide)

def back_kernel(n, dt_ref, dte_ref, dtx_ref, gs_ref, rate_ref, rawrate_ref, b_ref, c_ref, bblk_ref, oblk_ref, check_ref, next_ref,
                gdtx_ref, gdt_ref, glog_ref, gb_ref, gc_ref, us, decs, hs, ls, ps):
    rows, wide = dte_ref.shape
    tiles = wide // 128
    rates = [rate_ref[:, j*128:(j+1)*128] for j in range(tiles)]
    @pl.when(pl.program_id(0) == 0)
    def _():
        gb_ref[...] = jnp.zeros_like(gb_ref)
        gc_ref[...] = jnp.zeros_like(gc_ref)
    glog_ref[...] = jnp.zeros_like(glog_ref)
    def block(k, later):
        kk = rows // STEP - 1 - k
        at = pl.multiple_of(kk * STEP, STEP)
        kn = pl.multiple_of(kk * n, n)
        dte = dte_ref[pl.ds(at, STEP), :]
        dtx = dtx_ref[pl.ds(at, STEP), :]
        state = [check_ref[pl.ds(kn, n), j*128:(j+1)*128] for j in range(tiles)]
        for i in range(STEP):
            bs = b_ref[pl.ds((at + i) * n, n), :]
            for j in range(tiles):
                c = slice(j*128, (j+1)*128)
                decay = jnp.exp2(rowb(dte[:, c], i, n) * rates[j])
                kept = decay * state[j]
                state[j] = kept + bs * rowb(dtx[:, c], i, n)
                decs[i*n:(i+1)*n, c] = decay
                us[i*n:(i+1)*n, c] = kept
                hs[i*n:(i+1)*n, c] = state[j].astype(BF)
        later = list(later)
        dt = dt_ref[pl.ds(at, STEP), :]
        gs = gs_ref[pl.ds(at, STEP), :]
        logs = [glog_ref[:, j*128:(j+1)*128] for j in range(tiles)]
        for i in reversed(range(STEP)):
            cs = c_ref[pl.ds((at + i) * n, n), :]
            for j in range(tiles):
                c = slice(j*128, (j+1)*128)
                adj = later[j] + cs * rowb(gs[:, c], i, n)
                part = adj * us[i*n:(i+1)*n, c] * rawrate_ref[:, c]
                later[j] = adj * decs[i*n:(i+1)*n, c]
                logs[j] = logs[j] + part * rowb(dt[:, c], i, n)
                ls[i*n:(i+1)*n, c] = adj.astype(BF)
                ps[i*n:(i+1)*n, c] = part.astype(BF)
        for j in range(tiles):
            glog_ref[:, j*128:(j+1)*128] = logs[j]
        gdtx_ref[pl.ds(at, STEP), :] = jnp.dot(bblk_ref[pl.ds(at, STEP), :], ls[...], preferred_element_type=F32)
        gdt_ref[pl.ds(at, STEP), :] = jnp.dot(oblk_ref[...], ps[...], preferred_element_type=F32)
        nt = (((1,), (1,)), ((), ()))
        gb_ref[pl.ds(at, STEP), :] += lax.dot_general(dtx.astype(BF), ls[...], nt, preferred_element_type=F32)
        gc_ref[pl.ds(at, STEP), :] += lax.dot_general(gs.astype(BF), hs[...], nt, preferred_element_type=F32)
        return tuple(later)
    start = tuple(next_ref[:, j*128:(j+1)*128] for j in range(tiles))
    lax.fori_loop(0, rows // STEP, block, start)

def back_pass(dt, dte, dtx, gs, rates2, rates, b_wide, c_wide, b_blk, o_blk, check, nxt, wide):
    rows, chans = dte.shape
    n = rates2.shape[0]
    col = lambda r: pl.BlockSpec((r, wide), lambda g: (0, g))
    whole = lambda a: pl.BlockSpec(a.shape, lambda g: (0, 0))
    return pl.pallas_call(
        functools.partial(back_kernel, n),
        grid=(chans // wide,),
        in_specs=[col(rows)] * 4 + [col(n)] * 2 + [whole(b_wide), whole(c_wide), whole(b_blk), whole(o_blk), col(rows // STEP * n), col(n)],
        out_specs=[col(rows), col(rows), col(n), pl.BlockSpec((rows, STEP * n), lambda g: (0, 0)), pl.BlockSpec((rows, STEP * n), lambda g: (0, 0))],
        out_shape=[jax.ShapeDtypeStruct((rows, chans), F32)] * 2 + [jax.ShapeDtypeStruct((n, chans), F32)] + [jax.ShapeDtypeStruct((rows, STEP * n), F32)] * 2,
        scratch_shapes=[pltpu.VMEM((STEP * n, wide), F32)] * 2 + [pltpu.VMEM((STEP * n, wide), BF)] * 3,
        compiler_params=pltpu.CompilerParams(vmem_limit_bytes=VM),
        cost_estimate=pl.CostEstimate(flops=26*rows*chans*n, bytes_accessed=24*rows*chans, transcendentals=rows*chans*n),
    )(dt, dte, dtx, gs, rates2, rates, b_wide, c_wide, b_blk, o_blk, check, nxt)

def block_diag(vals):
    rows, n = vals.shape
    same = (jnp.arange(rows)[:, None] % STEP) == (jnp.arange(STEP * n)[None, :] // n)
    return jnp.where(same, jnp.tile(vals, (1, STEP)), 0)

def block_undiag(full, n):
    rows = full.shape[0]
    same = (jnp.arange(rows)[:, None] % STEP) == (jnp.arange(STEP * n)[None, :] // n)
    return jnp.sum(jnp.where(same, full, 0).reshape(rows, STEP, n), axis=1)


def expert_kernel(slot_ref, grad_ref, up_ref, down_ref, out_ref, disp_ref, gup_ref, gdown_ref):
    slots, grads, up, down = slot_ref[...], grad_ref[...], up_ref[...], down_ref[...]
    hidden = lax.dot_general(slots, up, NT, preferred_element_type=F32)
    phi = 0.5 * (1.0 + lax.erf(hidden * (1.0 / math.sqrt(2.0))))
    act = (hidden * phi).astype(BF)
    slope = phi + hidden * jnp.exp(hidden * hidden * -0.5) * (1.0 / math.sqrt(2.0 * math.pi))
    gact = lax.dot_general(grads, down, NT, preferred_element_type=F32)
    ghid = (gact * slope).astype(BF)
    @pl.when(pl.program_id(0) == 0)
    def _():
        out_ref[...] = jnp.zeros_like(out_ref)
        disp_ref[...] = jnp.zeros_like(disp_ref)
    out_ref[...] += jnp.dot(act, down, preferred_element_type=F32)
    disp_ref[...] += jnp.dot(ghid, up, preferred_element_type=F32)
    gup_ref[...] = lax.dot_general(ghid, slots, TN, preferred_element_type=F32).astype(gup_ref.dtype)
    gdown_ref[...] = lax.dot_general(act, grads, TN, preferred_element_type=F32).astype(gdown_ref.dtype)

def expert_pass(slots, grads, up, down, block):
    rows, width = slots.shape
    units = up.shape[0]
    whole = pl.BlockSpec((rows, width), lambda g: (0, 0))
    part = pl.BlockSpec((block, width), lambda g: (g, 0))
    return pl.pallas_call(
        expert_kernel,
        grid=(units // block,),
        in_specs=[whole, whole, part, part],
        out_specs=[whole, whole, part, part],
        out_shape=[jax.ShapeDtypeStruct((rows, width), F32)] * 2 + [jax.ShapeDtypeStruct((units, width), BF)] * 2,
        compiler_params=pltpu.CompilerParams(vmem_limit_bytes=VM),
        cost_estimate=pl.CostEstimate(flops=12*rows*units*width, bytes_accessed=8*units*width + 12*rows*width, transcendentals=2*rows*units),
    )(slots, grads, up, down)


def flip(value, bit):
    return value + bit - 2 * bit * (lax.rem(value // bit, 2))


def greet(partners):
    barrier = pltpu.get_barrier_semaphore()
    for partner in partners:
        pl.semaphore_signal(barrier, inc=1, device_id=partner, device_id_type=MESH)
    pl.semaphore_wait(barrier, len(partners))


class ZSwap:
    def __init__(self, pairs, local, send, recv, count):
        self.pairs, self.local, self.send, self.recv, self.count = pairs, local, send, recv, count

    def own(self):
        z = lax.axis_index("seq")
        return [pltpu.make_async_copy(src.at[z], dst.at[z], self.local.at[i]) for i, (src, dst) in enumerate(self.pairs)]

    def out(self):
        dp, z = lax.axis_index("dp"), lax.axis_index("seq")
        made = []
        for j in range(1, self.count):
            peer = lax.rem(z + j, self.count)
            for i, (src, dst) in enumerate(self.pairs):
                made.append(pltpu.make_async_remote_copy(src.at[peer], dst.at[z], self.send.at[i, j - 1], self.recv.at[i, j - 1], device_id=(dp, peer), device_id_type=MESH))
        return made

    def start(self):
        for copy in self.out() + self.own():
            copy.start()

    def wait(self):
        dp, z = lax.axis_index("dp"), lax.axis_index("seq")
        for copy in self.own():
            copy.wait()
        for copy in self.out():
            copy.wait_send()
        for j in range(1, self.count):
            source = lax.rem(z + self.count - j, self.count)
            for i, (src, dst) in enumerate(self.pairs):
                pltpu.make_async_remote_copy(src.at[z], dst.at[source], self.send.at[i, j - 1], self.recv.at[i, j - 1], device_id=(dp, source), device_id_type=MESH).wait_recv()


def gather_kernel(parts, count, in_ref, rest_ref, up_ref, down_ref, tok_ref, ids_ref, gin_ref, grest_ref, gup_ref, gdown_ref, rim_ref, rimids_ref,
                  local_sem, send, recv, share_send, share_recv, pair_send, pair_recv, swap_local, swap_send, swap_recv, rim_send, rim_recv):
    dp, z = lax.axis_index("dp"), lax.axis_index("seq")
    chip, core = dp // 2, lax.rem(dp, 2)
    srcs, dsts = (in_ref, rest_ref), (gin_ref, grest_ref)
    sibling = (flip(dp, 1), z)
    peers = [lax.rem(z + j, count) for j in range(1, count)]
    greet([sibling, (flip(dp, 4), z), (flip(dp, 2), z)] + [(dp, peer) for peer in peers])

    tail = pl.ds(tok_ref.shape[0] - rim_ref.shape[0], rim_ref.shape[0])
    rims = [pltpu.make_async_remote_copy(src, dst, rim_send.at[i], rim_recv.at[i], device_id=(dp, lax.rem(z + 1, count)), device_id_type=MESH)
            for i, (src, dst) in enumerate(((tok_ref.at[tail], rim_ref), (ids_ref, rimids_ref)))]
    for copy in rims:
        copy.start()
    mine = []
    for i, (src, dst) in enumerate(zip(srcs, dsts)):
        local = pltpu.make_async_copy(src, dst.at[chip, core, z], local_sem.at[i])
        pair = pltpu.make_async_remote_copy(src, dst.at[chip, core, z], pair_send.at[i], pair_recv.at[i], device_id=sibling, device_id_type=MESH)
        local.start()
        pair.start()
        mine += [local, pair]
    for copy in mine:
        copy.wait()
    swap = ZSwap(((up_ref, gup_ref), (down_ref, gdown_ref)), swap_local, swap_send, swap_recv, count)

    def role(which, first_bit, second_bit):
        chunks = parts[which]
        first, second = (flip(dp, first_bit), z), (flip(dp, second_bit), z)
        first_chip, second_chip = flip(chip, first_bit // 2), flip(chip, second_bit // 2)
        both_chip = flip(first_chip, second_bit // 2)

        def copies(at_chip, at_z, slot, to, send_s, recv_s):
            made = []
            for i, (ref, lo, size) in enumerate(chunks):
                view = dsts[ref].at[at_chip, :, at_z, pl.ds(lo, size)]
                made.append(pltpu.make_async_remote_copy(view, view, send_s.at[slot, i], recv_s.at[slot, i], device_id=to, device_id_type=MESH))
            return made

        def start(made):
            for copy in made:
                copy.start()

        def wait_recv(made):
            for copy in made:
                copy.wait_recv()

        def along_first(k):
            return copies(chip, k, 4 + k, first, send, recv)

        def along_second(k, far):
            return copies(first_chip if far else chip, k, 8 + 4 * far + k, second, send, recv)

        def came_first(k):
            return copies(first_chip, k, 4 + k, first, send, recv)

        def came_second(k, far):
            return copies(both_chip if far else second_chip, k, 8 + 4 * far + k, second, send, recv)

        def share(at_chip, k, offset):
            return copies(at_chip, k, 4 * offset + k, sibling, share_send, share_recv)

        def spread(k):
            start(along_second(k, 0))
            start(along_first(k))

        def rest(k):
            wait_recv(came_first(k))
            start(along_second(k, 1))
            start(share(first_chip, k, 1))

        @pl.when(z > 0)
        def _():
            start(copies(chip, z, z, (dp, z - 1), send, recv))

        @pl.when(z < count - 1)
        def _():
            start(copies(chip, z, z + count * 5, (dp, z + 1), send, recv))

        def below(hop, work):
            pl.when(z - hop >= 0)(lambda: work(z - hop))

        def above(hop, work):
            pl.when(z + hop <= count - 1)(lambda: work(z + hop))

        def from_below(k):
            wait_recv(copies(chip, k, k + count * 5, (dp, z), send, recv))

            @pl.when(z < count - 1)
            def _():
                start(copies(chip, k, k + count * 5, (dp, z + 1), send, recv))

            spread(k)
            start(share(chip, k, 0))

        def from_above(k):
            wait_recv(copies(chip, k, k, (dp, z), send, recv))

            @pl.when(z > 0)
            def _():
                start(copies(chip, k, k, (dp, z - 1), send, recv))

            spread(k)
            start(share(chip, k, 0))

        spread(z)
        for hop in range(1, count):
            below(hop, from_below)
            above(hop, from_above)
            if hop == 1:
                rest(z)
            else:
                below(hop - 1, rest)
                above(hop - 1, rest)
        swap.start()
        below(count - 1, rest)
        above(count - 1, rest)

        def finish(k, _):
            for far in (0, 1):
                wait_recv(came_second(k, far))
                start(share(both_chip if far else second_chip, k, 2 + far))
            return 0

        lax.fori_loop(0, count, finish, 0)

        def drain(k, _):
            for copy in along_first(k) + along_second(k, 0) + along_second(k, 1):
                copy.wait_send()
            for offset, at_chip in enumerate((chip, first_chip, second_chip, both_chip)):
                if offset:
                    for copy in share(at_chip, k, offset):
                        copy.wait_send()
                else:
                    @pl.when(k != z)
                    def _():
                        for copy in share(at_chip, k, offset):
                            copy.wait_send()

            @pl.when((k <= z) & (z < count - 1))
            def _():
                for copy in copies(chip, k, k + count * 5, (dp, z), send, recv):
                    copy.wait_send()

            @pl.when((k >= z) & (z > 0))
            def _():
                for copy in copies(chip, k, k, (dp, z), send, recv):
                    copy.wait_send()
            return 0

        lax.fori_loop(0, count, drain, 0)

        other = parts[1 - which]

        def shared(k, _):
            for offset, at_chip in enumerate((chip, second_chip, first_chip, both_chip)):
                def wait():
                    for i, (ref, lo, size) in enumerate(other):
                        view = dsts[ref].at[at_chip, :, k, pl.ds(lo, size)]
                        pltpu.make_async_remote_copy(view, view, share_send.at[4 * offset + k, i], share_recv.at[4 * offset + k, i], device_id=sibling, device_id_type=MESH).wait_recv()
                if offset:
                    wait()
                else:
                    pl.when(k != z)(wait)
            return 0

        lax.fori_loop(0, count, shared, 0)

    pl.when(core == 0)(lambda: role(0, 4, 2))
    pl.when(core == 1)(lambda: role(1, 2, 4))
    swap.wait()
    for copy in rims:
        copy.wait()


def gather_all(w_in, rest, up, down, tok, ids, cut, count):
    parts = (((0, 0, cut),), ((0, cut, w_in.shape[0] - cut), (1, 0, rest.shape[0])))
    shape = lambda a: jax.ShapeDtypeStruct((4, 2, count) + a.shape, a.dtype)
    sems = lambda *s: pltpu.SemaphoreType.DMA(s)
    return pl.pallas_call(
        functools.partial(gather_kernel, parts, count),
        in_specs=[pl.BlockSpec(memory_space=pl.ANY)] * 6,
        out_specs=[pl.BlockSpec(memory_space=pl.ANY)] * 6,
        out_shape=[shape(w_in), shape(rest), jax.ShapeDtypeStruct(up.shape, up.dtype), jax.ShapeDtypeStruct(down.shape, down.dtype),
                   jax.ShapeDtypeStruct((16, tok.shape[1]), tok.dtype), jax.ShapeDtypeStruct(ids.shape, ids.dtype)],
        scratch_shapes=[sems(2), sems(24, 2), sems(24, 2), sems(16, 2), sems(16, 2), sems(2), sems(2), sems(2), sems(2, count - 1), sems(2, count - 1), sems(2), sems(2)],
        compiler_params=pltpu.CompilerParams(collective_id=1, has_side_effects=True),
        cost_estimate=pl.CostEstimate(flops=0, bytes_accessed=200_000_000, transcendentals=0),
        name="gather_all",
    )(w_in, rest, up, down, tok, ids)


def scatter_kernel(parts, count, in_ref, rest_ref, up_ref, down_ref, oin_ref, orest_ref, oup_ref, odown_ref, mine_a, mine_b, sib_a, sib_b, far_a, far_b, near_a, near_b, zgot_a, zgot_b, final_a, final_b,
                   load_sem, sib_send, sib_recv, two_send, two_recv, one_send, one_recv, z_send, z_recv, end_send, end_recv, end_local,
                   swap_local, swap_send, swap_recv):
    dp, z = lax.axis_index("dp"), lax.axis_index("seq")
    chip, core = dp // 2, lax.rem(dp, 2)
    srcs, outs = (in_ref, rest_ref), (oin_ref, orest_ref)
    mine, sib, far_got, near_got, z_got, final = (mine_a, mine_b), (sib_a, sib_b), (far_a, far_b), (near_a, near_b), (zgot_a, zgot_b), (final_a, final_b)
    sibling = (flip(dp, 1), z)
    peers = [(dp, lax.rem(z + j, count)) for j in range(1, count)]
    greet([sibling, (flip(dp, 4), z), (flip(dp, 2), z)] + peers)

    swap = ZSwap(((up_ref, oup_ref), (down_ref, odown_ref)), swap_local, swap_send, swap_recv, count)

    def role(which, first_bit, second_bit):
        chunks, other = parts[which], parts[1 - which]
        first, second = (flip(dp, first_bit), z), (flip(dp, second_bit), z)
        first_chip, second_chip = flip(chip, first_bit // 2), flip(chip, second_bit // 2)
        both_chip = flip(first_chip, second_bit // 2)
        steps = [lax.rem(z + 1 + j, count) for j in range(count)]

        def loads(col, k):
            slot = col * count + k
            return [pltpu.make_async_copy(srcs[ref].at[col, :, k, pl.ds(lo, size)], mine[ref].at[slot, :, pl.ds(0, size)], load_sem.at[slot, ref])
                    for ref, lo, size in chunks]

        def sibling_copies(col, k, pieces):
            slot = col * count + k
            return [pltpu.make_async_remote_copy(srcs[ref].at[col, :, k, pl.ds(lo, size)], sib[ref].at[slot, :, pl.ds(0, size)],
                                                 sib_send.at[slot, ref], sib_recv.at[slot, ref], device_id=sibling, device_id_type=MESH)
                    for ref, lo, size in pieces]

        def send(col, k, dst, slot, send_s, recv_s, to):
            return [pltpu.make_async_remote_copy(mine[ref].at[col * count + k, :, pl.ds(0, size)], dst[ref].at[slot, :, pl.ds(0, size)],
                                                 send_s.at[slot, ref], recv_s.at[slot, ref], device_id=to, device_id_type=MESH)
                    for ref, lo, size in chunks]

        def start(copies):
            for copy in copies:
                copy.start()

        def wait_recv(copies):
            for copy in copies:
                copy.wait_recv()

        def wait_send(copies):
            for copy in copies:
                copy.wait_send()

        def add(col, k, terms, last=False):
            slot = col * count + k
            for copy in loads(col, k):
                copy.wait()
            wait_recv(sibling_copies(col, k, chunks))
            for ref, lo, size in chunks:
                def rows(r, _):
                    at = pl.ds(pl.multiple_of(r * 16, 16), 16)
                    for c in range(2):
                        total = mine[ref][slot, c, at, :].astype(F32) + sib[ref][slot, c, at, :].astype(F32)
                        for buf, place in terms:
                            total = total + buf[ref][place, c, at, :].astype(F32)
                        if last:
                            final[ref][c, at, :] = total
                        else:
                            mine[ref][slot, c, at, :] = total.astype(BF)
                    return 0

                lax.fori_loop(0, size // 16, rows, 0)

        for k in steps:
            for col, sib_col in ((both_chip, both_chip), (second_chip, first_chip), (first_chip, second_chip), (chip, chip)):
                start(sibling_copies(sib_col, k, other) + loads(col, k))

        swap.start()

        def stage_one(k):
            for far, col in ((1, both_chip), (0, second_chip)):
                add(col, k, ())
                start(send(col, k, far_got, far * count + k, two_send, two_recv, second))

        def stage_two(k):
            wait_recv(send(first_chip, k, far_got, count + k, two_send, two_recv, second))
            add(first_chip, k, ((far_got, count + k),))
            start(send(first_chip, k, near_got, k, one_send, one_recv, first))

        def stage_three(j, k):
            wait_recv(send(chip, k, far_got, k, two_send, two_recv, second))
            wait_recv(send(chip, k, near_got, k, one_send, one_recv, first))
            if j < count - 1:
                add(chip, k, ((far_got, k), (near_got, k)))
                start(send(chip, k, z_got, j, z_send, z_recv, (dp, k)))

        for j in range(count + 2):
            if j < count:
                stage_one(steps[j])
            if 1 <= j <= count:
                stage_two(steps[j - 1])
            if j >= 2:
                stage_three(j - 2, steps[j - 2])

        for j in range(count - 1):
            wait_recv(send(chip, z, z_got, j, z_send, z_recv, (dp, z)))
        add(chip, z, ((far_got, z), (near_got, z)) + tuple((z_got, j) for j in range(count - 1)), last=True)
        locals_, remotes = [], []
        for ref, lo, size in chunks:
            locals_.append(pltpu.make_async_copy(final[ref].at[which, pl.ds(0, size)], outs[ref].at[pl.ds(lo, size)], end_local.at[ref]))
            remotes.append(pltpu.make_async_remote_copy(final[ref].at[1 - which, pl.ds(0, size)], outs[ref].at[pl.ds(lo, size)],
                                                        end_send.at[which, ref], end_recv.at[which, ref], device_id=sibling, device_id_type=MESH))
        start(locals_ + remotes)
        for copy in locals_:
            copy.wait()
        wait_send(remotes)
        for ref, lo, size in other:
            pltpu.make_async_remote_copy(final[ref].at[which, pl.ds(0, size)], outs[ref].at[pl.ds(lo, size)],
                                         end_send.at[1 - which, ref], end_recv.at[1 - which, ref], device_id=sibling, device_id_type=MESH).wait_recv()
        for j, k in enumerate(steps):
            for col in (chip, first_chip, second_chip, both_chip):
                wait_send(sibling_copies(col, k, other))
            wait_send(send(both_chip, k, far_got, count + k, two_send, two_recv, second))
            wait_send(send(second_chip, k, far_got, k, two_send, two_recv, second))
            wait_send(send(first_chip, k, near_got, k, one_send, one_recv, first))
            if j < count - 1:
                wait_send(send(chip, k, z_got, j, z_send, z_recv, (dp, k)))

    pl.when(core == 0)(lambda: role(0, 4, 2))
    pl.when(core == 1)(lambda: role(1, 2, 4))
    swap.wait()


def scatter_all(g_in, g_rest, up, down, cut, collective_id):
    count = g_in.shape[2]
    rows_in, rows_rest = g_in.shape[3], g_rest.shape[3]
    parts = (((0, 0, cut),), ((0, cut, rows_in - cut), (1, 0, rows_rest)))
    sems = lambda *s: pltpu.SemaphoreType.DMA(s)
    places = 4 * count

    def bufs(k, kind=BF):
        lead = (k, 2) if k else (2,)
        return [pltpu.VMEM(lead + (max(cut, rows_in - cut), g_in.shape[4]), kind), pltpu.VMEM(lead + (rows_rest, g_rest.shape[4]), kind)]

    return pl.pallas_call(
        functools.partial(scatter_kernel, parts, count),
        in_specs=[pl.BlockSpec(memory_space=pl.ANY)] * 4,
        out_specs=[pl.BlockSpec(memory_space=pl.ANY)] * 4,
        out_shape=[jax.ShapeDtypeStruct(g_in.shape[3:], F32), jax.ShapeDtypeStruct(g_rest.shape[3:], F32), jax.ShapeDtypeStruct(up.shape, up.dtype), jax.ShapeDtypeStruct(down.shape, down.dtype)],
        scratch_shapes=bufs(places) + bufs(places) + bufs(2 * count) + bufs(count) + bufs(count - 1) + bufs(0, F32)
        + [sems(places, 2), sems(places, 2), sems(places, 2), sems(2 * count, 2), sems(2 * count, 2), sems(count, 2), sems(count, 2),
           sems(count - 1, 2), sems(count - 1, 2), sems(2, 2), sems(2, 2), sems(2), sems(2), sems(2, count - 1), sems(2, count - 1)],
        compiler_params=pltpu.CompilerParams(collective_id=collective_id, has_side_effects=True, vmem_limit_bytes=VM),
        cost_estimate=pl.CostEstimate(flops=0, bytes_accessed=200_000_000, transcendentals=0),
        name="scatter_all",
    )(g_in, g_rest, up, down)


def unpack_kernel(own, width_b, pack_ref, low_ref, high_ref, small_ref, tall):
    blocks = pack_ref.shape[0]
    for b in range(blocks):
        block = pack_ref[b].astype(F32)
        tall[b * own : (b + 1) * own, :] = block[:own]
        small_ref[b : b + 1, :] = block[own : own + 1]
    for j in range(tall.shape[0] // 128):
        turned = tall[j * 128 : (j + 1) * 128, :].T
        low_ref[:, j * 128 : (j + 1) * 128] = turned[:width_b].astype(BF)
        high_ref[:, j * 128 : (j + 1) * 128] = turned[width_b:]


def unpack(pack, own, width_b):
    blocks, _, cols = pack.shape
    chans = blocks * own
    if own % 8:
        turned = pack[:, :own].reshape(chans, cols).T
        return turned[:width_b], turned[width_b:].astype(F32), pack[:, own].astype(F32)
    return pl.pallas_call(
        functools.partial(unpack_kernel, own, width_b),
        out_shape=[jax.ShapeDtypeStruct((width_b, chans), BF), jax.ShapeDtypeStruct((cols - width_b, chans), F32), jax.ShapeDtypeStruct((blocks, cols), F32)],
        scratch_shapes=[pltpu.VMEM((chans, cols), F32)],
        compiler_params=pltpu.CompilerParams(vmem_limit_bytes=VM),
        name="unpack_small",
    )(pack)


def pack_kernel(own, x_ref, dt_ref, log_ref, misc_ref, small_ref, out_ref, wide, tall):
    at = 0
    for ref in (x_ref, dt_ref, log_ref, misc_ref):
        wide[at : at + ref.shape[0], :] = ref[...]
        at += ref.shape[0]
    wide[at:, :] = jnp.zeros((wide.shape[0] - at, wide.shape[1]), F32)
    for j in range(tall.shape[0] // 128):
        tall[j * 128 : (j + 1) * 128, :] = wide[:, j * 128 : (j + 1) * 128].T
    cols = wide.shape[0]
    first = lax.broadcasted_iota(jnp.int32, (8, cols), 0) == 0
    for b in range(out_ref.shape[0]):
        tail = jnp.where(first, jnp.broadcast_to(small_ref[b : b + 1, :], (8, cols)), 0.0)
        out_ref[b] = jnp.concatenate([tall[b * own : (b + 1) * own, :], tail], axis=0).astype(BF)


def pack_grads(x_t, dt_t, log_t, misc, small, own):
    blocks, cols = small.shape
    chans = x_t.shape[1]
    rows = own + -own % 16
    if own % 8:
        turned = jnp.concatenate([x_t, dt_t, log_t, misc]).T.reshape(blocks, own, -1)
        turned = jnp.pad(turned, ((0, 0), (0, 0), (0, cols - turned.shape[2])))
        return jnp.concatenate([turned, small[:, None], jnp.zeros((blocks, rows - own - 1, cols), F32)], axis=1).astype(BF)
    return pl.pallas_call(
        functools.partial(pack_kernel, own),
        out_shape=jax.ShapeDtypeStruct((blocks, rows, cols), BF),
        scratch_shapes=[pltpu.VMEM((cols, chans), F32), pltpu.VMEM((chans, cols), F32)],
        compiler_params=pltpu.CompilerParams(vmem_limit_bytes=VM),
        name="pack_small",
    )(x_t, dt_t, log_t, misc, small)


def finish_kernel(own, cuts, pack_ref, up_ref, down_ref, up_out, down_out, row_out, *col_outs):
    piece, width = up_ref.shape[1:]
    filler = -piece % 128

    down_out[0] = down_ref[0].astype(F32)
    tall = up_ref[0].astype(F32)
    if filler:
        tall = jnp.concatenate([tall, jnp.zeros((filler, width), F32)], axis=0)
    for j in range(width // 128):
        up_out[0, j * 128 : (j + 1) * 128, :] = tall[:, j * 128 : (j + 1) * 128].T[:, :piece]

    @pl.when(pl.program_id(0) == 0)
    def _():
        row_out[...] = pack_ref[own : own + 1, :]
        for (lo, size), out in zip(cuts, col_outs):
            out[...] = pack_ref[0:own, lo : lo + size]


def finish(pack, up, down, own, cuts):
    experts, piece, width = up.shape
    if own % 8:
        return [jnp.swapaxes(up.astype(F32), 1, 2), down.astype(F32), pack[own : own + 1]] + [pack[:own, lo : lo + size] for lo, size in cuts]
    whole = lambda shape: pl.BlockSpec(shape, lambda e: (0,) * len(shape))
    part = lambda shape: pl.BlockSpec((1,) + shape[1:], lambda e: (e, 0, 0))
    shapes = [(experts, width, piece), (experts, piece, width), (1, pack.shape[1])] + [(own, size) for _, size in cuts]
    return pl.pallas_call(
        functools.partial(finish_kernel, own, cuts),
        grid=(experts,),
        in_specs=[whole(pack.shape), part(up.shape), part(down.shape)],
        out_specs=[part(shapes[0]), part(shapes[1])] + [whole(s) for s in shapes[2:]],
        out_shape=[jax.ShapeDtypeStruct(s, F32) for s in shapes],
        compiler_params=pltpu.CompilerParams(vmem_limit_bytes=VM),
        name="finish",
    )(pack, up, down)


def chain_kernel(step, pieces, carry_ref, own_ref, out_ref, inbox, outbox, send, recv):
    dp, z = lax.axis_index("dp"), lax.axis_index("seq")
    last = lax.axis_size("seq") - 1
    has_before = z > 0 if step > 0 else z < last
    has_after = z < last if step > 0 else z > 0
    barrier = pltpu.get_barrier_semaphore()

    def neighbours(act):
        pl.when(has_before)(lambda: act(z - step))
        pl.when(has_after)(lambda: act(z + step))

    neighbours(lambda peer: pl.semaphore_signal(barrier, inc=1, device_id=(dp, peer), device_id_type=MESH))
    count = last + 1
    pl.semaphore_wait(barrier, (z + last) // count + (2 * last - z) // count)
    wide = own_ref.shape[1] // pieces

    def copy(g):
        return pltpu.make_async_remote_copy(outbox.at[g], inbox.at[g], send.at[g], recv.at[g], device_id=(dp, z + step), device_id_type=MESH)

    def back(g):
        return pltpu.make_async_remote_copy(outbox.at[g], inbox.at[g], send.at[g], recv.at[g], device_id=(dp, z - step), device_id_type=MESH)

    for g in range(pieces):
        c = slice(g * wide, (g + 1) * wide)

        @pl.when(has_before)
        def _():
            back(g).wait_recv()
            out_ref[:, c] = inbox[g].astype(F32)

        @pl.when(jnp.logical_not(has_before))
        def _():
            out_ref[:, c] = jnp.zeros((out_ref.shape[0], wide), F32)

        @pl.when(has_after)
        def _():
            outbox[g] = (carry_ref[:, c] * out_ref[:, c] + own_ref[:, c]).astype(BF)
            copy(g).start()

    @pl.when(has_after)
    def _():
        for g in range(pieces):
            copy(g).wait_send()


def chain(carry, own, step, collective_id):
    pieces = 3
    n, chans = own.shape
    return pl.pallas_call(
        functools.partial(chain_kernel, step, pieces),
        in_specs=[pl.BlockSpec(memory_space=pltpu.VMEM)] * 2,
        out_specs=pl.BlockSpec(memory_space=pltpu.VMEM),
        out_shape=jax.ShapeDtypeStruct((n, chans), F32),
        scratch_shapes=[pltpu.VMEM((pieces, n, chans // pieces), BF)] * 2 + [pltpu.SemaphoreType.DMA((pieces,))] * 2,
        compiler_params=pltpu.CompilerParams(collective_id=collective_id, has_side_effects=True),
        name="chain",
    )(carry, own)


def dot(a, b):
    return jnp.dot(a, b, preferred_element_type=F32)


def dot_nt(a, b):
    return lax.dot_general(a, b, NT, preferred_element_type=F32)


def dot_tn(a, b):
    return lax.dot_general(a, b, TN, preferred_element_type=F32)


def shift(value, axis, steps):
    count = lax.axis_size(axis)
    first, last = (max(0, -steps), min(count, count - steps))
    return lax.ppermute(value, axis, [(source, source + steps) for source in range(first, last)])


def rms_scale(value):
    return lax.rsqrt(jnp.mean(value * value, axis=-1, keepdims=True) + EPS)


def rms_back(value, gain, grad):
    scale = rms_scale(value)
    scaled = grad * gain
    grad_gain = jnp.sum(grad * (value * scale), axis=0)
    return scale * scaled - value * (scale * scale * scale) * jnp.mean(value * scaled, axis=-1, keepdims=True), grad_gain


def swap(value):
    return lax.all_to_all(value, "seq", 0, 0)


def shards(tokens, segment_ids, routes, cotangent, small_params, w_in, conv_w, conv_b, w_x, w_dt, dt_bias, a_log, d_skip, w_out, w_up, w_down):
    both = ("dp", "seq")
    devices = lax.axis_size(both)
    width = tokens.shape[2]
    rows = tokens.shape[1]
    experts = w_up.shape[0]
    chans = w_in.shape[0] * devices // 2
    own = w_out.shape[0]
    rank = w_dt.shape[1]
    n = a_log.shape[1]
    taps = conv_w.shape[1]
    slots = rows // 2
    halo = 16
    wide = 768

    tok_b = tokens[0]
    seg_plus = segment_ids[0] + 1

    columns = (w_x, w_dt, a_log, conv_w, conv_b[:, None], dt_bias[:, None], d_skip[:, None])
    packed = jnp.concatenate(columns, axis=1)
    share = small_params.shape[0]
    packed = jnp.pad(packed, ((0, -own % 16), (0, 256 - packed.shape[1])))
    packed = packed + jnp.pad(small_params[None], ((own, -own % 16 - 1), (0, 256 - share)))
    direct = lax.axis_size("dp") == 8 and lax.axis_size("seq") == 4
    up_t = jnp.swapaxes(w_up, 1, 2)
    full_out = lax.all_gather(w_out, both, axis=0, tiled=True)
    if direct:
        last_ids = jnp.broadcast_to(seg_plus[rows - halo :, None], (halo, 128))
        all_in, all_pack, part_up, part_down, rim_tok, rim_ids = gather_all(w_in, packed, up_t, w_down, tok_b, last_ids, 80, 4)
        rim_ids = jnp.where(lax.axis_index("seq") > 0, rim_ids[:, 0], 0)
    else:
        all_in, all_pack = lax.all_gather(w_in, both), lax.all_gather(packed, both)
        part_up, part_down = swap(up_t), swap(w_down)
        rim_tok = shift(tok_b[rows - halo :], "seq", 1)
        rim_ids = shift(seg_plus[rows - halo :], "seq", 1)
    full_in = all_in.reshape(2 * chans, width)
    low_t, high_t, small = unpack(all_pack.reshape(devices, -1, 256), own, rank + w_x.shape[1])
    full_up = lax.all_gather(part_up, "dp", axis=0).reshape(-1, width)
    full_down = lax.all_gather(part_down, "dp", axis=0).reshape(-1, width)
    xcols = w_x.shape[1]
    full_x_t, full_dt_t = low_t[:xcols], low_t[xcols:]
    alog_t, conv_f, bias_row, dtb_row, skip = high_t[:n], high_t[n : n + taps], high_t[n + taps : n + taps + 1], high_t[n + taps + 1 : n + taps + 2], high_t[n + taps + 2 : n + taps + 3]
    flat_small = small[:, :share].reshape(-1)
    gain_one = flat_small[:width]
    gain_two = flat_small[width : 2 * width]
    router = flat_small[2 * width :].reshape(width, experts).astype(BF)
    route_ids = routes[0]
    onehot = (route_ids == jnp.arange(experts)[None, :]).astype(BF)
    before = (jnp.arange(rows)[:, None] > jnp.arange(rows)[None, :]).astype(BF)
    place = jnp.sum(dot(before, onehot) * onehot.astype(F32), axis=1).astype(jnp.int32)
    slot_of = route_ids[:, 0] * slots + place
    gather_mat = (slot_of[:, None] == jnp.arange(experts * slots)[None, :]).astype(BF)
    grad_out_b = cotangent[0]
    grad_out = grad_out_b.astype(F32)
    go_local, full_in = lax.optimization_barrier((dot_tn(gather_mat, grad_out_b).astype(BF), full_in))
    go_slots = swap(go_local.reshape(experts, slots, width)).reshape(-1, width)

    tok_ext = jnp.concatenate([rim_tok, tok_b]).astype(F32)
    tok_f = tok_b.astype(F32)
    ids_ext = jnp.concatenate([rim_ids, seg_plus])
    same = jnp.stack([ids_ext[halo - taps + 1 + k : halo - taps + 1 + k + rows] == seg_plus for k in range(taps)], axis=1).astype(F32)
    keep = same[:, taps - 2 : taps - 1]
    normed_ext = (tok_ext * rms_scale(tok_ext) * gain_one).astype(BF)
    normed = normed_ext[halo:]
    conv_in = dot_nt(normed_ext, full_in[:chans]).astype(BF).astype(F32)
    z = dot_nt(normed, full_in[chans:])
    conv_sum = bias_row
    for k in range(taps):
        lo = halo - taps + 1 + k
        conv_sum = conv_sum + conv_f[k : k + 1] * conv_in[lo : lo + rows] * same[:, k : k + 1]
    values = conv_sum * jax.nn.sigmoid(conv_sum)
    values_b = values.astype(BF)
    projected = dot_nt(values_b, full_x_t)
    low_rank = projected[:, :rank].astype(BF)
    b_rows = projected[:, rank : rank + n]
    c_rows = projected[:, rank + n :]
    pre_dt = dot(low_rank, full_dt_t) + dtb_row
    dt = jax.nn.softplus(pre_dt)
    dt_keep = jnp.where(keep > 0, dt, 1e30)
    dtx, go_slots = lax.optimization_barrier((dt * values, go_slots))
    rates = -jnp.exp(alog_t)
    rates2 = rates * math.log2(math.e)
    b_wide = jnp.broadcast_to(b_rows[:, :, None], (rows, n, 128)).reshape(rows * n, 128)
    c_wide = jnp.broadcast_to(c_rows[:, :, None], (rows, n, 128)).reshape(rows * n, 128)
    own_state, carry = state_pass(dt_keep, dtx, rates2, b_wide, wide)
    start = chain(carry, own_state, 1, 3)
    scanned, checks = scan_pass(dt_keep, dtx, rates2, b_wide, block_diag(c_rows).astype(BF), start, wide)
    sig_z = jax.nn.sigmoid(z)
    gated = ((scanned + skip * values) * (z * sig_z)).astype(BF)
    first_sum = tok_f + dot(gated, full_out)
    normed_two = (first_sum * rms_scale(first_sum) * gain_two).astype(BF)

    n2_slots = swap(dot_tn(gather_mat, normed_two).astype(BF).reshape(experts, slots, width)).reshape(-1, width)
    probs = jax.nn.softmax(dot(n2_slots, router), axis=-1)
    mine = (jnp.arange(experts) == lax.axis_index("seq")).astype(F32)[None]
    gate = jnp.sum(probs * mine, axis=1, keepdims=True)
    ge_slots = (gate * go_slots.astype(F32)).astype(BF)
    expert_out, grad_disp, grad_up, grad_down = expert_pass(n2_slots, ge_slots, full_up, full_down, 768)
    grad_gate = jnp.sum(go_slots.astype(F32) * expert_out, axis=1, keepdims=True)
    grad_logits = (grad_gate * gate * (mine - probs)).astype(BF)
    grad_router = dot_tn(n2_slots, grad_logits)
    grad_n2_slots = (grad_disp + dot_nt(grad_logits, router)).astype(BF)
    grad_n2 = dot(gather_mat, swap(grad_n2_slots.reshape(experts, slots, width)).reshape(-1, width))
    mixed_slots = swap((gate * expert_out).astype(BF).reshape(experts, slots, width)).reshape(-1, width)
    mixed_out = (first_sum + dot(gather_mat, mixed_slots)).astype(BF)
    part_gup = lax.psum_scatter(grad_up, "dp", scatter_dimension=0, tiled=True).reshape(experts, -1, width)
    part_gdown = lax.psum_scatter(grad_down, "dp", scatter_dimension=0, tiled=True).reshape(experts, -1, width)

    grad_norm_two, grad_gain_two = rms_back(first_sum, gain_two, grad_n2)
    grad_first = grad_out + grad_norm_two
    grad_mixer = grad_first.astype(BF)
    grad_w_out = dot_tn(gated, grad_mixer)
    grad_gated = dot_nt(grad_mixer, full_out)
    silu_z = z * sig_z
    grad_scanned = grad_gated * silu_z
    grad_z = grad_gated * (scanned + skip * values) * (sig_z * (1.0 + z * (1.0 - sig_z)))
    grad_z_b = grad_z.astype(BF)
    grad_skip = jnp.sum(grad_scanned * values, axis=0)
    grad_start = back_state_pass(dt_keep, grad_scanned, rates2, c_wide, wide)
    nxt = chain(carry, grad_start, -1, 4)
    ones_blk = block_diag(jnp.ones((STEP, n), F32)).astype(BF)
    g_dtx, g_dt, g_log, gb_full, gc_full = back_pass(
        dt, dt_keep, dtx, grad_scanned, rates2, rates, b_wide, c_wide, block_diag(b_rows).astype(BF), ones_blk, checks, nxt, wide
    )
    grad_dt = g_dt + g_dtx * values
    grad_pre_f = grad_dt * jax.nn.sigmoid(pre_dt)
    grad_dtb = jnp.sum(grad_pre_f, axis=0)
    grad_pre = grad_pre_f.astype(BF)
    grad_dt_t = dot_tn(low_rank, grad_pre)
    grad_proj = jnp.concatenate([dot_nt(grad_pre, full_dt_t), block_undiag(gb_full, n), block_undiag(gc_full, n)], axis=1).astype(BF)
    grad_x_t = dot_tn(grad_proj, values_b)
    grad_values = grad_scanned * skip + g_dtx * dt + dot(grad_proj, full_x_t)
    sig_c = jax.nn.sigmoid(conv_sum)
    grad_conv_sum = grad_values * (sig_c * (1.0 + conv_sum * (1.0 - sig_c)))
    grad_bias = jnp.sum(grad_conv_sum, axis=0)
    grad_taps = []
    grad_ext = None
    for k in range(taps):
        lo = halo - taps + 1 + k
        masked = grad_conv_sum * same[:, k : k + 1]
        grad_taps.append(jnp.sum(masked * conv_in[lo : lo + rows], axis=0))
        term = jnp.pad(masked * conv_f[k : k + 1], ((lo, halo - lo), (0, 0)))
        grad_ext = term if grad_ext is None else grad_ext + term
    rim_back = shift(grad_ext[halo - 8 : halo], "seq", -1)
    grad_conv_in = (grad_ext[halo:] + jnp.pad(rim_back, ((rows - 8, 0), (0, 0)))).astype(BF)
    grad_w_in = dot_tn(jnp.concatenate([grad_conv_in, grad_z_b], axis=1), normed).astype(BF)
    grad_normed = dot(grad_conv_in, full_in[:chans]) + dot(grad_z_b, full_in[chans:])
    grad_norm_one, grad_gain_one = rms_back(tok_f, gain_one, grad_normed)
    tokens_grad = (grad_first + grad_norm_one).astype(BF)

    grad_small = jnp.concatenate([grad_gain_one, grad_gain_two, grad_router.reshape(-1)])
    misc = jnp.stack(grad_taps + [grad_bias, grad_dtb, grad_skip, jnp.zeros_like(grad_bias)])
    grad_packed = pack_grads(grad_x_t, grad_dt_t, g_log, misc, jnp.pad(grad_small.reshape(devices, -1), ((0, 0), (0, 256 - share))), own)
    if direct:
        sum_in, sum_pack, sum_up, sum_down = scatter_all(
            grad_w_in.reshape(4, 2, 4, 2 * own, width), grad_packed.reshape((4, 2, 4) + grad_packed.shape[1:]), part_gup, part_gdown, 80, 2
        )
    else:
        sum_in = lax.psum_scatter(grad_w_in, both, scatter_dimension=0, tiled=True).astype(F32)
        sum_pack = lax.psum_scatter(grad_packed, both, scatter_dimension=0, tiled=True)[0].astype(F32)
        sum_up, sum_down = swap(part_gup), swap(part_gdown)
    grad_w_out = lax.optimization_barrier((grad_w_out.astype(BF), part_gup, part_gdown))[0]
    sum_out = lax.psum_scatter(grad_w_out, both, scatter_dimension=0, tiled=True).astype(F32)
    cuts, at = [], 0
    for column in columns:
        cuts.append((at, column.shape[1]))
        at += column.shape[1]
    up_out, down_out, s_row, s_x, s_dt, s_log, s_conv, s_bias, s_dtb, s_skip = finish(sum_pack, sum_up, sum_down, own, tuple(cuts))
    return (
        mixed_out[None],
        tokens_grad[None],
        s_row[0, :share],
        sum_in,
        s_conv,
        s_bias[:, 0],
        s_x,
        s_dt,
        s_dtb[:, 0],
        s_log,
        s_skip[:, 0],
        sum_out,
        up_out,
        down_out,
    )


def solution(mesh):
    split = ("dp", "seq")
    token, row, mat, vec = P("dp", "seq", None), P("dp", "seq"), P(split, None), P(split)
    return jax.shard_map(
        shards,
        mesh=mesh,
        in_specs=(token, row, token, token, vec, mat, mat, vec, mat, mat, vec, mat, vec, mat, P(None, None, split), P(None, split, None)),
        out_specs=(token, token, vec, mat, mat, vec, mat, mat, vec, mat, vec, mat, P(None, None, split), P(None, split, None)),
        check_vma=False,
    )
```

```python
import functools
import math

import jax
import jax.numpy as jnp
from jax import lax
from jax.experimental import pallas as pl
from jax.experimental.pallas import tpu as pltpu
from jax.sharding import PartitionSpec as P

F32, BF = jnp.float32, jnp.bfloat16
EPS = 1e-05
STEP = 16
VM = 56 * 1024 * 1024
MESH = pl.DeviceIdType.MESH
NT = (((1,), (1,)), ((), ()))
TN = (((0,), (0,)), ((), ()))


def rowb(block, i, n):
    return jnp.broadcast_to(block[i:i+1, :], (n, block.shape[1]))

def state_kernel(n, dte_ref, dtx_ref, rate_ref, b_ref, state_ref, carry_ref):
    rows, wide = dte_ref.shape
    tiles = wide // 128
    rates = [rate_ref[:, j*128:(j+1)*128] for j in range(tiles)]
    def block(k, carry):
        state, total = carry
        at = pl.multiple_of(k * STEP, STEP)
        dte = dte_ref[pl.ds(at, STEP), :]
        dtx = dtx_ref[pl.ds(at, STEP), :]
        state = list(state)
        for i in range(STEP):
            bs = b_ref[pl.ds((at + i) * n, n), :]
            for j in range(tiles):
                c = slice(j*128, (j+1)*128)
                decay = jnp.exp2(rowb(dte[:, c], i, n) * rates[j])
                state[j] = decay * state[j] + bs * rowb(dtx[:, c], i, n)
        return tuple(state), total + dte
    zero = tuple(jnp.zeros((n, 128), F32) for _ in range(tiles))
    state, total = lax.fori_loop(0, rows // STEP, block, (zero, jnp.zeros((STEP, wide), F32)))
    summed = jnp.sum(total, axis=0, keepdims=True)
    for j in range(tiles):
        c = slice(j*128, (j+1)*128)
        state_ref[:, c] = state[j]
        carry_ref[:, c] = jnp.exp2(jnp.broadcast_to(summed[:, c], (n, 128)) * rates[j])

def state_pass(dte, dtx, rates2, b_wide, wide):
    rows, chans = dte.shape
    n = rates2.shape[0]
    return pl.pallas_call(
        functools.partial(state_kernel, n),
        grid=(chans // wide,),
        in_specs=[pl.BlockSpec((rows, wide), lambda g: (0, g)),
                  pl.BlockSpec((rows, wide), lambda g: (0, g)),
                  pl.BlockSpec((n, wide), lambda g: (0, g)),
                  pl.BlockSpec(b_wide.shape, lambda g: (0, 0))],
        out_specs=[pl.BlockSpec((n, wide), lambda g: (0, g))] * 2,
        out_shape=[jax.ShapeDtypeStruct((n, chans), F32)] * 2,
        compiler_params=pltpu.CompilerParams(vmem_limit_bytes=VM),
        cost_estimate=pl.CostEstimate(flops=8*rows*chans*n, bytes_accessed=8*rows*chans, transcendentals=rows*chans*n),
    )(dte, dtx, rates2, b_wide)

def scan_kernel(n, dte_ref, dtx_ref, rate_ref, b_ref, cblk_ref, start_ref, y_ref, check_ref, hs):
    rows, wide = dte_ref.shape
    tiles = wide // 128
    rates = [rate_ref[:, j*128:(j+1)*128] for j in range(tiles)]
    def block(k, state):
        at = pl.multiple_of(k * STEP, STEP)
        dte = dte_ref[pl.ds(at, STEP), :]
        dtx = dtx_ref[pl.ds(at, STEP), :]
        state = list(state)
        kn = pl.multiple_of(k * n, n)
        for j in range(tiles):
            check_ref[pl.ds(kn, n), j*128:(j+1)*128] = state[j]
        for i in range(STEP):
            bs = b_ref[pl.ds((at + i) * n, n), :]
            for j in range(tiles):
                c = slice(j*128, (j+1)*128)
                decay = jnp.exp2(rowb(dte[:, c], i, n) * rates[j])
                state[j] = decay * state[j] + bs * rowb(dtx[:, c], i, n)
                hs[i*n:(i+1)*n, c] = state[j].astype(BF)
        y_ref[pl.ds(at, STEP), :] = jnp.dot(cblk_ref[pl.ds(at, STEP), :], hs[...], preferred_element_type=F32)
        return tuple(state)
    start = tuple(start_ref[:, j*128:(j+1)*128] for j in range(tiles))
    lax.fori_loop(0, rows // STEP, block, start)

def scan_pass(dte, dtx, rates2, b_wide, c_blk, start, wide):
    rows, chans = dte.shape
    n = rates2.shape[0]
    return pl.pallas_call(
        functools.partial(scan_kernel, n),
        grid=(chans // wide,),
        in_specs=[pl.BlockSpec((rows, wide), lambda g: (0, g)),
                  pl.BlockSpec((rows, wide), lambda g: (0, g)),
                  pl.BlockSpec((n, wide), lambda g: (0, g)),
                  pl.BlockSpec(b_wide.shape, lambda g: (0, 0)),
                  pl.BlockSpec(c_blk.shape, lambda g: (0, 0)),
                  pl.BlockSpec((n, wide), lambda g: (0, g))],
        out_specs=[pl.BlockSpec((rows, wide), lambda g: (0, g)),
                   pl.BlockSpec((rows // STEP * n, wide), lambda g: (0, g))],
        out_shape=[jax.ShapeDtypeStruct((rows, chans), F32),
                   jax.ShapeDtypeStruct((rows // STEP * n, chans), F32)],
        scratch_shapes=[pltpu.VMEM((STEP * n, wide), BF)],
        compiler_params=pltpu.CompilerParams(vmem_limit_bytes=VM),
        cost_estimate=pl.CostEstimate(flops=10*rows*chans*n, bytes_accessed=12*rows*chans, transcendentals=rows*chans*n),
    )(dte, dtx, rates2, b_wide, c_blk, start)

def back_state_kernel(n, dte_ref, gs_ref, rate_ref, c_ref, out_ref):
    rows, wide = dte_ref.shape
    tiles = wide // 128
    rates = [rate_ref[:, j*128:(j+1)*128] for j in range(tiles)]
    def block(k, state):
        at = pl.multiple_of(rows - STEP - k * STEP, STEP)
        dte = dte_ref[pl.ds(at, STEP), :]
        gs = gs_ref[pl.ds(at, STEP), :]
        state = list(state)
        for i in reversed(range(STEP)):
            cs = c_ref[pl.ds((at + i) * n, n), :]
            for j in range(tiles):
                c = slice(j*128, (j+1)*128)
                decay = jnp.exp2(rowb(dte[:, c], i, n) * rates[j])
                state[j] = decay * (state[j] + cs * rowb(gs[:, c], i, n))
        return tuple(state)
    zero = tuple(jnp.zeros((n, 128), F32) for _ in range(tiles))
    state = lax.fori_loop(0, rows // STEP, block, zero)
    for j in range(tiles):
        out_ref[:, j*128:(j+1)*128] = state[j]

def back_state_pass(dte, gs, rates2, c_wide, wide):
    rows, chans = dte.shape
    n = rates2.shape[0]
    return pl.pallas_call(
        functools.partial(back_state_kernel, n),
        grid=(chans // wide,),
        in_specs=[pl.BlockSpec((rows, wide), lambda g: (0, g)),
                  pl.BlockSpec((rows, wide), lambda g: (0, g)),
                  pl.BlockSpec((n, wide), lambda g: (0, g)),
                  pl.BlockSpec(c_wide.shape, lambda g: (0, 0))],
        out_specs=pl.BlockSpec((n, wide), lambda g: (0, g)),
        out_shape=jax.ShapeDtypeStruct((n, chans), F32),
        compiler_params=pltpu.CompilerParams(vmem_limit_bytes=VM),
        cost_estimate=pl.CostEstimate(flops=8*rows*chans*n, bytes_accessed=8*rows*chans, transcendentals=rows*chans*n),
    )(dte, gs, rates2, c_wide)

def back_kernel(n, dt_ref, dte_ref, dtx_ref, gs_ref, rate_ref, rawrate_ref, b_ref, c_ref, bblk_ref, oblk_ref, check_ref, next_ref,
                gdtx_ref, gdt_ref, glog_ref, gb_ref, gc_ref, us, decs, hs, ls, ps):
    rows, wide = dte_ref.shape
    tiles = wide // 128
    rates = [rate_ref[:, j*128:(j+1)*128] for j in range(tiles)]
    @pl.when(pl.program_id(0) == 0)
    def _():
        gb_ref[...] = jnp.zeros_like(gb_ref)
        gc_ref[...] = jnp.zeros_like(gc_ref)
    glog_ref[...] = jnp.zeros_like(glog_ref)
    def block(k, later):
        kk = rows // STEP - 1 - k
        at = pl.multiple_of(kk * STEP, STEP)
        kn = pl.multiple_of(kk * n, n)
        dte = dte_ref[pl.ds(at, STEP), :]
        dtx = dtx_ref[pl.ds(at, STEP), :]
        state = [check_ref[pl.ds(kn, n), j*128:(j+1)*128] for j in range(tiles)]
        for i in range(STEP):
            bs = b_ref[pl.ds((at + i) * n, n), :]
            for j in range(tiles):
                c = slice(j*128, (j+1)*128)
                decay = jnp.exp2(rowb(dte[:, c], i, n) * rates[j])
                kept = decay * state[j]
                state[j] = kept + bs * rowb(dtx[:, c], i, n)
                decs[i*n:(i+1)*n, c] = decay
                us[i*n:(i+1)*n, c] = kept
                hs[i*n:(i+1)*n, c] = state[j].astype(BF)
        later = list(later)
        dt = dt_ref[pl.ds(at, STEP), :]
        gs = gs_ref[pl.ds(at, STEP), :]
        logs = [glog_ref[:, j*128:(j+1)*128] for j in range(tiles)]
        for i in reversed(range(STEP)):
            cs = c_ref[pl.ds((at + i) * n, n), :]
            for j in range(tiles):
                c = slice(j*128, (j+1)*128)
                adj = later[j] + cs * rowb(gs[:, c], i, n)
                part = adj * us[i*n:(i+1)*n, c] * rawrate_ref[:, c]
                later[j] = adj * decs[i*n:(i+1)*n, c]
                logs[j] = logs[j] + part * rowb(dt[:, c], i, n)
                ls[i*n:(i+1)*n, c] = adj.astype(BF)
                ps[i*n:(i+1)*n, c] = part.astype(BF)
        for j in range(tiles):
            glog_ref[:, j*128:(j+1)*128] = logs[j]
        gdtx_ref[pl.ds(at, STEP), :] = jnp.dot(bblk_ref[pl.ds(at, STEP), :], ls[...], preferred_element_type=F32)
        gdt_ref[pl.ds(at, STEP), :] = jnp.dot(oblk_ref[...], ps[...], preferred_element_type=F32)
        nt = (((1,), (1,)), ((), ()))
        gb_ref[pl.ds(at, STEP), :] += lax.dot_general(dtx.astype(BF), ls[...], nt, preferred_element_type=F32)
        gc_ref[pl.ds(at, STEP), :] += lax.dot_general(gs.astype(BF), hs[...], nt, preferred_element_type=F32)
        return tuple(later)
    start = tuple(next_ref[:, j*128:(j+1)*128] for j in range(tiles))
    lax.fori_loop(0, rows // STEP, block, start)

def back_pass(dt, dte, dtx, gs, rates2, rates, b_wide, c_wide, b_blk, o_blk, check, nxt, wide):
    rows, chans = dte.shape
    n = rates2.shape[0]
    col = lambda r: pl.BlockSpec((r, wide), lambda g: (0, g))
    whole = lambda a: pl.BlockSpec(a.shape, lambda g: (0, 0))
    return pl.pallas_call(
        functools.partial(back_kernel, n),
        grid=(chans // wide,),
        in_specs=[col(rows)] * 4 + [col(n)] * 2 + [whole(b_wide), whole(c_wide), whole(b_blk), whole(o_blk), col(rows // STEP * n), col(n)],
        out_specs=[col(rows), col(rows), col(n), pl.BlockSpec((rows, STEP * n), lambda g: (0, 0)), pl.BlockSpec((rows, STEP * n), lambda g: (0, 0))],
        out_shape=[jax.ShapeDtypeStruct((rows, chans), F32)] * 2 + [jax.ShapeDtypeStruct((n, chans), F32)] + [jax.ShapeDtypeStruct((rows, STEP * n), F32)] * 2,
        scratch_shapes=[pltpu.VMEM((STEP * n, wide), F32)] * 2 + [pltpu.VMEM((STEP * n, wide), BF)] * 3,
        compiler_params=pltpu.CompilerParams(vmem_limit_bytes=VM),
        cost_estimate=pl.CostEstimate(flops=26*rows*chans*n, bytes_accessed=24*rows*chans, transcendentals=rows*chans*n),
    )(dt, dte, dtx, gs, rates2, rates, b_wide, c_wide, b_blk, o_blk, check, nxt)

def block_diag(vals):
    rows, n = vals.shape
    same = (jnp.arange(rows)[:, None] % STEP) == (jnp.arange(STEP * n)[None, :] // n)
    return jnp.where(same, jnp.tile(vals, (1, STEP)), 0)

def block_undiag(full, n):
    rows = full.shape[0]
    same = (jnp.arange(rows)[:, None] % STEP) == (jnp.arange(STEP * n)[None, :] // n)
    return jnp.sum(jnp.where(same, full, 0).reshape(rows, STEP, n), axis=1)


def flip(value, bit):
    return value + bit - 2 * bit * (lax.rem(value // bit, 2))


def greet(partners):
    barrier = pltpu.get_barrier_semaphore()
    for partner in partners:
        pl.semaphore_signal(barrier, inc=1, device_id=partner, device_id_type=MESH)
    pl.semaphore_wait(barrier, len(partners))


class ZSwap:
    def __init__(self, pairs, local, send, recv, count):
        self.pairs, self.local, self.send, self.recv, self.count = pairs, local, send, recv, count

    def own(self):
        z = lax.axis_index("seq")
        return [pltpu.make_async_copy(src.at[z], dst.at[z], self.local.at[i]) for i, (src, dst) in enumerate(self.pairs)]

    def out(self):
        dp, z = lax.axis_index("dp"), lax.axis_index("seq")
        made = []
        for j in range(1, self.count):
            peer = lax.rem(z + j, self.count)
            for i, (src, dst) in enumerate(self.pairs):
                made.append(pltpu.make_async_remote_copy(src.at[peer], dst.at[z], self.send.at[i, j - 1], self.recv.at[i, j - 1], device_id=(dp, peer), device_id_type=MESH))
        return made

    def start(self):
        for copy in self.out() + self.own():
            copy.start()

    def wait(self):
        dp, z = lax.axis_index("dp"), lax.axis_index("seq")
        for copy in self.own():
            copy.wait()
        for copy in self.out():
            copy.wait_send()
        for j in range(1, self.count):
            source = lax.rem(z + self.count - j, self.count)
            for i, (src, dst) in enumerate(self.pairs):
                pltpu.make_async_remote_copy(src.at[z], dst.at[source], self.send.at[i, j - 1], self.recv.at[i, j - 1], device_id=(dp, source), device_id_type=MESH).wait_recv()


def gather_kernel(parts, count, in_ref, rest_ref, up_ref, tok_ref, ids_ref, gin_ref, grest_ref, gup_ref, rim_ref, rimids_ref,
                  local_sem, send, recv, share_send, share_recv, pair_send, pair_recv, swap_local, swap_send, swap_recv, rim_send, rim_recv):
    dp, z = lax.axis_index("dp"), lax.axis_index("seq")
    chip, core = dp // 2, lax.rem(dp, 2)
    srcs, dsts = (in_ref, rest_ref), (gin_ref, grest_ref)
    sibling = (flip(dp, 1), z)
    peers = [lax.rem(z + j, count) for j in range(1, count)]
    greet([sibling, (flip(dp, 4), z), (flip(dp, 2), z)] + [(dp, peer) for peer in peers])

    tail = pl.ds(tok_ref.shape[0] - rim_ref.shape[0], rim_ref.shape[0])
    rims = [pltpu.make_async_remote_copy(src, dst, rim_send.at[i], rim_recv.at[i], device_id=(dp, lax.rem(z + 1, count)), device_id_type=MESH)
            for i, (src, dst) in enumerate(((tok_ref.at[tail], rim_ref), (ids_ref, rimids_ref)))]
    for copy in rims:
        copy.start()
    mine = []
    for i, (src, dst) in enumerate(zip(srcs, dsts)):
        local = pltpu.make_async_copy(src, dst.at[chip, core, z], local_sem.at[i])
        pair = pltpu.make_async_remote_copy(src, dst.at[chip, core, z], pair_send.at[i], pair_recv.at[i], device_id=sibling, device_id_type=MESH)
        local.start()
        pair.start()
        mine += [local, pair]
    for copy in mine:
        copy.wait()
    swap = ZSwap(((up_ref, gup_ref),), swap_local, swap_send, swap_recv, count)

    def role(which, first_bit, second_bit):
        subs = parts[which]
        first, second = (flip(dp, first_bit), z), (flip(dp, second_bit), z)
        first_chip, second_chip = flip(chip, first_bit // 2), flip(chip, second_bit // 2)
        both_chip = flip(first_chip, second_bit // 2)

        def copies(sub, at_chip, at_z, slot, to, send_s, recv_s):
            made = []
            for i, (ref, lo, size) in enumerate(subs[sub]):
                view = dsts[ref].at[at_chip, :, at_z, pl.ds(lo, size)]
                made.append(pltpu.make_async_remote_copy(view, view, send_s.at[sub, slot, i], recv_s.at[sub, slot, i], device_id=to, device_id_type=MESH))
            return made

        def start(made):
            for copy in made:
                copy.start()

        def wait_recv(made):
            for copy in made:
                copy.wait_recv()

        def along_first(sub, k):
            return copies(sub, chip, k, 4 + k, first, send, recv)

        def along_second(sub, k, far):
            return copies(sub, first_chip if far else chip, k, 8 + 4 * far + k, second, send, recv)

        def came_first(sub, k):
            return copies(sub, first_chip, k, 4 + k, first, send, recv)

        def came_second(sub, k, far):
            return copies(sub, both_chip if far else second_chip, k, 8 + 4 * far + k, second, send, recv)

        def share(sub, at_chip, k, offset):
            return copies(sub, at_chip, k, 4 * offset + k, sibling, share_send, share_recv)

        def up(sub, k):
            return copies(sub, chip, k, k + count * 5, (dp, z + 1), send, recv)

        def down(sub, k):
            return copies(sub, chip, k, k, (dp, z - 1), send, recv)

        both = range(len(subs))

        def spread(sub, k):
            start(along_first(sub, k))
            start(along_second(sub, k, 0))

        def rest(k):
            for sub in both:
                wait_recv(came_first(sub, k))
                start(along_second(sub, k, 1))
                start(share(sub, first_chip, k, 1))

        def below(hop, work):
            pl.when(z - hop >= 0)(lambda: work(z - hop))

        def above(hop, work):
            pl.when(z + hop <= count - 1)(lambda: work(z + hop))

        def from_below(k):
            for sub in both:
                wait_recv(up(sub, k))
                pl.when(z < count - 1)(lambda: start(up(sub, k)))
                spread(sub, k)
                start(share(sub, chip, k, 0))

        def from_above(k):
            for sub in both:
                wait_recv(down(sub, k))
                pl.when(z > 0)(lambda: start(down(sub, k)))
                spread(sub, k)
                start(share(sub, chip, k, 0))

        for sub in both:
            pl.when(z > 0)(lambda: start(down(sub, z)))
            pl.when(z < count - 1)(lambda: start(up(sub, z)))
            spread(sub, z)
        for hop in range(1, count):
            below(hop, from_below)
            above(hop, from_above)
            if hop == count - 2:
                swap.start()
            if hop == 1:
                rest(z)
            else:
                below(hop - 1, rest)
                above(hop - 1, rest)
        below(count - 1, rest)
        above(count - 1, rest)

        def finish(k, _):
            for far in (0, 1):
                for sub in both:
                    wait_recv(came_second(sub, k, far))
                    start(share(sub, both_chip if far else second_chip, k, 2 + far))
            return 0

        lax.fori_loop(0, count, finish, 0)

        def drain(k, _):
            def wait_send(made):
                for copy in made:
                    copy.wait_send()

            for sub in both:
                wait_send(along_first(sub, k) + along_second(sub, k, 0) + along_second(sub, k, 1))
                for offset, at_chip in ((1, first_chip), (2, second_chip), (3, both_chip)):
                    wait_send(share(sub, at_chip, k, offset))
                pl.when(k != z)(lambda: wait_send(share(sub, chip, k, 0)))
                pl.when((k <= z) & (z < count - 1))(lambda: wait_send(up(sub, k)))
                pl.when((k >= z) & (z > 0))(lambda: wait_send(down(sub, k)))
            return 0

        lax.fori_loop(0, count, drain, 0)

        def shared(k, _):
            for offset, at_chip in enumerate((chip, second_chip, first_chip, both_chip)):
                def wait():
                    for sub, chunks in enumerate(parts[1 - which]):
                        for i, (ref, lo, size) in enumerate(chunks):
                            view = dsts[ref].at[at_chip, :, k, pl.ds(lo, size)]
                            pltpu.make_async_remote_copy(view, view, share_send.at[sub, 4 * offset + k, i], share_recv.at[sub, 4 * offset + k, i], device_id=sibling, device_id_type=MESH).wait_recv()
                if offset:
                    wait()
                else:
                    pl.when(k != z)(wait)
            return 0

        lax.fori_loop(0, count, shared, 0)

    pl.when(core == 0)(lambda: role(0, 4, 2))
    pl.when(core == 1)(lambda: role(1, 2, 4))
    swap.wait()
    for copy in rims:
        copy.wait()


def gather_all(w_in, rest, up, tok, ids, cut, count):
    parts = ((((0, 0, 48),), ((0, 48, cut - 48),)), (((0, cut, 48),), ((0, cut + 48, w_in.shape[0] - cut - 48), (1, 0, rest.shape[0]))))
    shape = lambda a: jax.ShapeDtypeStruct((4, 2, count) + a.shape, a.dtype)
    sems = lambda *s: pltpu.SemaphoreType.DMA(s)
    return pl.pallas_call(
        functools.partial(gather_kernel, parts, count),
        in_specs=[pl.BlockSpec(memory_space=pl.ANY)] * 5,
        out_specs=[pl.BlockSpec(memory_space=pl.ANY)] * 5,
        out_shape=[shape(w_in), shape(rest), jax.ShapeDtypeStruct(up.shape, up.dtype),
                   jax.ShapeDtypeStruct((16, tok.shape[1]), tok.dtype), jax.ShapeDtypeStruct(ids.shape, ids.dtype)],
        scratch_shapes=[sems(2), sems(2, 24, 2), sems(2, 24, 2), sems(2, 16, 2), sems(2, 16, 2), sems(2), sems(2), sems(1), sems(1, count - 1), sems(1, count - 1), sems(2), sems(2)],
        compiler_params=pltpu.CompilerParams(collective_id=1, has_side_effects=True),
        cost_estimate=pl.CostEstimate(flops=0, bytes_accessed=200_000_000, transcendentals=0),
        name="gather_all",
    )(w_in, rest, up, tok, ids)


def scatter_kernel(parts, count, in_ref, rest_ref, proj_ref, oin_ref, orest_ref, oproj_ref, mine_a, mine_b, sib_a, sib_b, far_a, far_b, near_a, near_b, zgot_a, zgot_b, final_a, final_b,
                   load_sem, sib_send, sib_recv, two_send, two_recv, one_send, one_recv, z_send, z_recv, end_send, end_recv, end_local,
                   swap_local, swap_send, swap_recv):
    dp, z = lax.axis_index("dp"), lax.axis_index("seq")
    chip, core = dp // 2, lax.rem(dp, 2)
    srcs, outs = (in_ref, rest_ref), (oin_ref, orest_ref)
    mine, sib, far_got, near_got, z_got, final = (mine_a, mine_b), (sib_a, sib_b), (far_a, far_b), (near_a, near_b), (zgot_a, zgot_b), (final_a, final_b)
    sibling = (flip(dp, 1), z)
    peers = [(dp, lax.rem(z + j, count)) for j in range(1, count)]
    greet([sibling, (flip(dp, 4), z), (flip(dp, 2), z)] + peers)

    swap = ZSwap(((proj_ref, oproj_ref),), swap_local, swap_send, swap_recv, count)

    def role(which, first_bit, second_bit):
        chunks, other = parts[which], parts[1 - which]
        first, second = (flip(dp, first_bit), z), (flip(dp, second_bit), z)
        first_chip, second_chip = flip(chip, first_bit // 2), flip(chip, second_bit // 2)
        both_chip = flip(first_chip, second_bit // 2)
        steps = [lax.rem(z + 1 + j, count) for j in range(count)]

        def loads(col, k):
            slot = col * count + k
            return [pltpu.make_async_copy(srcs[ref].at[col, :, k, pl.ds(lo, size)], mine[ref].at[slot, :, pl.ds(0, size)], load_sem.at[slot, ref])
                    for ref, lo, size in chunks]

        def sibling_copies(col, k, pieces):
            slot = col * count + k
            return [pltpu.make_async_remote_copy(srcs[ref].at[col, :, k, pl.ds(lo, size)], sib[ref].at[slot, :, pl.ds(0, size)],
                                                 sib_send.at[slot, ref], sib_recv.at[slot, ref], device_id=sibling, device_id_type=MESH)
                    for ref, lo, size in pieces]

        def send(col, k, dst, slot, send_s, recv_s, to):
            return [pltpu.make_async_remote_copy(mine[ref].at[col * count + k, :, pl.ds(0, size)], dst[ref].at[slot, :, pl.ds(0, size)],
                                                 send_s.at[slot, ref], recv_s.at[slot, ref], device_id=to, device_id_type=MESH)
                    for ref, lo, size in chunks]

        def start(copies):
            for copy in copies:
                copy.start()

        def wait_recv(copies):
            for copy in copies:
                copy.wait_recv()

        def wait_send(copies):
            for copy in copies:
                copy.wait_send()

        def add(col, k, terms, last=False):
            slot = col * count + k
            for copy in loads(col, k):
                copy.wait()
            wait_recv(sibling_copies(col, k, chunks))
            for ref, lo, size in chunks:
                def rows(r, _):
                    at = pl.ds(pl.multiple_of(r * 16, 16), 16)
                    for c in range(2):
                        total = mine[ref][slot, c, at, :].astype(F32) + sib[ref][slot, c, at, :].astype(F32)
                        for buf, place in terms:
                            total = total + buf[ref][place, c, at, :].astype(F32)
                        if last:
                            final[ref][c, at, :] = total
                        else:
                            mine[ref][slot, c, at, :] = total.astype(BF)
                    return 0

                lax.fori_loop(0, size // 16, rows, 0)

        for k in steps:
            for col, sib_col in ((both_chip, both_chip), (second_chip, first_chip), (first_chip, second_chip), (chip, chip)):
                start(sibling_copies(sib_col, k, other) + loads(col, k))

        swap.start()

        def stage_one(k):
            for far, col in ((1, both_chip), (0, second_chip)):
                add(col, k, ())
                start(send(col, k, far_got, far * count + k, two_send, two_recv, second))

        def stage_two(k):
            wait_recv(send(first_chip, k, far_got, count + k, two_send, two_recv, second))
            add(first_chip, k, ((far_got, count + k),))
            start(send(first_chip, k, near_got, k, one_send, one_recv, first))

        def stage_three(j, k):
            wait_recv(send(chip, k, far_got, k, two_send, two_recv, second))
            wait_recv(send(chip, k, near_got, k, one_send, one_recv, first))
            if j < count - 1:
                add(chip, k, ((far_got, k), (near_got, k)))
                start(send(chip, k, z_got, j, z_send, z_recv, (dp, k)))

        for j in range(count + 2):
            if j < count:
                stage_one(steps[j])
            if 1 <= j <= count:
                stage_two(steps[j - 1])
            if j >= 2:
                stage_three(j - 2, steps[j - 2])

        for j in range(count - 1):
            wait_recv(send(chip, z, z_got, j, z_send, z_recv, (dp, z)))
        add(chip, z, ((far_got, z), (near_got, z)) + tuple((z_got, j) for j in range(count - 1)), last=True)
        locals_, remotes = [], []
        for ref, lo, size in chunks:
            locals_.append(pltpu.make_async_copy(final[ref].at[which, pl.ds(0, size)], outs[ref].at[pl.ds(lo, size)], end_local.at[ref]))
            remotes.append(pltpu.make_async_remote_copy(final[ref].at[1 - which, pl.ds(0, size)], outs[ref].at[pl.ds(lo, size)],
                                                        end_send.at[which, ref], end_recv.at[which, ref], device_id=sibling, device_id_type=MESH))
        start(locals_ + remotes)
        for copy in locals_:
            copy.wait()
        wait_send(remotes)
        for ref, lo, size in other:
            pltpu.make_async_remote_copy(final[ref].at[which, pl.ds(0, size)], outs[ref].at[pl.ds(lo, size)],
                                         end_send.at[1 - which, ref], end_recv.at[1 - which, ref], device_id=sibling, device_id_type=MESH).wait_recv()
        for j, k in enumerate(steps):
            for col in (chip, first_chip, second_chip, both_chip):
                wait_send(sibling_copies(col, k, other))
            wait_send(send(both_chip, k, far_got, count + k, two_send, two_recv, second))
            wait_send(send(second_chip, k, far_got, k, two_send, two_recv, second))
            wait_send(send(first_chip, k, near_got, k, one_send, one_recv, first))
            if j < count - 1:
                wait_send(send(chip, k, z_got, j, z_send, z_recv, (dp, k)))

    pl.when(core == 0)(lambda: role(0, 4, 2))
    pl.when(core == 1)(lambda: role(1, 2, 4))
    swap.wait()


def scatter_all(g_in, g_rest, proj, cut, collective_id):
    count = g_in.shape[2]
    rows_in, rows_rest = g_in.shape[3], g_rest.shape[3]
    parts = (((0, 0, cut),), ((0, cut, rows_in - cut), (1, 0, rows_rest)))
    sems = lambda *s: pltpu.SemaphoreType.DMA(s)
    places = 4 * count

    def bufs(k, kind=BF):
        lead = (k, 2) if k else (2,)
        return [pltpu.VMEM(lead + (max(cut, rows_in - cut), g_in.shape[4]), kind), pltpu.VMEM(lead + (rows_rest, g_rest.shape[4]), kind)]

    return pl.pallas_call(
        functools.partial(scatter_kernel, parts, count),
        in_specs=[pl.BlockSpec(memory_space=pl.ANY)] * 3,
        out_specs=[pl.BlockSpec(memory_space=pl.ANY)] * 3,
        out_shape=[jax.ShapeDtypeStruct(g_in.shape[3:], F32), jax.ShapeDtypeStruct(g_rest.shape[3:], F32), jax.ShapeDtypeStruct(proj.shape, proj.dtype)],
        scratch_shapes=bufs(places) + bufs(places) + bufs(2 * count) + bufs(count) + bufs(count - 1) + bufs(0, F32)
        + [sems(places, 2), sems(places, 2), sems(places, 2), sems(2 * count, 2), sems(2 * count, 2), sems(count, 2), sems(count, 2),
           sems(count - 1, 2), sems(count - 1, 2), sems(2, 2), sems(2, 2), sems(2), sems(1), sems(1, count - 1), sems(1, count - 1)],
        compiler_params=pltpu.CompilerParams(collective_id=collective_id, has_side_effects=True, vmem_limit_bytes=VM),
        cost_estimate=pl.CostEstimate(flops=0, bytes_accessed=200_000_000, transcendentals=0),
        name="scatter_all",
    )(g_in, g_rest, proj)


def unpack_kernel(own, width_b, pack_ref, low_ref, high_ref, small_ref, tall):
    blocks = pack_ref.shape[0]
    for b in range(blocks):
        block = pack_ref[b].astype(F32)
        tall[b * own : (b + 1) * own, :] = block[:own]
        small_ref[b : b + 1, :] = block[own : own + 1]
    for j in range(tall.shape[0] // 128):
        turned = tall[j * 128 : (j + 1) * 128, :].T
        low_ref[:, j * 128 : (j + 1) * 128] = turned[:width_b].astype(BF)
        high_ref[:, j * 128 : (j + 1) * 128] = turned[width_b:]


def unpack(pack, own, width_b):
    blocks, _, cols = pack.shape
    chans = blocks * own
    if own % 8:
        turned = pack[:, :own].reshape(chans, cols).T
        return turned[:width_b], turned[width_b:].astype(F32), pack[:, own].astype(F32)
    return pl.pallas_call(
        functools.partial(unpack_kernel, own, width_b),
        out_shape=[jax.ShapeDtypeStruct((width_b, chans), BF), jax.ShapeDtypeStruct((cols - width_b, chans), F32), jax.ShapeDtypeStruct((blocks, cols), F32)],
        scratch_shapes=[pltpu.VMEM((chans, cols), F32)],
        compiler_params=pltpu.CompilerParams(vmem_limit_bytes=VM),
        name="unpack_small",
    )(pack)


def pack_kernel(own, x_ref, dt_ref, log_ref, misc_ref, small_ref, out_ref, wide, tall):
    at = 0
    for ref in (x_ref, dt_ref, log_ref, misc_ref):
        wide[at : at + ref.shape[0], :] = ref[...]
        at += ref.shape[0]
    wide[at:, :] = jnp.zeros((wide.shape[0] - at, wide.shape[1]), F32)
    for j in range(tall.shape[0] // 128):
        tall[j * 128 : (j + 1) * 128, :] = wide[:, j * 128 : (j + 1) * 128].T
    cols = wide.shape[0]
    first = lax.broadcasted_iota(jnp.int32, (8, cols), 0) == 0
    for b in range(out_ref.shape[0]):
        tail = jnp.where(first, jnp.broadcast_to(small_ref[b : b + 1, :], (8, cols)), 0.0)
        out_ref[b] = jnp.concatenate([tall[b * own : (b + 1) * own, :], tail], axis=0).astype(BF)


def pack_grads(x_t, dt_t, log_t, misc, small, own):
    blocks, cols = small.shape
    chans = x_t.shape[1]
    rows = own + -own % 16
    if own % 8:
        turned = jnp.concatenate([x_t, dt_t, log_t, misc]).T.reshape(blocks, own, -1)
        turned = jnp.pad(turned, ((0, 0), (0, 0), (0, cols - turned.shape[2])))
        return jnp.concatenate([turned, small[:, None], jnp.zeros((blocks, rows - own - 1, cols), F32)], axis=1).astype(BF)
    return pl.pallas_call(
        functools.partial(pack_kernel, own),
        out_shape=jax.ShapeDtypeStruct((blocks, rows, cols), BF),
        scratch_shapes=[pltpu.VMEM((cols, chans), F32), pltpu.VMEM((chans, cols), F32)],
        compiler_params=pltpu.CompilerParams(vmem_limit_bytes=VM),
        name="pack_small",
    )(x_t, dt_t, log_t, misc, small)


def finish_kernel(own, cuts, pack_ref, exp_ref, proj_ref, up_out, down_out, row_out, proj_out, *col_outs):
    piece, width = exp_ref.shape[2:]
    filler = -piece % 128

    down_out[0] = exp_ref[0, 1].astype(F32)
    tall = exp_ref[0, 0].astype(F32)
    if filler:
        tall = jnp.concatenate([tall, jnp.zeros((filler, width), F32)], axis=0)
    for j in range(width // 128):
        up_out[0, j * 128 : (j + 1) * 128, :] = tall[:, j * 128 : (j + 1) * 128].T[:, :piece]

    @pl.when(pl.program_id(0) == 0)
    def _():
        row_out[...] = pack_ref[own : own + 1, :]
        proj_out[...] = sum(proj_ref[k].astype(F32) for k in range(proj_ref.shape[0]))[:own]
        for (lo, size), out in zip(cuts, col_outs):
            out[...] = pack_ref[0:own, lo : lo + size]


def finish(pack, both, proj, own, cuts):
    experts, _, piece, width = both.shape
    if own % 8:
        return [jnp.swapaxes(both[:, 0].astype(F32), 1, 2), both[:, 1].astype(F32), pack[own : own + 1], jnp.sum(proj[:, :own].astype(F32), axis=0)] + [pack[:own, lo : lo + size] for lo, size in cuts]
    whole = lambda shape: pl.BlockSpec(shape, lambda e: (0,) * len(shape))
    part = lambda shape: pl.BlockSpec((1,) + shape[1:], lambda e: (e, 0, 0))
    shapes = [(experts, width, piece), (experts, piece, width), (1, pack.shape[1]), (own, width)] + [(own, size) for _, size in cuts]
    return pl.pallas_call(
        functools.partial(finish_kernel, own, cuts),
        grid=(experts,),
        in_specs=[whole(pack.shape), pl.BlockSpec((1,) + both.shape[1:], lambda e: (e, 0, 0, 0)), whole(proj.shape)],
        out_specs=[part(shapes[0]), part(shapes[1])] + [whole(s) for s in shapes[2:]],
        out_shape=[jax.ShapeDtypeStruct(s, F32) for s in shapes],
        compiler_params=pltpu.CompilerParams(vmem_limit_bytes=VM),
        name="finish",
    )(pack, both, proj)


def chain_kernel(step, pieces, carry_ref, own_ref, out_ref, inbox, outbox, send, recv):
    dp, z = lax.axis_index("dp"), lax.axis_index("seq")
    last = lax.axis_size("seq") - 1
    has_before = z > 0 if step > 0 else z < last
    has_after = z < last if step > 0 else z > 0
    barrier = pltpu.get_barrier_semaphore()

    def neighbours(act):
        pl.when(has_before)(lambda: act(z - step))
        pl.when(has_after)(lambda: act(z + step))

    neighbours(lambda peer: pl.semaphore_signal(barrier, inc=1, device_id=(dp, peer), device_id_type=MESH))
    count = last + 1
    pl.semaphore_wait(barrier, (z + last) // count + (2 * last - z) // count)
    wide = own_ref.shape[1] // pieces

    def copy(g):
        return pltpu.make_async_remote_copy(outbox.at[g], inbox.at[g], send.at[g], recv.at[g], device_id=(dp, z + step), device_id_type=MESH)

    def back(g):
        return pltpu.make_async_remote_copy(outbox.at[g], inbox.at[g], send.at[g], recv.at[g], device_id=(dp, z - step), device_id_type=MESH)

    for g in range(pieces):
        c = slice(g * wide, (g + 1) * wide)

        @pl.when(has_before)
        def _():
            back(g).wait_recv()
            out_ref[:, c] = inbox[g].astype(F32)

        @pl.when(jnp.logical_not(has_before))
        def _():
            out_ref[:, c] = jnp.zeros((out_ref.shape[0], wide), F32)

        @pl.when(has_after)
        def _():
            outbox[g] = (carry_ref[:, c] * out_ref[:, c] + own_ref[:, c]).astype(BF)
            copy(g).start()

    @pl.when(has_after)
    def _():
        for g in range(pieces):
            copy(g).wait_send()


def chain(carry, own, step, collective_id):
    pieces = 3
    n, chans = own.shape
    return pl.pallas_call(
        functools.partial(chain_kernel, step, pieces),
        in_specs=[pl.BlockSpec(memory_space=pltpu.VMEM)] * 2,
        out_specs=pl.BlockSpec(memory_space=pltpu.VMEM),
        out_shape=jax.ShapeDtypeStruct((n, chans), F32),
        scratch_shapes=[pltpu.VMEM((pieces, n, chans // pieces), BF)] * 2 + [pltpu.SemaphoreType.DMA((pieces,))] * 2,
        compiler_params=pltpu.CompilerParams(collective_id=collective_id, has_side_effects=True),
        name="chain",
    )(carry, own)


def experts_kernel(block, piece, pick_ref, n2_ref, go_ref, router_ref, up_hbm, down_hbm, back_ref, late_ref, mixed_ref, grouter_ref, gexp_hbm,
                   up, down, gup, gdown, outbox, inbox, ret, total, disp, load_sem, store_sem, own_sem, out_send, out_recv, back_own, back_send, back_recv):
    dp, z = lax.axis_index("dp"), lax.axis_index("seq")
    count = lax.axis_size("seq")
    peers = [lax.rem(z + j, count) for j in range(1, count)]
    blocks = up.shape[0] // block
    rows, width = total.shape
    each = rows // count

    def loads(b):
        at = pl.ds(pl.multiple_of(b * block, block), block)
        return [pltpu.make_async_copy(up_hbm.at[at], up.at[at], load_sem.at[b, 0]), pltpu.make_async_copy(down_hbm.at[at], down.at[at], load_sem.at[b, 1])]

    def stores(b):
        made = []
        for i in range(block // piece):
            at = pl.ds(pl.multiple_of(b * block + i * piece, 16), piece)
            to = b * (block // piece) + i
            made.append(pltpu.make_async_copy(gup.at[at], gexp_hbm.at[to, 0], store_sem.at[to, 0]))
            made.append(pltpu.make_async_copy(gdown.at[at], gexp_hbm.at[to, 1], store_sem.at[to, 1]))
        return made

    def send(half, j):
        return pltpu.make_async_remote_copy(outbox.at[half, peers[j]], inbox.at[half, z], out_send.at[half, j], out_recv.at[half, j], device_id=(dp, peers[j]), device_id_type=MESH)

    def came(half, j):
        return pltpu.make_async_remote_copy(outbox.at[half, z], inbox.at[half, lax.rem(z + count - 1 - j, count)], out_send.at[half, j], out_recv.at[half, j], device_id=(dp, z), device_id_type=MESH)

    def kept(half):
        return pltpu.make_async_copy(outbox.at[half, z], inbox.at[half, z], own_sem.at[half])

    def give(half, j):
        return pltpu.make_async_remote_copy(ret.at[half, peers[j]], back_ref.at[z], back_send.at[half, j], back_recv.at[half, j], device_id=(dp, peers[j]), device_id_type=MESH)

    def got(half, j):
        return pltpu.make_async_remote_copy(ret.at[half, z], back_ref.at[lax.rem(z + count - 1 - j, count)], back_send.at[half, j], back_recv.at[half, j], device_id=(dp, z), device_id_type=MESH)

    def give_own(half):
        return pltpu.make_async_copy(ret.at[half, z], back_ref.at[z], back_own.at[half])

    greet([(dp, peer) for peer in peers])
    for half in range(2):
        picked = lax.dot_general(pick_ref[:, half * rows : (half + 1) * rows], n2_ref[...], TN, preferred_element_type=F32)
        outbox[half] = picked.astype(BF).reshape(count, each, width)
        for j in range(count - 1):
            send(half, j).start()
        kept(half).start()
    for b in range(blocks):
        for copy in loads(b):
            copy.start()
    lanes = lax.broadcasted_iota(jnp.int32, (rows, router_ref.shape[1]), 1)
    mine = (lanes == z).astype(F32)
    for half in range(2):
        kept(half).wait()
        for j in range(count - 1):
            came(half, j).wait_recv()
        slots = inbox[half].reshape(rows, width)
        go = go_ref[:, half * each : (half + 1) * each, :].reshape(rows, width).astype(F32)
        logits = jnp.where(lanes < count, jnp.dot(slots, router_ref[...], preferred_element_type=F32), -1e30)
        powers = jnp.exp(logits - jnp.max(logits, axis=1, keepdims=True))
        probs = jnp.where(lanes < count, powers / jnp.sum(powers, axis=1, keepdims=True), 0.0)
        gate = jnp.sum(probs * mine, axis=1, keepdims=True)
        grads = (gate * go).astype(BF)
        total[...] = jnp.zeros_like(total)
        disp[...] = jnp.zeros_like(disp)

        def units(b, _):
            at = pl.ds(pl.multiple_of(b * block, block), block)
            if half == 0:
                for copy in loads(b):
                    copy.wait()
            hidden = lax.dot_general(slots, up[at, :], NT, preferred_element_type=F32)
            phi = 0.5 * (1.0 + lax.erf(hidden * (1.0 / math.sqrt(2.0))))
            act = (hidden * phi).astype(BF)
            slope = phi + hidden * jnp.exp(hidden * hidden * -0.5) * (1.0 / math.sqrt(2.0 * math.pi))
            ghid = (lax.dot_general(grads, down[at, :], NT, preferred_element_type=F32) * slope).astype(BF)
            total[...] += jnp.dot(act, down[at, :], preferred_element_type=F32)
            disp[...] += jnp.dot(ghid, up[at, :], preferred_element_type=F32)
            new_up = lax.dot_general(ghid, slots, TN, preferred_element_type=F32)
            new_down = lax.dot_general(act, grads, TN, preferred_element_type=F32)
            if half == 0:
                gup[at, :] = new_up.astype(BF)
                gdown[at, :] = new_down.astype(BF)
            else:
                gup[at, :] = (gup[at, :].astype(F32) + new_up).astype(BF)
                gdown[at, :] = (gdown[at, :].astype(F32) + new_down).astype(BF)
                for copy in stores(b):
                    copy.start()
            return 0

        lax.fori_loop(0, blocks, units, 0)
        expert_out = total[...]
        mixed_ref[:, half * each : (half + 1) * each, :] = (gate * expert_out).astype(BF).reshape(count, each, width)
        grad_gate = jnp.sum(go * expert_out, axis=1, keepdims=True)
        grad_logits = (grad_gate * gate * (mine - probs)).astype(BF)
        grad_n2 = disp[...] + lax.dot_general(grad_logits, router_ref[...], NT, preferred_element_type=F32)
        if half == 0:
            ret[half] = grad_n2.astype(BF).reshape(count, each, width)
            for j in range(count - 1):
                give(half, j).start()
            give_own(half).start()
        else:
            late_ref[...] = grad_n2.astype(BF).reshape(count, each, width)
        grouter = lax.dot_general(slots, grad_logits, TN, preferred_element_type=F32)
        if half == 0:
            grouter_ref[...] = grouter
        else:
            grouter_ref[...] += grouter
    for b in range(blocks):
        for copy in stores(b):
            copy.wait()
    give_own(0).wait()
    for j in range(count - 1):
        send(0, j).wait_send()
        send(1, j).wait_send()
        give(0, j).wait_send()
        got(0, j).wait_recv()


def experts_pass(pick, n2, go, router, up, down, block, piece, collective_id):
    count, slots, width = go.shape
    units = up.shape[0]
    rows = count * slots // 2
    vmem = pl.BlockSpec(memory_space=pltpu.VMEM)
    hbm = pl.BlockSpec(memory_space=pl.ANY)
    sems = lambda *s: pltpu.SemaphoreType.DMA(s)
    blocks = units // block
    return pl.pallas_call(
        functools.partial(experts_kernel, block, piece),
        in_specs=[vmem] * 4 + [hbm] * 2,
        out_specs=[hbm, vmem, vmem, vmem, hbm],
        out_shape=[jax.ShapeDtypeStruct((count, slots // 2, width), BF)] * 2 + [jax.ShapeDtypeStruct((count, slots, width), BF), jax.ShapeDtypeStruct(router.shape, F32),
                   jax.ShapeDtypeStruct((units // piece, 2, piece, width), BF)],
        scratch_shapes=[pltpu.VMEM(up.shape, BF)] * 4
        + [pltpu.VMEM((2, count, slots // 2, width), BF)] * 2 + [pltpu.VMEM((1, count, slots // 2, width), BF)] + [pltpu.VMEM((rows, width), F32)] * 2
        + [sems(blocks, 2), sems(units // piece, 2), sems(2), sems(2, count - 1), sems(2, count - 1), sems(1), sems(1, count - 1), sems(1, count - 1)],
        compiler_params=pltpu.CompilerParams(collective_id=collective_id, has_side_effects=True, vmem_limit_bytes=VM),
        cost_estimate=pl.CostEstimate(flops=24 * rows * units * width, bytes_accessed=100_000_000, transcendentals=4 * rows * units),
        name="experts",
    )(pick, n2, go, router, up, down)


def dot(a, b):
    return jnp.dot(a, b, preferred_element_type=F32)


def dot_nt(a, b):
    return lax.dot_general(a, b, NT, preferred_element_type=F32)


def dot_tn(a, b):
    return lax.dot_general(a, b, TN, preferred_element_type=F32)


def shift(value, axis, steps):
    count = lax.axis_size(axis)
    first, last = (max(0, -steps), min(count, count - steps))
    return lax.ppermute(value, axis, [(source, source + steps) for source in range(first, last)])


def rms_scale(value):
    return lax.rsqrt(jnp.mean(value * value, axis=-1, keepdims=True) + EPS)


def rms_back(value, gain, grad):
    scale = rms_scale(value)
    scaled = grad * gain
    grad_gain = jnp.sum(grad * (value * scale), axis=0)
    return scale * scaled - value * (scale * scale * scale) * jnp.mean(value * scaled, axis=-1, keepdims=True), grad_gain


def swap(value):
    return lax.all_to_all(value, "seq", 0, 0)


def shards(tokens, segment_ids, routes, cotangent, small_params, w_in, conv_w, conv_b, w_x, w_dt, dt_bias, a_log, d_skip, w_out, w_up, w_down):
    both = ("dp", "seq")
    devices = lax.axis_size(both)
    width = tokens.shape[2]
    rows = tokens.shape[1]
    experts = w_up.shape[0]
    chans = w_in.shape[0] * devices // 2
    own = w_out.shape[0]
    rank = w_dt.shape[1]
    n = a_log.shape[1]
    taps = conv_w.shape[1]
    slots = rows // 2
    halo = 16
    wide = 768

    tok_b = tokens[0]
    seg_plus = segment_ids[0] + 1

    columns = (w_x, w_dt, a_log, conv_w, conv_b[:, None], dt_bias[:, None], d_skip[:, None])
    packed = jnp.concatenate(columns, axis=1)
    share = small_params.shape[0]
    packed = jnp.pad(packed, ((0, -own % 16), (0, 256 - packed.shape[1])))
    packed = packed + jnp.pad(small_params[None], ((own, -own % 16 - 1), (0, 256 - share)))
    direct = lax.axis_size("dp") == 8 and lax.axis_size("seq") == 4
    up_t = jnp.swapaxes(w_up, 1, 2)
    full_out = lax.all_gather(w_out, both, axis=0, tiled=True)
    if direct:
        last_ids = jnp.broadcast_to(seg_plus[rows - halo :, None], (halo, 128))
        all_in, all_pack, part_up, rim_tok, rim_ids = gather_all(w_in, packed, up_t, tok_b, last_ids, 80, 4)
        down_late, all_in = lax.optimization_barrier((w_down, all_in))
        part_down = swap(down_late)
        rim_ids = jnp.where(lax.axis_index("seq") > 0, rim_ids[:, 0], 0)
    else:
        all_in, all_pack = lax.all_gather(w_in, both), lax.all_gather(packed, both)
        part_up, part_down = swap(up_t), swap(w_down)
        rim_tok = shift(tok_b[rows - halo :], "seq", 1)
        rim_ids = shift(seg_plus[rows - halo :], "seq", 1)
    full_in = lax.optimization_barrier(all_in.reshape(2 * chans, width))
    low_t, high_t, small = unpack(all_pack.reshape(devices, -1, 256), own, rank + w_x.shape[1])
    small, part_up = lax.optimization_barrier((small, part_up))
    full_up = lax.all_gather(part_up, "dp", axis=0).reshape(-1, width)
    xcols = w_x.shape[1]
    full_x_t, full_dt_t = low_t[:xcols], low_t[xcols:]
    alog_t, conv_f, bias_row, dtb_row, skip = high_t[:n], high_t[n : n + taps], high_t[n + taps : n + taps + 1], high_t[n + taps + 1 : n + taps + 2], high_t[n + taps + 2 : n + taps + 3]
    flat_small = small[:, :share].reshape(-1)
    gain_one = flat_small[:width]
    gain_two = flat_small[width : 2 * width]
    router = flat_small[2 * width :].reshape(width, experts).astype(BF)
    route_ids = routes[0]
    onehot = (route_ids == jnp.arange(experts)[None, :]).astype(BF)
    before = (jnp.arange(rows)[:, None] > jnp.arange(rows)[None, :]).astype(BF)
    place = jnp.sum(dot(before, onehot) * onehot.astype(F32), axis=1).astype(jnp.int32)
    slot_of = route_ids[:, 0] * slots + place
    gather_mat = (slot_of[:, None] == jnp.arange(experts * slots)[None, :]).astype(BF)
    half = slots // 2
    pick_of = place // half * (experts * half) + route_ids[:, 0] * half + place % half
    pick = (pick_of[:, None] == jnp.arange(experts * slots)[None, :]).astype(BF)
    grad_out_b = cotangent[0]
    grad_out = grad_out_b.astype(F32)
    tok_ext = jnp.concatenate([rim_tok, tok_b]).astype(F32)
    tok_f = tok_b.astype(F32)
    ids_ext = jnp.concatenate([rim_ids, seg_plus])
    same = jnp.stack([ids_ext[halo - taps + 1 + k : halo - taps + 1 + k + rows] == seg_plus for k in range(taps)], axis=1).astype(F32)
    keep = same[:, taps - 2 : taps - 1]
    normed_ext = (tok_ext * rms_scale(tok_ext) * gain_one).astype(BF)
    normed = normed_ext[halo:]
    conv_in = dot_nt(normed_ext, full_in[:chans]).astype(BF).astype(F32)
    z = dot_nt(normed, full_in[chans:])
    conv_sum = bias_row
    for k in range(taps):
        lo = halo - taps + 1 + k
        conv_sum = conv_sum + conv_f[k : k + 1] * conv_in[lo : lo + rows] * same[:, k : k + 1]
    values = conv_sum * jax.nn.sigmoid(conv_sum)
    values_b = values.astype(BF)
    projected = dot_nt(values_b, full_x_t)
    low_rank = projected[:, :rank].astype(BF)
    b_rows = projected[:, rank : rank + n]
    c_rows = projected[:, rank + n :]
    pre_dt = dot(low_rank, full_dt_t) + dtb_row
    dt = jax.nn.softplus(pre_dt)
    dt_keep = jnp.where(keep > 0, dt, 1e30)
    dtx = dt * values
    rates = -jnp.exp(alog_t)
    rates2 = rates * math.log2(math.e)
    b_wide = jnp.broadcast_to(b_rows[:, :, None], (rows, n, 128)).reshape(rows * n, 128)
    c_wide = jnp.broadcast_to(c_rows[:, :, None], (rows, n, 128)).reshape(rows * n, 128)
    own_state, carry = state_pass(dt_keep, dtx, rates2, b_wide, wide)
    carry, part_down = lax.optimization_barrier((carry, part_down))
    full_down = lax.all_gather(part_down, "dp", axis=0).reshape(-1, width)
    start = chain(carry, own_state, 1, 3)
    go_local, start = lax.optimization_barrier((dot_tn(gather_mat, grad_out_b).astype(BF), start))
    go_slots = swap(go_local.reshape(experts, slots, width))
    scanned, checks = scan_pass(dt_keep, dtx, rates2, b_wide, block_diag(c_rows).astype(BF), start, wide)
    scanned, go_slots = lax.optimization_barrier((scanned, go_slots))
    sig_z = jax.nn.sigmoid(z)
    gated = ((scanned + skip * values) * (z * sig_z)).astype(BF)
    first_sum = tok_f + dot(gated, full_out)
    normed_two = (first_sum * rms_scale(first_sum) * gain_two).astype(BF)

    piece = w_up.shape[2]
    router_wide = jnp.pad(router, ((0, 0), (0, 128 - experts)))
    back_n2, late_n2, mixed_back, grad_router, grad_exp = experts_pass(pick, normed_two, go_slots, router_wide, full_up, full_down, 768, piece if piece % 16 == 0 else 768, 5)
    grad_router = grad_router[:, :experts]
    late_n2 = swap(late_n2)
    grad_n2 = dot(pick, jnp.concatenate([back_n2.reshape(-1, width), late_n2.reshape(-1, width)]))
    mixed_slots = swap(mixed_back).reshape(-1, width)
    if piece % 16:
        grad_exp = jnp.swapaxes(jnp.swapaxes(grad_exp, 0, 1).reshape(2, -1, piece, width), 0, 1)
    part_exp = lax.psum_scatter(grad_exp, "dp", scatter_dimension=0, tiled=True)

    grad_norm_two, grad_gain_two = rms_back(first_sum, gain_two, grad_n2)
    grad_first = grad_out + grad_norm_two
    grad_mixer = grad_first.astype(BF)
    grad_w_out = dot_tn(gated, grad_mixer)
    grad_gated = dot_nt(grad_mixer, full_out)
    silu_z = z * sig_z
    grad_scanned = grad_gated * silu_z
    grad_z = grad_gated * (scanned + skip * values) * (sig_z * (1.0 + z * (1.0 - sig_z)))
    grad_z_b = grad_z.astype(BF)
    grad_skip = jnp.sum(grad_scanned * values, axis=0)
    grad_start = back_state_pass(dt_keep, grad_scanned, rates2, c_wide, wide)
    nxt = chain(carry, grad_start, -1, 4)
    ones_blk = block_diag(jnp.ones((STEP, n), F32)).astype(BF)
    g_dtx, g_dt, g_log, gb_full, gc_full = back_pass(
        dt, dt_keep, dtx, grad_scanned, rates2, rates, b_wide, c_wide, block_diag(b_rows).astype(BF), ones_blk, checks, nxt, wide
    )
    g_dtx, mixed_slots, part_exp, grad_w_out = lax.optimization_barrier((g_dtx, mixed_slots, part_exp, grad_w_out.astype(BF)))
    sum_exp = swap(part_exp)
    mixed_out = (first_sum + dot(gather_mat, mixed_slots)).astype(BF)
    grad_dt = g_dt + g_dtx * values
    grad_pre_f = grad_dt * jax.nn.sigmoid(pre_dt)
    grad_dtb = jnp.sum(grad_pre_f, axis=0)
    grad_pre = grad_pre_f.astype(BF)
    grad_dt_t = dot_tn(low_rank, grad_pre)
    grad_proj = jnp.concatenate([dot_nt(grad_pre, full_dt_t), block_undiag(gb_full, n), block_undiag(gc_full, n)], axis=1).astype(BF)
    grad_x_t = dot_tn(grad_proj, values_b)
    grad_values = grad_scanned * skip + g_dtx * dt + dot(grad_proj, full_x_t)
    sig_c = jax.nn.sigmoid(conv_sum)
    grad_conv_sum = grad_values * (sig_c * (1.0 + conv_sum * (1.0 - sig_c)))
    grad_bias = jnp.sum(grad_conv_sum, axis=0)
    grad_taps = []
    grad_ext = None
    for k in range(taps):
        lo = halo - taps + 1 + k
        masked = grad_conv_sum * same[:, k : k + 1]
        grad_taps.append(jnp.sum(masked * conv_in[lo : lo + rows], axis=0))
        term = jnp.pad(masked * conv_f[k : k + 1], ((lo, halo - lo), (0, 0)))
        grad_ext = term if grad_ext is None else grad_ext + term
    rim_back = shift(grad_ext[halo - 8 : halo], "seq", -1)
    grad_conv_in = (grad_ext[halo:] + jnp.pad(rim_back, ((rows - 8, 0), (0, 0)))).astype(BF)
    grad_w_in = dot_tn(jnp.concatenate([grad_conv_in, grad_z_b], axis=1), normed).astype(BF)
    grad_normed = dot(grad_conv_in, full_in[:chans]) + dot(grad_z_b, full_in[chans:])
    grad_norm_one, grad_gain_one = rms_back(tok_f, gain_one, grad_normed)
    tokens_grad = (grad_first + grad_norm_one).astype(BF)

    grad_small = jnp.concatenate([grad_gain_one, grad_gain_two, grad_router.reshape(-1)])
    misc = jnp.stack(grad_taps + [grad_bias, grad_dtb, grad_skip, jnp.zeros_like(grad_bias)])
    grad_packed = pack_grads(grad_x_t, grad_dt_t, g_log, misc, jnp.pad(grad_small.reshape(devices, -1), ((0, 0), (0, 256 - share))), own)
    part_out = lax.psum_scatter(grad_w_out, "dp", scatter_dimension=0, tiled=True).reshape(-1, own, width)
    part_out = jnp.pad(part_out, ((0, 0), (0, -own % 16), (0, 0)))
    if direct:
        grad_packed, sum_exp = lax.optimization_barrier((grad_packed, sum_exp))
        sum_in, sum_pack, all_out = scatter_all(
            grad_w_in.reshape(4, 2, 4, 2 * own, width), grad_packed.reshape((4, 2, 4) + grad_packed.shape[1:]), part_out, 80, 2
        )
    else:
        sum_in = lax.psum_scatter(grad_w_in, both, scatter_dimension=0, tiled=True).astype(F32)
        sum_pack = lax.psum_scatter(grad_packed, both, scatter_dimension=0, tiled=True)[0].astype(F32)
        all_out = swap(part_out)
    cuts, at = [], 0
    for column in columns:
        cuts.append((at, column.shape[1]))
        at += column.shape[1]
    up_out, down_out, s_row, sum_out, s_x, s_dt, s_log, s_conv, s_bias, s_dtb, s_skip = finish(sum_pack, sum_exp, all_out, own, tuple(cuts))
    return (
        mixed_out[None],
        tokens_grad[None],
        s_row[0, :share],
        sum_in,
        s_conv,
        s_bias[:, 0],
        s_x,
        s_dt,
        s_dtb[:, 0],
        s_log,
        s_skip[:, 0],
        sum_out,
        up_out,
        down_out,
    )


def solution(mesh):
    split = ("dp", "seq")
    token, row, mat, vec = P("dp", "seq", None), P("dp", "seq"), P(split, None), P(split)
    return jax.shard_map(
        shards,
        mesh=mesh,
        in_specs=(token, row, token, token, vec, mat, mat, vec, mat, mat, vec, mat, vec, mat, P(None, None, split), P(None, split, None)),
        out_specs=(token, token, vec, mat, mat, vec, mat, mat, vec, mat, vec, mat, P(None, None, split), P(None, split, None)),
        check_vma=False,
    )
```

```python
import functools
import math

import jax
import jax.numpy as jnp
from jax import lax
from jax.experimental import pallas as pl
from jax.experimental.pallas import tpu as pltpu
from jax.sharding import PartitionSpec as P

F32, BF = jnp.float32, jnp.bfloat16
EPS = 1e-05
STEP = 16
VM = 56 * 1024 * 1024
MESH = pl.DeviceIdType.MESH
NT = (((1,), (1,)), ((), ()))
TN = (((0,), (0,)), ((), ()))


def rowb(block, i, n):
    return jnp.broadcast_to(block[i:i+1, :], (n, block.shape[1]))

def state_kernel(n, dte_ref, dtx_ref, rate_ref, b_ref, state_ref, carry_ref):
    rows, wide = dte_ref.shape
    tiles = wide // 128
    rates = [rate_ref[:, j*128:(j+1)*128] for j in range(tiles)]
    def block(k, carry):
        state, total = carry
        at = pl.multiple_of(k * STEP, STEP)
        dte = dte_ref[pl.ds(at, STEP), :]
        dtx = dtx_ref[pl.ds(at, STEP), :]
        state = list(state)
        for i in range(STEP):
            bs = b_ref[pl.ds((at + i) * n, n), :]
            for j in range(tiles):
                c = slice(j*128, (j+1)*128)
                decay = jnp.exp2(rowb(dte[:, c], i, n) * rates[j])
                state[j] = decay * state[j] + bs * rowb(dtx[:, c], i, n)
        return tuple(state), total + dte
    zero = tuple(jnp.zeros((n, 128), F32) for _ in range(tiles))
    state, total = lax.fori_loop(0, rows // STEP, block, (zero, jnp.zeros((STEP, wide), F32)))
    summed = jnp.sum(total, axis=0, keepdims=True)
    for j in range(tiles):
        c = slice(j*128, (j+1)*128)
        state_ref[:, c] = state[j]
        carry_ref[:, c] = jnp.exp2(jnp.broadcast_to(summed[:, c], (n, 128)) * rates[j])

def front_kernel(halo, ext_ref, normed_ref, wc_ref, wz_ref, xt_ref, taps_ref, bias_ref, same_ref, conv_ref, sum_ref, values_ref, z_ref, proj_ref):
    rows, wide = sum_ref.shape
    taps = taps_ref.shape[0]
    conv_ref[...] = lax.dot_general(ext_ref[...], wc_ref[...], NT, preferred_element_type=F32).astype(BF).astype(F32)
    z_ref[...] = lax.dot_general(normed_ref[...], wz_ref[...], NT, preferred_element_type=F32)
    for j in range(wide // 128):
        c = slice(j * 128, (j + 1) * 128)
        total = jnp.broadcast_to(bias_ref[:, c], (rows, 128))
        for k in range(taps):
            lo = halo - taps + 1 + k
            total = total + taps_ref[k : k + 1, c] * conv_ref[lo : lo + rows, c] * same_ref[k]
        sum_ref[:, c] = total
        values_ref[:, c] = total * jax.nn.sigmoid(total)

    @pl.when(pl.program_id(0) == 0)
    def _():
        proj_ref[...] = jnp.zeros_like(proj_ref)

    proj_ref[...] += lax.dot_general(values_ref[...].astype(BF), xt_ref[...], NT, preferred_element_type=F32)


def front(normed_ext, normed, full_in, x_t, conv_taps, bias, same, halo, wide):
    rows, width = normed.shape
    chans = full_in.shape[0] // 2
    taps = conv_taps.shape[0]
    wide_same = jnp.broadcast_to(same.T[:, :, None], (taps, rows, 128))
    col = lambda r: pl.BlockSpec((r, wide), lambda g: (0, g))
    whole = lambda a: pl.BlockSpec(a.shape, lambda g: (0,) * len(a.shape))
    steps = chans // wide
    f32 = lambda r: jax.ShapeDtypeStruct((r, chans), F32)
    return pl.pallas_call(
        functools.partial(front_kernel, halo),
        grid=(steps,),
        in_specs=[whole(normed_ext), whole(normed), pl.BlockSpec((wide, width), lambda g: (g, 0)), pl.BlockSpec((wide, width), lambda g: (g + steps, 0)),
                  col(128), col(taps), col(1), whole(wide_same)],
        out_specs=[col(rows + halo), col(rows), col(rows), col(rows), pl.BlockSpec((rows, 128), lambda g: (0, 0))],
        out_shape=[f32(rows + halo), f32(rows), f32(rows), f32(rows), jax.ShapeDtypeStruct((rows, 128), F32)],
        compiler_params=pltpu.CompilerParams(vmem_limit_bytes=VM),
        cost_estimate=pl.CostEstimate(flops=4*rows*chans*width, bytes_accessed=4*chans*width + 16*rows*chans, transcendentals=rows*chans),
        name="front",
    )(normed_ext, normed, full_in, full_in, x_t, conv_taps, bias, wide_same)


def steps_kernel(n, rank_cols, proj_ref, keep_ref, values_ref, dtt_ref, dtb_ref, alog_ref,
                 low_ref, bw_ref, cw_ref, bblk_ref, cblk_ref, pre_ref, dt_ref, dte_ref, dtx_ref, rate_ref, rate2_ref, state_ref, carry_ref):
    rows, wide = pre_ref.shape
    groups = STEP * n

    @pl.when(pl.program_id(0) == 0)
    def _():
        proj = proj_ref[...]
        lanes = lax.broadcasted_iota(jnp.int32, proj.shape, 1)
        low_ref[...] = jnp.where(lanes < rank_cols, proj, 0.0).astype(BF)
        row = lax.broadcasted_iota(jnp.int32, (rows, groups), 0)
        col = lax.broadcasted_iota(jnp.int32, (rows, groups), 1)
        own = lax.rem(row, STEP) == col // n
        to_col = lax.rem(lax.broadcasted_iota(jnp.int32, (128, groups), 1), n)
        from_col = lax.broadcasted_iota(jnp.int32, (128, groups), 0)
        for i, (wide_ref, blk_ref) in enumerate(((bw_ref, bblk_ref), (cw_ref, cblk_ref))):
            pick = (from_col == to_col + rank_cols + i * n).astype(F32)
            tiled = jnp.where(own, jnp.dot(proj, pick, precision=lax.Precision.HIGHEST, preferred_element_type=F32), 0.0)
            blk_ref[...] = tiled.astype(BF)
            ones = jnp.ones((STEP, 128), F32)
            for k in range(rows // STEP):
                block = tiled[k * STEP : (k + 1) * STEP, :]
                wide_ref[k * groups : (k + 1) * groups, :] = lax.dot_general(block, ones, TN, precision=lax.Precision.HIGHEST, preferred_element_type=F32)

    pre = jnp.dot(low_ref[...], dtt_ref[...], preferred_element_type=F32) + dtb_ref[...]
    dt = jax.nn.softplus(pre)
    pre_ref[...] = pre
    dt_ref[...] = dt
    dtx_ref[...] = dt * values_ref[...]
    for j in range(wide // 128):
        c = slice(j * 128, (j + 1) * 128)
        dte_ref[:, c] = jnp.where(keep_ref[...] > 0, dt[:, c], 1e30)
    rate = -jnp.exp(alog_ref[...])
    rate_ref[...] = rate
    rate2_ref[...] = rate * math.log2(math.e)
    state_kernel(n, dte_ref, dtx_ref, rate2_ref, bw_ref, state_ref, carry_ref)


def steps(proj, keep, values, dt_t, dtb, alog_t, rank_cols, wide):
    rows, chans = values.shape
    n = alog_t.shape[0]
    groups = STEP * n
    wide_keep = jnp.broadcast_to(keep, (rows, 128))
    col = lambda r: pl.BlockSpec((r, wide), lambda g: (0, g))
    fixed = lambda *s: pl.BlockSpec(s, lambda g: (0, 0))
    f32 = lambda *s: jax.ShapeDtypeStruct(s, F32)
    bf = lambda *s: jax.ShapeDtypeStruct(s, BF)
    return pl.pallas_call(
        functools.partial(steps_kernel, n, rank_cols),
        grid=(chans // wide,),
        in_specs=[fixed(rows, 128), fixed(rows, 128), col(rows), col(128), col(1), col(n)],
        out_specs=[fixed(rows, 128), fixed(rows * n, 128), fixed(rows * n, 128), fixed(rows, groups), fixed(rows, groups)] + [col(rows)] * 4 + [col(n)] * 4,
        out_shape=[bf(rows, 128), f32(rows * n, 128), f32(rows * n, 128), bf(rows, groups), bf(rows, groups)] + [f32(rows, chans)] * 4 + [f32(n, chans)] * 4,
        compiler_params=pltpu.CompilerParams(vmem_limit_bytes=VM),
        cost_estimate=pl.CostEstimate(flops=10*rows*chans*n, bytes_accessed=24*rows*chans, transcendentals=rows*chans*n),
        name="steps",
    )(proj, wide_keep, values, dt_t, dtb, alog_t)


def scan_kernel(n, dte_ref, dtx_ref, rate_ref, b_ref, cblk_ref, start_ref, values_ref, z_ref, skip_ref, out_ref, tok_ref, gain_ref,
                y_ref, check_ref, gated_ref, first_ref, normed_ref, hs):
    rows, wide = dte_ref.shape
    tiles = wide // 128
    rates = [rate_ref[:, j*128:(j+1)*128] for j in range(tiles)]

    def block(k, state):
        at = pl.multiple_of(k * STEP, STEP)
        dte = dte_ref[pl.ds(at, STEP), :]
        dtx = dtx_ref[pl.ds(at, STEP), :]
        state = list(state)
        kn = pl.multiple_of(k * n, n)
        for j in range(tiles):
            check_ref[pl.ds(kn, n), j*128:(j+1)*128] = state[j]
        for i in range(STEP):
            bs = b_ref[pl.ds((at + i) * n, n), :]
            for j in range(tiles):
                c = slice(j*128, (j+1)*128)
                decay = jnp.exp2(rowb(dte[:, c], i, n) * rates[j])
                state[j] = decay * state[j] + bs * rowb(dtx[:, c], i, n)
                hs[i*n:(i+1)*n, c] = state[j].astype(BF)
        y_ref[pl.ds(at, STEP), :] = jnp.dot(cblk_ref[pl.ds(at, STEP), :], hs[...], preferred_element_type=F32)
        return tuple(state)

    start = tuple(start_ref[:, j*128:(j+1)*128] for j in range(tiles))
    lax.fori_loop(0, rows // STEP, block, start)

    @pl.when(pl.program_id(0) == 0)
    def _():
        first_ref[...] = tok_ref[...].astype(F32)

    z = z_ref[...]
    gated_ref[...] = ((y_ref[...] + skip_ref[...] * values_ref[...]) * (z * jax.nn.sigmoid(z))).astype(BF)
    first_ref[...] += jnp.dot(gated_ref[...], out_ref[...], preferred_element_type=F32)

    @pl.when(pl.program_id(0) == pl.num_programs(0) - 1)
    def _():
        first = first_ref[...]
        scale = lax.rsqrt(jnp.mean(first * first, axis=1, keepdims=True) + EPS)
        normed_ref[...] = (first * scale * gain_ref[...]).astype(BF)


def scan_pass(dte, dtx, rates2, b_wide, c_blk, start, values, z, skip, full_out, tok, gain, wide):
    rows, chans = dte.shape
    n = rates2.shape[0]
    width = tok.shape[1]
    col = lambda r: pl.BlockSpec((r, wide), lambda g: (0, g))
    whole = lambda a: pl.BlockSpec(a.shape, lambda g: (0, 0))
    return pl.pallas_call(
        functools.partial(scan_kernel, n),
        grid=(chans // wide,),
        in_specs=[col(rows), col(rows), col(n), whole(b_wide), whole(c_blk), col(n), col(rows), col(rows), col(1), pl.BlockSpec((wide, width), lambda g: (g, 0)), whole(tok), whole(gain)],
        out_specs=[col(rows), col(rows // STEP * n), col(rows), whole(tok), whole(tok)],
        out_shape=[jax.ShapeDtypeStruct((rows, chans), F32), jax.ShapeDtypeStruct((rows // STEP * n, chans), F32), jax.ShapeDtypeStruct((rows, chans), BF),
                   jax.ShapeDtypeStruct((rows, width), F32), jax.ShapeDtypeStruct((rows, width), BF)],
        scratch_shapes=[pltpu.VMEM((STEP * n, wide), BF)],
        compiler_params=pltpu.CompilerParams(vmem_limit_bytes=VM),
        cost_estimate=pl.CostEstimate(flops=10*rows*chans*n, bytes_accessed=12*rows*chans, transcendentals=rows*chans*n),
        name="scan_pass",
    )(dte, dtx, rates2, b_wide, c_blk, start, values, z, skip, full_out, tok, gain)


def back_state_kernel(n, dte_ref, gs_ref, rate_ref, c_ref, out_ref):
    rows, wide = dte_ref.shape
    tiles = wide // 128
    rates = [rate_ref[:, j*128:(j+1)*128] for j in range(tiles)]
    def block(k, state):
        at = pl.multiple_of(rows - STEP - k * STEP, STEP)
        dte = dte_ref[pl.ds(at, STEP), :]
        gs = gs_ref[pl.ds(at, STEP), :]
        state = list(state)
        for i in reversed(range(STEP)):
            cs = c_ref[pl.ds((at + i) * n, n), :]
            for j in range(tiles):
                c = slice(j*128, (j+1)*128)
                decay = jnp.exp2(rowb(dte[:, c], i, n) * rates[j])
                state[j] = decay * (state[j] + cs * rowb(gs[:, c], i, n))
        return tuple(state)
    zero = tuple(jnp.zeros((n, 128), F32) for _ in range(tiles))
    state = lax.fori_loop(0, rows // STEP, block, zero)
    for j in range(tiles):
        out_ref[:, j*128:(j+1)*128] = state[j]

def back_state_pass(dte, gs, rates2, c_wide, wide):
    rows, chans = dte.shape
    n = rates2.shape[0]
    return pl.pallas_call(
        functools.partial(back_state_kernel, n),
        grid=(chans // wide,),
        in_specs=[pl.BlockSpec((rows, wide), lambda g: (0, g)),
                  pl.BlockSpec((rows, wide), lambda g: (0, g)),
                  pl.BlockSpec((n, wide), lambda g: (0, g)),
                  pl.BlockSpec(c_wide.shape, lambda g: (0, 0))],
        out_specs=pl.BlockSpec((n, wide), lambda g: (0, g)),
        out_shape=jax.ShapeDtypeStruct((n, chans), F32),
        compiler_params=pltpu.CompilerParams(vmem_limit_bytes=VM),
        cost_estimate=pl.CostEstimate(flops=8*rows*chans*n, bytes_accessed=8*rows*chans, transcendentals=rows*chans*n),
    )(dte, gs, rates2, c_wide)

def back_kernel(n, rank_cols, dt_ref, dte_ref, dtx_ref, gs_ref, values_ref, pre_ref, skip_ref, rate_ref, rawrate_ref, b_ref, c_ref, bblk_ref, check_ref, next_ref, low_ref, wdt_ref,
                gval_ref, glog_ref, gwdt_ref, gdtb_ref, gskip_ref, proj_ref, us, decs, hs, ls, ps, gdtx, gdt, gb, gc, rank):
    rows, wide = dte_ref.shape
    tiles = wide // 128
    rates = [rate_ref[:, j*128:(j+1)*128] for j in range(tiles)]

    @pl.when(pl.program_id(0) == 0)
    def _():
        gb[...] = jnp.zeros_like(gb)
        gc[...] = jnp.zeros_like(gc)
        rank[...] = jnp.zeros_like(rank)

    ones = (lax.broadcasted_iota(jnp.int32, (STEP, STEP * n), 0) == lax.broadcasted_iota(jnp.int32, (STEP, STEP * n), 1) // n).astype(BF)
    glog_ref[...] = jnp.zeros_like(glog_ref)

    def block(k, later):
        kk = rows // STEP - 1 - k
        at = pl.multiple_of(kk * STEP, STEP)
        kn = pl.multiple_of(kk * n, n)
        dte = dte_ref[pl.ds(at, STEP), :]
        dtx = dtx_ref[pl.ds(at, STEP), :]
        state = [check_ref[pl.ds(kn, n), j*128:(j+1)*128] for j in range(tiles)]
        for i in range(STEP):
            bs = b_ref[pl.ds((at + i) * n, n), :]
            for j in range(tiles):
                c = slice(j*128, (j+1)*128)
                decay = jnp.exp2(rowb(dte[:, c], i, n) * rates[j])
                kept = decay * state[j]
                state[j] = kept + bs * rowb(dtx[:, c], i, n)
                decs[i*n:(i+1)*n, c] = decay
                us[i*n:(i+1)*n, c] = kept
                hs[i*n:(i+1)*n, c] = state[j].astype(BF)
        later = list(later)
        dt = dt_ref[pl.ds(at, STEP), :]
        gs = gs_ref[pl.ds(at, STEP), :]
        logs = [glog_ref[:, j*128:(j+1)*128] for j in range(tiles)]
        for i in reversed(range(STEP)):
            cs = c_ref[pl.ds((at + i) * n, n), :]
            for j in range(tiles):
                c = slice(j*128, (j+1)*128)
                adj = later[j] + cs * rowb(gs[:, c], i, n)
                part = adj * us[i*n:(i+1)*n, c] * rawrate_ref[:, c]
                later[j] = adj * decs[i*n:(i+1)*n, c]
                logs[j] = logs[j] + part * rowb(dt[:, c], i, n)
                ls[i*n:(i+1)*n, c] = adj.astype(BF)
                ps[i*n:(i+1)*n, c] = part.astype(BF)
        for j in range(tiles):
            glog_ref[:, j*128:(j+1)*128] = logs[j]
        gdtx[pl.ds(at, STEP), :] = jnp.dot(bblk_ref[pl.ds(at, STEP), :], ls[...], preferred_element_type=F32)
        gdt[pl.ds(at, STEP), :] = jnp.dot(ones, ps[...], preferred_element_type=F32)
        gb[pl.ds(at, STEP), :] += lax.dot_general(dtx.astype(BF), ls[...], NT, preferred_element_type=F32)
        gc[pl.ds(at, STEP), :] += lax.dot_general(gs.astype(BF), hs[...], NT, preferred_element_type=F32)
        return tuple(later)

    start = tuple(next_ref[:, j*128:(j+1)*128] for j in range(tiles))
    lax.fori_loop(0, rows // STEP, block, start)

    values = values_ref[...]
    grad_pre = (gdt[...] + gdtx[...] * values) * jax.nn.sigmoid(pre_ref[...])
    gdtb_ref[...] = jnp.sum(grad_pre, axis=0, keepdims=True)
    grad_pre = grad_pre.astype(BF)
    gwdt_ref[...] = lax.dot_general(low_ref[...], grad_pre, TN, preferred_element_type=F32)
    rank[...] += lax.dot_general(grad_pre, wdt_ref[...], NT, preferred_element_type=F32)
    gs = gs_ref[...]
    gskip_ref[...] = jnp.sum(gs * values, axis=0, keepdims=True)
    gval_ref[...] = gs * skip_ref[...] + gdtx[...] * dt_ref[...]

    @pl.when(pl.program_id(0) == pl.num_programs(0) - 1)
    def _():
        groups = STEP * n
        row = lax.broadcasted_iota(jnp.int32, (rows, groups), 0)
        col = lax.broadcasted_iota(jnp.int32, (rows, groups), 1)
        own = lax.rem(row, STEP) == col // n
        from_col = lax.rem(lax.broadcasted_iota(jnp.int32, (groups, rank.shape[1]), 0), n)
        to_col = lax.broadcasted_iota(jnp.int32, (groups, rank.shape[1]), 1)
        total = rank[...]
        for i, acc in enumerate((gb, gc)):
            place = (to_col == from_col + rank_cols + i * n).astype(BF)
            total = total + jnp.dot(jnp.where(own, acc[...], 0.0).astype(BF), place, preferred_element_type=F32)
        proj_ref[...] = total.astype(BF)


def back_pass(dt, dte, dtx, gs, values, pre, skip, rates2, rates, b_wide, c_wide, b_blk, check, nxt, low, wdt, rank_cols, wide):
    rows, chans = dte.shape
    n = rates2.shape[0]
    col = lambda r: pl.BlockSpec((r, wide), lambda g: (0, g))
    whole = lambda a: pl.BlockSpec(a.shape, lambda g: (0, 0))
    sq = lambda kind, w=wide: pltpu.VMEM((STEP * n, w), kind)
    return pl.pallas_call(
        functools.partial(back_kernel, n, rank_cols),
        grid=(chans // wide,),
        in_specs=[col(rows)] * 6 + [col(1)] + [col(n)] * 2 + [whole(b_wide), whole(c_wide), whole(b_blk), col(rows // STEP * n), col(n), whole(low), col(wdt.shape[0])],
        out_specs=[col(rows), col(n), col(low.shape[1]), col(1), col(1), pl.BlockSpec((rows, 128), lambda g: (0, 0))],
        out_shape=[jax.ShapeDtypeStruct((rows, chans), F32), jax.ShapeDtypeStruct((n, chans), F32), jax.ShapeDtypeStruct((low.shape[1], chans), F32),
                   jax.ShapeDtypeStruct((1, chans), F32), jax.ShapeDtypeStruct((1, chans), F32), jax.ShapeDtypeStruct((rows, 128), BF)],
        scratch_shapes=[sq(F32), sq(F32), sq(BF), sq(BF), sq(BF), pltpu.VMEM((rows, wide), F32), pltpu.VMEM((rows, wide), F32),
                        pltpu.VMEM((rows, STEP * n), F32), pltpu.VMEM((rows, STEP * n), F32), pltpu.VMEM((rows, 128), F32)],
        compiler_params=pltpu.CompilerParams(vmem_limit_bytes=VM),
        cost_estimate=pl.CostEstimate(flops=26*rows*chans*n, bytes_accessed=24*rows*chans, transcendentals=rows*chans*n),
        name="back_pass",
    )(dt, dte, dtx, gs, values, pre, skip, rates2, rates, b_wide, c_wide, b_blk, check, nxt, low, wdt)


def conv_back_kernel(halo, gval_ref, proj_ref, xt_ref, values_ref, sum_ref, ext_ref, same_ref, later_ref, taps_ref,
                     gconv_ref, last_ref, rim_ref, gxt_ref, gtaps_ref, pad):
    rows, wide = gval_ref.shape
    taps = taps_ref.shape[0]
    proj = proj_ref[...]
    grad_values = gval_ref[...] + jnp.dot(proj, xt_ref[...], preferred_element_type=F32)
    gxt_ref[...] = lax.dot_general(proj, values_ref[...].astype(BF), TN, preferred_element_type=F32)
    sums = sum_ref[...]
    sig = jax.nn.sigmoid(sums)
    pad[0:rows, :] = grad_values * (sig * (1.0 + sums * (1.0 - sig)))
    pad[rows:, :] = jnp.zeros((pad.shape[0] - rows, wide), F32)
    row = lax.broadcasted_iota(jnp.int32, (8, 128), 0)
    for j in range(wide // 128):
        c = slice(j * 128, (j + 1) * 128)
        grads = pad[0:rows, c]
        sums_of = [jnp.sum(grads * same_ref[k] * ext_ref[halo - taps + 1 + k : halo - taps + 1 + k + rows, c], axis=0, keepdims=True) for k in range(taps)]
        sums_of.append(jnp.sum(grads, axis=0, keepdims=True))
        total = jnp.zeros((rows, 128), F32)
        rim = jnp.zeros((8, 128), F32)
        for k in range(taps):
            weight = taps_ref[k : k + 1, c]
            total = total + pad[taps - 1 - k : taps - 1 - k + rows, c] * later_ref[k] * weight
            if k < taps - 1:
                moved = pltpu.roll(grads[0:8] * same_ref[k, 0:8, :], 8 - taps + 1 + k, 0)
                rim = rim + jnp.where(row >= 8 - taps + 1 + k, moved, 0.0) * weight
        gconv_ref[:, c] = total.astype(BF)
        last_ref[:, c] = total[rows - 8 :]
        rim_ref[:, c] = rim
        gtaps_ref[:, c] = jnp.concatenate(sums_of + [jnp.zeros((8 - len(sums_of), 128), F32)], axis=0)


def conv_back(gval, proj, x_t, values, sums, ext, same, conv_taps, halo, wide):
    rows, chans = gval.shape
    taps = conv_taps.shape[0]
    later = jnp.stack([jnp.pad(same[taps - 1 - k :, k], (0, taps - 1 - k)) for k in range(taps)])
    cover = lambda a: jnp.broadcast_to(a[:, :, None], (taps, rows, 128))
    col = lambda r: pl.BlockSpec((r, wide), lambda g: (0, g))
    mask = pl.BlockSpec((taps, rows, 128), lambda g: (0, 0, 0))
    f32 = lambda r: jax.ShapeDtypeStruct((r, chans), F32)
    return pl.pallas_call(
        functools.partial(conv_back_kernel, halo),
        grid=(chans // wide,),
        in_specs=[col(rows), pl.BlockSpec(proj.shape, lambda g: (0, 0)), col(x_t.shape[0]), col(rows), col(rows), col(ext.shape[0]), mask, mask, col(taps)],
        out_specs=[col(rows), col(8), col(8), col(x_t.shape[0]), col(8)],
        out_shape=[jax.ShapeDtypeStruct((rows, chans), BF), f32(8), f32(8), f32(x_t.shape[0]), f32(8)],
        scratch_shapes=[pltpu.VMEM((rows + 8, wide), F32)],
        compiler_params=pltpu.CompilerParams(vmem_limit_bytes=VM),
        cost_estimate=pl.CostEstimate(flops=60*rows*chans, bytes_accessed=20*rows*chans, transcendentals=rows*chans),
        name="conv_back",
    )(gval, proj, x_t, values, sums, ext, cover(same.T), cover(later), conv_taps)


def flip(value, bit):
    return value + bit - 2 * bit * (lax.rem(value // bit, 2))


def greet(partners):
    barrier = pltpu.get_barrier_semaphore()
    for partner in partners:
        pl.semaphore_signal(barrier, inc=1, device_id=partner, device_id_type=MESH)
    pl.semaphore_wait(barrier, len(partners))


class ZSwap:
    def __init__(self, pairs, local, send, recv, count):
        self.pairs, self.local, self.send, self.recv, self.count = pairs, local, send, recv, count

    def own(self):
        z = lax.axis_index("seq")
        return [pltpu.make_async_copy(src.at[z], dst.at[z], self.local.at[i]) for i, (src, dst) in enumerate(self.pairs)]

    def out(self):
        dp, z = lax.axis_index("dp"), lax.axis_index("seq")
        made = []
        for j in range(1, self.count):
            peer = lax.rem(z + j, self.count)
            for i, (src, dst) in enumerate(self.pairs):
                made.append(pltpu.make_async_remote_copy(src.at[peer], dst.at[z], self.send.at[i, j - 1], self.recv.at[i, j - 1], device_id=(dp, peer), device_id_type=MESH))
        return made

    def start(self):
        for copy in self.out() + self.own():
            copy.start()

    def wait(self):
        dp, z = lax.axis_index("dp"), lax.axis_index("seq")
        for copy in self.own():
            copy.wait()
        for copy in self.out():
            copy.wait_send()
        for j in range(1, self.count):
            source = lax.rem(z + self.count - j, self.count)
            for i, (src, dst) in enumerate(self.pairs):
                pltpu.make_async_remote_copy(src.at[z], dst.at[source], self.send.at[i, j - 1], self.recv.at[i, j - 1], device_id=(dp, source), device_id_type=MESH).wait_recv()


def gather_kernel(parts, count, in_ref, rest_ref, up_ref, tok_ref, ids_ref, gin_ref, grest_ref, gup_ref, rim_ref, rimids_ref,
                  local_sem, send, recv, share_send, share_recv, pair_send, pair_recv, swap_local, swap_send, swap_recv, rim_send, rim_recv):
    dp, z = lax.axis_index("dp"), lax.axis_index("seq")
    chip, core = dp // 2, lax.rem(dp, 2)
    srcs, dsts = (in_ref, rest_ref), (gin_ref, grest_ref)
    sibling = (flip(dp, 1), z)
    peers = [lax.rem(z + j, count) for j in range(1, count)]
    greet([sibling, (flip(dp, 4), z), (flip(dp, 2), z)] + [(dp, peer) for peer in peers])

    tail = pl.ds(tok_ref.shape[0] - rim_ref.shape[0], rim_ref.shape[0])
    rims = [pltpu.make_async_remote_copy(src, dst, rim_send.at[i], rim_recv.at[i], device_id=(dp, lax.rem(z + 1, count)), device_id_type=MESH)
            for i, (src, dst) in enumerate(((tok_ref.at[tail], rim_ref), (ids_ref, rimids_ref)))]
    for copy in rims:
        copy.start()
    mine = []
    for i, (src, dst) in enumerate(zip(srcs, dsts)):
        local = pltpu.make_async_copy(src, dst.at[chip, core, z], local_sem.at[i])
        pair = pltpu.make_async_remote_copy(src, dst.at[chip, core, z], pair_send.at[i], pair_recv.at[i], device_id=sibling, device_id_type=MESH)
        local.start()
        pair.start()
        mine += [local, pair]
    for copy in mine:
        copy.wait()
    swap = ZSwap(((up_ref, gup_ref),), swap_local, swap_send, swap_recv, count)

    def role(which, first_bit, second_bit):
        subs = parts[which]
        first, second = (flip(dp, first_bit), z), (flip(dp, second_bit), z)
        first_chip, second_chip = flip(chip, first_bit // 2), flip(chip, second_bit // 2)
        both_chip = flip(first_chip, second_bit // 2)

        def copies(sub, at_chip, at_z, slot, to, send_s, recv_s):
            made = []
            for i, (ref, lo, size) in enumerate(subs[sub]):
                view = dsts[ref].at[at_chip, :, at_z, pl.ds(lo, size)]
                made.append(pltpu.make_async_remote_copy(view, view, send_s.at[sub, slot, i], recv_s.at[sub, slot, i], device_id=to, device_id_type=MESH))
            return made

        def start(made):
            for copy in made:
                copy.start()

        def wait_recv(made):
            for copy in made:
                copy.wait_recv()

        def along_first(sub, k):
            return copies(sub, chip, k, 4 + k, first, send, recv)

        def along_second(sub, k, far):
            return copies(sub, first_chip if far else chip, k, 8 + 4 * far + k, second, send, recv)

        def came_first(sub, k):
            return copies(sub, first_chip, k, 4 + k, first, send, recv)

        def came_second(sub, k, far):
            return copies(sub, both_chip if far else second_chip, k, 8 + 4 * far + k, second, send, recv)

        def share(sub, at_chip, k, offset):
            return copies(sub, at_chip, k, 4 * offset + k, sibling, share_send, share_recv)

        def up(sub, k):
            return copies(sub, chip, k, k + count * 5, (dp, z + 1), send, recv)

        def down(sub, k):
            return copies(sub, chip, k, k, (dp, z - 1), send, recv)

        both = range(len(subs))

        def spread(sub, k):
            start(along_first(sub, k))
            start(along_second(sub, k, 0))

        def rest(k):
            for sub in both:
                wait_recv(came_first(sub, k))
                start(along_second(sub, k, 1))
                start(share(sub, first_chip, k, 1))

        def below(hop, work):
            pl.when(z - hop >= 0)(lambda: work(z - hop))

        def above(hop, work):
            pl.when(z + hop <= count - 1)(lambda: work(z + hop))

        def from_below(k):
            for sub in both:
                wait_recv(up(sub, k))
                pl.when(z < count - 1)(lambda: start(up(sub, k)))
                spread(sub, k)
                start(share(sub, chip, k, 0))

        def from_above(k):
            for sub in both:
                wait_recv(down(sub, k))
                pl.when(z > 0)(lambda: start(down(sub, k)))
                spread(sub, k)
                start(share(sub, chip, k, 0))

        for sub in both:
            pl.when(z > 0)(lambda: start(down(sub, z)))
            pl.when(z < count - 1)(lambda: start(up(sub, z)))
            spread(sub, z)
        for hop in range(1, count):
            below(hop, from_below)
            above(hop, from_above)
            if hop == count - 2:
                swap.start()
            if hop == 1:
                rest(z)
            else:
                below(hop - 1, rest)
                above(hop - 1, rest)
        below(count - 1, rest)
        above(count - 1, rest)

        def finish(k, _):
            for far in (0, 1):
                for sub in both:
                    wait_recv(came_second(sub, k, far))
                    start(share(sub, both_chip if far else second_chip, k, 2 + far))
            return 0

        lax.fori_loop(0, count, finish, 0)

        def drain(k, _):
            def wait_send(made):
                for copy in made:
                    copy.wait_send()

            for sub in both:
                wait_send(along_first(sub, k) + along_second(sub, k, 0) + along_second(sub, k, 1))
                for offset, at_chip in ((1, first_chip), (2, second_chip), (3, both_chip)):
                    wait_send(share(sub, at_chip, k, offset))
                pl.when(k != z)(lambda: wait_send(share(sub, chip, k, 0)))
                pl.when((k <= z) & (z < count - 1))(lambda: wait_send(up(sub, k)))
                pl.when((k >= z) & (z > 0))(lambda: wait_send(down(sub, k)))
            return 0

        lax.fori_loop(0, count, drain, 0)

        def shared(k, _):
            for offset, at_chip in enumerate((chip, second_chip, first_chip, both_chip)):
                def wait():
                    for sub, chunks in enumerate(parts[1 - which]):
                        for i, (ref, lo, size) in enumerate(chunks):
                            view = dsts[ref].at[at_chip, :, k, pl.ds(lo, size)]
                            pltpu.make_async_remote_copy(view, view, share_send.at[sub, 4 * offset + k, i], share_recv.at[sub, 4 * offset + k, i], device_id=sibling, device_id_type=MESH).wait_recv()
                if offset:
                    wait()
                else:
                    pl.when(k != z)(wait)
            return 0

        lax.fori_loop(0, count, shared, 0)

    pl.when(core == 0)(lambda: role(0, 4, 2))
    pl.when(core == 1)(lambda: role(1, 2, 4))
    swap.wait()
    for copy in rims:
        copy.wait()


def gather_all(w_in, rest, up, tok, ids, cut, count):
    parts = ((((0, 0, 48),), ((0, 48, cut - 48),)), (((0, cut, 48),), ((0, cut + 48, w_in.shape[0] - cut - 48), (1, 0, rest.shape[0]))))
    shape = lambda a: jax.ShapeDtypeStruct((4, 2, count) + a.shape, a.dtype)
    sems = lambda *s: pltpu.SemaphoreType.DMA(s)
    return pl.pallas_call(
        functools.partial(gather_kernel, parts, count),
        in_specs=[pl.BlockSpec(memory_space=pl.ANY)] * 5,
        out_specs=[pl.BlockSpec(memory_space=pl.ANY)] * 5,
        out_shape=[shape(w_in), shape(rest), jax.ShapeDtypeStruct(up.shape, up.dtype),
                   jax.ShapeDtypeStruct((16, tok.shape[1]), tok.dtype), jax.ShapeDtypeStruct(ids.shape, ids.dtype)],
        scratch_shapes=[sems(2), sems(2, 24, 2), sems(2, 24, 2), sems(2, 16, 2), sems(2, 16, 2), sems(2), sems(2), sems(1), sems(1, count - 1), sems(1, count - 1), sems(2), sems(2)],
        compiler_params=pltpu.CompilerParams(collective_id=1, has_side_effects=True),
        cost_estimate=pl.CostEstimate(flops=0, bytes_accessed=200_000_000, transcendentals=0),
        name="gather_all",
    )(w_in, rest, up, tok, ids)


def scatter_kernel(parts, count, in_ref, rest_ref, proj_ref, oin_ref, orest_ref, oproj_ref, mine_a, mine_b, sib_a, sib_b, far_a, far_b, near_a, near_b, zgot_a, zgot_b, final_a, final_b,
                   load_sem, sib_send, sib_recv, two_send, two_recv, one_send, one_recv, z_send, z_recv, end_send, end_recv, end_local,
                   swap_local, swap_send, swap_recv):
    dp, z = lax.axis_index("dp"), lax.axis_index("seq")
    chip, core = dp // 2, lax.rem(dp, 2)
    srcs, outs = (in_ref, rest_ref), (oin_ref, orest_ref)
    mine, sib, far_got, near_got, z_got, final = (mine_a, mine_b), (sib_a, sib_b), (far_a, far_b), (near_a, near_b), (zgot_a, zgot_b), (final_a, final_b)
    sibling = (flip(dp, 1), z)
    peers = [(dp, lax.rem(z + j, count)) for j in range(1, count)]
    greet([sibling, (flip(dp, 4), z), (flip(dp, 2), z)] + peers)

    swap = ZSwap(((proj_ref, oproj_ref),), swap_local, swap_send, swap_recv, count)

    def role(which, first_bit, second_bit):
        chunks, other = parts[which], parts[1 - which]
        first, second = (flip(dp, first_bit), z), (flip(dp, second_bit), z)
        first_chip, second_chip = flip(chip, first_bit // 2), flip(chip, second_bit // 2)
        both_chip = flip(first_chip, second_bit // 2)
        steps = [lax.rem(z + 1 + j, count) for j in range(count)]

        def loads(col, k):
            slot = col * count + k
            return [pltpu.make_async_copy(srcs[ref].at[col, :, k, pl.ds(lo, size)], mine[ref].at[slot, :, pl.ds(0, size)], load_sem.at[slot, ref])
                    for ref, lo, size in chunks]

        def sibling_copies(col, k, pieces):
            slot = col * count + k
            return [pltpu.make_async_remote_copy(srcs[ref].at[col, :, k, pl.ds(lo, size)], sib[ref].at[slot, :, pl.ds(0, size)],
                                                 sib_send.at[slot, ref], sib_recv.at[slot, ref], device_id=sibling, device_id_type=MESH)
                    for ref, lo, size in pieces]

        def send(col, k, dst, slot, send_s, recv_s, to):
            return [pltpu.make_async_remote_copy(mine[ref].at[col * count + k, :, pl.ds(0, size)], dst[ref].at[slot, :, pl.ds(0, size)],
                                                 send_s.at[slot, ref], recv_s.at[slot, ref], device_id=to, device_id_type=MESH)
                    for ref, lo, size in chunks]

        def start(copies):
            for copy in copies:
                copy.start()

        def wait_recv(copies):
            for copy in copies:
                copy.wait_recv()

        def wait_send(copies):
            for copy in copies:
                copy.wait_send()

        def add(col, k, terms, last=False):
            slot = col * count + k
            for copy in loads(col, k):
                copy.wait()
            wait_recv(sibling_copies(col, k, chunks))
            for ref, lo, size in chunks:
                def rows(r, _):
                    at = pl.ds(pl.multiple_of(r * 16, 16), 16)
                    for c in range(2):
                        total = mine[ref][slot, c, at, :].astype(F32) + sib[ref][slot, c, at, :].astype(F32)
                        for buf, place in terms:
                            total = total + buf[ref][place, c, at, :].astype(F32)
                        if last:
                            final[ref][c, at, :] = total
                        else:
                            mine[ref][slot, c, at, :] = total.astype(BF)
                    return 0

                lax.fori_loop(0, size // 16, rows, 0)

        for k in steps:
            for col, sib_col in ((both_chip, both_chip), (second_chip, first_chip), (first_chip, second_chip), (chip, chip)):
                start(sibling_copies(sib_col, k, other) + loads(col, k))

        swap.start()

        def stage_one(k):
            for far, col in ((1, both_chip), (0, second_chip)):
                add(col, k, ())
                start(send(col, k, far_got, far * count + k, two_send, two_recv, second))

        def stage_two(k):
            wait_recv(send(first_chip, k, far_got, count + k, two_send, two_recv, second))
            add(first_chip, k, ((far_got, count + k),))
            start(send(first_chip, k, near_got, k, one_send, one_recv, first))

        def stage_three(j, k):
            wait_recv(send(chip, k, far_got, k, two_send, two_recv, second))
            wait_recv(send(chip, k, near_got, k, one_send, one_recv, first))
            if j < count - 1:
                add(chip, k, ((far_got, k), (near_got, k)))
                start(send(chip, k, z_got, j, z_send, z_recv, (dp, k)))

        for j in range(count + 2):
            if j < count:
                stage_one(steps[j])
            if 1 <= j <= count:
                stage_two(steps[j - 1])
            if j >= 2:
                stage_three(j - 2, steps[j - 2])

        for j in range(count - 1):
            wait_recv(send(chip, z, z_got, j, z_send, z_recv, (dp, z)))
        add(chip, z, ((far_got, z), (near_got, z)) + tuple((z_got, j) for j in range(count - 1)), last=True)
        locals_, remotes = [], []
        for ref, lo, size in chunks:
            locals_.append(pltpu.make_async_copy(final[ref].at[which, pl.ds(0, size)], outs[ref].at[pl.ds(lo, size)], end_local.at[ref]))
            remotes.append(pltpu.make_async_remote_copy(final[ref].at[1 - which, pl.ds(0, size)], outs[ref].at[pl.ds(lo, size)],
                                                        end_send.at[which, ref], end_recv.at[which, ref], device_id=sibling, device_id_type=MESH))
        start(locals_ + remotes)
        for copy in locals_:
            copy.wait()
        wait_send(remotes)
        for ref, lo, size in other:
            pltpu.make_async_remote_copy(final[ref].at[which, pl.ds(0, size)], outs[ref].at[pl.ds(lo, size)],
                                         end_send.at[1 - which, ref], end_recv.at[1 - which, ref], device_id=sibling, device_id_type=MESH).wait_recv()
        for j, k in enumerate(steps):
            for col in (chip, first_chip, second_chip, both_chip):
                wait_send(sibling_copies(col, k, other))
            wait_send(send(both_chip, k, far_got, count + k, two_send, two_recv, second))
            wait_send(send(second_chip, k, far_got, k, two_send, two_recv, second))
            wait_send(send(first_chip, k, near_got, k, one_send, one_recv, first))
            if j < count - 1:
                wait_send(send(chip, k, z_got, j, z_send, z_recv, (dp, k)))

    pl.when(core == 0)(lambda: role(0, 4, 2))
    pl.when(core == 1)(lambda: role(1, 2, 4))
    swap.wait()


def scatter_all(g_in, g_rest, proj, cut, collective_id):
    count = g_in.shape[2]
    rows_in, rows_rest = g_in.shape[3], g_rest.shape[3]
    parts = (((0, 0, cut),), ((0, cut, rows_in - cut), (1, 0, rows_rest)))
    sems = lambda *s: pltpu.SemaphoreType.DMA(s)
    places = 4 * count

    def bufs(k, kind=BF):
        lead = (k, 2) if k else (2,)
        return [pltpu.VMEM(lead + (max(cut, rows_in - cut), g_in.shape[4]), kind), pltpu.VMEM(lead + (rows_rest, g_rest.shape[4]), kind)]

    return pl.pallas_call(
        functools.partial(scatter_kernel, parts, count),
        in_specs=[pl.BlockSpec(memory_space=pl.ANY)] * 3,
        out_specs=[pl.BlockSpec(memory_space=pl.ANY)] * 3,
        out_shape=[jax.ShapeDtypeStruct(g_in.shape[3:], F32), jax.ShapeDtypeStruct(g_rest.shape[3:], F32), jax.ShapeDtypeStruct(proj.shape, proj.dtype)],
        scratch_shapes=bufs(places) + bufs(places) + bufs(2 * count) + bufs(count) + bufs(count - 1) + bufs(0, F32)
        + [sems(places, 2), sems(places, 2), sems(places, 2), sems(2 * count, 2), sems(2 * count, 2), sems(count, 2), sems(count, 2),
           sems(count - 1, 2), sems(count - 1, 2), sems(2, 2), sems(2, 2), sems(2), sems(1), sems(1, count - 1), sems(1, count - 1)],
        compiler_params=pltpu.CompilerParams(collective_id=collective_id, has_side_effects=True, vmem_limit_bytes=VM),
        cost_estimate=pl.CostEstimate(flops=0, bytes_accessed=200_000_000, transcendentals=0),
        name="scatter_all",
    )(g_in, g_rest, proj)


def unpack_kernel(own, x_cols, dt_cols, pack_ref, xt_ref, dtt_ref, high_ref, small_ref, tall):
    for b in range(pack_ref.shape[0]):
        block = pack_ref[b].astype(F32)
        tall[b * own : (b + 1) * own, :] = block[:own]
        small_ref[b : b + 1, :] = block[own : own + 1]
    for j in range(tall.shape[0] // 128):
        c = slice(j * 128, (j + 1) * 128)
        turned = tall[c, :].T
        for ref, lo, size in ((xt_ref, 0, x_cols), (dtt_ref, x_cols, dt_cols)):
            ref[:, c] = jnp.concatenate([turned[lo : lo + size], jnp.zeros((ref.shape[0] - size, 128), F32)], axis=0).astype(BF)
        high_ref[:, c] = turned[x_cols + dt_cols :]


def unpack(pack, own, x_cols, dt_cols):
    blocks, _, cols = pack.shape
    chans = blocks * own
    if own % 8:
        turned = pack[:, :own].reshape(chans, cols).T
        grown = lambda a: jnp.pad(a, ((0, 128 - a.shape[0]), (0, 0)))
        return grown(turned[:x_cols]), grown(turned[x_cols : x_cols + dt_cols]), turned[x_cols + dt_cols :].astype(F32), pack[:, own].astype(F32)
    return pl.pallas_call(
        functools.partial(unpack_kernel, own, x_cols, dt_cols),
        out_shape=[jax.ShapeDtypeStruct((128, chans), BF)] * 2 + [jax.ShapeDtypeStruct((cols - x_cols - dt_cols, chans), F32), jax.ShapeDtypeStruct((blocks, cols), F32)],
        scratch_shapes=[pltpu.VMEM((chans, cols), F32)],
        compiler_params=pltpu.CompilerParams(vmem_limit_bytes=VM),
        name="unpack_small",
    )(pack)


def pack_kernel(own, sizes, x_ref, dt_ref, log_ref, taps_ref, dtb_ref, skip_ref, small_ref, out_ref, wide, tall):
    at = 0
    for ref, size in zip((x_ref, dt_ref, log_ref, taps_ref, dtb_ref, skip_ref), sizes):
        wide[at : at + size, :] = ref[0:size, :]
        at += size
    wide[at:, :] = jnp.zeros((wide.shape[0] - at, wide.shape[1]), F32)
    for j in range(tall.shape[0] // 128):
        tall[j * 128 : (j + 1) * 128, :] = wide[:, j * 128 : (j + 1) * 128].T
    cols = wide.shape[0]
    first = lax.broadcasted_iota(jnp.int32, (8, cols), 0) == 0
    for b in range(out_ref.shape[0]):
        tail = jnp.where(first, jnp.broadcast_to(small_ref[b : b + 1, :], (8, cols)), 0.0)
        out_ref[b] = jnp.concatenate([tall[b * own : (b + 1) * own, :], tail], axis=0).astype(BF)


def pack_grads(parts, sizes, small, own):
    blocks, cols = small.shape
    chans = parts[0].shape[1]
    rows = own + -own % 16
    if own % 8:
        turned = jnp.concatenate([part[:size] for part, size in zip(parts, sizes)]).T.reshape(blocks, own, -1)
        turned = jnp.pad(turned, ((0, 0), (0, 0), (0, cols - turned.shape[2])))
        return jnp.concatenate([turned, small[:, None], jnp.zeros((blocks, rows - own - 1, cols), F32)], axis=1).astype(BF)
    return pl.pallas_call(
        functools.partial(pack_kernel, own, sizes),
        out_shape=jax.ShapeDtypeStruct((blocks, rows, cols), BF),
        scratch_shapes=[pltpu.VMEM((cols, chans), F32), pltpu.VMEM((chans, cols), F32)],
        compiler_params=pltpu.CompilerParams(vmem_limit_bytes=VM),
        name="pack_small",
    )(*parts, small)


def finish_kernel(own, cuts, pack_ref, up_ref, down_ref, proj_ref, up_out, down_out, row_out, proj_out, *small_outs):
    up_out[0] = up_ref[0].astype(F32)
    down_out[0] = down_ref[0].astype(F32)

    @pl.when(pl.program_id(0) == 0)
    def _():
        row_out[...] = pack_ref[own : own + 1, :]
        proj_out[...] = sum(proj_ref[k].astype(F32) for k in range(proj_ref.shape[0]))[:own]
        tall = pack_ref[...]
        turned = jnp.concatenate([tall, jnp.zeros((-tall.shape[0] % 128, tall.shape[1]), F32)], axis=0).T
        for (lo, size, turn), out in zip(cuts, small_outs):
            out[...] = turned[lo : lo + size, :own] if turn else pack_ref[0:own, lo : lo + size]


def finish(pack, up, down, proj, own, cuts):
    experts, piece, width = up.shape
    if own % 8:
        small = [pack[:own, lo : lo + size].T if turn else pack[:own, lo : lo + size] for lo, size, turn in cuts]
        return [up.astype(F32), down.astype(F32), pack[own : own + 1], jnp.sum(proj[:, :own].astype(F32), axis=0)] + small
    whole = lambda shape: pl.BlockSpec(shape, lambda e: (0,) * len(shape))
    part = lambda shape: pl.BlockSpec((1,) + shape[1:], lambda e: (e, 0, 0))
    shapes = [(experts, piece, width)] * 2 + [(1, pack.shape[1]), (own, width)] + [(size, own) if turn else (own, size) for _, size, turn in cuts]
    return pl.pallas_call(
        functools.partial(finish_kernel, own, cuts),
        grid=(experts,),
        in_specs=[whole(pack.shape), part(up.shape), part(up.shape), whole(proj.shape)],
        out_specs=[part(shapes[0]), part(shapes[1])] + [whole(s) for s in shapes[2:]],
        out_shape=[jax.ShapeDtypeStruct(s, F32) for s in shapes],
        compiler_params=pltpu.CompilerParams(vmem_limit_bytes=VM),
        name="finish",
    )(pack, up, down, proj)


def pack_params_kernel(x_ref, dt_ref, log_ref, taps_ref, bias_ref, dtb_ref, skip_ref, small_ref, out_ref, thin, tall):
    own, x_cols = x_ref.shape
    thin[...] = jnp.zeros_like(thin)
    at = 0
    for ref in (log_ref, taps_ref, bias_ref, dtb_ref, skip_ref):
        thin[at : at + ref.shape[0], 0:own] = ref[...].astype(F32)
        at += ref.shape[0]
    tall[...] = jnp.zeros_like(tall)
    at = x_cols + dt_ref.shape[1]
    tall[0:own, 0:x_cols] = x_ref[...].astype(F32)
    tall[0:own, x_cols:at] = dt_ref[...].astype(F32)
    tall[0:own, at : at + thin.shape[0]] = thin[...].T[:own]
    tall[own : own + 1, 0 : small_ref.shape[1]] = small_ref[...].astype(F32)
    out_ref[...] = tall[...].astype(BF)


def pack_params(w_x, w_dt, log_t, taps_t, bias, dtb, skip, small):
    own = w_x.shape[0]
    rows = own + -own % 16
    if own % 8:
        wide = jnp.concatenate([w_x, w_dt, log_t.T, taps_t.T, bias.T, dtb.T, skip.T], axis=1)
        wide = jnp.pad(wide, ((0, -own % 16), (0, 256 - wide.shape[1])))
        return wide + jnp.pad(small, ((own, -own % 16 - 1), (0, 256 - small.shape[1])))
    return pl.pallas_call(
        pack_params_kernel,
        out_shape=jax.ShapeDtypeStruct((rows, 256), BF),
        scratch_shapes=[pltpu.VMEM((32, 128), F32), pltpu.VMEM((rows, 256), F32)],
        name="pack_params",
    )(w_x, w_dt, log_t, taps_t, bias, dtb, skip, small)


def chain_kernel(step, pieces, carry_ref, own_ref, out_ref, inbox, outbox, send, recv):
    dp, z = lax.axis_index("dp"), lax.axis_index("seq")
    last = lax.axis_size("seq") - 1
    has_before = z > 0 if step > 0 else z < last
    has_after = z < last if step > 0 else z > 0
    barrier = pltpu.get_barrier_semaphore()

    def neighbours(act):
        pl.when(has_before)(lambda: act(z - step))
        pl.when(has_after)(lambda: act(z + step))

    neighbours(lambda peer: pl.semaphore_signal(barrier, inc=1, device_id=(dp, peer), device_id_type=MESH))
    count = last + 1
    pl.semaphore_wait(barrier, (z + last) // count + (2 * last - z) // count)
    wide = own_ref.shape[1] // pieces

    def copy(g):
        return pltpu.make_async_remote_copy(outbox.at[g], inbox.at[g], send.at[g], recv.at[g], device_id=(dp, z + step), device_id_type=MESH)

    def back(g):
        return pltpu.make_async_remote_copy(outbox.at[g], inbox.at[g], send.at[g], recv.at[g], device_id=(dp, z - step), device_id_type=MESH)

    for g in range(pieces):
        c = slice(g * wide, (g + 1) * wide)

        @pl.when(has_before)
        def _():
            back(g).wait_recv()
            out_ref[:, c] = inbox[g].astype(F32)

        @pl.when(jnp.logical_not(has_before))
        def _():
            out_ref[:, c] = jnp.zeros((out_ref.shape[0], wide), F32)

        @pl.when(has_after)
        def _():
            outbox[g] = (carry_ref[:, c] * out_ref[:, c] + own_ref[:, c]).astype(BF)
            copy(g).start()

    @pl.when(has_after)
    def _():
        for g in range(pieces):
            copy(g).wait_send()


def chain(carry, own, step, collective_id):
    pieces = 3
    n, chans = own.shape
    return pl.pallas_call(
        functools.partial(chain_kernel, step, pieces),
        in_specs=[pl.BlockSpec(memory_space=pltpu.VMEM)] * 2,
        out_specs=pl.BlockSpec(memory_space=pltpu.VMEM),
        out_shape=jax.ShapeDtypeStruct((n, chans), F32),
        scratch_shapes=[pltpu.VMEM((pieces, n, chans // pieces), BF)] * 2 + [pltpu.SemaphoreType.DMA((pieces,))] * 2,
        compiler_params=pltpu.CompilerParams(collective_id=collective_id, has_side_effects=True),
        name="chain",
    )(carry, own)


def experts_kernel(block, piece, pick_ref, n2_ref, go_ref, router_ref, up_hbm, down_hbm, back_ref, late_ref, mixed_ref, grouter_ref, gexp_hbm,
                   up, down, gup, gdown, outbox, inbox, ret, total, disp, load_sem, store_sem, own_sem, out_send, out_recv, back_own, back_send, back_recv):
    dp, z = lax.axis_index("dp"), lax.axis_index("seq")
    count = lax.axis_size("seq")
    peers = [lax.rem(z + j, count) for j in range(1, count)]
    blocks = up.shape[0] // block
    rows, width = total.shape
    each = rows // count

    def loads(b):
        at = pl.ds(pl.multiple_of(b * block, block), block)
        return [pltpu.make_async_copy(up_hbm.at[at], up.at[at], load_sem.at[b, 0]), pltpu.make_async_copy(down_hbm.at[at], down.at[at], load_sem.at[b, 1])]

    def stores(b):
        made = []
        for i in range(block // piece):
            at = pl.ds(pl.multiple_of(b * block + i * piece, 16), piece)
            to = b * (block // piece) + i
            made.append(pltpu.make_async_copy(gup.at[at], gexp_hbm.at[to, 0], store_sem.at[to, 0]))
            made.append(pltpu.make_async_copy(gdown.at[at], gexp_hbm.at[to, 1], store_sem.at[to, 1]))
        return made

    def send(half, j):
        return pltpu.make_async_remote_copy(outbox.at[half, peers[j]], inbox.at[half, z], out_send.at[half, j], out_recv.at[half, j], device_id=(dp, peers[j]), device_id_type=MESH)

    def came(half, j):
        return pltpu.make_async_remote_copy(outbox.at[half, z], inbox.at[half, lax.rem(z + count - 1 - j, count)], out_send.at[half, j], out_recv.at[half, j], device_id=(dp, z), device_id_type=MESH)

    def kept(half):
        return pltpu.make_async_copy(outbox.at[half, z], inbox.at[half, z], own_sem.at[half])

    def give(half, j):
        return pltpu.make_async_remote_copy(ret.at[half, peers[j]], back_ref.at[z], back_send.at[half, j], back_recv.at[half, j], device_id=(dp, peers[j]), device_id_type=MESH)

    def got(half, j):
        return pltpu.make_async_remote_copy(ret.at[half, z], back_ref.at[lax.rem(z + count - 1 - j, count)], back_send.at[half, j], back_recv.at[half, j], device_id=(dp, z), device_id_type=MESH)

    def give_own(half):
        return pltpu.make_async_copy(ret.at[half, z], back_ref.at[z], back_own.at[half])

    greet([(dp, peer) for peer in peers])
    for half in range(2):
        picked = lax.dot_general(pick_ref[:, half * rows : (half + 1) * rows], n2_ref[...], TN, preferred_element_type=F32)
        outbox[half] = picked.astype(BF).reshape(count, each, width)
        for j in range(count - 1):
            send(half, j).start()
        kept(half).start()
    for b in range(blocks):
        for copy in loads(b):
            copy.start()
    lanes = lax.broadcasted_iota(jnp.int32, (rows, router_ref.shape[1]), 1)
    mine = (lanes == z).astype(F32)
    for half in range(2):
        kept(half).wait()
        for j in range(count - 1):
            came(half, j).wait_recv()
        slots = inbox[half].reshape(rows, width)
        go = go_ref[:, half * each : (half + 1) * each, :].reshape(rows, width).astype(F32)
        logits = jnp.where(lanes < count, jnp.dot(slots, router_ref[...], preferred_element_type=F32), -1e30)
        powers = jnp.exp(logits - jnp.max(logits, axis=1, keepdims=True))
        probs = jnp.where(lanes < count, powers / jnp.sum(powers, axis=1, keepdims=True), 0.0)
        gate = jnp.sum(probs * mine, axis=1, keepdims=True)
        grads = (gate * go).astype(BF)
        total[...] = jnp.zeros_like(total)
        disp[...] = jnp.zeros_like(disp)

        def units(b, _):
            at = pl.ds(pl.multiple_of(b * block, block), block)
            if half == 0:
                for copy in loads(b):
                    copy.wait()
            hidden = lax.dot_general(slots, up[at, :], NT, preferred_element_type=F32)
            phi = 0.5 * (1.0 + lax.erf(hidden * (1.0 / math.sqrt(2.0))))
            act = (hidden * phi).astype(BF)
            slope = phi + hidden * jnp.exp(hidden * hidden * -0.5) * (1.0 / math.sqrt(2.0 * math.pi))
            ghid = (lax.dot_general(grads, down[at, :], NT, preferred_element_type=F32) * slope).astype(BF)
            total[...] += jnp.dot(act, down[at, :], preferred_element_type=F32)
            disp[...] += jnp.dot(ghid, up[at, :], preferred_element_type=F32)
            new_up = lax.dot_general(ghid, slots, TN, preferred_element_type=F32)
            new_down = lax.dot_general(act, grads, TN, preferred_element_type=F32)
            if half == 0:
                gup[at, :] = new_up.astype(BF)
                gdown[at, :] = new_down.astype(BF)
            else:
                gup[at, :] = (gup[at, :].astype(F32) + new_up).astype(BF)
                gdown[at, :] = (gdown[at, :].astype(F32) + new_down).astype(BF)
                for copy in stores(b):
                    copy.start()
            return 0

        lax.fori_loop(0, blocks, units, 0)
        expert_out = total[...]
        mixed_ref[:, half * each : (half + 1) * each, :] = (gate * expert_out).astype(BF).reshape(count, each, width)
        grad_gate = jnp.sum(go * expert_out, axis=1, keepdims=True)
        grad_logits = (grad_gate * gate * (mine - probs)).astype(BF)
        grad_n2 = disp[...] + lax.dot_general(grad_logits, router_ref[...], NT, preferred_element_type=F32)
        if half == 0:
            ret[half] = grad_n2.astype(BF).reshape(count, each, width)
            for j in range(count - 1):
                give(half, j).start()
            give_own(half).start()
        else:
            late_ref[...] = grad_n2.astype(BF).reshape(count, each, width)
        grouter = lax.dot_general(slots, grad_logits, TN, preferred_element_type=F32)
        if half == 0:
            grouter_ref[...] = grouter
        else:
            grouter_ref[...] += grouter
    for b in range(blocks):
        for copy in stores(b):
            copy.wait()
    give_own(0).wait()
    for j in range(count - 1):
        send(0, j).wait_send()
        send(1, j).wait_send()
        give(0, j).wait_send()
        got(0, j).wait_recv()


def experts_pass(pick, n2, go, router, up, down, block, piece, collective_id):
    count, slots, width = go.shape
    units = up.shape[0]
    rows = count * slots // 2
    vmem = pl.BlockSpec(memory_space=pltpu.VMEM)
    hbm = pl.BlockSpec(memory_space=pl.ANY)
    sems = lambda *s: pltpu.SemaphoreType.DMA(s)
    blocks = units // block
    return pl.pallas_call(
        functools.partial(experts_kernel, block, piece),
        in_specs=[vmem] * 4 + [hbm] * 2,
        out_specs=[hbm, vmem, vmem, vmem, hbm],
        out_shape=[jax.ShapeDtypeStruct((count, slots // 2, width), BF)] * 2 + [jax.ShapeDtypeStruct((count, slots, width), BF), jax.ShapeDtypeStruct(router.shape, F32),
                   jax.ShapeDtypeStruct((units // piece, 2, piece, width), BF)],
        scratch_shapes=[pltpu.VMEM(up.shape, BF)] * 4
        + [pltpu.VMEM((2, count, slots // 2, width), BF)] * 2 + [pltpu.VMEM((1, count, slots // 2, width), BF)] + [pltpu.VMEM((rows, width), F32)] * 2
        + [sems(blocks, 2), sems(units // piece, 2), sems(2), sems(2, count - 1), sems(2, count - 1), sems(1), sems(1, count - 1), sems(1, count - 1)],
        compiler_params=pltpu.CompilerParams(collective_id=collective_id, has_side_effects=True, vmem_limit_bytes=VM),
        cost_estimate=pl.CostEstimate(flops=24 * rows * units * width, bytes_accessed=100_000_000, transcendentals=4 * rows * units),
        name="experts",
    )(pick, n2, go, router, up, down)


def dot(a, b):
    return jnp.dot(a, b, preferred_element_type=F32)


def dot_nt(a, b):
    return lax.dot_general(a, b, NT, preferred_element_type=F32)


def dot_tn(a, b):
    return lax.dot_general(a, b, TN, preferred_element_type=F32)


def shift(value, axis, steps):
    count = lax.axis_size(axis)
    first, last = (max(0, -steps), min(count, count - steps))
    return lax.ppermute(value, axis, [(source, source + steps) for source in range(first, last)])


def rms_scale(value):
    return lax.rsqrt(jnp.mean(value * value, axis=-1, keepdims=True) + EPS)


def rms_back(value, gain, grad):
    scale = rms_scale(value)
    scaled = grad * gain
    grad_gain = jnp.sum(grad * (value * scale), axis=0)
    return scale * scaled - value * (scale * scale * scale) * jnp.mean(value * scaled, axis=-1, keepdims=True), grad_gain


def swap(value):
    return lax.all_to_all(value, "seq", 0, 0)


def shards(tokens, segment_ids, routes, cotangent, small_params, w_in, conv_w, conv_b, w_x, w_dt, dt_bias, a_log, d_skip, w_out, w_up, w_down):
    both = ("dp", "seq")
    devices = lax.axis_size(both)
    width = tokens.shape[2]
    rows = tokens.shape[1]
    experts = w_up.shape[0]
    chans = w_in.shape[0] * devices // 2
    own = w_out.shape[0]
    rank = w_dt.shape[1]
    n = a_log.shape[1]
    taps = conv_w.shape[1]
    slots = rows // 2
    halo = 16
    wide = 768

    tok_b = tokens[0]
    seg_plus = segment_ids[0] + 1

    share = small_params.shape[0]
    packed = pack_params(w_x, w_dt, a_log.T, conv_w.T, conv_b[None], dt_bias[None], d_skip[None], small_params[None])
    direct = lax.axis_size("dp") == 8 and lax.axis_size("seq") == 4
    up_t = jnp.swapaxes(w_up, 1, 2)
    full_out = lax.all_gather(w_out, both, axis=0, tiled=True)
    if direct:
        last_ids = jnp.broadcast_to(seg_plus[rows - halo :, None], (halo, 128))
        all_in, all_pack, part_up, rim_tok, rim_ids = gather_all(w_in, packed, up_t, tok_b, last_ids, 80, 4)
        down_late, all_in = lax.optimization_barrier((w_down, all_in))
        part_down = swap(down_late)
        rim_ids = jnp.where(lax.axis_index("seq") > 0, rim_ids[:, 0], 0)
    else:
        all_in, all_pack = lax.all_gather(w_in, both), lax.all_gather(packed, both)
        part_up, part_down = swap(up_t), swap(w_down)
        rim_tok = shift(tok_b[rows - halo :], "seq", 1)
        rim_ids = shift(seg_plus[rows - halo :], "seq", 1)
    full_in = lax.optimization_barrier(all_in.reshape(2 * chans, width))
    full_x_t, full_dt_t, high_t, small = unpack(all_pack.reshape(devices, -1, 256), own, w_x.shape[1], rank)
    small, part_up = lax.optimization_barrier((small, part_up))
    full_up = lax.all_gather(part_up, "dp", axis=0).reshape(-1, width)
    alog_t, conv_f, bias_row, dtb_row, skip = high_t[:n], high_t[n : n + taps], high_t[n + taps : n + taps + 1], high_t[n + taps + 1 : n + taps + 2], high_t[n + taps + 2 : n + taps + 3]
    flat_small = small[:, :share].reshape(-1)
    gain_one = flat_small[:width]
    gain_two = flat_small[width : 2 * width]
    router = flat_small[2 * width :].reshape(width, experts).astype(BF)
    route_ids = routes[0]
    onehot = (route_ids == jnp.arange(experts)[None, :]).astype(BF)
    before = (jnp.arange(rows)[:, None] > jnp.arange(rows)[None, :]).astype(BF)
    place = jnp.sum(dot(before, onehot) * onehot.astype(F32), axis=1).astype(jnp.int32)
    slot_of = route_ids[:, 0] * slots + place
    gather_mat = (slot_of[:, None] == jnp.arange(experts * slots)[None, :]).astype(BF)
    half = slots // 2
    pick_of = place // half * (experts * half) + route_ids[:, 0] * half + place % half
    pick = (pick_of[:, None] == jnp.arange(experts * slots)[None, :]).astype(BF)
    grad_out_b = cotangent[0]
    grad_out = grad_out_b.astype(F32)
    tok_ext = jnp.concatenate([rim_tok, tok_b]).astype(F32)
    tok_f = tok_b.astype(F32)
    ids_ext = jnp.concatenate([rim_ids, seg_plus])
    same = jnp.stack([ids_ext[halo - taps + 1 + k : halo - taps + 1 + k + rows] == seg_plus for k in range(taps)], axis=1).astype(F32)
    keep = same[:, taps - 2 : taps - 1]
    normed_ext = (tok_ext * rms_scale(tok_ext) * gain_one).astype(BF)
    normed = normed_ext[halo:]
    conv_in, conv_sum, values, z, projected = front(normed_ext, normed, full_in, full_x_t, conv_f, bias_row, same, halo, wide)
    low_wide, b_wide, c_wide, b_blk, c_blk, pre_dt, dt, dt_keep, dtx, rates, rates2, own_state, carry = steps(projected, keep, values, full_dt_t, dtb_row, alog_t, rank, wide)
    carry, part_down = lax.optimization_barrier((carry, part_down))
    full_down = lax.all_gather(part_down, "dp", axis=0).reshape(-1, width)
    start = chain(carry, own_state, 1, 3)
    go_local, start = lax.optimization_barrier((dot_tn(gather_mat, grad_out_b).astype(BF), start))
    go_slots = swap(go_local.reshape(experts, slots, width))
    scanned, checks, gated, first_sum, normed_two = scan_pass(
        dt_keep, dtx, rates2, b_wide, c_blk, start, values, z, skip, full_out, tok_b, gain_two[None], wide
    )
    normed_two, go_slots = lax.optimization_barrier((normed_two, go_slots))
    sig_z = jax.nn.sigmoid(z)

    piece = w_up.shape[2]
    router_wide = jnp.pad(router, ((0, 0), (0, 128 - experts)))
    back_n2, late_n2, mixed_back, grad_router, grad_exp = experts_pass(pick, normed_two, go_slots, router_wide, full_up, full_down, 768, piece if piece % 16 == 0 else 768, 5)
    grad_router = grad_router[:, :experts]
    late_n2 = swap(late_n2)
    grad_n2 = dot(pick, jnp.concatenate([back_n2.reshape(-1, width), late_n2.reshape(-1, width)]))
    mixed_slots = swap(mixed_back).reshape(-1, width)
    if piece % 16:
        grad_exp = jnp.swapaxes(jnp.swapaxes(grad_exp, 0, 1).reshape(2, -1, piece, width), 0, 1)
    part_exp = lax.psum_scatter(grad_exp.reshape(-1, width), "dp", scatter_dimension=0, tiled=True)

    grad_norm_two, grad_gain_two = rms_back(first_sum, gain_two, grad_n2)
    grad_first = grad_out + grad_norm_two
    grad_mixer = grad_first.astype(BF)
    grad_w_out = dot_tn(gated, grad_mixer).astype(BF)
    grad_gated = dot_nt(grad_mixer, full_out)
    silu_z = z * sig_z
    grad_scanned = grad_gated * silu_z
    grad_z = grad_gated * (scanned + skip * values) * (sig_z * (1.0 + z * (1.0 - sig_z)))
    grad_z_b = grad_z.astype(BF)
    grad_start = back_state_pass(dt_keep, grad_scanned, rates2, c_wide, wide)
    nxt = chain(carry, grad_start, -1, 4)
    nxt, grad_w_out = lax.optimization_barrier((nxt, grad_w_out))
    grad_vals, g_log, grad_dt_t, grad_dtb, grad_skip, grad_proj = back_pass(
        dt, dt_keep, dtx, grad_scanned, values, pre_dt, skip, rates2, rates, b_wide, c_wide, b_blk, checks, nxt, low_wide, full_dt_t, rank, wide
    )
    grad_vals, mixed_slots, part_exp, grad_w_out = lax.optimization_barrier((grad_vals, mixed_slots, part_exp, grad_w_out))
    sum_exp = swap(part_exp.reshape(experts, 2, piece, width))
    mixed_out = (first_sum + dot(gather_mat, mixed_slots)).astype(BF)
    grad_conv_b, grad_last, grad_rim, grad_x_t, grad_taps = conv_back(grad_vals, grad_proj, full_x_t, values, conv_sum, conv_in, same, conv_f, halo, wide)
    grad_last = (grad_last + shift(grad_rim, "seq", -1)).astype(BF)
    grad_conv_in = jnp.concatenate([grad_conv_b[: rows - 8], grad_last])
    grad_w_in = dot_tn(jnp.concatenate([grad_conv_in, grad_z_b], axis=1), normed).astype(BF)
    grad_normed = dot(grad_conv_in, full_in[:chans]) + dot(grad_z_b, full_in[chans:])
    grad_norm_one, grad_gain_one = rms_back(tok_f, gain_one, grad_normed)
    tokens_grad = (grad_first + grad_norm_one).astype(BF)

    grad_small = jnp.concatenate([grad_gain_one, grad_gain_two, grad_router.reshape(-1)])
    grad_packed = pack_grads(
        (grad_x_t, grad_dt_t, g_log, grad_taps, grad_dtb, grad_skip), (w_x.shape[1], rank, n, taps + 1, 1, 1), jnp.pad(grad_small.reshape(devices, -1), ((0, 0), (0, 256 - share))), own
    )
    part_out = lax.psum_scatter(grad_w_out, "dp", scatter_dimension=0, tiled=True).reshape(-1, own, width)
    part_out = jnp.pad(part_out, ((0, 0), (0, -own % 16), (0, 0)))
    if direct:
        grad_packed, sum_exp = lax.optimization_barrier((grad_packed, sum_exp))
        sum_in, sum_pack, all_out = scatter_all(
            grad_w_in.reshape(4, 2, 4, 2 * own, width), grad_packed.reshape((4, 2, 4) + grad_packed.shape[1:]), part_out, 80, 2
        )
    else:
        sum_in = lax.psum_scatter(grad_w_in, both, scatter_dimension=0, tiled=True).astype(F32)
        sum_pack = lax.psum_scatter(grad_packed, both, scatter_dimension=0, tiled=True)[0].astype(F32)
        all_out = swap(part_out)
    cuts, at = [], 0
    for size, turn in ((w_x.shape[1], False), (rank, False), (n, True), (taps, True), (1, True), (1, True), (1, True)):
        cuts.append((at, size, turn))
        at += size
    up_out, down_out, s_row, sum_out, s_x, s_dt, s_log, s_conv, s_bias, s_dtb, s_skip = finish(sum_pack, sum_exp[:, 0], sum_exp[:, 1], all_out, own, tuple(cuts))
    return (
        mixed_out[None],
        tokens_grad[None],
        s_row[0, :share],
        sum_in,
        s_conv.T,
        s_bias[0],
        s_x,
        s_dt,
        s_dtb[0],
        s_log.T,
        s_skip[0],
        sum_out,
        jnp.swapaxes(up_out, 1, 2),
        down_out,
    )


def solution(mesh):
    split = ("dp", "seq")
    token, row, mat, vec = P("dp", "seq", None), P("dp", "seq"), P(split, None), P(split)
    return jax.shard_map(
        shards,
        mesh=mesh,
        in_specs=(token, row, token, token, vec, mat, mat, vec, mat, mat, vec, mat, vec, mat, P(None, None, split), P(None, split, None)),
        out_specs=(token, token, vec, mat, mat, vec, mat, mat, vec, mat, vec, mat, P(None, None, split), P(None, split, None)),
        check_vma=False,
    )
```

```python
import functools
import math

import jax
import jax.numpy as jnp
from jax import lax
from jax.experimental import pallas as pl
from jax.experimental.pallas import tpu as pltpu
from jax.sharding import PartitionSpec as P

F32, BF = jnp.float32, jnp.bfloat16
EPS = 1e-05
STEP = 16
VM = 56 * 1024 * 1024
MESH = pl.DeviceIdType.MESH
SMALL = pl.CostEstimate(flops=0, bytes_accessed=0, transcendentals=0)
NT = (((1,), (1,)), ((), ()))
TN = (((0,), (0,)), ((), ()))


def rowb(block, i, n):
    return jnp.broadcast_to(block[i:i+1, :], (n, block.shape[1]))

def state_kernel(n, dte_ref, dtx_ref, rate_ref, b_ref, state_ref, carry_ref):
    rows, wide = dte_ref.shape
    tiles = wide // 128
    rates = [rate_ref[:, j*128:(j+1)*128] for j in range(tiles)]
    def block(k, carry):
        state, total = carry
        at = pl.multiple_of(k * STEP, STEP)
        dte = dte_ref[pl.ds(at, STEP), :]
        dtx = dtx_ref[pl.ds(at, STEP), :]
        state = list(state)
        for i in range(STEP):
            bs = b_ref[pl.ds((at + i) * n, n), :]
            for j in range(tiles):
                c = slice(j*128, (j+1)*128)
                decay = jnp.exp2(rowb(dte[:, c], i, n) * rates[j])
                state[j] = decay * state[j] + bs * rowb(dtx[:, c], i, n)
        return tuple(state), total + dte
    zero = tuple(jnp.zeros((n, 128), F32) for _ in range(tiles))
    state, total = lax.fori_loop(0, rows // STEP, block, (zero, jnp.zeros((STEP, wide), F32)))
    summed = jnp.sum(total, axis=0, keepdims=True)
    for j in range(tiles):
        c = slice(j*128, (j+1)*128)
        state_ref[:, c] = state[j]
        carry_ref[:, c] = jnp.exp2(jnp.broadcast_to(summed[:, c], (n, 128)) * rates[j])

def front_kernel(rim_ref, tok_ref, gain_ref, wc_ref, wz_ref, xt_ref, taps_ref, bias_ref, same_ref, normed_ref, conv_ref, sum_ref, values_ref, z_ref, proj_ref, ext):
    rows, wide = sum_ref.shape
    halo = rim_ref.shape[0]
    taps = taps_ref.shape[0]

    @pl.when(pl.program_id(0) == 0)
    def _():
        for ref, lo in ((rim_ref, 0), (tok_ref, halo)):
            tok = ref[...].astype(F32)
            scale = lax.rsqrt(jnp.mean(tok * tok, axis=1, keepdims=True) + EPS)
            ext[lo : lo + ref.shape[0], :] = (tok * scale * gain_ref[...]).astype(BF)
        normed_ref[...] = ext[halo:, :]
        proj_ref[...] = jnp.zeros_like(proj_ref)

    conv_ref[...] = lax.dot_general(ext[...], wc_ref[...], NT, preferred_element_type=F32).astype(BF).astype(F32)
    z_ref[...] = lax.dot_general(ext[halo:, :], wz_ref[...], NT, preferred_element_type=F32)
    same = [jnp.broadcast_to(same_ref[:, k : k + 1], (rows, 128)) for k in range(taps)]
    for j in range(wide // 128):
        c = slice(j * 128, (j + 1) * 128)
        total = jnp.broadcast_to(bias_ref[:, c], (rows, 128))
        for k in range(taps):
            lo = halo - taps + 1 + k
            total = total + taps_ref[k : k + 1, c] * conv_ref[lo : lo + rows, c] * same[k]
        sum_ref[:, c] = total
        values_ref[:, c] = total * jax.nn.sigmoid(total)
    proj_ref[...] += lax.dot_general(values_ref[...].astype(BF), xt_ref[...], NT, preferred_element_type=F32)


def front(rim, tok, gain, full_in, x_t, conv_taps, bias, same, wide):
    rows, width = tok.shape
    halo = rim.shape[0]
    chans = full_in.shape[0] // 2
    taps = conv_taps.shape[0]
    col = lambda r: pl.BlockSpec((r, wide), lambda g: (0, g))
    whole = lambda a: pl.BlockSpec(a.shape, lambda g: (0, 0))
    steps = chans // wide
    f32 = lambda r: jax.ShapeDtypeStruct((r, chans), F32)
    return pl.pallas_call(
        front_kernel,
        grid=(steps,),
        in_specs=[whole(rim), whole(tok), whole(gain), pl.BlockSpec((wide, width), lambda g: (g, 0)), pl.BlockSpec((wide, width), lambda g: (g + steps, 0)),
                  col(128), col(taps), col(1), whole(same)],
        out_specs=[whole(tok), col(rows + halo), col(rows), col(rows), col(rows), pl.BlockSpec((rows, 128), lambda g: (0, 0))],
        out_shape=[jax.ShapeDtypeStruct((rows, width), BF), f32(rows + halo), f32(rows), f32(rows), f32(rows), jax.ShapeDtypeStruct((rows, 128), F32)],
        scratch_shapes=[pltpu.VMEM((rows + halo, width), BF)],
        compiler_params=pltpu.CompilerParams(vmem_limit_bytes=VM),
        cost_estimate=pl.CostEstimate(flops=4*rows*chans*width, bytes_accessed=4*chans*width + 16*rows*chans, transcendentals=rows*chans),
        name="front",
    )(rim, tok, gain, full_in, full_in, x_t, conv_taps, bias, same)


def steps_kernel(n, rank_cols, proj_ref, keep_ref, values_ref, dtt_ref, dtb_ref, alog_ref,
                 low_ref, bw_ref, cw_ref, bblk_ref, cblk_ref, pre_ref, dt_ref, dte_ref, dtx_ref, rate_ref, rate2_ref, state_ref, carry_ref):
    rows, wide = pre_ref.shape
    groups = STEP * n

    @pl.when(pl.program_id(0) == 0)
    def _():
        proj = proj_ref[...]
        lanes = lax.broadcasted_iota(jnp.int32, proj.shape, 1)
        low_ref[...] = jnp.where(lanes < rank_cols, proj, 0.0).astype(BF)
        row = lax.broadcasted_iota(jnp.int32, (rows, groups), 0)
        col = lax.broadcasted_iota(jnp.int32, (rows, groups), 1)
        own = lax.rem(row, STEP) == col // n
        to_col = lax.rem(lax.broadcasted_iota(jnp.int32, (128, groups), 1), n)
        from_col = lax.broadcasted_iota(jnp.int32, (128, groups), 0)
        for i, (wide_ref, blk_ref) in enumerate(((bw_ref, bblk_ref), (cw_ref, cblk_ref))):
            pick = (from_col == to_col + rank_cols + i * n).astype(F32)
            tiled = jnp.where(own, jnp.dot(proj, pick, precision=lax.Precision.HIGHEST, preferred_element_type=F32), 0.0)
            blk_ref[...] = tiled.astype(BF)
            ones = jnp.ones((STEP, 128), F32)
            for k in range(rows // STEP):
                block = tiled[k * STEP : (k + 1) * STEP, :]
                wide_ref[k * groups : (k + 1) * groups, :] = lax.dot_general(block, ones, TN, precision=lax.Precision.HIGHEST, preferred_element_type=F32)

    pre = jnp.dot(low_ref[...], dtt_ref[...], preferred_element_type=F32) + dtb_ref[...]
    dt = jax.nn.softplus(pre)
    pre_ref[...] = pre
    dt_ref[...] = dt
    dtx_ref[...] = dt * values_ref[...]
    taps = keep_ref.shape[1]
    keep = jnp.broadcast_to(keep_ref[:, taps - 2 : taps - 1], (rows, 128))
    for j in range(wide // 128):
        c = slice(j * 128, (j + 1) * 128)
        dte_ref[:, c] = jnp.where(keep > 0, dt[:, c], 1e30)
    rate = -jnp.exp(alog_ref[...])
    rate_ref[...] = rate
    rate2_ref[...] = rate * math.log2(math.e)
    state_kernel(n, dte_ref, dtx_ref, rate2_ref, bw_ref, state_ref, carry_ref)


def steps(proj, same, values, dt_t, dtb, alog_t, rank_cols, wide):
    rows, chans = values.shape
    n = alog_t.shape[0]
    groups = STEP * n
    col = lambda r: pl.BlockSpec((r, wide), lambda g: (0, g))
    fixed = lambda *s: pl.BlockSpec(s, lambda g: (0, 0))
    f32 = lambda *s: jax.ShapeDtypeStruct(s, F32)
    bf = lambda *s: jax.ShapeDtypeStruct(s, BF)
    return pl.pallas_call(
        functools.partial(steps_kernel, n, rank_cols),
        grid=(chans // wide,),
        in_specs=[fixed(rows, 128), fixed(*same.shape), col(rows), col(128), col(1), col(n)],
        out_specs=[fixed(rows, 128), fixed(rows * n, 128), fixed(rows * n, 128), fixed(rows, groups), fixed(rows, groups)] + [col(rows)] * 4 + [col(n)] * 4,
        out_shape=[bf(rows, 128), f32(rows * n, 128), f32(rows * n, 128), bf(rows, groups), bf(rows, groups)] + [f32(rows, chans)] * 4 + [f32(n, chans)] * 4,
        compiler_params=pltpu.CompilerParams(vmem_limit_bytes=VM),
        cost_estimate=pl.CostEstimate(flops=10*rows*chans*n, bytes_accessed=24*rows*chans, transcendentals=rows*chans*n),
        name="steps",
    )(proj, same, values, dt_t, dtb, alog_t)


def scan_kernel(n, dte_ref, dtx_ref, rate_ref, b_ref, cblk_ref, start_ref, values_ref, z_ref, skip_ref, out_ref, tok_ref, gain_ref, pick_ref,
                y_ref, check_ref, gated_ref, first_ref, normed_ref, sent_ref, hs):
    rows, wide = dte_ref.shape
    tiles = wide // 128
    rates = [rate_ref[:, j*128:(j+1)*128] for j in range(tiles)]

    def block(k, state):
        at = pl.multiple_of(k * STEP, STEP)
        dte = dte_ref[pl.ds(at, STEP), :]
        dtx = dtx_ref[pl.ds(at, STEP), :]
        state = list(state)
        kn = pl.multiple_of(k * n, n)
        for j in range(tiles):
            check_ref[pl.ds(kn, n), j*128:(j+1)*128] = state[j]
        for i in range(STEP):
            bs = b_ref[pl.ds((at + i) * n, n), :]
            for j in range(tiles):
                c = slice(j*128, (j+1)*128)
                decay = jnp.exp2(rowb(dte[:, c], i, n) * rates[j])
                state[j] = decay * state[j] + bs * rowb(dtx[:, c], i, n)
                hs[i*n:(i+1)*n, c] = state[j].astype(BF)
        y_ref[pl.ds(at, STEP), :] = jnp.dot(cblk_ref[pl.ds(at, STEP), :], hs[...], preferred_element_type=F32)
        return tuple(state)

    start = tuple(start_ref[:, j*128:(j+1)*128] for j in range(tiles))
    lax.fori_loop(0, rows // STEP, block, start)

    @pl.when(pl.program_id(0) == 0)
    def _():
        first_ref[...] = tok_ref[...].astype(F32)

    z = z_ref[...]
    gated_ref[...] = ((y_ref[...] + skip_ref[...] * values_ref[...]) * (z * jax.nn.sigmoid(z))).astype(BF)
    first_ref[...] += jnp.dot(gated_ref[...], out_ref[...], preferred_element_type=F32)

    @pl.when(pl.program_id(0) == pl.num_programs(0) - 1)
    def _():
        first = first_ref[...]
        scale = lax.rsqrt(jnp.mean(first * first, axis=1, keepdims=True) + EPS)
        normed_ref[...] = (first * scale * gain_ref[...]).astype(BF)
        sent_ref[...] = lax.dot_general(pick_ref[...], normed_ref[...], TN, preferred_element_type=F32).astype(BF)


def scan_pass(dte, dtx, rates2, b_wide, c_blk, start, values, z, skip, full_out, tok, gain, pick, wide):
    rows, chans = dte.shape
    n = rates2.shape[0]
    width = tok.shape[1]
    col = lambda r: pl.BlockSpec((r, wide), lambda g: (0, g))
    whole = lambda a: pl.BlockSpec(a.shape, lambda g: (0, 0))
    return pl.pallas_call(
        functools.partial(scan_kernel, n),
        grid=(chans // wide,),
        in_specs=[col(rows), col(rows), col(n), whole(b_wide), whole(c_blk), col(n), col(rows), col(rows), col(1), pl.BlockSpec((wide, width), lambda g: (g, 0)), whole(tok), whole(gain), whole(pick)],
        out_specs=[col(rows), col(rows // STEP * n), col(rows), whole(tok), whole(tok), pl.BlockSpec((pick.shape[1], width), lambda g: (0, 0))],
        out_shape=[jax.ShapeDtypeStruct((rows, chans), F32), jax.ShapeDtypeStruct((rows // STEP * n, chans), F32), jax.ShapeDtypeStruct((rows, chans), BF),
                   jax.ShapeDtypeStruct((rows, width), F32), jax.ShapeDtypeStruct((rows, width), BF), jax.ShapeDtypeStruct((pick.shape[1], width), BF)],
        scratch_shapes=[pltpu.VMEM((STEP * n, wide), BF)],
        compiler_params=pltpu.CompilerParams(vmem_limit_bytes=VM),
        cost_estimate=pl.CostEstimate(flops=10*rows*chans*n, bytes_accessed=12*rows*chans, transcendentals=rows*chans*n),
        name="scan_pass",
    )(dte, dtx, rates2, b_wide, c_blk, start, values, z, skip, full_out, tok, gain, pick)


def back_state_kernel(n, dte_ref, gs_ref, rate_ref, c_ref, out_ref):
    rows, wide = dte_ref.shape
    tiles = wide // 128
    rates = [rate_ref[:, j*128:(j+1)*128] for j in range(tiles)]
    def block(k, state):
        at = pl.multiple_of(rows - STEP - k * STEP, STEP)
        dte = dte_ref[pl.ds(at, STEP), :]
        gs = gs_ref[pl.ds(at, STEP), :]
        state = list(state)
        for i in reversed(range(STEP)):
            cs = c_ref[pl.ds((at + i) * n, n), :]
            for j in range(tiles):
                c = slice(j*128, (j+1)*128)
                decay = jnp.exp2(rowb(dte[:, c], i, n) * rates[j])
                state[j] = decay * (state[j] + cs * rowb(gs[:, c], i, n))
        return tuple(state)
    zero = tuple(jnp.zeros((n, 128), F32) for _ in range(tiles))
    state = lax.fori_loop(0, rows // STEP, block, zero)
    for j in range(tiles):
        out_ref[:, j*128:(j+1)*128] = state[j]

def back_front_kernel(n, order, steps, grad_ref, out_ref, z_ref, y_ref, values_ref, skip_ref, gated_ref, dte_ref, rate_ref, c_ref, gs_ref, gz_ref, gwo_ref, state_ref):
    grad = grad_ref[...]
    gated = lax.dot_general(grad, out_ref[...], NT, preferred_element_type=F32)
    z = z_ref[...]
    sig = jax.nn.sigmoid(z)
    gs_ref[...] = gated * (z * sig)
    gz_ref[...] = (gated * (y_ref[...] + skip_ref[...] * values_ref[...]) * (sig * (1.0 + z * (1.0 - sig)))).astype(BF)
    grad_out = lax.dot_general(gated_ref[...], grad, TN, preferred_element_type=F32).astype(BF)
    if order is None:
        gwo_ref[...] = grad_out
    else:
        per = len(order) // steps
        size = grad_out.shape[0] // per
        for g in range(steps):

            @pl.when(pl.program_id(0) == g)
            def _():
                for to, share in enumerate(order[g * per : (g + 1) * per]):
                    at = (share - g * per) * size
                    gwo_ref[to * size : (to + 1) * size, :] = grad_out[at : at + size]

    back_state_kernel(n, dte_ref, gs_ref, rate_ref, c_ref, state_ref)


def back_front(grad, full_out, z, scanned, values, skip, gated, dte, rates2, c_wide, wide, order=None):
    rows, chans = dte.shape
    width = grad.shape[1]
    n = rates2.shape[0]
    col = lambda r: pl.BlockSpec((r, wide), lambda g: (0, g))
    whole = lambda a: pl.BlockSpec(a.shape, lambda g: (0, 0))
    flat = pl.BlockSpec((wide, width), lambda g: (g, 0))
    return pl.pallas_call(
        functools.partial(back_front_kernel, n, order, chans // wide),
        grid=(chans // wide,),
        in_specs=[whole(grad), flat, col(rows), col(rows), col(rows), col(1), col(rows), col(rows), col(n), whole(c_wide)],
        out_specs=[col(rows), col(rows), flat, col(n)],
        out_shape=[jax.ShapeDtypeStruct((rows, chans), F32), jax.ShapeDtypeStruct((rows, chans), BF), jax.ShapeDtypeStruct((chans, width), BF), jax.ShapeDtypeStruct((n, chans), F32)],
        compiler_params=pltpu.CompilerParams(vmem_limit_bytes=VM),
        cost_estimate=pl.CostEstimate(flops=8*rows*chans*n, bytes_accessed=8*rows*chans, transcendentals=rows*chans*n),
        name="back_front",
    )(grad, full_out, z, scanned, values, skip, gated, dte, rates2, c_wide)


def back_kernel(n, rank_cols, dt_ref, dte_ref, dtx_ref, gs_ref, values_ref, pre_ref, skip_ref, rate_ref, rawrate_ref, b_ref, c_ref, bblk_ref, check_ref, next_ref, low_ref, wdt_ref,
                gval_ref, glog_ref, gwdt_ref, gdtb_ref, gskip_ref, proj_ref, us, decs, hs, ls, ps, gdtx, gdt, gb, gc, rank):
    rows, wide = dte_ref.shape
    tiles = wide // 128
    rates = [rate_ref[:, j*128:(j+1)*128] for j in range(tiles)]

    @pl.when(pl.program_id(0) == 0)
    def _():
        gb[...] = jnp.zeros_like(gb)
        gc[...] = jnp.zeros_like(gc)
        rank[...] = jnp.zeros_like(rank)

    ones = (lax.broadcasted_iota(jnp.int32, (STEP, STEP * n), 0) == lax.broadcasted_iota(jnp.int32, (STEP, STEP * n), 1) // n).astype(BF)
    glog_ref[...] = jnp.zeros_like(glog_ref)

    def block(k, later):
        kk = rows // STEP - 1 - k
        at = pl.multiple_of(kk * STEP, STEP)
        kn = pl.multiple_of(kk * n, n)
        dte = dte_ref[pl.ds(at, STEP), :]
        dtx = dtx_ref[pl.ds(at, STEP), :]
        state = [check_ref[pl.ds(kn, n), j*128:(j+1)*128] for j in range(tiles)]
        for i in range(STEP):
            bs = b_ref[pl.ds((at + i) * n, n), :]
            for j in range(tiles):
                c = slice(j*128, (j+1)*128)
                decay = jnp.exp2(rowb(dte[:, c], i, n) * rates[j])
                kept = decay * state[j]
                state[j] = kept + bs * rowb(dtx[:, c], i, n)
                decs[i*n:(i+1)*n, c] = decay
                us[i*n:(i+1)*n, c] = kept
                hs[i*n:(i+1)*n, c] = state[j].astype(BF)
        later = list(later)
        dt = dt_ref[pl.ds(at, STEP), :]
        gs = gs_ref[pl.ds(at, STEP), :]
        logs = [glog_ref[:, j*128:(j+1)*128] for j in range(tiles)]
        for i in reversed(range(STEP)):
            cs = c_ref[pl.ds((at + i) * n, n), :]
            for j in range(tiles):
                c = slice(j*128, (j+1)*128)
                adj = later[j] + cs * rowb(gs[:, c], i, n)
                part = adj * us[i*n:(i+1)*n, c] * rawrate_ref[:, c]
                later[j] = adj * decs[i*n:(i+1)*n, c]
                logs[j] = logs[j] + part * rowb(dt[:, c], i, n)
                ls[i*n:(i+1)*n, c] = adj.astype(BF)
                ps[i*n:(i+1)*n, c] = part.astype(BF)
        for j in range(tiles):
            glog_ref[:, j*128:(j+1)*128] = logs[j]
        gdtx[pl.ds(at, STEP), :] = jnp.dot(bblk_ref[pl.ds(at, STEP), :], ls[...], preferred_element_type=F32)
        gdt[pl.ds(at, STEP), :] = jnp.dot(ones, ps[...], preferred_element_type=F32)
        gb[pl.ds(at, STEP), :] += lax.dot_general(dtx.astype(BF), ls[...], NT, preferred_element_type=F32)
        gc[pl.ds(at, STEP), :] += lax.dot_general(gs.astype(BF), hs[...], NT, preferred_element_type=F32)
        return tuple(later)

    start = tuple(next_ref[:, j*128:(j+1)*128] for j in range(tiles))
    lax.fori_loop(0, rows // STEP, block, start)

    values = values_ref[...]
    grad_pre = (gdt[...] + gdtx[...] * values) * jax.nn.sigmoid(pre_ref[...])
    gdtb_ref[...] = jnp.sum(grad_pre, axis=0, keepdims=True)
    grad_pre = grad_pre.astype(BF)
    gwdt_ref[...] = lax.dot_general(low_ref[...], grad_pre, TN, preferred_element_type=F32)
    rank[...] += lax.dot_general(grad_pre, wdt_ref[...], NT, preferred_element_type=F32)
    gs = gs_ref[...]
    gskip_ref[...] = jnp.sum(gs * values, axis=0, keepdims=True)
    gval_ref[...] = gs * skip_ref[...] + gdtx[...] * dt_ref[...]

    @pl.when(pl.program_id(0) == pl.num_programs(0) - 1)
    def _():
        groups = STEP * n
        row = lax.broadcasted_iota(jnp.int32, (rows, groups), 0)
        col = lax.broadcasted_iota(jnp.int32, (rows, groups), 1)
        own = lax.rem(row, STEP) == col // n
        from_col = lax.rem(lax.broadcasted_iota(jnp.int32, (groups, rank.shape[1]), 0), n)
        to_col = lax.broadcasted_iota(jnp.int32, (groups, rank.shape[1]), 1)
        total = rank[...]
        for i, acc in enumerate((gb, gc)):
            place = (to_col == from_col + rank_cols + i * n).astype(BF)
            total = total + jnp.dot(jnp.where(own, acc[...], 0.0).astype(BF), place, preferred_element_type=F32)
        proj_ref[...] = total.astype(BF)


def back_pass(dt, dte, dtx, gs, values, pre, skip, rates2, rates, b_wide, c_wide, b_blk, check, nxt, low, wdt, rank_cols, wide):
    rows, chans = dte.shape
    n = rates2.shape[0]
    col = lambda r: pl.BlockSpec((r, wide), lambda g: (0, g))
    whole = lambda a: pl.BlockSpec(a.shape, lambda g: (0, 0))
    sq = lambda kind, w=wide: pltpu.VMEM((STEP * n, w), kind)
    return pl.pallas_call(
        functools.partial(back_kernel, n, rank_cols),
        grid=(chans // wide,),
        in_specs=[col(rows)] * 6 + [col(1)] + [col(n)] * 2 + [whole(b_wide), whole(c_wide), whole(b_blk), col(rows // STEP * n), col(n), whole(low), col(wdt.shape[0])],
        out_specs=[col(rows), col(n), col(low.shape[1]), col(1), col(1), pl.BlockSpec((rows, 128), lambda g: (0, 0))],
        out_shape=[jax.ShapeDtypeStruct((rows, chans), F32), jax.ShapeDtypeStruct((n, chans), F32), jax.ShapeDtypeStruct((low.shape[1], chans), F32),
                   jax.ShapeDtypeStruct((1, chans), F32), jax.ShapeDtypeStruct((1, chans), F32), jax.ShapeDtypeStruct((rows, 128), BF)],
        scratch_shapes=[sq(F32), sq(F32), sq(BF), sq(BF), sq(BF), pltpu.VMEM((rows, wide), F32), pltpu.VMEM((rows, wide), F32),
                        pltpu.VMEM((rows, STEP * n), F32), pltpu.VMEM((rows, STEP * n), F32), pltpu.VMEM((rows, 128), F32)],
        compiler_params=pltpu.CompilerParams(vmem_limit_bytes=VM),
        cost_estimate=pl.CostEstimate(flops=26*rows*chans*n, bytes_accessed=24*rows*chans, transcendentals=rows*chans*n),
        name="back_pass",
    )(dt, dte, dtx, gs, values, pre, skip, rates2, rates, b_wide, c_wide, b_blk, check, nxt, low, wdt)


def conv_back_kernel(halo, gval_ref, proj_ref, xt_ref, values_ref, sum_ref, ext_ref, same_ref, taps_ref,
                     gconv_ref, last_ref, rim_ref, gxt_ref, gtaps_ref, pad):
    rows, wide = gval_ref.shape
    taps = taps_ref.shape[0]
    proj = proj_ref[...]
    grad_values = gval_ref[...] + jnp.dot(proj, xt_ref[...], preferred_element_type=F32)
    gxt_ref[...] = lax.dot_general(proj, values_ref[...].astype(BF), TN, preferred_element_type=F32)
    sums = sum_ref[...]
    sig = jax.nn.sigmoid(sums)
    pad[0:rows, :] = grad_values * (sig * (1.0 + sums * (1.0 - sig)))
    pad[rows:, :] = jnp.zeros((pad.shape[0] - rows, wide), F32)
    row = lax.broadcasted_iota(jnp.int32, (8, 128), 0)
    same = [jnp.broadcast_to(same_ref[:, k : k + 1], (rows, 128)) for k in range(taps)]
    rowed = lax.broadcasted_iota(jnp.int32, (rows, 128), 0)
    later = [jnp.where(rowed < rows - (taps - 1 - k), pltpu.roll(same[k], (rows - (taps - 1 - k)) % rows, 0), 0.0) for k in range(taps)]
    for j in range(wide // 128):
        c = slice(j * 128, (j + 1) * 128)
        grads = pad[0:rows, c]
        sums_of = [jnp.sum(grads * same[k] * ext_ref[halo - taps + 1 + k : halo - taps + 1 + k + rows, c], axis=0, keepdims=True) for k in range(taps)]
        sums_of.append(jnp.sum(grads, axis=0, keepdims=True))
        total = jnp.zeros((rows, 128), F32)
        rim = jnp.zeros((8, 128), F32)
        for k in range(taps):
            weight = taps_ref[k : k + 1, c]
            total = total + pad[taps - 1 - k : taps - 1 - k + rows, c] * later[k] * weight
            if k < taps - 1:
                moved = pltpu.roll(grads[0:8] * same[k][0:8], 8 - taps + 1 + k, 0)
                rim = rim + jnp.where(row >= 8 - taps + 1 + k, moved, 0.0) * weight
        gconv_ref[:, c] = total.astype(BF)
        last_ref[:, c] = total[rows - 8 :]
        rim_ref[:, c] = rim
        gtaps_ref[:, c] = jnp.concatenate(sums_of + [jnp.zeros((8 - len(sums_of), 128), F32)], axis=0)


def conv_back(gval, proj, x_t, values, sums, ext, same, conv_taps, halo, wide):
    rows, chans = gval.shape
    taps = conv_taps.shape[0]
    col = lambda r: pl.BlockSpec((r, wide), lambda g: (0, g))
    mask = pl.BlockSpec(same.shape, lambda g: (0, 0))
    f32 = lambda r: jax.ShapeDtypeStruct((r, chans), F32)
    return pl.pallas_call(
        functools.partial(conv_back_kernel, halo),
        grid=(chans // wide,),
        in_specs=[col(rows), pl.BlockSpec(proj.shape, lambda g: (0, 0)), col(x_t.shape[0]), col(rows), col(rows), col(ext.shape[0]), mask, col(taps)],
        out_specs=[col(rows), col(8), col(8), col(x_t.shape[0]), col(8)],
        out_shape=[jax.ShapeDtypeStruct((rows, chans), BF), f32(8), f32(8), f32(x_t.shape[0]), f32(8)],
        scratch_shapes=[pltpu.VMEM((rows + 8, wide), F32)],
        compiler_params=pltpu.CompilerParams(vmem_limit_bytes=VM),
        cost_estimate=pl.CostEstimate(flops=60*rows*chans, bytes_accessed=20*rows*chans, transcendentals=rows*chans),
        name="conv_back",
    )(gval, proj, x_t, values, sums, ext, same, conv_taps)


def flip(value, bit):
    return value + bit - 2 * bit * (lax.rem(value // bit, 2))


def greet(partners):
    barrier = pltpu.get_barrier_semaphore()
    for partner in partners:
        pl.semaphore_signal(barrier, inc=1, device_id=partner, device_id_type=MESH)
    pl.semaphore_wait(barrier, len(partners))


class ZSwap:
    def __init__(self, pairs, local, send, recv, count):
        self.pairs, self.local, self.send, self.recv, self.count = pairs, local, send, recv, count

    def own(self):
        z = lax.axis_index("seq")
        return [pltpu.make_async_copy(src.at[z], dst.at[z], self.local.at[i]) for i, (src, dst) in enumerate(self.pairs)]

    def out(self):
        dp, z = lax.axis_index("dp"), lax.axis_index("seq")
        made = []
        for j in range(1, self.count):
            peer = lax.rem(z + j, self.count)
            for i, (src, dst) in enumerate(self.pairs):
                made.append(pltpu.make_async_remote_copy(src.at[peer], dst.at[z], self.send.at[i, j - 1], self.recv.at[i, j - 1], device_id=(dp, peer), device_id_type=MESH))
        return made

    def start(self):
        for copy in self.out() + self.own():
            copy.start()

    def wait(self):
        dp, z = lax.axis_index("dp"), lax.axis_index("seq")
        for copy in self.own():
            copy.wait()
        for copy in self.out():
            copy.wait_send()
        for j in range(1, self.count):
            source = lax.rem(z + self.count - j, self.count)
            for i, (src, dst) in enumerate(self.pairs):
                pltpu.make_async_remote_copy(src.at[z], dst.at[source], self.send.at[i, j - 1], self.recv.at[i, j - 1], device_id=(dp, source), device_id_type=MESH).wait_recv()


def gather_kernel(parts, count, in_ref, rest_ref, up_ref, tok_ref, ids_ref, gin_ref, grest_ref, gup_ref, rim_ref, rimids_ref,
                  local_sem, send, recv, share_send, share_recv, pair_send, pair_recv, swap_local, swap_send, swap_recv, rim_send, rim_recv):
    dp, z = lax.axis_index("dp"), lax.axis_index("seq")
    chip, core = dp // 2, lax.rem(dp, 2)
    srcs, dsts = (in_ref, rest_ref), (gin_ref, grest_ref)
    sibling = (flip(dp, 1), z)
    peers = [lax.rem(z + j, count) for j in range(1, count)]
    greet([sibling, (flip(dp, 4), z), (flip(dp, 2), z)] + [(dp, peer) for peer in peers])

    tail = pl.ds(tok_ref.shape[0] - rim_ref.shape[0], rim_ref.shape[0])
    rims = [pltpu.make_async_remote_copy(src, dst, rim_send.at[i], rim_recv.at[i], device_id=(dp, lax.rem(z + 1, count)), device_id_type=MESH)
            for i, (src, dst) in enumerate(((tok_ref.at[tail], rim_ref), (ids_ref, rimids_ref)))]
    for copy in rims:
        copy.start()
    mine = []
    for i, (src, dst) in enumerate(zip(srcs, dsts)):
        local = pltpu.make_async_copy(src, dst.at[chip, core, z], local_sem.at[i])
        pair = pltpu.make_async_remote_copy(src, dst.at[chip, core, z], pair_send.at[i], pair_recv.at[i], device_id=sibling, device_id_type=MESH)
        local.start()
        pair.start()
        mine += [local, pair]
    for copy in mine:
        copy.wait()
    swap = ZSwap(((up_ref, gup_ref),), swap_local, swap_send, swap_recv, count)

    def role(which, first_bit, second_bit):
        subs = parts[which]
        first, second = (flip(dp, first_bit), z), (flip(dp, second_bit), z)
        first_chip, second_chip = flip(chip, first_bit // 2), flip(chip, second_bit // 2)
        both_chip = flip(first_chip, second_bit // 2)

        def copies(sub, at_chip, at_z, slot, to, send_s, recv_s):
            made = []
            for i, (ref, lo, size) in enumerate(subs[sub]):
                view = dsts[ref].at[at_chip, :, at_z, pl.ds(lo, size)]
                made.append(pltpu.make_async_remote_copy(view, view, send_s.at[sub, slot, i], recv_s.at[sub, slot, i], device_id=to, device_id_type=MESH))
            return made

        def start(made):
            for copy in made:
                copy.start()

        def wait_recv(made):
            for copy in made:
                copy.wait_recv()

        def along_first(sub, k):
            return copies(sub, chip, k, 4 + k, first, send, recv)

        def along_second(sub, k, far):
            return copies(sub, first_chip if far else chip, k, 8 + 4 * far + k, second, send, recv)

        def came_first(sub, k):
            return copies(sub, first_chip, k, 4 + k, first, send, recv)

        def came_second(sub, k, far):
            return copies(sub, both_chip if far else second_chip, k, 8 + 4 * far + k, second, send, recv)

        def share(sub, at_chip, k, offset):
            return copies(sub, at_chip, k, 4 * offset + k, sibling, share_send, share_recv)

        def up(sub, k):
            return copies(sub, chip, k, k + count * 5, (dp, z + 1), send, recv)

        def down(sub, k):
            return copies(sub, chip, k, k, (dp, z - 1), send, recv)

        both = range(len(subs))

        def spread(sub, k):
            start(along_first(sub, k))
            start(along_second(sub, k, 0))

        def rest(k):
            for sub in both:
                wait_recv(came_first(sub, k))
                start(along_second(sub, k, 1))
                start(share(sub, first_chip, k, 1))

        def below(hop, work):
            pl.when(z - hop >= 0)(lambda: work(z - hop))

        def above(hop, work):
            pl.when(z + hop <= count - 1)(lambda: work(z + hop))

        def from_below(k):
            for sub in both:
                wait_recv(up(sub, k))
                pl.when(z < count - 1)(lambda: start(up(sub, k)))
                spread(sub, k)
                start(share(sub, chip, k, 0))

        def from_above(k):
            for sub in both:
                wait_recv(down(sub, k))
                pl.when(z > 0)(lambda: start(down(sub, k)))
                spread(sub, k)
                start(share(sub, chip, k, 0))

        for sub in both:
            pl.when(z > 0)(lambda: start(down(sub, z)))
            pl.when(z < count - 1)(lambda: start(up(sub, z)))
            spread(sub, z)
        for hop in range(1, count):
            below(hop, from_below)
            above(hop, from_above)
            if hop == count - 2:
                swap.start()
            if hop == 1:
                rest(z)
            else:
                below(hop - 1, rest)
                above(hop - 1, rest)
        below(count - 1, rest)
        above(count - 1, rest)

        def finish(k, _):
            for far in (0, 1):
                for sub in both:
                    wait_recv(came_second(sub, k, far))
                    start(share(sub, both_chip if far else second_chip, k, 2 + far))
            return 0

        lax.fori_loop(0, count, finish, 0)

        def drain(k, _):
            def wait_send(made):
                for copy in made:
                    copy.wait_send()

            for sub in both:
                wait_send(along_first(sub, k) + along_second(sub, k, 0) + along_second(sub, k, 1))
                for offset, at_chip in ((1, first_chip), (2, second_chip), (3, both_chip)):
                    wait_send(share(sub, at_chip, k, offset))
                pl.when(k != z)(lambda: wait_send(share(sub, chip, k, 0)))
                pl.when((k <= z) & (z < count - 1))(lambda: wait_send(up(sub, k)))
                pl.when((k >= z) & (z > 0))(lambda: wait_send(down(sub, k)))
            return 0

        lax.fori_loop(0, count, drain, 0)

        def shared(k, _):
            for offset, at_chip in enumerate((chip, second_chip, first_chip, both_chip)):
                def wait():
                    for sub, chunks in enumerate(parts[1 - which]):
                        for i, (ref, lo, size) in enumerate(chunks):
                            view = dsts[ref].at[at_chip, :, k, pl.ds(lo, size)]
                            pltpu.make_async_remote_copy(view, view, share_send.at[sub, 4 * offset + k, i], share_recv.at[sub, 4 * offset + k, i], device_id=sibling, device_id_type=MESH).wait_recv()
                if offset:
                    wait()
                else:
                    pl.when(k != z)(wait)
            return 0

        lax.fori_loop(0, count, shared, 0)

    pl.when(core == 0)(lambda: role(0, 4, 2))
    pl.when(core == 1)(lambda: role(1, 2, 4))
    swap.wait()
    for copy in rims:
        copy.wait()


def gather_all(w_in, rest, up, tok, ids, cut, count):
    parts = ((((0, 0, 48),), ((0, 48, cut - 48),)), (((0, cut, 48),), ((0, cut + 48, w_in.shape[0] - cut - 48), (1, 0, rest.shape[0]))))
    shape = lambda a: jax.ShapeDtypeStruct((4, 2, count) + a.shape, a.dtype)
    sems = lambda *s: pltpu.SemaphoreType.DMA(s)
    return pl.pallas_call(
        functools.partial(gather_kernel, parts, count),
        in_specs=[pl.BlockSpec(memory_space=pl.ANY)] * 5,
        out_specs=[pl.BlockSpec(memory_space=pl.ANY)] * 5,
        out_shape=[shape(w_in), shape(rest), jax.ShapeDtypeStruct(up.shape, up.dtype),
                   jax.ShapeDtypeStruct((16, tok.shape[1]), tok.dtype), jax.ShapeDtypeStruct(ids.shape, ids.dtype)],
        scratch_shapes=[sems(2), sems(2, 24, 2), sems(2, 24, 2), sems(2, 16, 2), sems(2, 16, 2), sems(2), sems(2), sems(1), sems(1, count - 1), sems(1, count - 1), sems(2), sems(2)],
        compiler_params=pltpu.CompilerParams(collective_id=1, has_side_effects=True),
        cost_estimate=pl.CostEstimate(flops=0, bytes_accessed=200_000_000, transcendentals=0),
        name="gather_all",
    )(w_in, rest, up, tok, ids)


def scatter_kernel(parts, count, in_ref, rest_ref, proj_ref, down_ref, oin_ref, orest_ref, oproj_ref, odown_ref, mine_a, mine_b, sib_a, sib_b, far_a, far_b, near_a, near_b, zgot_a, zgot_b, final_a, final_b,
                   load_sem, sib_send, sib_recv, two_send, two_recv, one_send, one_recv, z_send, z_recv, end_send, end_recv, end_local,
                   swap_local, swap_send, swap_recv):
    dp, z = lax.axis_index("dp"), lax.axis_index("seq")
    chip, core = dp // 2, lax.rem(dp, 2)
    srcs, outs = (in_ref, rest_ref), (oin_ref, orest_ref)
    mine, sib, far_got, near_got, z_got, final = (mine_a, mine_b), (sib_a, sib_b), (far_a, far_b), (near_a, near_b), (zgot_a, zgot_b), (final_a, final_b)
    sibling = (flip(dp, 1), z)
    peers = [(dp, lax.rem(z + j, count)) for j in range(1, count)]
    greet([sibling, (flip(dp, 4), z), (flip(dp, 2), z)] + peers)

    swap = ZSwap(((proj_ref, oproj_ref), (down_ref, odown_ref)), swap_local, swap_send, swap_recv, count)

    def role(which, first_bit, second_bit):
        chunks, other = parts[which], parts[1 - which]
        first, second = (flip(dp, first_bit), z), (flip(dp, second_bit), z)
        first_chip, second_chip = flip(chip, first_bit // 2), flip(chip, second_bit // 2)
        both_chip = flip(first_chip, second_bit // 2)
        steps = [lax.rem(z + 1 + j, count) for j in range(count)]

        def loads(col, k):
            slot = col * count + k
            return [pltpu.make_async_copy(srcs[ref].at[col, :, k, pl.ds(lo, size)], mine[ref].at[slot, :, pl.ds(0, size)], load_sem.at[slot, ref])
                    for ref, lo, size in chunks]

        def sibling_copies(col, k, pieces):
            slot = col * count + k
            return [pltpu.make_async_remote_copy(srcs[ref].at[col, :, k, pl.ds(lo, size)], sib[ref].at[slot, :, pl.ds(0, size)],
                                                 sib_send.at[slot, ref], sib_recv.at[slot, ref], device_id=sibling, device_id_type=MESH)
                    for ref, lo, size in pieces]

        def send(col, k, dst, slot, send_s, recv_s, to):
            return [pltpu.make_async_remote_copy(mine[ref].at[col * count + k, :, pl.ds(0, size)], dst[ref].at[slot, :, pl.ds(0, size)],
                                                 send_s.at[slot, ref], recv_s.at[slot, ref], device_id=to, device_id_type=MESH)
                    for ref, lo, size in chunks]

        def start(copies):
            for copy in copies:
                copy.start()

        def wait_recv(copies):
            for copy in copies:
                copy.wait_recv()

        def wait_send(copies):
            for copy in copies:
                copy.wait_send()

        def add(col, k, terms, last=False):
            slot = col * count + k
            for copy in loads(col, k):
                copy.wait()
            wait_recv(sibling_copies(col, k, chunks))
            for ref, lo, size in chunks:
                def rows(r, _):
                    at = pl.ds(pl.multiple_of(r * 16, 16), 16)
                    for c in range(2):
                        total = mine[ref][slot, c, at, :].astype(F32) + sib[ref][slot, c, at, :].astype(F32)
                        for buf, place in terms:
                            total = total + buf[ref][place, c, at, :].astype(F32)
                        if last:
                            final[ref][c, at, :] = total
                        else:
                            mine[ref][slot, c, at, :] = total.astype(BF)
                    return 0

                lax.fori_loop(0, size // 16, rows, 0)

        for k in steps:
            for col, sib_col in ((both_chip, both_chip), (second_chip, first_chip), (first_chip, second_chip), (chip, chip)):
                start(sibling_copies(sib_col, k, other) + loads(col, k))

        swap.start()

        def stage_one(k):
            for far, col in ((1, both_chip), (0, second_chip)):
                add(col, k, ())
                start(send(col, k, far_got, far * count + k, two_send, two_recv, second))

        def stage_two(k):
            wait_recv(send(first_chip, k, far_got, count + k, two_send, two_recv, second))
            add(first_chip, k, ((far_got, count + k),))
            start(send(first_chip, k, near_got, k, one_send, one_recv, first))

        def stage_three(j, k):
            wait_recv(send(chip, k, far_got, k, two_send, two_recv, second))
            wait_recv(send(chip, k, near_got, k, one_send, one_recv, first))
            if j < count - 1:
                add(chip, k, ((far_got, k), (near_got, k)))
                start(send(chip, k, z_got, j, z_send, z_recv, (dp, k)))

        for j in range(count + 2):
            if j < count:
                stage_one(steps[j])
            if 1 <= j <= count:
                stage_two(steps[j - 1])
            if j >= 2:
                stage_three(j - 2, steps[j - 2])

        for j in range(count - 1):
            wait_recv(send(chip, z, z_got, j, z_send, z_recv, (dp, z)))
        add(chip, z, ((far_got, z), (near_got, z)) + tuple((z_got, j) for j in range(count - 1)), last=True)
        locals_, remotes = [], []
        for ref, lo, size in chunks:
            locals_.append(pltpu.make_async_copy(final[ref].at[which, pl.ds(0, size)], outs[ref].at[pl.ds(lo, size)], end_local.at[ref]))
            remotes.append(pltpu.make_async_remote_copy(final[ref].at[1 - which, pl.ds(0, size)], outs[ref].at[pl.ds(lo, size)],
                                                        end_send.at[which, ref], end_recv.at[which, ref], device_id=sibling, device_id_type=MESH))
        start(locals_ + remotes)
        for copy in locals_:
            copy.wait()
        wait_send(remotes)
        for ref, lo, size in other:
            pltpu.make_async_remote_copy(final[ref].at[which, pl.ds(0, size)], outs[ref].at[pl.ds(lo, size)],
                                         end_send.at[1 - which, ref], end_recv.at[1 - which, ref], device_id=sibling, device_id_type=MESH).wait_recv()
        for j, k in enumerate(steps):
            for col in (chip, first_chip, second_chip, both_chip):
                wait_send(sibling_copies(col, k, other))
            wait_send(send(both_chip, k, far_got, count + k, two_send, two_recv, second))
            wait_send(send(second_chip, k, far_got, k, two_send, two_recv, second))
            wait_send(send(first_chip, k, near_got, k, one_send, one_recv, first))
            if j < count - 1:
                wait_send(send(chip, k, z_got, j, z_send, z_recv, (dp, k)))

    pl.when(core == 0)(lambda: role(0, 4, 2))
    pl.when(core == 1)(lambda: role(1, 2, 4))
    swap.wait()


def scatter_all(g_in, g_rest, proj, down, cut, collective_id):
    count = g_in.shape[2]
    rows_in, rows_rest = g_in.shape[3], g_rest.shape[3]
    parts = (((0, 0, cut),), ((0, cut, rows_in - cut), (1, 0, rows_rest)))
    sems = lambda *s: pltpu.SemaphoreType.DMA(s)
    places = 4 * count

    def bufs(k, kind=BF):
        lead = (k, 2) if k else (2,)
        return [pltpu.VMEM(lead + (max(cut, rows_in - cut), g_in.shape[4]), kind), pltpu.VMEM(lead + (rows_rest, g_rest.shape[4]), kind)]

    return pl.pallas_call(
        functools.partial(scatter_kernel, parts, count),
        in_specs=[pl.BlockSpec(memory_space=pl.ANY)] * 4,
        out_specs=[pl.BlockSpec(memory_space=pl.ANY)] * 4,
        out_shape=[jax.ShapeDtypeStruct(g_in.shape[3:], F32), jax.ShapeDtypeStruct(g_rest.shape[3:], F32), jax.ShapeDtypeStruct(proj.shape, proj.dtype), jax.ShapeDtypeStruct(down.shape, down.dtype)],
        scratch_shapes=bufs(places) + bufs(places) + bufs(2 * count) + bufs(count) + bufs(count - 1) + bufs(0, F32)
        + [sems(places, 2), sems(places, 2), sems(places, 2), sems(2 * count, 2), sems(2 * count, 2), sems(count, 2), sems(count, 2),
           sems(count - 1, 2), sems(count - 1, 2), sems(2, 2), sems(2, 2), sems(2), sems(2), sems(2, count - 1), sems(2, count - 1)],
        compiler_params=pltpu.CompilerParams(collective_id=collective_id, has_side_effects=True, vmem_limit_bytes=VM),
        cost_estimate=pl.CostEstimate(flops=0, bytes_accessed=200_000_000, transcendentals=0),
        name="scatter_all",
    )(g_in, g_rest, proj, down)


def unpack_kernel(own, cuts, pack_ref, small_ref, *refs):
    outs, tall = refs[:-1], refs[-1]
    for b in range(pack_ref.shape[0]):
        block = pack_ref[b].astype(F32)
        tall[b * own : (b + 1) * own, :] = block[:own]
        small_ref[b : b + 1, :] = block[own : own + 1]
    for j in range(tall.shape[0] // 128):
        c = slice(j * 128, (j + 1) * 128)
        turned = tall[c, :].T
        for ref, (lo, size) in zip(outs, cuts):
            part = turned[lo : lo + size]
            if ref.shape[0] > size:
                part = jnp.concatenate([part, jnp.zeros((ref.shape[0] - size, 128), F32)], axis=0)
            ref[:, c] = part.astype(ref.dtype)


def unpack(pack, own, sizes):
    blocks, _, cols = pack.shape
    chans = blocks * own
    cuts, at = [], 0
    for size in sizes:
        cuts.append((at, size))
        at += size
    rows = [128, 128] + list(sizes[2:])
    kinds = [BF, BF] + [F32] * (len(sizes) - 2)
    if own % 8:
        turned = pack[:, :own].reshape(chans, cols).T
        parts = [jnp.pad(turned[lo : lo + size], ((0, r - size), (0, 0))).astype(kind) for (lo, size), r, kind in zip(cuts, rows, kinds)]
        return [pack[:, own].astype(F32)] + parts
    return pl.pallas_call(
        functools.partial(unpack_kernel, own, tuple(cuts)),
        out_shape=[jax.ShapeDtypeStruct((blocks, cols), F32)] + [jax.ShapeDtypeStruct((r, chans), kind) for r, kind in zip(rows, kinds)],
        scratch_shapes=[pltpu.VMEM((chans, cols), F32)],
        compiler_params=pltpu.CompilerParams(vmem_limit_bytes=VM),
        name="unpack_small",
    )(pack)


def pack_kernel(own, sizes, x_ref, dt_ref, log_ref, taps_ref, dtb_ref, skip_ref, small_ref, out_ref, wide, tall):
    at = 0
    for ref, size in zip((x_ref, dt_ref, log_ref, taps_ref, dtb_ref, skip_ref), sizes):
        wide[at : at + size, :] = ref[0:size, :]
        at += size
    wide[at:, :] = jnp.zeros((wide.shape[0] - at, wide.shape[1]), F32)
    for j in range(tall.shape[0] // 128):
        tall[j * 128 : (j + 1) * 128, :] = wide[:, j * 128 : (j + 1) * 128].T
    cols = wide.shape[0]
    first = lax.broadcasted_iota(jnp.int32, (8, cols), 0) == 0
    for b in range(out_ref.shape[0]):
        tail = jnp.where(first, jnp.broadcast_to(small_ref[b : b + 1, :], (8, cols)), 0.0)
        out_ref[b] = jnp.concatenate([tall[b * own : (b + 1) * own, :], tail], axis=0).astype(BF)


def pack_grads(parts, sizes, small, own):
    blocks, cols = small.shape
    chans = parts[0].shape[1]
    rows = own + -own % 16
    if own % 8:
        turned = jnp.concatenate([part[:size] for part, size in zip(parts, sizes)]).T.reshape(blocks, own, -1)
        turned = jnp.pad(turned, ((0, 0), (0, 0), (0, cols - turned.shape[2])))
        return jnp.concatenate([turned, small[:, None], jnp.zeros((blocks, rows - own - 1, cols), F32)], axis=1).astype(BF)
    return pl.pallas_call(
        functools.partial(pack_kernel, own, sizes),
        out_shape=jax.ShapeDtypeStruct((blocks, rows, cols), BF),
        scratch_shapes=[pltpu.VMEM((cols, chans), F32), pltpu.VMEM((chans, cols), F32)],
        compiler_params=pltpu.CompilerParams(vmem_limit_bytes=VM),
        name="pack_small",
    )(*parts, small)


def finish_kernel(own, cuts, pack_ref, up_ref, down_ref, proj_ref, up_out, down_out, row_out, proj_out, *small_outs):
    up_out[0] = up_ref[0].astype(F32)
    down_out[0] = down_ref[0].astype(F32)

    @pl.when(pl.program_id(0) == 0)
    def _():
        row_out[...] = pack_ref[own : own + 1, :]
        proj_out[...] = sum(proj_ref[k].astype(F32) for k in range(proj_ref.shape[0]))[:own]
        tall = pack_ref[...]
        turned = jnp.concatenate([tall, jnp.zeros((-tall.shape[0] % 128, tall.shape[1]), F32)], axis=0).T
        for (lo, size, turn), out in zip(cuts, small_outs):
            out[...] = turned[lo : lo + size, :own] if turn else pack_ref[0:own, lo : lo + size]


def finish(pack, up, down, proj, own, cuts):
    experts, piece, width = up.shape
    if own % 8:
        small = [pack[:own, lo : lo + size].T if turn else pack[:own, lo : lo + size] for lo, size, turn in cuts]
        return [up.astype(F32), down.astype(F32), pack[own : own + 1], jnp.sum(proj[:, :own].astype(F32), axis=0)] + small
    whole = lambda shape: pl.BlockSpec(shape, lambda e: (0,) * len(shape))
    part = lambda shape: pl.BlockSpec((1,) + shape[1:], lambda e: (e, 0, 0))
    shapes = [(experts, piece, width)] * 2 + [(1, pack.shape[1]), (own, width)] + [(size, own) if turn else (own, size) for _, size, turn in cuts]
    return pl.pallas_call(
        functools.partial(finish_kernel, own, cuts),
        grid=(experts,),
        in_specs=[whole(pack.shape), part(up.shape), part(up.shape), whole(proj.shape)],
        out_specs=[part(shapes[0]), part(shapes[1])] + [whole(s) for s in shapes[2:]],
        out_shape=[jax.ShapeDtypeStruct(s, F32) for s in shapes],
        compiler_params=pltpu.CompilerParams(vmem_limit_bytes=VM),
        name="finish",
    )(pack, up, down, proj)


def pack_params_kernel(x_ref, dt_ref, log_ref, taps_ref, bias_ref, dtb_ref, skip_ref, small_ref, out_ref, thin, tall):
    own, x_cols = x_ref.shape
    thin[...] = jnp.zeros_like(thin)
    at = 0
    for ref in (log_ref, taps_ref, bias_ref, dtb_ref, skip_ref):
        thin[at : at + ref.shape[0], 0:own] = ref[...].astype(F32)
        at += ref.shape[0]
    tall[...] = jnp.zeros_like(tall)
    at = x_cols + dt_ref.shape[1]
    tall[0:own, 0:x_cols] = x_ref[...].astype(F32)
    tall[0:own, x_cols:at] = dt_ref[...].astype(F32)
    tall[0:own, at : at + thin.shape[0]] = thin[...].T[:own]
    tall[own : own + 1, 0 : small_ref.shape[1]] = small_ref[...].astype(F32)
    out_ref[...] = tall[...].astype(BF)


def pack_params(w_x, w_dt, log_t, taps_t, bias, dtb, skip, small):
    own = w_x.shape[0]
    rows = own + -own % 16
    if own % 8:
        wide = jnp.concatenate([w_x, w_dt, log_t.T, taps_t.T, bias.T, dtb.T, skip.T], axis=1)
        wide = jnp.pad(wide, ((0, -own % 16), (0, 256 - wide.shape[1])))
        return wide + jnp.pad(small, ((own, -own % 16 - 1), (0, 256 - small.shape[1])))
    return pl.pallas_call(
        pack_params_kernel,
        out_shape=jax.ShapeDtypeStruct((rows, 256), BF),
        scratch_shapes=[pltpu.VMEM((32, 128), F32), pltpu.VMEM((rows, 256), F32)],
        name="pack_params",
    )(w_x, w_dt, log_t, taps_t, bias, dtb, skip, small)


def chain_kernel(step, pieces, carry_ref, own_ref, out_ref, inbox, outbox, send, recv):
    dp, z = lax.axis_index("dp"), lax.axis_index("seq")
    last = lax.axis_size("seq") - 1
    has_before = z > 0 if step > 0 else z < last
    has_after = z < last if step > 0 else z > 0
    barrier = pltpu.get_barrier_semaphore()

    def neighbours(act):
        pl.when(has_before)(lambda: act(z - step))
        pl.when(has_after)(lambda: act(z + step))

    neighbours(lambda peer: pl.semaphore_signal(barrier, inc=1, device_id=(dp, peer), device_id_type=MESH))
    count = last + 1
    pl.semaphore_wait(barrier, (z + last) // count + (2 * last - z) // count)
    wide = own_ref.shape[1] // pieces

    def copy(g):
        return pltpu.make_async_remote_copy(outbox.at[g], inbox.at[g], send.at[g], recv.at[g], device_id=(dp, z + step), device_id_type=MESH)

    def back(g):
        return pltpu.make_async_remote_copy(outbox.at[g], inbox.at[g], send.at[g], recv.at[g], device_id=(dp, z - step), device_id_type=MESH)

    for g in range(pieces):
        c = slice(g * wide, (g + 1) * wide)

        @pl.when(has_before)
        def _():
            back(g).wait_recv()
            out_ref[:, c] = inbox[g].astype(F32)

        @pl.when(jnp.logical_not(has_before))
        def _():
            out_ref[:, c] = jnp.zeros((out_ref.shape[0], wide), F32)

        @pl.when(has_after)
        def _():
            outbox[g] = (carry_ref[:, c] * out_ref[:, c] + own_ref[:, c]).astype(BF)
            copy(g).start()

    @pl.when(has_after)
    def _():
        for g in range(pieces):
            copy(g).wait_send()


def chain(carry, own, step, collective_id):
    pieces = 3
    n, chans = own.shape
    return pl.pallas_call(
        functools.partial(chain_kernel, step, pieces),
        in_specs=[pl.BlockSpec(memory_space=pltpu.VMEM)] * 2,
        out_specs=pl.BlockSpec(memory_space=pltpu.VMEM),
        out_shape=jax.ShapeDtypeStruct((n, chans), F32),
        scratch_shapes=[pltpu.VMEM((pieces, n, chans // pieces), BF)] * 2 + [pltpu.SemaphoreType.DMA((pieces,))] * 2,
        compiler_params=pltpu.CompilerParams(collective_id=collective_id, has_side_effects=True),
        name="chain",
    )(carry, own)


def experts_kernel(block, piece, pick_ref, n2_ref, early_ref, go_ref, router_ref, up_hbm, down_hbm, back_ref, late_ref, mixed_ref, grouter_ref, gexp_hbm,
                   up, down, gup, gdown, outbox, inbox, ret, total, disp, load_sem, store_sem, own_sem, out_send, out_recv, back_own, back_send, back_recv):
    dp, z = lax.axis_index("dp"), lax.axis_index("seq")
    count = lax.axis_size("seq")
    peers = [lax.rem(z + j, count) for j in range(1, count)]
    blocks = up.shape[0] // block
    rows, width = total.shape
    each = rows // count

    def loads(b):
        at = pl.ds(pl.multiple_of(b * block, block), block)
        return [pltpu.make_async_copy(up_hbm.at[at], up.at[at], load_sem.at[b, 0]), pltpu.make_async_copy(down_hbm.at[at], down.at[at], load_sem.at[b, 1])]

    def stores(b):
        made = []
        for i in range(block // piece):
            at = pl.ds(pl.multiple_of(b * block + i * piece, 16), piece)
            to = b * (block // piece) + i
            made.append(pltpu.make_async_copy(gup.at[at], gexp_hbm.at[to, 0], store_sem.at[to, 0]))
            made.append(pltpu.make_async_copy(gdown.at[at], gexp_hbm.at[to, 1], store_sem.at[to, 1]))
        return made

    def send(j):
        return pltpu.make_async_remote_copy(outbox.at[peers[j]], inbox.at[z], out_send.at[j], out_recv.at[j], device_id=(dp, peers[j]), device_id_type=MESH)

    def came(j):
        return pltpu.make_async_remote_copy(outbox.at[z], inbox.at[lax.rem(z + count - 1 - j, count)], out_send.at[j], out_recv.at[j], device_id=(dp, z), device_id_type=MESH)

    def kept():
        return pltpu.make_async_copy(outbox.at[z], inbox.at[z], own_sem.at[0])

    def give(half, j):
        return pltpu.make_async_remote_copy(ret.at[half, peers[j]], back_ref.at[z], back_send.at[half, j], back_recv.at[half, j], device_id=(dp, peers[j]), device_id_type=MESH)

    def got(half, j):
        return pltpu.make_async_remote_copy(ret.at[half, z], back_ref.at[lax.rem(z + count - 1 - j, count)], back_send.at[half, j], back_recv.at[half, j], device_id=(dp, z), device_id_type=MESH)

    def give_own(half):
        return pltpu.make_async_copy(ret.at[half, z], back_ref.at[z], back_own.at[half])

    greet([(dp, peer) for peer in peers])
    picked = lax.dot_general(pick_ref[...], n2_ref[...], TN, preferred_element_type=F32)
    outbox[...] = picked.astype(BF).reshape(count, each, width)
    for j in range(count - 1):
        send(j).start()
    kept().start()
    for b in range(blocks):
        for copy in loads(b):
            copy.start()
    lanes = lax.broadcasted_iota(jnp.int32, (rows, router_ref.shape[1]), 1)
    mine = (lanes == z).astype(F32)
    for half in range(2):
        if half:
            kept().wait()
            for j in range(count - 1):
                came(j).wait_recv()
        slots = (inbox if half else early_ref)[...].reshape(rows, width)
        go = go_ref[:, half * each : (half + 1) * each, :].reshape(rows, width).astype(F32)
        logits = jnp.where(lanes < count, jnp.dot(slots, router_ref[...], preferred_element_type=F32), -1e30)
        powers = jnp.exp(logits - jnp.max(logits, axis=1, keepdims=True))
        probs = jnp.where(lanes < count, powers / jnp.sum(powers, axis=1, keepdims=True), 0.0)
        gate = jnp.sum(probs * mine, axis=1, keepdims=True)
        grads = (gate * go).astype(BF)
        total[...] = jnp.zeros_like(total)
        disp[...] = jnp.zeros_like(disp)

        def units(b, _):
            at = pl.ds(pl.multiple_of(b * block, block), block)
            if half == 0:
                for copy in loads(b):
                    copy.wait()
            hidden = lax.dot_general(slots, up[at, :], NT, preferred_element_type=F32)
            phi = 0.5 * (1.0 + lax.erf(hidden * (1.0 / math.sqrt(2.0))))
            act = (hidden * phi).astype(BF)
            slope = phi + hidden * jnp.exp(hidden * hidden * -0.5) * (1.0 / math.sqrt(2.0 * math.pi))
            ghid = (lax.dot_general(grads, down[at, :], NT, preferred_element_type=F32) * slope).astype(BF)
            total[...] += jnp.dot(act, down[at, :], preferred_element_type=F32)
            disp[...] += jnp.dot(ghid, up[at, :], preferred_element_type=F32)
            new_up = lax.dot_general(ghid, slots, TN, preferred_element_type=F32)
            new_down = lax.dot_general(act, grads, TN, preferred_element_type=F32)
            if half == 0:
                gup[at, :] = new_up.astype(BF)
                gdown[at, :] = new_down.astype(BF)
            else:
                gup[at, :] = (gup[at, :].astype(F32) + new_up).astype(BF)
                gdown[at, :] = (gdown[at, :].astype(F32) + new_down).astype(BF)
                for copy in stores(b):
                    copy.start()
            return 0

        lax.fori_loop(0, blocks, units, 0)
        expert_out = total[...]
        mixed_ref[:, half * each : (half + 1) * each, :] = (gate * expert_out).astype(BF).reshape(count, each, width)
        grad_gate = jnp.sum(go * expert_out, axis=1, keepdims=True)
        grad_logits = (grad_gate * gate * (mine - probs)).astype(BF)
        grad_n2 = disp[...] + lax.dot_general(grad_logits, router_ref[...], NT, preferred_element_type=F32)
        if half == 0:
            ret[half] = grad_n2.astype(BF).reshape(count, each, width)
            for j in range(count - 1):
                give(half, j).start()
            give_own(half).start()
        else:
            late_ref[...] = grad_n2.astype(BF).reshape(count, each, width)
        grouter = lax.dot_general(slots, grad_logits, TN, preferred_element_type=F32)
        if half == 0:
            grouter_ref[...] = grouter
        else:
            grouter_ref[...] += grouter
    for b in range(blocks):
        for copy in stores(b):
            copy.wait()
    give_own(0).wait()
    for j in range(count - 1):
        send(j).wait_send()
        give(0, j).wait_send()
        got(0, j).wait_recv()


def experts_pass(pick, n2, early, go, router, up, down, block, piece, collective_id):
    count, slots, width = go.shape
    units = up.shape[0]
    rows = count * slots // 2
    vmem = pl.BlockSpec(memory_space=pltpu.VMEM)
    hbm = pl.BlockSpec(memory_space=pl.ANY)
    sems = lambda *s: pltpu.SemaphoreType.DMA(s)
    blocks = units // block
    return pl.pallas_call(
        functools.partial(experts_kernel, block, piece),
        in_specs=[vmem] * 5 + [hbm] * 2,
        out_specs=[hbm, vmem, vmem, vmem, hbm],
        out_shape=[jax.ShapeDtypeStruct((count, slots // 2, width), BF)] * 2 + [jax.ShapeDtypeStruct((count, slots, width), BF), jax.ShapeDtypeStruct(router.shape, F32),
                   jax.ShapeDtypeStruct((units // piece, 2, piece, width), BF)],
        scratch_shapes=[pltpu.VMEM(up.shape, BF)] * 4
        + [pltpu.VMEM((count, slots // 2, width), BF)] * 2 + [pltpu.VMEM((1, count, slots // 2, width), BF)] + [pltpu.VMEM((rows, width), F32)] * 2
        + [sems(blocks, 2), sems(units // piece, 2), sems(1), sems(count - 1), sems(count - 1), sems(1), sems(1, count - 1), sems(1, count - 1)],
        compiler_params=pltpu.CompilerParams(collective_id=collective_id, has_side_effects=True, vmem_limit_bytes=VM),
        cost_estimate=pl.CostEstimate(flops=24 * rows * units * width, bytes_accessed=100_000_000, transcendentals=4 * rows * units),
        name="experts",
    )(pick, n2, early, go, router, up, down)


def dot(a, b):
    return jnp.dot(a, b, preferred_element_type=F32)


def dot_nt(a, b):
    return lax.dot_general(a, b, NT, preferred_element_type=F32)


def dot_tn(a, b):
    return lax.dot_general(a, b, TN, preferred_element_type=F32)


def shift(value, axis, steps):
    count = lax.axis_size(axis)
    first, last = (max(0, -steps), min(count, count - steps))
    return lax.ppermute(value, axis, [(source, source + steps) for source in range(first, last)])


def rms_scale(value):
    return lax.rsqrt(jnp.mean(value * value, axis=-1, keepdims=True) + EPS)


def rms_back(value, gain, grad):
    scale = rms_scale(value)
    scaled = grad * gain
    grad_gain = jnp.sum(grad * (value * scale), axis=0)
    return scale * scaled - value * (scale * scale * scale) * jnp.mean(value * scaled, axis=-1, keepdims=True), grad_gain


def swap(value):
    return lax.all_to_all(value, "seq", 0, 0)


def shards(tokens, segment_ids, routes, cotangent, small_params, w_in, conv_w, conv_b, w_x, w_dt, dt_bias, a_log, d_skip, w_out, w_up, w_down):
    both = ("dp", "seq")
    devices = lax.axis_size(both)
    width = tokens.shape[2]
    rows = tokens.shape[1]
    experts = w_up.shape[0]
    chans = w_in.shape[0] * devices // 2
    own = w_out.shape[0]
    rank = w_dt.shape[1]
    n = a_log.shape[1]
    taps = conv_w.shape[1]
    slots = rows // 2
    halo = 16
    wide = 768

    tok_b = tokens[0]
    seg_plus = segment_ids[0] + 1

    share = small_params.shape[0]
    packed = pack_params(w_x, w_dt, a_log.T, conv_w.T, conv_b[None], dt_bias[None], d_skip[None], small_params[None])
    direct = lax.axis_size("dp") == 8 and lax.axis_size("seq") == 4
    ring = [[r ^ (r >> 1) for r in range(8)]] if direct else None
    up_t = jnp.swapaxes(w_up, 1, 2)
    full_out = lax.all_gather(w_out, both, axis=0, tiled=True)
    if direct:
        last_ids = jnp.broadcast_to(seg_plus[rows - halo :, None], (halo, 128))
        all_in, all_pack, part_up, rim_tok, rim_ids = gather_all(w_in, packed, up_t, tok_b, last_ids, 80, 4)
        down_late, all_in = lax.optimization_barrier((w_down, all_in))
        part_down = swap(down_late)
        rim_ids = jnp.where(lax.axis_index("seq") > 0, rim_ids[:, 0], 0)
    else:
        all_in, all_pack = lax.all_gather(w_in, both), lax.all_gather(packed, both)
        part_up, part_down = swap(up_t), swap(w_down)
        rim_tok = shift(tok_b[rows - halo :], "seq", 1)
        rim_ids = shift(seg_plus[rows - halo :], "seq", 1)
    full_in = lax.optimization_barrier(all_in.reshape(2 * chans, width))
    small, full_x_t, full_dt_t, alog_t, conv_f, bias_row, dtb_row, skip = unpack(all_pack.reshape(devices, -1, 256), own, (w_x.shape[1], rank, n, taps, 1, 1, 1))
    small, part_up = lax.optimization_barrier((small, part_up))
    full_up = lax.all_gather(part_up, "dp", axis=0, axis_index_groups=ring).reshape(-1, width)
    flat_small = small[:, :share].reshape(-1)
    gain_one = flat_small[:width]
    gain_two = flat_small[width : 2 * width]
    router = flat_small[2 * width :].reshape(width, experts).astype(BF)
    route_ids = routes[0]
    onehot = (route_ids == jnp.arange(experts)[None, :]).astype(BF)
    before = (jnp.arange(rows)[:, None] > jnp.arange(rows)[None, :]).astype(BF)
    place = jnp.sum(dot(before, onehot) * onehot.astype(F32), axis=1).astype(jnp.int32)
    slot_of = route_ids[:, 0] * slots + place
    gather_mat = (slot_of[:, None] == jnp.arange(experts * slots)[None, :]).astype(BF)
    half = slots // 2
    pick_of = place // half * (experts * half) + route_ids[:, 0] * half + place % half
    pick = (pick_of[:, None] == jnp.arange(experts * slots)[None, :]).astype(BF)
    grad_out_b = cotangent[0]
    grad_out = grad_out_b.astype(F32)
    tok_f = tok_b.astype(F32)
    ids_ext = jnp.concatenate([rim_ids, seg_plus])
    same = jnp.stack([ids_ext[halo - taps + 1 + k : halo - taps + 1 + k + rows] == seg_plus for k in range(taps)], axis=1).astype(F32)
    normed, conv_in, conv_sum, values, z, projected = front(rim_tok, tok_b, gain_one[None], full_in, full_x_t, conv_f, bias_row, same, wide)
    low_wide, b_wide, c_wide, b_blk, c_blk, pre_dt, dt, dt_keep, dtx, rates, rates2, own_state, carry = steps(projected, same, values, full_dt_t, dtb_row, alog_t, rank, wide)
    carry, part_down = lax.optimization_barrier((carry, part_down))
    full_down = lax.all_gather(part_down, "dp", axis=0, axis_index_groups=ring).reshape(-1, width)
    start = chain(carry, own_state, 1, 3)
    go_local, start = lax.optimization_barrier((dot_tn(gather_mat, grad_out_b).astype(BF), start))
    go_slots = swap(go_local.reshape(experts, slots, width))
    scanned, checks, gated, first_sum, normed_two, sent = scan_pass(
        dt_keep, dtx, rates2, b_wide, c_blk, start, values, z, skip, full_out, tok_b, gain_two[None], pick[:, : experts * half], wide
    )
    sent, go_slots = lax.optimization_barrier((sent, go_slots))
    early = swap(sent.reshape(experts, half, width))

    piece = w_up.shape[2]
    router_wide = jnp.pad(router, ((0, 0), (0, 128 - experts)))
    back_n2, late_n2, mixed_back, grad_router, grad_exp = experts_pass(pick[:, experts * half :], normed_two, early, go_slots, router_wide, full_up, full_down, 768, piece if piece % 16 == 0 else 768, 5)
    grad_router = grad_router[:, :experts]
    late_n2 = swap(late_n2)
    grad_n2 = dot(pick, jnp.concatenate([back_n2.reshape(-1, width), late_n2.reshape(-1, width)]))
    mixed_slots = swap(mixed_back).reshape(-1, width)
    if piece % 16:
        grad_exp = jnp.swapaxes(jnp.swapaxes(grad_exp, 0, 1).reshape(2, -1, piece, width), 0, 1)
    part_exp = lax.psum_scatter(grad_exp.reshape(-1, width), "dp", scatter_dimension=0, tiled=True, axis_index_groups=ring)

    grad_norm_two, grad_gain_two = rms_back(first_sum, gain_two, grad_n2)
    grad_first = grad_out + grad_norm_two
    grad_mixer = grad_first.astype(BF)
    grad_scanned, grad_z_b, grad_w_out, grad_start = back_front(grad_mixer, full_out, z, scanned, values, skip, gated, dt_keep, rates2, c_wide, chans // 2, ring[0] if direct else None)
    nxt = chain(carry, grad_start, -1, 4)
    grad_vals, g_log, grad_dt_t, grad_dtb, grad_skip, grad_proj = back_pass(
        dt, dt_keep, dtx, grad_scanned, values, pre_dt, skip, rates2, rates, b_wide, c_wide, b_blk, checks, nxt, low_wide, full_dt_t, rank, wide
    )
    grad_vals, mixed_slots, part_exp, grad_w_out = lax.optimization_barrier((grad_vals, mixed_slots, part_exp, grad_w_out))
    part_exp = part_exp.reshape(experts, 2, piece, width)
    part_down = part_exp[:, 1]
    sum_up = swap(part_exp[:, 0])
    mixed_out = (first_sum + dot(gather_mat, mixed_slots)).astype(BF)
    grad_conv_b, grad_last, grad_rim, grad_x_t, grad_taps = conv_back(grad_vals, grad_proj, full_x_t, values, conv_sum, conv_in, same, conv_f, halo, wide)
    grad_last = (grad_last + shift(grad_rim, "seq", -1)).astype(BF)
    grad_conv_in = jnp.concatenate([grad_conv_b[: rows - 8], grad_last])
    grad_w_in = dot_tn(jnp.concatenate([grad_conv_in, grad_z_b], axis=1), normed).astype(BF)
    grad_normed = dot(grad_conv_in, full_in[:chans]) + dot(grad_z_b, full_in[chans:])
    grad_norm_one, grad_gain_one = rms_back(tok_f, gain_one, grad_normed)
    tokens_grad = (grad_first + grad_norm_one).astype(BF)

    grad_small = jnp.concatenate([grad_gain_one, grad_gain_two, grad_router.reshape(-1)])
    grad_packed = pack_grads(
        (grad_x_t, grad_dt_t, g_log, grad_taps, grad_dtb, grad_skip), (w_x.shape[1], rank, n, taps + 1, 1, 1), jnp.pad(grad_small.reshape(devices, -1), ((0, 0), (0, 256 - share))), own
    )
    part_out = lax.psum_scatter(grad_w_out, "dp", scatter_dimension=0, tiled=True, axis_index_groups=ring).reshape(-1, own, width)
    part_out = jnp.pad(part_out, ((0, 0), (0, -own % 16), (0, 0)))
    if direct:
        grad_packed, sum_up = lax.optimization_barrier((grad_packed, sum_up))
        sum_in, sum_pack, all_out, sum_down = scatter_all(
            grad_w_in.reshape(4, 2, 4, 2 * own, width), grad_packed.reshape((4, 2, 4) + grad_packed.shape[1:]), part_out, part_down, 80, 2
        )
    else:
        sum_in = lax.psum_scatter(grad_w_in, both, scatter_dimension=0, tiled=True).astype(F32)
        sum_pack = lax.psum_scatter(grad_packed, both, scatter_dimension=0, tiled=True)[0].astype(F32)
        all_out, sum_down = swap(part_out), swap(part_down)
    cuts, at = [], 0
    for size, turn in ((w_x.shape[1], False), (rank, False), (n, True), (taps, True), (1, True), (1, True), (1, True)):
        cuts.append((at, size, turn))
        at += size
    up_out, down_out, s_row, sum_out, s_x, s_dt, s_log, s_conv, s_bias, s_dtb, s_skip = finish(sum_pack, sum_up, sum_down, all_out, own, tuple(cuts))
    return (
        mixed_out[None],
        tokens_grad[None],
        s_row[0, :share],
        sum_in,
        s_conv.T,
        s_bias[0],
        s_x,
        s_dt,
        s_dtb[0],
        s_log.T,
        s_skip[0],
        sum_out,
        jnp.swapaxes(up_out, 1, 2),
        down_out,
    )


def solution(mesh):
    split = ("dp", "seq")
    token, row, mat, vec = P("dp", "seq", None), P("dp", "seq"), P(split, None), P(split)
    return jax.shard_map(
        shards,
        mesh=mesh,
        in_specs=(token, row, token, token, vec, mat, mat, vec, mat, mat, vec, mat, vec, mat, P(None, None, split), P(None, split, None)),
        out_specs=(token, token, vec, mat, mat, vec, mat, mat, vec, mat, vec, mat, P(None, None, split), P(None, split, None)),
        check_vma=False,
    )
```

```python
import functools
import math

import jax
import jax.numpy as jnp
from jax import lax
from jax.experimental import pallas as pl
from jax.experimental.pallas import tpu as pltpu
from jax.sharding import PartitionSpec as P

F32, BF = jnp.float32, jnp.bfloat16
EPS = 1e-05
STEP = 16
VM = 56 * 1024 * 1024
MESH = pl.DeviceIdType.MESH
SMALL = pl.CostEstimate(flops=0, bytes_accessed=0, transcendentals=0)
NT = (((1,), (1,)), ((), ()))
TN = (((0,), (0,)), ((), ()))


def rowr(ref, at, i, c, n):
    return jnp.broadcast_to(ref.at[pl.ds(at, STEP), c][i : i + 1, :], (n, 128))

def state_kernel(n, dte_ref, dtx_ref, rate_ref, b_ref, state_ref, carry_ref):
    rows, wide = dte_ref.shape
    tiles = wide // 128
    rates = [rate_ref[:, j*128:(j+1)*128] for j in range(tiles)]
    def block(k, carry):
        state, total = carry
        at = pl.multiple_of(k * STEP, STEP)
        dte = dte_ref[pl.ds(at, STEP), :]
        dtx = dtx_ref[pl.ds(at, STEP), :]
        state = list(state)
        for i in range(STEP):
            bs = b_ref[pl.ds((at + i) * n, n), :]
            for j in range(tiles):
                c = slice(j*128, (j+1)*128)
                decay = jnp.exp2(rowr(dte_ref, at, i, c, n) * rates[j])
                state[j] = decay * state[j] + bs * rowr(dtx_ref, at, i, c, n)
        return tuple(state), total + dte
    zero = tuple(jnp.zeros((n, 128), F32) for _ in range(tiles))
    state, total = lax.fori_loop(0, rows // STEP, block, (zero, jnp.zeros((STEP, wide), F32)))
    summed = jnp.sum(total, axis=0, keepdims=True)
    for j in range(tiles):
        c = slice(j*128, (j+1)*128)
        state_ref[:, c] = state[j]
        carry_ref[:, c] = jnp.exp2(jnp.broadcast_to(summed[:, c], (n, 128)) * rates[j])

def front_kernel(rim_ref, tok_ref, gain_ref, wc_ref, wz_ref, xt_ref, taps_ref, bias_ref, same_ref, normed_ref, conv_ref, sum_ref, values_ref, z_ref, proj_ref, ext):
    rows, wide = sum_ref.shape
    halo = rim_ref.shape[0]
    taps = taps_ref.shape[0]

    @pl.when(pl.program_id(0) == 0)
    def _():
        for ref, lo in ((rim_ref, 0), (tok_ref, halo)):
            tok = ref[...].astype(F32)
            scale = lax.rsqrt(jnp.mean(tok * tok, axis=1, keepdims=True) + EPS)
            ext[lo : lo + ref.shape[0], :] = (tok * scale * gain_ref[...]).astype(BF)
        normed_ref[...] = ext[halo:, :]
        proj_ref[...] = jnp.zeros_like(proj_ref)

    conv_ref[...] = lax.dot_general(ext[...], wc_ref[...], NT, preferred_element_type=F32).astype(BF).astype(F32)
    z_ref[...] = lax.dot_general(ext[halo:, :], wz_ref[...], NT, preferred_element_type=F32)
    same = [jnp.broadcast_to(same_ref[:, k : k + 1], (rows, 128)) for k in range(taps)]
    for j in range(wide // 128):
        c = slice(j * 128, (j + 1) * 128)
        total = jnp.broadcast_to(bias_ref[:, c], (rows, 128))
        for k in range(taps):
            lo = halo - taps + 1 + k
            total = total + taps_ref[k : k + 1, c] * conv_ref[lo : lo + rows, c] * same[k]
        sum_ref[:, c] = total
        values_ref[:, c] = total * jax.nn.sigmoid(total)
    proj_ref[...] += lax.dot_general(values_ref[...].astype(BF), xt_ref[...], NT, preferred_element_type=F32)


def front(rim, tok, gain, full_in, x_t, conv_taps, bias, same, wide):
    rows, width = tok.shape
    halo = rim.shape[0]
    chans = full_in.shape[0] // 2
    taps = conv_taps.shape[0]
    col = lambda r: pl.BlockSpec((r, wide), lambda g: (0, g))
    whole = lambda a: pl.BlockSpec(a.shape, lambda g: (0, 0))
    steps = chans // wide
    f32 = lambda r: jax.ShapeDtypeStruct((r, chans), F32)
    return pl.pallas_call(
        front_kernel,
        grid=(steps,),
        in_specs=[whole(rim), whole(tok), whole(gain), pl.BlockSpec((wide, width), lambda g: (g, 0)), pl.BlockSpec((wide, width), lambda g: (g + steps, 0)),
                  col(128), col(taps), col(1), whole(same)],
        out_specs=[whole(tok), col(rows + halo), col(rows), col(rows), col(rows), pl.BlockSpec((rows, 128), lambda g: (0, 0))],
        out_shape=[jax.ShapeDtypeStruct((rows, width), BF), f32(rows + halo), f32(rows), f32(rows), f32(rows), jax.ShapeDtypeStruct((rows, 128), F32)],
        scratch_shapes=[pltpu.VMEM((rows + halo, width), BF)],
        compiler_params=pltpu.CompilerParams(vmem_limit_bytes=VM),
        cost_estimate=pl.CostEstimate(flops=4*rows*chans*width, bytes_accessed=4*chans*width + 16*rows*chans, transcendentals=rows*chans),
        name="front",
    )(rim, tok, gain, full_in, full_in, x_t, conv_taps, bias, same)


def steps_kernel(n, rank_cols, proj_ref, keep_ref, values_ref, dtt_ref, dtb_ref, alog_ref,
                 low_ref, bw_ref, cw_ref, bblk_ref, cblk_ref, pre_ref, dt_ref, dte_ref, dtx_ref, rate_ref, rate2_ref, state_ref, carry_ref):
    rows, wide = pre_ref.shape
    groups = STEP * n

    @pl.when(pl.program_id(0) == 0)
    def _():
        proj = proj_ref[...]
        lanes = lax.broadcasted_iota(jnp.int32, proj.shape, 1)
        low_ref[...] = jnp.where(lanes < rank_cols, proj, 0.0).astype(BF)
        row = lax.broadcasted_iota(jnp.int32, (rows, groups), 0)
        col = lax.broadcasted_iota(jnp.int32, (rows, groups), 1)
        own = lax.rem(row, STEP) == col // n
        to_col = lax.rem(lax.broadcasted_iota(jnp.int32, (128, groups), 1), n)
        from_col = lax.broadcasted_iota(jnp.int32, (128, groups), 0)
        for i, (wide_ref, blk_ref) in enumerate(((bw_ref, bblk_ref), (cw_ref, cblk_ref))):
            pick = (from_col == to_col + rank_cols + i * n).astype(F32)
            tiled = jnp.where(own, jnp.dot(proj, pick, precision=lax.Precision.HIGHEST, preferred_element_type=F32), 0.0)
            high = tiled.astype(BF)
            low = (tiled - high.astype(F32)).astype(BF)
            blk_ref[...] = high
            ones = jnp.ones((STEP, 128), BF)
            for k in range(rows // STEP):
                at = slice(k * STEP, (k + 1) * STEP)
                wide_ref[k * groups : (k + 1) * groups, :] = lax.dot_general(high[at], ones, TN, preferred_element_type=F32) + lax.dot_general(low[at], ones, TN, preferred_element_type=F32)

    pre = jnp.dot(low_ref[...], dtt_ref[...], preferred_element_type=F32) + dtb_ref[...]
    dt = jax.nn.softplus(pre)
    pre_ref[...] = pre
    dt_ref[...] = dt
    dtx_ref[...] = dt * values_ref[...]
    taps = keep_ref.shape[1]
    keep = jnp.broadcast_to(keep_ref[:, taps - 2 : taps - 1], (rows, 128))
    for j in range(wide // 128):
        c = slice(j * 128, (j + 1) * 128)
        dte_ref[:, c] = jnp.where(keep > 0, dt[:, c], 1e30)
    rate = -jnp.exp(alog_ref[...])
    rate_ref[...] = rate
    rate2_ref[...] = rate * math.log2(math.e)
    state_kernel(n, dte_ref, dtx_ref, rate2_ref, bw_ref, state_ref, carry_ref)


def steps(proj, same, values, dt_t, dtb, alog_t, rank_cols, wide):
    rows, chans = values.shape
    n = alog_t.shape[0]
    groups = STEP * n
    col = lambda r: pl.BlockSpec((r, wide), lambda g: (0, g))
    fixed = lambda *s: pl.BlockSpec(s, lambda g: (0, 0))
    f32 = lambda *s: jax.ShapeDtypeStruct(s, F32)
    bf = lambda *s: jax.ShapeDtypeStruct(s, BF)
    return pl.pallas_call(
        functools.partial(steps_kernel, n, rank_cols),
        grid=(chans // wide,),
        in_specs=[fixed(rows, 128), fixed(*same.shape), col(rows), col(128), col(1), col(n)],
        out_specs=[fixed(rows, 128), fixed(rows * n, 128), fixed(rows * n, 128), fixed(rows, groups), fixed(rows, groups)] + [col(rows)] * 4 + [col(n)] * 4,
        out_shape=[bf(rows, 128), f32(rows * n, 128), f32(rows * n, 128), bf(rows, groups), bf(rows, groups)] + [f32(rows, chans)] * 4 + [f32(n, chans)] * 4,
        compiler_params=pltpu.CompilerParams(vmem_limit_bytes=VM),
        cost_estimate=pl.CostEstimate(flops=10*rows*chans*n, bytes_accessed=24*rows*chans, transcendentals=rows*chans*n),
        name="steps",
    )(proj, same, values, dt_t, dtb, alog_t)


def scan_kernel(n, dte_ref, dtx_ref, rate_ref, b_ref, cblk_ref, start_ref, values_ref, z_ref, skip_ref, out_ref, tok_ref, gain_ref, pick_ref,
                y_ref, check_ref, gated_ref, first_ref, normed_ref, sent_ref, hs):
    rows, wide = dte_ref.shape
    tiles = wide // 128
    rates = [rate_ref[:, j*128:(j+1)*128] for j in range(tiles)]

    def block(k, state):
        at = pl.multiple_of(k * STEP, STEP)
        dte = dte_ref[pl.ds(at, STEP), :]
        dtx = dtx_ref[pl.ds(at, STEP), :]
        state = list(state)
        kn = pl.multiple_of(k * n, n)
        for j in range(tiles):
            check_ref[pl.ds(kn, n), j*128:(j+1)*128] = state[j]
        for i in range(STEP):
            bs = b_ref[pl.ds((at + i) * n, n), :]
            for j in range(tiles):
                c = slice(j*128, (j+1)*128)
                decay = jnp.exp2(rowr(dte_ref, at, i, c, n) * rates[j])
                state[j] = decay * state[j] + bs * rowr(dtx_ref, at, i, c, n)
                hs[i*n:(i+1)*n, c] = state[j].astype(BF)
        y_ref[pl.ds(at, STEP), :] = jnp.dot(cblk_ref[pl.ds(at, STEP), :], hs[...], preferred_element_type=F32)
        return tuple(state)

    start = tuple(start_ref[:, j*128:(j+1)*128] for j in range(tiles))
    lax.fori_loop(0, rows // STEP, block, start)

    @pl.when(pl.program_id(0) == 0)
    def _():
        first_ref[...] = tok_ref[...].astype(F32)

    z = z_ref[...]
    gated_ref[...] = ((y_ref[...] + skip_ref[...] * values_ref[...]) * (z * jax.nn.sigmoid(z))).astype(BF)
    first_ref[...] += jnp.dot(gated_ref[...], out_ref[...], preferred_element_type=F32)

    @pl.when(pl.program_id(0) == pl.num_programs(0) - 1)
    def _():
        first = first_ref[...]
        scale = lax.rsqrt(jnp.mean(first * first, axis=1, keepdims=True) + EPS)
        normed_ref[...] = (first * scale * gain_ref[...]).astype(BF)
        sent_ref[...] = lax.dot_general(pick_ref[...], normed_ref[...], TN, preferred_element_type=F32).astype(BF)


def scan_pass(dte, dtx, rates2, b_wide, c_blk, start, values, z, skip, full_out, tok, gain, pick, wide):
    rows, chans = dte.shape
    n = rates2.shape[0]
    width = tok.shape[1]
    col = lambda r: pl.BlockSpec((r, wide), lambda g: (0, g))
    whole = lambda a: pl.BlockSpec(a.shape, lambda g: (0, 0))
    return pl.pallas_call(
        functools.partial(scan_kernel, n),
        grid=(chans // wide,),
        in_specs=[col(rows), col(rows), col(n), whole(b_wide), whole(c_blk), col(n), col(rows), col(rows), col(1), pl.BlockSpec((wide, width), lambda g: (g, 0)), whole(tok), whole(gain), whole(pick)],
        out_specs=[col(rows), col(rows // STEP * n), col(rows), whole(tok), whole(tok), pl.BlockSpec((pick.shape[1], width), lambda g: (0, 0))],
        out_shape=[jax.ShapeDtypeStruct((rows, chans), F32), jax.ShapeDtypeStruct((rows // STEP * n, chans), F32), jax.ShapeDtypeStruct((rows, chans), BF),
                   jax.ShapeDtypeStruct((rows, width), F32), jax.ShapeDtypeStruct((rows, width), BF), jax.ShapeDtypeStruct((pick.shape[1], width), BF)],
        scratch_shapes=[pltpu.VMEM((STEP * n, wide), BF)],
        compiler_params=pltpu.CompilerParams(vmem_limit_bytes=VM),
        cost_estimate=pl.CostEstimate(flops=10*rows*chans*n, bytes_accessed=12*rows*chans, transcendentals=rows*chans*n),
        name="scan_pass",
    )(dte, dtx, rates2, b_wide, c_blk, start, values, z, skip, full_out, tok, gain, pick)


def back_state_kernel(n, dte_ref, gs_ref, rate_ref, c_ref, out_ref):
    rows, wide = dte_ref.shape
    tiles = wide // 128
    rates = [rate_ref[:, j*128:(j+1)*128] for j in range(tiles)]
    def block(k, state):
        at = pl.multiple_of(rows - STEP - k * STEP, STEP)
        dte = dte_ref[pl.ds(at, STEP), :]
        gs = gs_ref[pl.ds(at, STEP), :]
        state = list(state)
        for i in reversed(range(STEP)):
            cs = c_ref[pl.ds((at + i) * n, n), :]
            for j in range(tiles):
                c = slice(j*128, (j+1)*128)
                decay = jnp.exp2(rowr(dte_ref, at, i, c, n) * rates[j])
                state[j] = decay * (state[j] + cs * rowr(gs_ref, at, i, c, n))
        return tuple(state)
    zero = tuple(jnp.zeros((n, 128), F32) for _ in range(tiles))
    state = lax.fori_loop(0, rows // STEP, block, zero)
    for j in range(tiles):
        out_ref[:, j*128:(j+1)*128] = state[j]

def back_front_kernel(n, order, steps, grad_ref, out_ref, z_ref, y_ref, values_ref, skip_ref, gated_ref, dte_ref, rate_ref, c_ref, gs_ref, gz_ref, gwo_ref, state_ref):
    grad = grad_ref[...]
    gated = lax.dot_general(grad, out_ref[...], NT, preferred_element_type=F32)
    z = z_ref[...]
    sig = jax.nn.sigmoid(z)
    gs_ref[...] = gated * (z * sig)
    gz_ref[...] = (gated * (y_ref[...] + skip_ref[...] * values_ref[...]) * (sig * (1.0 + z * (1.0 - sig)))).astype(BF)
    grad_out = lax.dot_general(gated_ref[...], grad, TN, preferred_element_type=F32).astype(BF)
    if order is None:
        gwo_ref[...] = grad_out
    else:
        per = len(order) // steps
        size = grad_out.shape[0] // per
        for g in range(steps):

            @pl.when(pl.program_id(0) == g)
            def _():
                for to, share in enumerate(order[g * per : (g + 1) * per]):
                    at = (share - g * per) * size
                    gwo_ref[to * size : (to + 1) * size, :] = grad_out[at : at + size]

    back_state_kernel(n, dte_ref, gs_ref, rate_ref, c_ref, state_ref)


def back_front(grad, full_out, z, scanned, values, skip, gated, dte, rates2, c_wide, wide, order=None):
    rows, chans = dte.shape
    width = grad.shape[1]
    n = rates2.shape[0]
    col = lambda r: pl.BlockSpec((r, wide), lambda g: (0, g))
    whole = lambda a: pl.BlockSpec(a.shape, lambda g: (0, 0))
    flat = pl.BlockSpec((wide, width), lambda g: (g, 0))
    return pl.pallas_call(
        functools.partial(back_front_kernel, n, order, chans // wide),
        grid=(chans // wide,),
        in_specs=[whole(grad), flat, col(rows), col(rows), col(rows), col(1), col(rows), col(rows), col(n), whole(c_wide)],
        out_specs=[col(rows), col(rows), flat, col(n)],
        out_shape=[jax.ShapeDtypeStruct((rows, chans), F32), jax.ShapeDtypeStruct((rows, chans), BF), jax.ShapeDtypeStruct((chans, width), BF), jax.ShapeDtypeStruct((n, chans), F32)],
        compiler_params=pltpu.CompilerParams(vmem_limit_bytes=VM),
        cost_estimate=pl.CostEstimate(flops=8*rows*chans*n, bytes_accessed=8*rows*chans, transcendentals=rows*chans*n),
        name="back_front",
    )(grad, full_out, z, scanned, values, skip, gated, dte, rates2, c_wide)


def back_kernel(n, rank_cols, dt_ref, dte_ref, dtx_ref, gs_ref, values_ref, pre_ref, skip_ref, rate_ref, rawrate_ref, b_ref, c_ref, bblk_ref, check_ref, next_ref, low_ref, wdt_ref,
                gval_ref, glog_ref, gwdt_ref, gdtb_ref, gskip_ref, proj_ref, us, decs, hs, ls, ps, gdtx, gdt, gb, gc, rank):
    rows, wide = dte_ref.shape
    tiles = wide // 128
    rates = [rate_ref[:, j*128:(j+1)*128] for j in range(tiles)]

    @pl.when(pl.program_id(0) == 0)
    def _():
        gb[...] = jnp.zeros_like(gb)
        gc[...] = jnp.zeros_like(gc)
        rank[...] = jnp.zeros_like(rank)

    ones = (lax.broadcasted_iota(jnp.int32, (STEP, STEP * n), 0) == lax.broadcasted_iota(jnp.int32, (STEP, STEP * n), 1) // n).astype(BF)
    glog_ref[...] = jnp.zeros_like(glog_ref)

    def block(k, later):
        kk = rows // STEP - 1 - k
        at = pl.multiple_of(kk * STEP, STEP)
        kn = pl.multiple_of(kk * n, n)
        dte = dte_ref[pl.ds(at, STEP), :]
        dtx = dtx_ref[pl.ds(at, STEP), :]
        state = [check_ref[pl.ds(kn, n), j*128:(j+1)*128] for j in range(tiles)]
        for i in range(STEP):
            bs = b_ref[pl.ds((at + i) * n, n), :]
            for j in range(tiles):
                c = slice(j*128, (j+1)*128)
                decay = jnp.exp2(rowr(dte_ref, at, i, c, n) * rates[j])
                kept = decay * state[j]
                state[j] = kept + bs * rowr(dtx_ref, at, i, c, n)
                decs[i*n:(i+1)*n, c] = decay
                us[i*n:(i+1)*n, c] = kept
                hs[i*n:(i+1)*n, c] = state[j].astype(BF)
        later = list(later)
        dt = dt_ref[pl.ds(at, STEP), :]
        gs = gs_ref[pl.ds(at, STEP), :]
        logs = [glog_ref[:, j*128:(j+1)*128] for j in range(tiles)]
        for i in reversed(range(STEP)):
            cs = c_ref[pl.ds((at + i) * n, n), :]
            for j in range(tiles):
                c = slice(j*128, (j+1)*128)
                adj = later[j] + cs * rowr(gs_ref, at, i, c, n)
                part = adj * us[i*n:(i+1)*n, c] * rawrate_ref[:, c]
                later[j] = adj * decs[i*n:(i+1)*n, c]
                logs[j] = logs[j] + part * rowr(dt_ref, at, i, c, n)
                ls[i*n:(i+1)*n, c] = adj.astype(BF)
                ps[i*n:(i+1)*n, c] = part.astype(BF)
        for j in range(tiles):
            glog_ref[:, j*128:(j+1)*128] = logs[j]
        gdtx[pl.ds(at, STEP), :] = jnp.dot(bblk_ref[pl.ds(at, STEP), :], ls[...], preferred_element_type=F32)
        gdt[pl.ds(at, STEP), :] = jnp.dot(ones, ps[...], preferred_element_type=F32)
        gb[pl.ds(at, STEP), :] += lax.dot_general(dtx.astype(BF), ls[...], NT, preferred_element_type=F32)
        gc[pl.ds(at, STEP), :] += lax.dot_general(gs.astype(BF), hs[...], NT, preferred_element_type=F32)
        return tuple(later)

    start = tuple(next_ref[:, j*128:(j+1)*128] for j in range(tiles))
    lax.fori_loop(0, rows // STEP, block, start)

    values = values_ref[...]
    grad_pre = (gdt[...] + gdtx[...] * values) * jax.nn.sigmoid(pre_ref[...])
    gdtb_ref[...] = jnp.sum(grad_pre, axis=0, keepdims=True)
    grad_pre = grad_pre.astype(BF)
    gwdt_ref[...] = lax.dot_general(low_ref[...], grad_pre, TN, preferred_element_type=F32)
    rank[...] += lax.dot_general(grad_pre, wdt_ref[...], NT, preferred_element_type=F32)
    gs = gs_ref[...]
    gskip_ref[...] = jnp.sum(gs * values, axis=0, keepdims=True)
    gval_ref[...] = gs * skip_ref[...] + gdtx[...] * dt_ref[...]

    @pl.when(pl.program_id(0) == pl.num_programs(0) - 1)
    def _():
        groups = STEP * n
        row = lax.broadcasted_iota(jnp.int32, (rows, groups), 0)
        col = lax.broadcasted_iota(jnp.int32, (rows, groups), 1)
        own = lax.rem(row, STEP) == col // n
        from_col = lax.rem(lax.broadcasted_iota(jnp.int32, (groups, rank.shape[1]), 0), n)
        to_col = lax.broadcasted_iota(jnp.int32, (groups, rank.shape[1]), 1)
        total = rank[...]
        for i, acc in enumerate((gb, gc)):
            place = (to_col == from_col + rank_cols + i * n).astype(BF)
            total = total + jnp.dot(jnp.where(own, acc[...], 0.0).astype(BF), place, preferred_element_type=F32)
        proj_ref[...] = total.astype(BF)


def back_pass(dt, dte, dtx, gs, values, pre, skip, rates2, rates, b_wide, c_wide, b_blk, check, nxt, low, wdt, rank_cols, wide):
    rows, chans = dte.shape
    n = rates2.shape[0]
    col = lambda r: pl.BlockSpec((r, wide), lambda g: (0, g))
    whole = lambda a: pl.BlockSpec(a.shape, lambda g: (0, 0))
    sq = lambda kind, w=wide: pltpu.VMEM((STEP * n, w), kind)
    return pl.pallas_call(
        functools.partial(back_kernel, n, rank_cols),
        grid=(chans // wide,),
        in_specs=[col(rows)] * 6 + [col(1)] + [col(n)] * 2 + [whole(b_wide), whole(c_wide), whole(b_blk), col(rows // STEP * n), col(n), whole(low), col(wdt.shape[0])],
        out_specs=[col(rows), col(n), col(low.shape[1]), col(1), col(1), pl.BlockSpec((rows, 128), lambda g: (0, 0))],
        out_shape=[jax.ShapeDtypeStruct((rows, chans), F32), jax.ShapeDtypeStruct((n, chans), F32), jax.ShapeDtypeStruct((low.shape[1], chans), F32),
                   jax.ShapeDtypeStruct((1, chans), F32), jax.ShapeDtypeStruct((1, chans), F32), jax.ShapeDtypeStruct((rows, 128), BF)],
        scratch_shapes=[sq(F32), sq(F32), sq(BF), sq(BF), sq(BF), pltpu.VMEM((rows, wide), F32), pltpu.VMEM((rows, wide), F32),
                        pltpu.VMEM((rows, STEP * n), F32), pltpu.VMEM((rows, STEP * n), F32), pltpu.VMEM((rows, 128), F32)],
        compiler_params=pltpu.CompilerParams(vmem_limit_bytes=VM),
        cost_estimate=pl.CostEstimate(flops=26*rows*chans*n, bytes_accessed=24*rows*chans, transcendentals=rows*chans*n),
        name="back_pass",
    )(dt, dte, dtx, gs, values, pre, skip, rates2, rates, b_wide, c_wide, b_blk, check, nxt, low, wdt)


def conv_back_kernel(halo, gval_ref, proj_ref, xt_ref, values_ref, sum_ref, ext_ref, same_ref, taps_ref, place_ref, slots_ref, first_ref,
                     mixed_ref, gconv_ref, last_ref, rim_ref, gxt_ref, gtaps_ref, pad):
    rows, wide = gval_ref.shape
    taps = taps_ref.shape[0]

    @pl.when(pl.program_id(0) == 0)
    def _():
        mixed_ref[...] = (first_ref[...] + jnp.dot(place_ref[...], slots_ref[...], preferred_element_type=F32)).astype(BF)

    proj = proj_ref[...]
    grad_values = gval_ref[...] + jnp.dot(proj, xt_ref[...], preferred_element_type=F32)
    gxt_ref[...] = lax.dot_general(proj, values_ref[...].astype(BF), TN, preferred_element_type=F32)
    sums = sum_ref[...]
    sig = jax.nn.sigmoid(sums)
    pad[0:rows, :] = grad_values * (sig * (1.0 + sums * (1.0 - sig)))
    pad[rows:, :] = jnp.zeros((pad.shape[0] - rows, wide), F32)
    row = lax.broadcasted_iota(jnp.int32, (8, 128), 0)
    same = [jnp.broadcast_to(same_ref[:, k : k + 1], (rows, 128)) for k in range(taps)]
    rowed = lax.broadcasted_iota(jnp.int32, (rows, 128), 0)
    later = [jnp.where(rowed < rows - (taps - 1 - k), pltpu.roll(same[k], (rows - (taps - 1 - k)) % rows, 0), 0.0) for k in range(taps)]
    for j in range(wide // 128):
        c = slice(j * 128, (j + 1) * 128)
        grads = pad[0:rows, c]
        sums_of = [jnp.sum(grads * same[k] * ext_ref[halo - taps + 1 + k : halo - taps + 1 + k + rows, c], axis=0, keepdims=True) for k in range(taps)]
        sums_of.append(jnp.sum(grads, axis=0, keepdims=True))
        total = jnp.zeros((rows, 128), F32)
        rim = jnp.zeros((8, 128), F32)
        for k in range(taps):
            weight = taps_ref[k : k + 1, c]
            total = total + pad[taps - 1 - k : taps - 1 - k + rows, c] * later[k] * weight
            if k < taps - 1:
                moved = pltpu.roll(grads[0:8] * same[k][0:8], 8 - taps + 1 + k, 0)
                rim = rim + jnp.where(row >= 8 - taps + 1 + k, moved, 0.0) * weight
        gconv_ref[:, c] = total.astype(BF)
        last_ref[:, c] = total[rows - 8 :]
        rim_ref[:, c] = rim
        gtaps_ref[:, c] = jnp.concatenate(sums_of + [jnp.zeros((8 - len(sums_of), 128), F32)], axis=0)


def conv_back(gval, proj, x_t, values, sums, ext, same, conv_taps, place, slots, first, halo, wide):
    rows, chans = gval.shape
    taps = conv_taps.shape[0]
    col = lambda r: pl.BlockSpec((r, wide), lambda g: (0, g))
    fixed = lambda a: pl.BlockSpec(a.shape, lambda g: (0, 0))
    mask = fixed(same)
    f32 = lambda r: jax.ShapeDtypeStruct((r, chans), F32)
    return pl.pallas_call(
        functools.partial(conv_back_kernel, halo),
        grid=(chans // wide,),
        in_specs=[col(rows), pl.BlockSpec(proj.shape, lambda g: (0, 0)), col(x_t.shape[0]), col(rows), col(rows), col(ext.shape[0]), mask, col(taps), fixed(place), fixed(slots), fixed(first)],
        out_specs=[fixed(first), col(rows), col(8), col(8), col(x_t.shape[0]), col(8)],
        out_shape=[jax.ShapeDtypeStruct(first.shape, BF), jax.ShapeDtypeStruct((rows, chans), BF), f32(8), f32(8), f32(x_t.shape[0]), f32(8)],
        scratch_shapes=[pltpu.VMEM((rows + 8, wide), F32)],
        compiler_params=pltpu.CompilerParams(vmem_limit_bytes=VM),
        cost_estimate=pl.CostEstimate(flops=60*rows*chans, bytes_accessed=20*rows*chans, transcendentals=rows*chans),
        name="conv_back",
    )(gval, proj, x_t, values, sums, ext, same, conv_taps, place, slots, first)


def tail_gate_kernel(gz_ref, normed_ref, win_ref, gwin_ref, total_ref):
    @pl.when(pl.program_id(0) == 0)
    def _():
        total_ref[...] = jnp.zeros_like(total_ref)

    grad = gz_ref[...]
    gwin_ref[...] = lax.dot_general(grad, normed_ref[...], TN, preferred_element_type=F32).astype(BF)
    total_ref[...] += jnp.dot(grad, win_ref[...], preferred_element_type=F32)


def tail_gate(grad_z, normed, full_in, wide):
    rows, width = normed.shape
    chans = grad_z.shape[1]
    steps = chans // wide
    whole = pl.BlockSpec((rows, width), lambda g: (0, 0))
    weights = pl.BlockSpec((wide, width), lambda g: (g + steps, 0))
    return pl.pallas_call(
        tail_gate_kernel,
        grid=(steps,),
        in_specs=[pl.BlockSpec((rows, wide), lambda g: (0, g)), whole, weights],
        out_specs=[weights, whole],
        out_shape=[jax.ShapeDtypeStruct((2 * chans, width), BF), jax.ShapeDtypeStruct((rows, width), F32)],
        compiler_params=pltpu.CompilerParams(vmem_limit_bytes=VM),
        cost_estimate=pl.CostEstimate(flops=4*rows*chans*width, bytes_accessed=4*chans*width, transcendentals=0),
        name="tail_gate",
    )(grad_z, normed, full_in)


def tail_kernel(conv_ref, last_ref, rim_ref, normed_ref, win_ref, tok_ref, gain_ref, first_ref, before_ref, _, gwin_ref, gtok_ref, ggain_ref, total, mixed):
    step = pl.program_id(0)
    rows = tok_ref.shape[0]

    @pl.when(step == 0)
    def _():
        total[...] = before_ref[...]

    mixed[0 : rows - 16, :] = conv_ref[0 : rows - 16, :]
    kept = conv_ref[rows - 16 : rows, :].astype(F32)
    mixed[rows - 16 : rows, :] = jnp.concatenate([kept[0:8], last_ref[...] + rim_ref[...]], axis=0).astype(BF)
    grad = mixed[...]
    gwin_ref[...] = lax.dot_general(grad, normed_ref[...], TN, preferred_element_type=F32).astype(BF)
    total[...] += jnp.dot(grad, win_ref[...], preferred_element_type=F32)

    @pl.when(step == pl.num_programs(0) - 1)
    def _():
        tok = tok_ref[...].astype(F32)
        grad_normed = total[...]
        scale = lax.rsqrt(jnp.mean(tok * tok, axis=1, keepdims=True) + EPS)
        scaled = grad_normed * gain_ref[...]
        ggain_ref[...] = jnp.sum(grad_normed * (tok * scale), axis=0, keepdims=True)
        back = scale * scaled - tok * (scale * scale * scale) * jnp.mean(tok * scaled, axis=1, keepdims=True)
        gtok_ref[...] = (first_ref[...] + back).astype(BF)


def tail(grad_conv, last, rim, normed, full_in, tok, gain, grad_first, before, gwin, wide):
    rows, width = tok.shape
    chans = grad_conv.shape[1]
    whole = lambda a: pl.BlockSpec(a.shape, lambda g: (0, 0))
    col = lambda r: pl.BlockSpec((r, wide), lambda g: (0, g))
    weights = pl.BlockSpec((wide, width), lambda g: (g, 0))
    return pl.pallas_call(
        tail_kernel,
        grid=(chans // wide,),
        in_specs=[col(rows), col(8), col(8), whole(normed), weights, whole(tok), whole(gain), whole(grad_first), whole(before), pl.BlockSpec(memory_space=pl.ANY)],
        out_specs=[weights, whole(tok), whole(gain)],
        out_shape=[jax.ShapeDtypeStruct(gwin.shape, BF), jax.ShapeDtypeStruct(tok.shape, BF), jax.ShapeDtypeStruct(gain.shape, F32)],
        input_output_aliases={9: 0},
        scratch_shapes=[pltpu.VMEM((rows, width), F32), pltpu.VMEM((rows, wide), BF)],
        compiler_params=pltpu.CompilerParams(vmem_limit_bytes=VM),
        cost_estimate=pl.CostEstimate(flops=4*rows*chans*width, bytes_accessed=4*chans*width, transcendentals=0),
        name="tail",
    )(grad_conv, last, rim, normed, full_in, tok, gain, grad_first, before, gwin)


def flip(value, bit):
    return value + bit - 2 * bit * (lax.rem(value // bit, 2))


def greet(partners):
    barrier = pltpu.get_barrier_semaphore()
    for partner in partners:
        pl.semaphore_signal(barrier, inc=1, device_id=partner, device_id_type=MESH)
    pl.semaphore_wait(barrier, len(partners))


class ZSwap:
    def __init__(self, pairs, local, send, recv, count):
        self.pairs, self.local, self.send, self.recv, self.count = pairs, local, send, recv, count

    def own(self):
        z = lax.axis_index("seq")
        return [pltpu.make_async_copy(src.at[z], dst.at[z], self.local.at[i]) for i, (src, dst) in enumerate(self.pairs)]

    def out(self):
        dp, z = lax.axis_index("dp"), lax.axis_index("seq")
        made = []
        for j in range(1, self.count):
            peer = lax.rem(z + j, self.count)
            for i, (src, dst) in enumerate(self.pairs):
                made.append(pltpu.make_async_remote_copy(src.at[peer], dst.at[z], self.send.at[i, j - 1], self.recv.at[i, j - 1], device_id=(dp, peer), device_id_type=MESH))
        return made

    def start(self):
        for copy in self.out() + self.own():
            copy.start()

    def wait(self):
        dp, z = lax.axis_index("dp"), lax.axis_index("seq")
        for copy in self.own():
            copy.wait()
        for copy in self.out():
            copy.wait_send()
        for j in range(1, self.count):
            source = lax.rem(z + self.count - j, self.count)
            for i, (src, dst) in enumerate(self.pairs):
                pltpu.make_async_remote_copy(src.at[z], dst.at[source], self.send.at[i, j - 1], self.recv.at[i, j - 1], device_id=(dp, source), device_id_type=MESH).wait_recv()


def gather_kernel(parts, count, in_ref, rest_ref, up_ref, tok_ref, ids_ref, gin_ref, grest_ref, gup_ref, rim_ref, rimids_ref,
                  local_sem, send, recv, share_send, share_recv, pair_send, pair_recv, swap_local, swap_send, swap_recv, rim_send, rim_recv):
    dp, z = lax.axis_index("dp"), lax.axis_index("seq")
    chip, core = dp // 2, lax.rem(dp, 2)
    srcs, dsts = (in_ref, rest_ref), (gin_ref, grest_ref)
    sibling = (flip(dp, 1), z)
    peers = [lax.rem(z + j, count) for j in range(1, count)]
    greet([sibling, (flip(dp, 4), z), (flip(dp, 2), z)] + [(dp, peer) for peer in peers])

    tail = pl.ds(tok_ref.shape[0] - rim_ref.shape[0], rim_ref.shape[0])
    rims = [pltpu.make_async_remote_copy(src, dst, rim_send.at[i], rim_recv.at[i], device_id=(dp, lax.rem(z + 1, count)), device_id_type=MESH)
            for i, (src, dst) in enumerate(((tok_ref.at[tail], rim_ref), (ids_ref, rimids_ref)))]
    for copy in rims:
        copy.start()
    mine = []
    for i, (src, dst) in enumerate(zip(srcs, dsts)):
        local = pltpu.make_async_copy(src, dst.at[chip, core, z], local_sem.at[i])
        pair = pltpu.make_async_remote_copy(src, dst.at[chip, core, z], pair_send.at[i], pair_recv.at[i], device_id=sibling, device_id_type=MESH)
        local.start()
        pair.start()
        mine += [local, pair]
    for copy in mine:
        copy.wait()
    swap = ZSwap(((up_ref, gup_ref),), swap_local, swap_send, swap_recv, count)

    def role(which, first_bit, second_bit):
        subs = parts[which]
        first, second = (flip(dp, first_bit), z), (flip(dp, second_bit), z)
        first_chip, second_chip = flip(chip, first_bit // 2), flip(chip, second_bit // 2)
        both_chip = flip(first_chip, second_bit // 2)

        def copies(sub, at_chip, at_z, slot, to, send_s, recv_s):
            made = []
            for i, (ref, lo, size) in enumerate(subs[sub]):
                view = dsts[ref].at[at_chip, :, at_z, pl.ds(lo, size)]
                made.append(pltpu.make_async_remote_copy(view, view, send_s.at[sub, slot, i], recv_s.at[sub, slot, i], device_id=to, device_id_type=MESH))
            return made

        def start(made):
            for copy in made:
                copy.start()

        def wait_recv(made):
            for copy in made:
                copy.wait_recv()

        def along_first(sub, k):
            return copies(sub, chip, k, 4 + k, first, send, recv)

        def along_second(sub, k, far):
            return copies(sub, first_chip if far else chip, k, 8 + 4 * far + k, second, send, recv)

        def came_first(sub, k):
            return copies(sub, first_chip, k, 4 + k, first, send, recv)

        def came_second(sub, k, far):
            return copies(sub, both_chip if far else second_chip, k, 8 + 4 * far + k, second, send, recv)

        def share(sub, at_chip, k, offset):
            return copies(sub, at_chip, k, 4 * offset + k, sibling, share_send, share_recv)

        def up(sub, k):
            return copies(sub, chip, k, k + count * 5, (dp, z + 1), send, recv)

        def down(sub, k):
            return copies(sub, chip, k, k, (dp, z - 1), send, recv)

        both = range(len(subs))

        def spread(sub, k):
            start(along_first(sub, k))
            start(along_second(sub, k, 0))

        def rest(k):
            for sub in both:
                wait_recv(came_first(sub, k))
                start(along_second(sub, k, 1))
                start(share(sub, first_chip, k, 1))

        def below(hop, work):
            pl.when(z - hop >= 0)(lambda: work(z - hop))

        def above(hop, work):
            pl.when(z + hop <= count - 1)(lambda: work(z + hop))

        def from_below(k):
            for sub in both:
                wait_recv(up(sub, k))
                pl.when(z < count - 1)(lambda: start(up(sub, k)))
                spread(sub, k)
                start(share(sub, chip, k, 0))

        def from_above(k):
            for sub in both:
                wait_recv(down(sub, k))
                pl.when(z > 0)(lambda: start(down(sub, k)))
                spread(sub, k)
                start(share(sub, chip, k, 0))

        for sub in both:
            pl.when(z > 0)(lambda: start(down(sub, z)))
            pl.when(z < count - 1)(lambda: start(up(sub, z)))
            spread(sub, z)
        for hop in range(1, count):
            below(hop, from_below)
            above(hop, from_above)
            if hop == count - 2:
                swap.start()
            if hop == 1:
                rest(z)
            else:
                below(hop - 1, rest)
                above(hop - 1, rest)
        below(count - 1, rest)
        above(count - 1, rest)

        def finish(k, _):
            for far in (0, 1):
                for sub in both:
                    wait_recv(came_second(sub, k, far))
                    start(share(sub, both_chip if far else second_chip, k, 2 + far))
            return 0

        lax.fori_loop(0, count, finish, 0)

        def drain(k, _):
            def wait_send(made):
                for copy in made:
                    copy.wait_send()

            for sub in both:
                wait_send(along_first(sub, k) + along_second(sub, k, 0) + along_second(sub, k, 1))
                for offset, at_chip in ((1, first_chip), (2, second_chip), (3, both_chip)):
                    wait_send(share(sub, at_chip, k, offset))
                pl.when(k != z)(lambda: wait_send(share(sub, chip, k, 0)))
                pl.when((k <= z) & (z < count - 1))(lambda: wait_send(up(sub, k)))
                pl.when((k >= z) & (z > 0))(lambda: wait_send(down(sub, k)))
            return 0

        lax.fori_loop(0, count, drain, 0)

        def shared(k, _):
            for offset, at_chip in enumerate((chip, second_chip, first_chip, both_chip)):
                def wait():
                    for sub, chunks in enumerate(parts[1 - which]):
                        for i, (ref, lo, size) in enumerate(chunks):
                            view = dsts[ref].at[at_chip, :, k, pl.ds(lo, size)]
                            pltpu.make_async_remote_copy(view, view, share_send.at[sub, 4 * offset + k, i], share_recv.at[sub, 4 * offset + k, i], device_id=sibling, device_id_type=MESH).wait_recv()
                if offset:
                    wait()
                else:
                    pl.when(k != z)(wait)
            return 0

        lax.fori_loop(0, count, shared, 0)

    pl.when(core == 0)(lambda: role(0, 4, 2))
    pl.when(core == 1)(lambda: role(1, 2, 4))
    swap.wait()
    for copy in rims:
        copy.wait()


def gather_all(w_in, rest, up, tok, ids, cut, count):
    parts = ((((0, 0, 48),), ((0, 48, cut - 48),)), (((0, cut, 48),), ((0, cut + 48, w_in.shape[0] - cut - 48), (1, 0, rest.shape[0]))))
    shape = lambda a: jax.ShapeDtypeStruct((4, 2, count) + a.shape, a.dtype)
    sems = lambda *s: pltpu.SemaphoreType.DMA(s)
    return pl.pallas_call(
        functools.partial(gather_kernel, parts, count),
        in_specs=[pl.BlockSpec(memory_space=pl.ANY)] * 5,
        out_specs=[pl.BlockSpec(memory_space=pl.ANY)] * 5,
        out_shape=[shape(w_in), shape(rest), jax.ShapeDtypeStruct(up.shape, up.dtype),
                   jax.ShapeDtypeStruct((16, tok.shape[1]), tok.dtype), jax.ShapeDtypeStruct(ids.shape, ids.dtype)],
        scratch_shapes=[sems(2), sems(2, 24, 2), sems(2, 24, 2), sems(2, 16, 2), sems(2, 16, 2), sems(2), sems(2), sems(1), sems(1, count - 1), sems(1, count - 1), sems(2), sems(2)],
        compiler_params=pltpu.CompilerParams(collective_id=1, has_side_effects=True),
        cost_estimate=pl.CostEstimate(flops=0, bytes_accessed=200_000_000, transcendentals=0),
        name="gather_all",
    )(w_in, rest, up, tok, ids)


def scatter_kernel(parts, count, in_ref, rest_ref, proj_ref, down_ref, oin_ref, orest_ref, oproj_ref, odown_ref, mine_a, mine_b, sib_a, sib_b, far_a, far_b, near_a, near_b, zgot_a, zgot_b, final_a, final_b,
                   load_sem, sib_send, sib_recv, two_send, two_recv, one_send, one_recv, z_send, z_recv, end_send, end_recv, end_local,
                   swap_local, swap_send, swap_recv):
    dp, z = lax.axis_index("dp"), lax.axis_index("seq")
    chip, core = dp // 2, lax.rem(dp, 2)
    srcs, outs = (in_ref, rest_ref), (oin_ref, orest_ref)
    mine, sib, far_got, near_got, z_got, final = (mine_a, mine_b), (sib_a, sib_b), (far_a, far_b), (near_a, near_b), (zgot_a, zgot_b), (final_a, final_b)
    sibling = (flip(dp, 1), z)
    peers = [(dp, lax.rem(z + j, count)) for j in range(1, count)]
    greet([sibling, (flip(dp, 4), z), (flip(dp, 2), z)] + peers)

    swap = ZSwap(((proj_ref, oproj_ref), (down_ref, odown_ref)), swap_local, swap_send, swap_recv, count)

    def role(which, first_bit, second_bit):
        chunks, other = parts[which], parts[1 - which]
        first, second = (flip(dp, first_bit), z), (flip(dp, second_bit), z)
        first_chip, second_chip = flip(chip, first_bit // 2), flip(chip, second_bit // 2)
        both_chip = flip(first_chip, second_bit // 2)
        steps = [lax.rem(z + 1 + j, count) for j in range(count)]

        def loads(col, k):
            slot = col * count + k
            return [pltpu.make_async_copy(srcs[ref].at[col, :, k, pl.ds(lo, size)], mine[ref].at[slot, :, pl.ds(0, size)], load_sem.at[slot, ref])
                    for ref, lo, size in chunks]

        def sibling_copies(col, k, pieces):
            slot = col * count + k
            return [pltpu.make_async_remote_copy(srcs[ref].at[col, :, k, pl.ds(lo, size)], sib[ref].at[slot, :, pl.ds(0, size)],
                                                 sib_send.at[slot, ref], sib_recv.at[slot, ref], device_id=sibling, device_id_type=MESH)
                    for ref, lo, size in pieces]

        def send(col, k, dst, slot, send_s, recv_s, to):
            return [pltpu.make_async_remote_copy(mine[ref].at[col * count + k, :, pl.ds(0, size)], dst[ref].at[slot, :, pl.ds(0, size)],
                                                 send_s.at[slot, ref], recv_s.at[slot, ref], device_id=to, device_id_type=MESH)
                    for ref, lo, size in chunks]

        def start(copies):
            for copy in copies:
                copy.start()

        def wait_recv(copies):
            for copy in copies:
                copy.wait_recv()

        def wait_send(copies):
            for copy in copies:
                copy.wait_send()

        def add(col, k, terms, last=False):
            slot = col * count + k
            for copy in loads(col, k):
                copy.wait()
            wait_recv(sibling_copies(col, k, chunks))
            for ref, lo, size in chunks:
                def rows(r, _):
                    at = pl.ds(pl.multiple_of(r * 16, 16), 16)
                    for c in range(2):
                        total = mine[ref][slot, c, at, :].astype(F32) + sib[ref][slot, c, at, :].astype(F32)
                        for buf, place in terms:
                            total = total + buf[ref][place, c, at, :].astype(F32)
                        if last:
                            final[ref][c, at, :] = total
                        else:
                            mine[ref][slot, c, at, :] = total.astype(BF)
                    return 0

                lax.fori_loop(0, size // 16, rows, 0)

        for k in steps:
            for col, sib_col in ((both_chip, both_chip), (second_chip, first_chip), (first_chip, second_chip), (chip, chip)):
                start(sibling_copies(sib_col, k, other) + loads(col, k))

        swap.start()

        def stage_one(k):
            for far, col in ((1, both_chip), (0, second_chip)):
                add(col, k, ())
                start(send(col, k, far_got, far * count + k, two_send, two_recv, second))

        def stage_two(k):
            wait_recv(send(first_chip, k, far_got, count + k, two_send, two_recv, second))
            add(first_chip, k, ((far_got, count + k),))
            start(send(first_chip, k, near_got, k, one_send, one_recv, first))

        def stage_three(j, k):
            wait_recv(send(chip, k, far_got, k, two_send, two_recv, second))
            wait_recv(send(chip, k, near_got, k, one_send, one_recv, first))
            if j < count - 1:
                add(chip, k, ((far_got, k), (near_got, k)))
                start(send(chip, k, z_got, j, z_send, z_recv, (dp, k)))

        for j in range(count + 2):
            if j < count:
                stage_one(steps[j])
            if 1 <= j <= count:
                stage_two(steps[j - 1])
            if j >= 2:
                stage_three(j - 2, steps[j - 2])

        for j in range(count - 1):
            wait_recv(send(chip, z, z_got, j, z_send, z_recv, (dp, z)))
        add(chip, z, ((far_got, z), (near_got, z)) + tuple((z_got, j) for j in range(count - 1)), last=True)
        locals_, remotes = [], []
        for ref, lo, size in chunks:
            locals_.append(pltpu.make_async_copy(final[ref].at[which, pl.ds(0, size)], outs[ref].at[pl.ds(lo, size)], end_local.at[ref]))
            remotes.append(pltpu.make_async_remote_copy(final[ref].at[1 - which, pl.ds(0, size)], outs[ref].at[pl.ds(lo, size)],
                                                        end_send.at[which, ref], end_recv.at[which, ref], device_id=sibling, device_id_type=MESH))
        start(locals_ + remotes)
        for copy in locals_:
            copy.wait()
        wait_send(remotes)
        for ref, lo, size in other:
            pltpu.make_async_remote_copy(final[ref].at[which, pl.ds(0, size)], outs[ref].at[pl.ds(lo, size)],
                                         end_send.at[1 - which, ref], end_recv.at[1 - which, ref], device_id=sibling, device_id_type=MESH).wait_recv()
        for j, k in enumerate(steps):
            for col in (chip, first_chip, second_chip, both_chip):
                wait_send(sibling_copies(col, k, other))
            wait_send(send(both_chip, k, far_got, count + k, two_send, two_recv, second))
            wait_send(send(second_chip, k, far_got, k, two_send, two_recv, second))
            wait_send(send(first_chip, k, near_got, k, one_send, one_recv, first))
            if j < count - 1:
                wait_send(send(chip, k, z_got, j, z_send, z_recv, (dp, k)))

    pl.when(core == 0)(lambda: role(0, 4, 2))
    pl.when(core == 1)(lambda: role(1, 2, 4))
    swap.wait()


def scatter_all(g_in, g_rest, proj, down, cut, collective_id):
    count = g_in.shape[2]
    rows_in, rows_rest = g_in.shape[3], g_rest.shape[3]
    parts = (((0, 0, cut),), ((0, cut, rows_in - cut), (1, 0, rows_rest)))
    sems = lambda *s: pltpu.SemaphoreType.DMA(s)
    places = 4 * count

    def bufs(k, kind=BF):
        lead = (k, 2) if k else (2,)
        return [pltpu.VMEM(lead + (max(cut, rows_in - cut), g_in.shape[4]), kind), pltpu.VMEM(lead + (rows_rest, g_rest.shape[4]), kind)]

    return pl.pallas_call(
        functools.partial(scatter_kernel, parts, count),
        in_specs=[pl.BlockSpec(memory_space=pl.ANY)] * 4,
        out_specs=[pl.BlockSpec(memory_space=pl.ANY)] * 4,
        out_shape=[jax.ShapeDtypeStruct(g_in.shape[3:], F32), jax.ShapeDtypeStruct(g_rest.shape[3:], F32), jax.ShapeDtypeStruct(proj.shape, proj.dtype), jax.ShapeDtypeStruct(down.shape, down.dtype)],
        scratch_shapes=bufs(places) + bufs(places) + bufs(2 * count) + bufs(count) + bufs(count - 1) + bufs(0, F32)
        + [sems(places, 2), sems(places, 2), sems(places, 2), sems(2 * count, 2), sems(2 * count, 2), sems(count, 2), sems(count, 2),
           sems(count - 1, 2), sems(count - 1, 2), sems(2, 2), sems(2, 2), sems(2), sems(2), sems(2, count - 1), sems(2, count - 1)],
        compiler_params=pltpu.CompilerParams(collective_id=collective_id, has_side_effects=True, vmem_limit_bytes=VM),
        cost_estimate=pl.CostEstimate(flops=0, bytes_accessed=200_000_000, transcendentals=0),
        name="scatter_all",
    )(g_in, g_rest, proj, down)


def unpack_kernel(own, cuts, pack_ref, small_ref, *refs):
    outs, tall = refs[:-1], refs[-1]
    for b in range(pack_ref.shape[0]):
        block = pack_ref[b].astype(F32)
        tall[b * own : (b + 1) * own, :] = block[:own]
        small_ref[b : b + 1, :] = block[own : own + 1]
    for j in range(tall.shape[0] // 128):
        c = slice(j * 128, (j + 1) * 128)
        turned = tall[c, :].T
        for ref, (lo, size) in zip(outs, cuts):
            part = turned[lo : lo + size]
            if ref.shape[0] > size:
                part = jnp.concatenate([part, jnp.zeros((ref.shape[0] - size, 128), F32)], axis=0)
            ref[:, c] = part.astype(ref.dtype)


def unpack(pack, own, sizes):
    blocks, _, cols = pack.shape
    chans = blocks * own
    cuts, at = [], 0
    for size in sizes:
        cuts.append((at, size))
        at += size
    rows = [128, 128] + list(sizes[2:])
    kinds = [BF, BF] + [F32] * (len(sizes) - 2)
    if own % 8:
        turned = pack[:, :own].reshape(chans, cols).T
        parts = [jnp.pad(turned[lo : lo + size], ((0, r - size), (0, 0))).astype(kind) for (lo, size), r, kind in zip(cuts, rows, kinds)]
        return [pack[:, own].astype(F32)] + parts
    return pl.pallas_call(
        functools.partial(unpack_kernel, own, tuple(cuts)),
        out_shape=[jax.ShapeDtypeStruct((blocks, cols), F32)] + [jax.ShapeDtypeStruct((r, chans), kind) for r, kind in zip(rows, kinds)],
        scratch_shapes=[pltpu.VMEM((chans, cols), F32)],
        compiler_params=pltpu.CompilerParams(vmem_limit_bytes=VM),
        name="unpack_small",
    )(pack)


def pack_kernel(own, sizes, x_ref, dt_ref, log_ref, taps_ref, dtb_ref, skip_ref, small_ref, out_ref, wide, tall):
    at = 0
    for ref, size in zip((x_ref, dt_ref, log_ref, taps_ref, dtb_ref, skip_ref), sizes):
        wide[at : at + size, :] = ref[0:size, :]
        at += size
    wide[at:, :] = jnp.zeros((wide.shape[0] - at, wide.shape[1]), F32)
    for j in range(tall.shape[0] // 128):
        tall[j * 128 : (j + 1) * 128, :] = wide[:, j * 128 : (j + 1) * 128].T
    cols = wide.shape[0]
    first = lax.broadcasted_iota(jnp.int32, (8, cols), 0) == 0
    for b in range(out_ref.shape[0]):
        tail = jnp.where(first, jnp.broadcast_to(small_ref[b : b + 1, :], (8, cols)), 0.0)
        out_ref[b] = jnp.concatenate([tall[b * own : (b + 1) * own, :], tail], axis=0).astype(BF)


def pack_grads(parts, sizes, small, own):
    blocks, cols = small.shape
    chans = parts[0].shape[1]
    rows = own + -own % 16
    if own % 8:
        turned = jnp.concatenate([part[:size] for part, size in zip(parts, sizes)]).T.reshape(blocks, own, -1)
        turned = jnp.pad(turned, ((0, 0), (0, 0), (0, cols - turned.shape[2])))
        return jnp.concatenate([turned, small[:, None], jnp.zeros((blocks, rows - own - 1, cols), F32)], axis=1).astype(BF)
    return pl.pallas_call(
        functools.partial(pack_kernel, own, sizes),
        out_shape=jax.ShapeDtypeStruct((blocks, rows, cols), BF),
        scratch_shapes=[pltpu.VMEM((cols, chans), F32), pltpu.VMEM((chans, cols), F32)],
        compiler_params=pltpu.CompilerParams(vmem_limit_bytes=VM),
        name="pack_small",
    )(*parts, small)


def finish_kernel(own, cuts, pack_ref, up_ref, down_ref, proj_ref, up_out, down_out, row_out, proj_out, *small_outs):
    up_out[0] = up_ref[0].astype(F32)
    down_out[0] = down_ref[0].astype(F32)

    @pl.when(pl.program_id(0) == 0)
    def _():
        row_out[...] = pack_ref[own : own + 1, :]
        proj_out[...] = sum(proj_ref[k].astype(F32) for k in range(proj_ref.shape[0]))[:own]
        tall = pack_ref[...]
        turned = jnp.concatenate([tall, jnp.zeros((-tall.shape[0] % 128, tall.shape[1]), F32)], axis=0).T
        for (lo, size, turn), out in zip(cuts, small_outs):
            out[...] = turned[lo : lo + size, :own] if turn else pack_ref[0:own, lo : lo + size]


def finish(pack, up, down, proj, own, cuts):
    experts, piece, width = up.shape
    if own % 8:
        small = [pack[:own, lo : lo + size].T if turn else pack[:own, lo : lo + size] for lo, size, turn in cuts]
        return [up.astype(F32), down.astype(F32), pack[own : own + 1], jnp.sum(proj[:, :own].astype(F32), axis=0)] + small
    whole = lambda shape: pl.BlockSpec(shape, lambda e: (0,) * len(shape))
    part = lambda shape: pl.BlockSpec((1,) + shape[1:], lambda e: (e, 0, 0))
    shapes = [(experts, piece, width)] * 2 + [(1, pack.shape[1]), (own, width)] + [(size, own) if turn else (own, size) for _, size, turn in cuts]
    return pl.pallas_call(
        functools.partial(finish_kernel, own, cuts),
        grid=(experts,),
        in_specs=[whole(pack.shape), part(up.shape), part(up.shape), whole(proj.shape)],
        out_specs=[part(shapes[0]), part(shapes[1])] + [whole(s) for s in shapes[2:]],
        out_shape=[jax.ShapeDtypeStruct(s, F32) for s in shapes],
        compiler_params=pltpu.CompilerParams(vmem_limit_bytes=VM),
        name="finish",
    )(pack, up, down, proj)


def pack_params_kernel(x_ref, dt_ref, log_ref, taps_ref, bias_ref, dtb_ref, skip_ref, small_ref, out_ref, thin, tall):
    own, x_cols = x_ref.shape
    thin[...] = jnp.zeros_like(thin)
    at = 0
    for ref in (log_ref, taps_ref, bias_ref, dtb_ref, skip_ref):
        thin[at : at + ref.shape[0], 0:own] = ref[...].astype(F32)
        at += ref.shape[0]
    tall[...] = jnp.zeros_like(tall)
    at = x_cols + dt_ref.shape[1]
    tall[0:own, 0:x_cols] = x_ref[...].astype(F32)
    tall[0:own, x_cols:at] = dt_ref[...].astype(F32)
    tall[0:own, at : at + thin.shape[0]] = thin[...].T[:own]
    tall[own : own + 1, 0 : small_ref.shape[1]] = small_ref[...].astype(F32)
    out_ref[...] = tall[...].astype(BF)


def pack_params(w_x, w_dt, log_t, taps_t, bias, dtb, skip, small):
    own = w_x.shape[0]
    rows = own + -own % 16
    if own % 8:
        wide = jnp.concatenate([w_x, w_dt, log_t.T, taps_t.T, bias.T, dtb.T, skip.T], axis=1)
        wide = jnp.pad(wide, ((0, -own % 16), (0, 256 - wide.shape[1])))
        return wide + jnp.pad(small, ((own, -own % 16 - 1), (0, 256 - small.shape[1])))
    return pl.pallas_call(
        pack_params_kernel,
        out_shape=jax.ShapeDtypeStruct((rows, 256), BF),
        scratch_shapes=[pltpu.VMEM((32, 128), F32), pltpu.VMEM((rows, 256), F32)],
        name="pack_params",
    )(w_x, w_dt, log_t, taps_t, bias, dtb, skip, small)


def chain_kernel(step, pieces, carry_ref, own_ref, out_ref, inbox, outbox, send, recv):
    dp, z = lax.axis_index("dp"), lax.axis_index("seq")
    last = lax.axis_size("seq") - 1
    has_before = z > 0 if step > 0 else z < last
    has_after = z < last if step > 0 else z > 0
    barrier = pltpu.get_barrier_semaphore()

    def neighbours(act):
        pl.when(has_before)(lambda: act(z - step))
        pl.when(has_after)(lambda: act(z + step))

    neighbours(lambda peer: pl.semaphore_signal(barrier, inc=1, device_id=(dp, peer), device_id_type=MESH))
    count = last + 1
    pl.semaphore_wait(barrier, (z + last) // count + (2 * last - z) // count)
    wide = own_ref.shape[1] // pieces

    def copy(g):
        return pltpu.make_async_remote_copy(outbox.at[g], inbox.at[g], send.at[g], recv.at[g], device_id=(dp, z + step), device_id_type=MESH)

    def back(g):
        return pltpu.make_async_remote_copy(outbox.at[g], inbox.at[g], send.at[g], recv.at[g], device_id=(dp, z - step), device_id_type=MESH)

    for g in range(pieces):
        c = slice(g * wide, (g + 1) * wide)

        @pl.when(has_before)
        def _():
            back(g).wait_recv()
            out_ref[:, c] = inbox[g].astype(F32)

        @pl.when(jnp.logical_not(has_before))
        def _():
            out_ref[:, c] = jnp.zeros((out_ref.shape[0], wide), F32)

        @pl.when(has_after)
        def _():
            outbox[g] = (carry_ref[:, c] * out_ref[:, c] + own_ref[:, c]).astype(BF)
            copy(g).start()

    @pl.when(has_after)
    def _():
        for g in range(pieces):
            copy(g).wait_send()


def chain(carry, own, step, collective_id):
    pieces = 3
    n, chans = own.shape
    return pl.pallas_call(
        functools.partial(chain_kernel, step, pieces),
        in_specs=[pl.BlockSpec(memory_space=pltpu.VMEM)] * 2,
        out_specs=pl.BlockSpec(memory_space=pltpu.VMEM),
        out_shape=jax.ShapeDtypeStruct((n, chans), F32),
        scratch_shapes=[pltpu.VMEM((pieces, n, chans // pieces), BF)] * 2 + [pltpu.SemaphoreType.DMA((pieces,))] * 2,
        compiler_params=pltpu.CompilerParams(collective_id=collective_id, has_side_effects=True),
        name="chain",
    )(carry, own)


def experts_kernel(block, piece, pick_ref, n2_ref, early_ref, go_ref, router_ref, up_hbm, down_hbm, back_ref, late_ref, mixed_ref, grouter_ref, gexp_hbm,
                   up, down, gup, gdown, outbox, inbox, ret, total, disp, load_sem, store_sem, own_sem, out_send, out_recv, back_own, back_send, back_recv):
    dp, z = lax.axis_index("dp"), lax.axis_index("seq")
    count = lax.axis_size("seq")
    peers = [lax.rem(z + j, count) for j in range(1, count)]
    blocks = up.shape[0] // block
    rows, width = total.shape
    each = rows // count

    def loads(b):
        at = pl.ds(pl.multiple_of(b * block, block), block)
        return [pltpu.make_async_copy(up_hbm.at[at], up.at[at], load_sem.at[b, 0]), pltpu.make_async_copy(down_hbm.at[at], down.at[at], load_sem.at[b, 1])]

    def stores(b):
        made = []
        for i in range(block // piece):
            at = pl.ds(pl.multiple_of(b * block + i * piece, 16), piece)
            to = b * (block // piece) + i
            made.append(pltpu.make_async_copy(gup.at[at], gexp_hbm.at[to, 0], store_sem.at[to, 0]))
            made.append(pltpu.make_async_copy(gdown.at[at], gexp_hbm.at[to, 1], store_sem.at[to, 1]))
        return made

    def send(j):
        return pltpu.make_async_remote_copy(outbox.at[peers[j]], inbox.at[z], out_send.at[j], out_recv.at[j], device_id=(dp, peers[j]), device_id_type=MESH)

    def came(j):
        return pltpu.make_async_remote_copy(outbox.at[z], inbox.at[lax.rem(z + count - 1 - j, count)], out_send.at[j], out_recv.at[j], device_id=(dp, z), device_id_type=MESH)

    def kept():
        return pltpu.make_async_copy(outbox.at[z], inbox.at[z], own_sem.at[0])

    def give(half, j):
        return pltpu.make_async_remote_copy(ret.at[half, peers[j]], back_ref.at[z], back_send.at[half, j], back_recv.at[half, j], device_id=(dp, peers[j]), device_id_type=MESH)

    def got(half, j):
        return pltpu.make_async_remote_copy(ret.at[half, z], back_ref.at[lax.rem(z + count - 1 - j, count)], back_send.at[half, j], back_recv.at[half, j], device_id=(dp, z), device_id_type=MESH)

    def give_own(half):
        return pltpu.make_async_copy(ret.at[half, z], back_ref.at[z], back_own.at[half])

    greet([(dp, peer) for peer in peers])
    picked = lax.dot_general(pick_ref[...], n2_ref[...], TN, preferred_element_type=F32)
    outbox[...] = picked.astype(BF).reshape(count, each, width)
    for j in range(count - 1):
        send(j).start()
    kept().start()
    for b in range(blocks):
        for copy in loads(b):
            copy.start()
    lanes = lax.broadcasted_iota(jnp.int32, (rows, router_ref.shape[1]), 1)
    mine = (lanes == z).astype(F32)
    for half in range(2):
        if half:
            kept().wait()
            for j in range(count - 1):
                came(j).wait_recv()
        slots = (inbox if half else early_ref)[...].reshape(rows, width)
        go = go_ref[:, half * each : (half + 1) * each, :].reshape(rows, width).astype(F32)
        logits = jnp.where(lanes < count, jnp.dot(slots, router_ref[...], preferred_element_type=F32), -1e30)
        powers = jnp.exp(logits - jnp.max(logits, axis=1, keepdims=True))
        probs = jnp.where(lanes < count, powers / jnp.sum(powers, axis=1, keepdims=True), 0.0)
        gate = jnp.sum(probs * mine, axis=1, keepdims=True)
        grads = (gate * go).astype(BF)
        total[...] = jnp.zeros_like(total)
        disp[...] = jnp.zeros_like(disp)

        def units(b, _):
            at = pl.ds(pl.multiple_of(b * block, block), block)
            if half == 0:
                for copy in loads(b):
                    copy.wait()
            hidden = lax.dot_general(slots, up[at, :], NT, preferred_element_type=F32)
            phi = 0.5 * (1.0 + lax.erf(hidden * (1.0 / math.sqrt(2.0))))
            act = (hidden * phi).astype(BF)
            slope = phi + hidden * jnp.exp(hidden * hidden * -0.5) * (1.0 / math.sqrt(2.0 * math.pi))
            ghid = (lax.dot_general(grads, down[at, :], NT, preferred_element_type=F32) * slope).astype(BF)
            total[...] += jnp.dot(act, down[at, :], preferred_element_type=F32)
            disp[...] += jnp.dot(ghid, up[at, :], preferred_element_type=F32)
            new_up = lax.dot_general(ghid, slots, TN, preferred_element_type=F32)
            new_down = lax.dot_general(act, grads, TN, preferred_element_type=F32)
            if half == 0:
                gup[at, :] = new_up.astype(BF)
                gdown[at, :] = new_down.astype(BF)
            else:
                gup[at, :] = (gup[at, :].astype(F32) + new_up).astype(BF)
                gdown[at, :] = (gdown[at, :].astype(F32) + new_down).astype(BF)
                for copy in stores(b):
                    copy.start()
            return 0

        lax.fori_loop(0, blocks, units, 0)
        expert_out = total[...]
        mixed_ref[:, half * each : (half + 1) * each, :] = (gate * expert_out).astype(BF).reshape(count, each, width)
        grad_gate = jnp.sum(go * expert_out, axis=1, keepdims=True)
        grad_logits = (grad_gate * gate * (mine - probs)).astype(BF)
        grad_n2 = disp[...] + lax.dot_general(grad_logits, router_ref[...], NT, preferred_element_type=F32)
        if half == 0:
            ret[half] = grad_n2.astype(BF).reshape(count, each, width)
            for j in range(count - 1):
                give(half, j).start()
            give_own(half).start()
        else:
            late_ref[...] = grad_n2.astype(BF).reshape(count, each, width)
        grouter = lax.dot_general(slots, grad_logits, TN, preferred_element_type=F32)
        if half == 0:
            grouter_ref[...] = grouter
        else:
            grouter_ref[...] += grouter
    for b in range(blocks):
        for copy in stores(b):
            copy.wait()
    give_own(0).wait()
    for j in range(count - 1):
        send(j).wait_send()
        give(0, j).wait_send()
        got(0, j).wait_recv()


def experts_pass(pick, n2, early, go, router, up, down, block, piece, collective_id):
    count, slots, width = go.shape
    units = up.shape[0]
    rows = count * slots // 2
    vmem = pl.BlockSpec(memory_space=pltpu.VMEM)
    hbm = pl.BlockSpec(memory_space=pl.ANY)
    sems = lambda *s: pltpu.SemaphoreType.DMA(s)
    blocks = units // block
    return pl.pallas_call(
        functools.partial(experts_kernel, block, piece),
        in_specs=[vmem] * 5 + [hbm] * 2,
        out_specs=[hbm, vmem, vmem, vmem, hbm],
        out_shape=[jax.ShapeDtypeStruct((count, slots // 2, width), BF)] * 2 + [jax.ShapeDtypeStruct((count, slots, width), BF), jax.ShapeDtypeStruct(router.shape, F32),
                   jax.ShapeDtypeStruct((units // piece, 2, piece, width), BF)],
        scratch_shapes=[pltpu.VMEM(up.shape, BF)] * 4
        + [pltpu.VMEM((count, slots // 2, width), BF)] * 2 + [pltpu.VMEM((1, count, slots // 2, width), BF)] + [pltpu.VMEM((rows, width), F32)] * 2
        + [sems(blocks, 2), sems(units // piece, 2), sems(1), sems(count - 1), sems(count - 1), sems(1), sems(1, count - 1), sems(1, count - 1)],
        compiler_params=pltpu.CompilerParams(collective_id=collective_id, has_side_effects=True, vmem_limit_bytes=VM),
        cost_estimate=pl.CostEstimate(flops=24 * rows * units * width, bytes_accessed=100_000_000, transcendentals=4 * rows * units),
        name="experts",
    )(pick, n2, early, go, router, up, down)


def dot(a, b):
    return jnp.dot(a, b, preferred_element_type=F32)


def dot_nt(a, b):
    return lax.dot_general(a, b, NT, preferred_element_type=F32)


def dot_tn(a, b):
    return lax.dot_general(a, b, TN, preferred_element_type=F32)


def shift(value, axis, steps):
    count = lax.axis_size(axis)
    first, last = (max(0, -steps), min(count, count - steps))
    return lax.ppermute(value, axis, [(source, source + steps) for source in range(first, last)])


def rms_scale(value):
    return lax.rsqrt(jnp.mean(value * value, axis=-1, keepdims=True) + EPS)


def rms_back(value, gain, grad):
    scale = rms_scale(value)
    scaled = grad * gain
    grad_gain = jnp.sum(grad * (value * scale), axis=0)
    return scale * scaled - value * (scale * scale * scale) * jnp.mean(value * scaled, axis=-1, keepdims=True), grad_gain


def swap(value):
    return lax.all_to_all(value, "seq", 0, 0)


def shards(tokens, segment_ids, routes, cotangent, small_params, w_in, conv_w, conv_b, w_x, w_dt, dt_bias, a_log, d_skip, w_out, w_up, w_down):
    both = ("dp", "seq")
    devices = lax.axis_size(both)
    width = tokens.shape[2]
    rows = tokens.shape[1]
    experts = w_up.shape[0]
    chans = w_in.shape[0] * devices // 2
    own = w_out.shape[0]
    rank = w_dt.shape[1]
    n = a_log.shape[1]
    taps = conv_w.shape[1]
    slots = rows // 2
    halo = 16
    wide = 768

    tok_b = tokens[0]
    seg_plus = segment_ids[0] + 1

    share = small_params.shape[0]
    packed = pack_params(w_x, w_dt, a_log.T, conv_w.T, conv_b[None], dt_bias[None], d_skip[None], small_params[None])
    direct = lax.axis_size("dp") == 8 and lax.axis_size("seq") == 4
    ring = [[r ^ (r >> 1) for r in range(8)]] if direct else None
    up_t = jnp.swapaxes(w_up, 1, 2)
    full_out = lax.all_gather(w_out, both, axis=0, tiled=True)
    if direct:
        last_ids = jnp.broadcast_to(seg_plus[rows - halo :, None], (halo, 128))
        all_in, all_pack, part_up, rim_tok, rim_ids = gather_all(w_in, packed, up_t, tok_b, last_ids, 80, 4)
        down_late, all_in = lax.optimization_barrier((w_down, all_in))
        part_down = swap(down_late)
        rim_ids = jnp.where(lax.axis_index("seq") > 0, rim_ids[:, 0], 0)
    else:
        all_in, all_pack = lax.all_gather(w_in, both), lax.all_gather(packed, both)
        part_up, part_down = swap(up_t), swap(w_down)
        rim_tok = shift(tok_b[rows - halo :], "seq", 1)
        rim_ids = shift(seg_plus[rows - halo :], "seq", 1)
    full_in = lax.optimization_barrier(all_in.reshape(2 * chans, width))
    small, full_x_t, full_dt_t, alog_t, conv_f, bias_row, dtb_row, skip = unpack(all_pack.reshape(devices, -1, 256), own, (w_x.shape[1], rank, n, taps, 1, 1, 1))
    small, part_up = lax.optimization_barrier((small, part_up))
    full_up = lax.all_gather(part_up, "dp", axis=0, axis_index_groups=ring).reshape(-1, width)
    flat_small = small[:, :share].reshape(-1)
    gain_one = flat_small[:width]
    gain_two = flat_small[width : 2 * width]
    router = flat_small[2 * width :].reshape(width, experts).astype(BF)
    route_ids = routes[0]
    onehot = (route_ids == jnp.arange(experts)[None, :]).astype(BF)
    before = (jnp.arange(rows)[:, None] > jnp.arange(rows)[None, :]).astype(BF)
    place = jnp.sum(dot(before, onehot) * onehot.astype(F32), axis=1).astype(jnp.int32)
    slot_of = route_ids[:, 0] * slots + place
    gather_mat = (slot_of[:, None] == jnp.arange(experts * slots)[None, :]).astype(BF)
    half = slots // 2
    pick_of = place // half * (experts * half) + route_ids[:, 0] * half + place % half
    pick = (pick_of[:, None] == jnp.arange(experts * slots)[None, :]).astype(BF)
    grad_out_b = cotangent[0]
    grad_out = grad_out_b.astype(F32)
    tok_f = tok_b.astype(F32)
    ids_ext = jnp.concatenate([rim_ids, seg_plus])
    same = jnp.stack([ids_ext[halo - taps + 1 + k : halo - taps + 1 + k + rows] == seg_plus for k in range(taps)], axis=1).astype(F32)
    normed, conv_in, conv_sum, values, z, projected = front(rim_tok, tok_b, gain_one[None], full_in, full_x_t, conv_f, bias_row, same, wide)
    low_wide, b_wide, c_wide, b_blk, c_blk, pre_dt, dt, dt_keep, dtx, rates, rates2, own_state, carry = steps(projected, same, values, full_dt_t, dtb_row, alog_t, rank, wide)
    carry, part_down = lax.optimization_barrier((carry, part_down))
    full_down = lax.all_gather(part_down, "dp", axis=0, axis_index_groups=ring).reshape(-1, width)
    start = chain(carry, own_state, 1, 3)
    go_local, start = lax.optimization_barrier((dot_tn(gather_mat, grad_out_b).astype(BF), start))
    go_slots = swap(go_local.reshape(experts, slots, width))
    scanned, checks, gated, first_sum, normed_two, sent = scan_pass(
        dt_keep, dtx, rates2, b_wide, c_blk, start, values, z, skip, full_out, tok_b, gain_two[None], pick[:, : experts * half], wide
    )
    sent, go_slots = lax.optimization_barrier((sent, go_slots))
    early = swap(sent.reshape(experts, half, width))

    piece = w_up.shape[2]
    router_wide = jnp.pad(router, ((0, 0), (0, 128 - experts)))
    back_n2, late_n2, mixed_back, grad_router, grad_exp = experts_pass(pick[:, experts * half :], normed_two, early, go_slots, router_wide, full_up, full_down, 768, piece if piece % 16 == 0 else 768, 5)
    grad_router = grad_router[:, :experts]
    late_n2 = swap(late_n2)
    grad_n2 = dot(pick, jnp.concatenate([back_n2.reshape(-1, width), late_n2.reshape(-1, width)]))
    mixed_slots = swap(mixed_back).reshape(-1, width)
    if piece % 16:
        grad_exp = jnp.swapaxes(jnp.swapaxes(grad_exp, 0, 1).reshape(2, -1, piece, width), 0, 1)
    part_exp = lax.psum_scatter(grad_exp.reshape(-1, width), "dp", scatter_dimension=0, tiled=True, axis_index_groups=ring)

    grad_norm_two, grad_gain_two = rms_back(first_sum, gain_two, grad_n2)
    grad_first = grad_out + grad_norm_two
    grad_mixer = grad_first.astype(BF)
    grad_scanned, grad_z_b, grad_w_out, grad_start = back_front(grad_mixer, full_out, z, scanned, values, skip, gated, dt_keep, rates2, c_wide, chans // 2, ring[0] if direct else None)
    nxt = chain(carry, grad_start, -1, 4)
    grad_vals, g_log, grad_dt_t, grad_dtb, grad_skip, grad_proj = back_pass(
        dt, dt_keep, dtx, grad_scanned, values, pre_dt, skip, rates2, rates, b_wide, c_wide, b_blk, checks, nxt, low_wide, full_dt_t, rank, wide
    )
    grad_vals, mixed_slots, part_exp, grad_w_out = lax.optimization_barrier((grad_vals, mixed_slots, part_exp, grad_w_out))
    part_exp = part_exp.reshape(experts, 2, piece, width)
    part_down = part_exp[:, 1]
    sum_up = swap(part_exp[:, 0])
    mixed_out, grad_conv_b, grad_last, grad_rim, grad_x_t, grad_taps = conv_back(
        grad_vals, grad_proj, full_x_t, values, conv_sum, conv_in, same, conv_f, gather_mat, mixed_slots, first_sum, halo, wide
    )
    grad_z_b, grad_rim = lax.optimization_barrier((grad_z_b, grad_rim))
    grad_w_in, gate_part = tail_gate(grad_z_b, normed, full_in, wide)
    grad_w_in, tokens_grad, grad_gain_one = tail(
        grad_conv_b, grad_last, shift(grad_rim, "seq", -1), normed, full_in, tok_b, gain_one[None], grad_first, gate_part, grad_w_in, wide
    )
    grad_small = jnp.concatenate([grad_gain_one[0], grad_gain_two, grad_router.reshape(-1)])
    grad_packed = pack_grads(
        (grad_x_t, grad_dt_t, g_log, grad_taps, grad_dtb, grad_skip), (w_x.shape[1], rank, n, taps + 1, 1, 1), jnp.pad(grad_small.reshape(devices, -1), ((0, 0), (0, 256 - share))), own
    )
    part_out = lax.psum_scatter(grad_w_out, "dp", scatter_dimension=0, tiled=True, axis_index_groups=ring).reshape(-1, own, width)
    part_out = jnp.pad(part_out, ((0, 0), (0, -own % 16), (0, 0)))
    if direct:
        grad_packed, sum_up = lax.optimization_barrier((grad_packed, sum_up))
        sum_in, sum_pack, all_out, sum_down = scatter_all(
            grad_w_in.reshape(4, 2, 4, 2 * own, width), grad_packed.reshape((4, 2, 4) + grad_packed.shape[1:]), part_out, part_down, 80, 2
        )
    else:
        sum_in = lax.psum_scatter(grad_w_in, both, scatter_dimension=0, tiled=True).astype(F32)
        sum_pack = lax.psum_scatter(grad_packed, both, scatter_dimension=0, tiled=True)[0].astype(F32)
        all_out, sum_down = swap(part_out), swap(part_down)
    cuts, at = [], 0
    for size, turn in ((w_x.shape[1], False), (rank, False), (n, True), (taps, True), (1, True), (1, True), (1, True)):
        cuts.append((at, size, turn))
        at += size
    up_out, down_out, s_row, sum_out, s_x, s_dt, s_log, s_conv, s_bias, s_dtb, s_skip = finish(sum_pack, sum_up, sum_down, all_out, own, tuple(cuts))
    return (
        mixed_out[None],
        tokens_grad[None],
        s_row[0, :share],
        sum_in,
        s_conv.T,
        s_bias[0],
        s_x,
        s_dt,
        s_dtb[0],
        s_log.T,
        s_skip[0],
        sum_out,
        jnp.swapaxes(up_out, 1, 2),
        down_out,
    )


def solution(mesh):
    split = ("dp", "seq")
    token, row, mat, vec = P("dp", "seq", None), P("dp", "seq"), P(split, None), P(split)
    return jax.shard_map(
        shards,
        mesh=mesh,
        in_specs=(token, row, token, token, vec, mat, mat, vec, mat, mat, vec, mat, vec, mat, P(None, None, split), P(None, split, None)),
        out_specs=(token, token, vec, mat, mat, vec, mat, mat, vec, mat, vec, mat, P(None, None, split), P(None, split, None)),
        check_vma=False,
    )
```

```python
import functools
import math

import jax
import jax.numpy as jnp
from jax import lax
from jax.experimental import pallas as pl
from jax.experimental.pallas import tpu as pltpu
from jax.sharding import PartitionSpec as P

F32, BF = jnp.float32, jnp.bfloat16
EPS = 1e-05
STEP = 16
VM = 56 * 1024 * 1024
MESH = pl.DeviceIdType.MESH
SMALL = pl.CostEstimate(flops=0, bytes_accessed=0, transcendentals=0)
NT = (((1,), (1,)), ((), ()))
TN = (((0,), (0,)), ((), ()))


def rowr(ref, at, i, c, n):
    return jnp.broadcast_to(ref.at[pl.ds(at, STEP), c][i : i + 1, :], (n, 128))

def state_kernel(n, dte_ref, dtx_ref, rate_ref, b_ref, state_ref, carry_ref):
    rows, wide = dte_ref.shape
    tiles = wide // 128
    rates = [rate_ref[:, j*128:(j+1)*128] for j in range(tiles)]
    def block(k, carry):
        state, total = carry
        at = pl.multiple_of(k * STEP, STEP)
        dte = dte_ref[pl.ds(at, STEP), :]
        dtx = dtx_ref[pl.ds(at, STEP), :]
        state = list(state)
        for i in range(STEP):
            bs = b_ref[pl.ds((at + i) * n, n), :]
            for j in range(tiles):
                c = slice(j*128, (j+1)*128)
                decay = jnp.exp2(rowr(dte_ref, at, i, c, n) * rates[j])
                state[j] = decay * state[j] + bs * rowr(dtx_ref, at, i, c, n)
        return tuple(state), total + dte
    zero = tuple(jnp.zeros((n, 128), F32) for _ in range(tiles))
    state, total = lax.fori_loop(0, rows // STEP, block, (zero, jnp.zeros((STEP, wide), F32)))
    summed = jnp.sum(total, axis=0, keepdims=True)
    for j in range(tiles):
        c = slice(j*128, (j+1)*128)
        state_ref[:, c] = state[j]
        carry_ref[:, c] = jnp.exp2(jnp.broadcast_to(summed[:, c], (n, 128)) * rates[j])

def front_kernel(rim_ref, tok_ref, gain_ref, wc_ref, wz_ref, xt_ref, taps_ref, bias_ref, same_ref, normed_ref, conv_ref, sum_ref, values_ref, z_ref, proj_ref, ext):
    rows, wide = sum_ref.shape
    halo = rim_ref.shape[0]
    taps = taps_ref.shape[0]

    @pl.when(pl.program_id(0) == 0)
    def _():
        for ref, lo in ((rim_ref, 0), (tok_ref, halo)):
            tok = ref[...].astype(F32)
            scale = lax.rsqrt(jnp.mean(tok * tok, axis=1, keepdims=True) + EPS)
            ext[lo : lo + ref.shape[0], :] = (tok * scale * gain_ref[...]).astype(BF)
        normed_ref[...] = ext[halo:, :]
        proj_ref[...] = jnp.zeros_like(proj_ref)

    conv_ref[...] = lax.dot_general(ext[...], wc_ref[...], NT, preferred_element_type=F32).astype(BF).astype(F32)
    z_ref[...] = lax.dot_general(ext[halo:, :], wz_ref[...], NT, preferred_element_type=F32)
    same = [jnp.broadcast_to(same_ref[:, k : k + 1], (rows, 128)) for k in range(taps)]
    for j in range(wide // 128):
        c = slice(j * 128, (j + 1) * 128)
        total = jnp.broadcast_to(bias_ref[:, c], (rows, 128))
        for k in range(taps):
            lo = halo - taps + 1 + k
            total = total + taps_ref[k : k + 1, c] * conv_ref[lo : lo + rows, c] * same[k]
        sum_ref[:, c] = total
        values_ref[:, c] = total * jax.nn.sigmoid(total)
    proj_ref[...] += lax.dot_general(values_ref[...].astype(BF), xt_ref[...], NT, preferred_element_type=F32)


def front(rim, tok, gain, full_in, x_t, conv_taps, bias, same, wide):
    rows, width = tok.shape
    halo = rim.shape[0]
    chans = full_in.shape[0] // 2
    taps = conv_taps.shape[0]
    col = lambda r: pl.BlockSpec((r, wide), lambda g: (0, g))
    whole = lambda a: pl.BlockSpec(a.shape, lambda g: (0, 0))
    steps = chans // wide
    f32 = lambda r: jax.ShapeDtypeStruct((r, chans), F32)
    return pl.pallas_call(
        front_kernel,
        grid=(steps,),
        in_specs=[whole(rim), whole(tok), whole(gain), pl.BlockSpec((wide, width), lambda g: (g, 0)), pl.BlockSpec((wide, width), lambda g: (g + steps, 0)),
                  col(128), col(taps), col(1), whole(same)],
        out_specs=[whole(tok), col(rows + halo), col(rows), col(rows), col(rows), pl.BlockSpec((rows, 128), lambda g: (0, 0))],
        out_shape=[jax.ShapeDtypeStruct((rows, width), BF), f32(rows + halo), f32(rows), f32(rows), f32(rows), jax.ShapeDtypeStruct((rows, 128), F32)],
        scratch_shapes=[pltpu.VMEM((rows + halo, width), BF)],
        compiler_params=pltpu.CompilerParams(vmem_limit_bytes=VM),
        cost_estimate=pl.CostEstimate(flops=4*rows*chans*width, bytes_accessed=4*chans*width + 16*rows*chans, transcendentals=rows*chans),
        name="front",
    )(rim, tok, gain, full_in, full_in, x_t, conv_taps, bias, same)


def steps_kernel(n, rank_cols, proj_ref, keep_ref, values_ref, dtt_ref, dtb_ref, alog_ref,
                 low_ref, bw_ref, cw_ref, bblk_ref, cblk_ref, pre_ref, dt_ref, dte_ref, dtx_ref, rate_ref, rate2_ref, state_ref, carry_ref):
    rows, wide = pre_ref.shape
    groups = STEP * n

    @pl.when(pl.program_id(0) == 0)
    def _():
        proj = proj_ref[...]
        lanes = lax.broadcasted_iota(jnp.int32, proj.shape, 1)
        low_ref[...] = jnp.where(lanes < rank_cols, proj, 0.0).astype(BF)
        row = lax.broadcasted_iota(jnp.int32, (rows, groups), 0)
        col = lax.broadcasted_iota(jnp.int32, (rows, groups), 1)
        own = lax.rem(row, STEP) == col // n
        to_col = lax.rem(lax.broadcasted_iota(jnp.int32, (128, groups), 1), n)
        from_col = lax.broadcasted_iota(jnp.int32, (128, groups), 0)
        for i, (wide_ref, blk_ref) in enumerate(((bw_ref, bblk_ref), (cw_ref, cblk_ref))):
            pick = (from_col == to_col + rank_cols + i * n).astype(F32)
            tiled = jnp.where(own, jnp.dot(proj, pick, precision=lax.Precision.HIGHEST, preferred_element_type=F32), 0.0)
            high = tiled.astype(BF)
            low = (tiled - high.astype(F32)).astype(BF)
            blk_ref[...] = high
            ones = jnp.ones((STEP, 128), BF)
            for k in range(rows // STEP):
                at = slice(k * STEP, (k + 1) * STEP)
                wide_ref[k * groups : (k + 1) * groups, :] = lax.dot_general(high[at], ones, TN, preferred_element_type=F32) + lax.dot_general(low[at], ones, TN, preferred_element_type=F32)

    pre = jnp.dot(low_ref[...], dtt_ref[...], preferred_element_type=F32) + dtb_ref[...]
    dt = jax.nn.softplus(pre)
    pre_ref[...] = pre
    dt_ref[...] = dt
    dtx_ref[...] = dt * values_ref[...]
    taps = keep_ref.shape[1]
    keep = jnp.broadcast_to(keep_ref[:, taps - 2 : taps - 1], (rows, 128))
    for j in range(wide // 128):
        c = slice(j * 128, (j + 1) * 128)
        dte_ref[:, c] = jnp.where(keep > 0, dt[:, c], 1e30)
    rate = -jnp.exp(alog_ref[...])
    rate_ref[...] = rate
    rate2_ref[...] = rate * math.log2(math.e)
    state_kernel(n, dte_ref, dtx_ref, rate2_ref, bw_ref, state_ref, carry_ref)


def steps(proj, same, values, dt_t, dtb, alog_t, rank_cols, wide):
    rows, chans = values.shape
    n = alog_t.shape[0]
    groups = STEP * n
    col = lambda r: pl.BlockSpec((r, wide), lambda g: (0, g))
    fixed = lambda *s: pl.BlockSpec(s, lambda g: (0, 0))
    f32 = lambda *s: jax.ShapeDtypeStruct(s, F32)
    bf = lambda *s: jax.ShapeDtypeStruct(s, BF)
    return pl.pallas_call(
        functools.partial(steps_kernel, n, rank_cols),
        grid=(chans // wide,),
        in_specs=[fixed(rows, 128), fixed(*same.shape), col(rows), col(128), col(1), col(n)],
        out_specs=[fixed(rows, 128), fixed(rows * n, 128), fixed(rows * n, 128), fixed(rows, groups), fixed(rows, groups)] + [col(rows)] * 4 + [col(n)] * 4,
        out_shape=[bf(rows, 128), f32(rows * n, 128), f32(rows * n, 128), bf(rows, groups), bf(rows, groups)] + [f32(rows, chans)] * 4 + [f32(n, chans)] * 4,
        compiler_params=pltpu.CompilerParams(vmem_limit_bytes=VM),
        cost_estimate=pl.CostEstimate(flops=10*rows*chans*n, bytes_accessed=24*rows*chans, transcendentals=rows*chans*n),
        name="steps",
    )(proj, same, values, dt_t, dtb, alog_t)


def scan_kernel(n, dte_ref, dtx_ref, rate_ref, b_ref, cblk_ref, start_ref, values_ref, z_ref, skip_ref, out_ref, tok_ref, gain_ref, pick_ref,
                y_ref, check_ref, gated_ref, first_ref, normed_ref, sent_ref, hs):
    rows, wide = dte_ref.shape
    tiles = wide // 128
    rates = [rate_ref[:, j*128:(j+1)*128] for j in range(tiles)]

    def block(k, state):
        at = pl.multiple_of(k * STEP, STEP)
        dte = dte_ref[pl.ds(at, STEP), :]
        dtx = dtx_ref[pl.ds(at, STEP), :]
        state = list(state)
        kn = pl.multiple_of(k * n, n)
        for j in range(tiles):
            check_ref[pl.ds(kn, n), j*128:(j+1)*128] = state[j]
        for i in range(STEP):
            bs = b_ref[pl.ds((at + i) * n, n), :]
            for j in range(tiles):
                c = slice(j*128, (j+1)*128)
                decay = jnp.exp2(rowr(dte_ref, at, i, c, n) * rates[j])
                state[j] = decay * state[j] + bs * rowr(dtx_ref, at, i, c, n)
                hs[i*n:(i+1)*n, c] = state[j].astype(BF)
        y_ref[pl.ds(at, STEP), :] = jnp.dot(cblk_ref[pl.ds(at, STEP), :], hs[...], preferred_element_type=F32)
        return tuple(state)

    start = tuple(start_ref[:, j*128:(j+1)*128] for j in range(tiles))
    lax.fori_loop(0, rows // STEP, block, start)

    @pl.when(pl.program_id(0) == 0)
    def _():
        first_ref[...] = tok_ref[...].astype(F32)

    z = z_ref[...]
    gated_ref[...] = ((y_ref[...] + skip_ref[...] * values_ref[...]) * (z * jax.nn.sigmoid(z))).astype(BF)
    first_ref[...] += jnp.dot(gated_ref[...], out_ref[...], preferred_element_type=F32)

    @pl.when(pl.program_id(0) == pl.num_programs(0) - 1)
    def _():
        first = first_ref[...]
        scale = lax.rsqrt(jnp.mean(first * first, axis=1, keepdims=True) + EPS)
        normed_ref[...] = (first * scale * gain_ref[...]).astype(BF)
        sent_ref[...] = lax.dot_general(pick_ref[...], normed_ref[...], TN, preferred_element_type=F32).astype(BF)


def scan_pass(dte, dtx, rates2, b_wide, c_blk, start, values, z, skip, full_out, tok, gain, pick, wide):
    rows, chans = dte.shape
    n = rates2.shape[0]
    width = tok.shape[1]
    col = lambda r: pl.BlockSpec((r, wide), lambda g: (0, g))
    whole = lambda a: pl.BlockSpec(a.shape, lambda g: (0, 0))
    return pl.pallas_call(
        functools.partial(scan_kernel, n),
        grid=(chans // wide,),
        in_specs=[col(rows), col(rows), col(n), whole(b_wide), whole(c_blk), col(n), col(rows), col(rows), col(1), pl.BlockSpec((wide, width), lambda g: (g, 0)), whole(tok), whole(gain), whole(pick)],
        out_specs=[col(rows), col(rows // STEP * n), col(rows), whole(tok), whole(tok), pl.BlockSpec((pick.shape[1], width), lambda g: (0, 0))],
        out_shape=[jax.ShapeDtypeStruct((rows, chans), F32), jax.ShapeDtypeStruct((rows // STEP * n, chans), F32), jax.ShapeDtypeStruct((rows, chans), BF),
                   jax.ShapeDtypeStruct((rows, width), F32), jax.ShapeDtypeStruct((rows, width), BF), jax.ShapeDtypeStruct((pick.shape[1], width), BF)],
        scratch_shapes=[pltpu.VMEM((STEP * n, wide), BF)],
        compiler_params=pltpu.CompilerParams(vmem_limit_bytes=VM),
        cost_estimate=pl.CostEstimate(flops=10*rows*chans*n, bytes_accessed=12*rows*chans, transcendentals=rows*chans*n),
        name="scan_pass",
    )(dte, dtx, rates2, b_wide, c_blk, start, values, z, skip, full_out, tok, gain, pick)


def back_state_kernel(n, dte_ref, gs_ref, rate_ref, c_ref, out_ref):
    rows, wide = dte_ref.shape
    tiles = wide // 128
    rates = [rate_ref[:, j*128:(j+1)*128] for j in range(tiles)]
    def block(k, state):
        at = pl.multiple_of(rows - STEP - k * STEP, STEP)
        dte = dte_ref[pl.ds(at, STEP), :]
        gs = gs_ref[pl.ds(at, STEP), :]
        state = list(state)
        for i in reversed(range(STEP)):
            cs = c_ref[pl.ds((at + i) * n, n), :]
            for j in range(tiles):
                c = slice(j*128, (j+1)*128)
                decay = jnp.exp2(rowr(dte_ref, at, i, c, n) * rates[j])
                state[j] = decay * (state[j] + cs * rowr(gs_ref, at, i, c, n))
        return tuple(state)
    zero = tuple(jnp.zeros((n, 128), F32) for _ in range(tiles))
    state = lax.fori_loop(0, rows // STEP, block, zero)
    for j in range(tiles):
        out_ref[:, j*128:(j+1)*128] = state[j]

def back_front_kernel(n, order, steps, grad_ref, out_ref, z_ref, y_ref, values_ref, skip_ref, gated_ref, dte_ref, rate_ref, c_ref, gs_ref, gz_ref, gwo_ref, state_ref):
    grad = grad_ref[...]
    gated = lax.dot_general(grad, out_ref[...], NT, preferred_element_type=F32)
    z = z_ref[...]
    sig = jax.nn.sigmoid(z)
    gs_ref[...] = gated * (z * sig)
    gz_ref[...] = (gated * (y_ref[...] + skip_ref[...] * values_ref[...]) * (sig * (1.0 + z * (1.0 - sig)))).astype(BF)
    grad_out = lax.dot_general(gated_ref[...], grad, TN, preferred_element_type=F32).astype(BF)
    if order is None:
        gwo_ref[...] = grad_out
    else:
        per = len(order) // steps
        size = grad_out.shape[0] // per
        for g in range(steps):

            @pl.when(pl.program_id(0) == g)
            def _():
                for to, share in enumerate(order[g * per : (g + 1) * per]):
                    at = (share - g * per) * size
                    gwo_ref[to * size : (to + 1) * size, :] = grad_out[at : at + size]

    back_state_kernel(n, dte_ref, gs_ref, rate_ref, c_ref, state_ref)


def back_front(grad, full_out, z, scanned, values, skip, gated, dte, rates2, c_wide, wide, order=None):
    rows, chans = dte.shape
    width = grad.shape[1]
    n = rates2.shape[0]
    col = lambda r: pl.BlockSpec((r, wide), lambda g: (0, g))
    whole = lambda a: pl.BlockSpec(a.shape, lambda g: (0, 0))
    flat = pl.BlockSpec((wide, width), lambda g: (g, 0))
    return pl.pallas_call(
        functools.partial(back_front_kernel, n, order, chans // wide),
        grid=(chans // wide,),
        in_specs=[whole(grad), flat, col(rows), col(rows), col(rows), col(1), col(rows), col(rows), col(n), whole(c_wide)],
        out_specs=[col(rows), col(rows), flat, col(n)],
        out_shape=[jax.ShapeDtypeStruct((rows, chans), F32), jax.ShapeDtypeStruct((rows, chans), BF), jax.ShapeDtypeStruct((chans, width), BF), jax.ShapeDtypeStruct((n, chans), F32)],
        compiler_params=pltpu.CompilerParams(vmem_limit_bytes=VM),
        cost_estimate=pl.CostEstimate(flops=8*rows*chans*n, bytes_accessed=8*rows*chans, transcendentals=rows*chans*n),
        name="back_front",
    )(grad, full_out, z, scanned, values, skip, gated, dte, rates2, c_wide)


def back_kernel(n, rank_cols, dt_ref, dte_ref, dtx_ref, gs_ref, values_ref, pre_ref, skip_ref, rate_ref, rawrate_ref, b_ref, c_ref, bblk_ref, check_ref, next_ref, low_ref, wdt_ref,
                gval_ref, glog_ref, gwdt_ref, gdtb_ref, gskip_ref, proj_ref, us, decs, hs, ls, ps, gdtx, gdt, gb, gc, rank):
    rows, wide = dte_ref.shape
    tiles = wide // 128
    rates = [rate_ref[:, j*128:(j+1)*128] for j in range(tiles)]

    @pl.when(pl.program_id(0) == 0)
    def _():
        gb[...] = jnp.zeros_like(gb)
        gc[...] = jnp.zeros_like(gc)
        rank[...] = jnp.zeros_like(rank)

    ones = (lax.broadcasted_iota(jnp.int32, (STEP, STEP * n), 0) == lax.broadcasted_iota(jnp.int32, (STEP, STEP * n), 1) // n).astype(BF)
    glog_ref[...] = jnp.zeros_like(glog_ref)

    def block(k, later):
        kk = rows // STEP - 1 - k
        at = pl.multiple_of(kk * STEP, STEP)
        kn = pl.multiple_of(kk * n, n)
        dte = dte_ref[pl.ds(at, STEP), :]
        dtx = dtx_ref[pl.ds(at, STEP), :]
        state = [check_ref[pl.ds(kn, n), j*128:(j+1)*128] for j in range(tiles)]
        for i in range(STEP):
            bs = b_ref[pl.ds((at + i) * n, n), :]
            for j in range(tiles):
                c = slice(j*128, (j+1)*128)
                decay = jnp.exp2(rowr(dte_ref, at, i, c, n) * rates[j])
                kept = decay * state[j]
                state[j] = kept + bs * rowr(dtx_ref, at, i, c, n)
                decs[i*n:(i+1)*n, c] = decay
                us[i*n:(i+1)*n, c] = kept
                hs[i*n:(i+1)*n, c] = state[j].astype(BF)
        later = list(later)
        dt = dt_ref[pl.ds(at, STEP), :]
        gs = gs_ref[pl.ds(at, STEP), :]
        logs = [glog_ref[:, j*128:(j+1)*128] for j in range(tiles)]
        for i in reversed(range(STEP)):
            cs = c_ref[pl.ds((at + i) * n, n), :]
            for j in range(tiles):
                c = slice(j*128, (j+1)*128)
                adj = later[j] + cs * rowr(gs_ref, at, i, c, n)
                part = adj * us[i*n:(i+1)*n, c] * rawrate_ref[:, c]
                later[j] = adj * decs[i*n:(i+1)*n, c]
                logs[j] = logs[j] + part * rowr(dt_ref, at, i, c, n)
                ls[i*n:(i+1)*n, c] = adj.astype(BF)
                ps[i*n:(i+1)*n, c] = part.astype(BF)
        for j in range(tiles):
            glog_ref[:, j*128:(j+1)*128] = logs[j]
        gdtx[pl.ds(at, STEP), :] = jnp.dot(bblk_ref[pl.ds(at, STEP), :], ls[...], preferred_element_type=F32)
        gdt[pl.ds(at, STEP), :] = jnp.dot(ones, ps[...], preferred_element_type=F32)
        gb[pl.ds(at, STEP), :] += lax.dot_general(dtx.astype(BF), ls[...], NT, preferred_element_type=F32)
        gc[pl.ds(at, STEP), :] += lax.dot_general(gs.astype(BF), hs[...], NT, preferred_element_type=F32)
        return tuple(later)

    start = tuple(next_ref[:, j*128:(j+1)*128] for j in range(tiles))
    lax.fori_loop(0, rows // STEP, block, start)

    values = values_ref[...]
    grad_pre = (gdt[...] + gdtx[...] * values) * jax.nn.sigmoid(pre_ref[...])
    gdtb_ref[...] = jnp.sum(grad_pre, axis=0, keepdims=True)
    grad_pre = grad_pre.astype(BF)
    gwdt_ref[...] = lax.dot_general(low_ref[...], grad_pre, TN, preferred_element_type=F32)
    rank[...] += lax.dot_general(grad_pre, wdt_ref[...], NT, preferred_element_type=F32)
    gs = gs_ref[...]
    gskip_ref[...] = jnp.sum(gs * values, axis=0, keepdims=True)
    gval_ref[...] = gs * skip_ref[...] + gdtx[...] * dt_ref[...]

    @pl.when(pl.program_id(0) == pl.num_programs(0) - 1)
    def _():
        groups = STEP * n
        row = lax.broadcasted_iota(jnp.int32, (rows, groups), 0)
        col = lax.broadcasted_iota(jnp.int32, (rows, groups), 1)
        own = lax.rem(row, STEP) == col // n
        from_col = lax.rem(lax.broadcasted_iota(jnp.int32, (groups, rank.shape[1]), 0), n)
        to_col = lax.broadcasted_iota(jnp.int32, (groups, rank.shape[1]), 1)
        total = rank[...]
        for i, acc in enumerate((gb, gc)):
            place = (to_col == from_col + rank_cols + i * n).astype(BF)
            total = total + jnp.dot(jnp.where(own, acc[...], 0.0).astype(BF), place, preferred_element_type=F32)
        proj_ref[...] = total.astype(BF)


def back_pass(dt, dte, dtx, gs, values, pre, skip, rates2, rates, b_wide, c_wide, b_blk, check, nxt, low, wdt, rank_cols, wide):
    rows, chans = dte.shape
    n = rates2.shape[0]
    col = lambda r: pl.BlockSpec((r, wide), lambda g: (0, g))
    whole = lambda a: pl.BlockSpec(a.shape, lambda g: (0, 0))
    sq = lambda kind, w=wide: pltpu.VMEM((STEP * n, w), kind)
    return pl.pallas_call(
        functools.partial(back_kernel, n, rank_cols),
        grid=(chans // wide,),
        in_specs=[col(rows)] * 6 + [col(1)] + [col(n)] * 2 + [whole(b_wide), whole(c_wide), whole(b_blk), col(rows // STEP * n), col(n), whole(low), col(wdt.shape[0])],
        out_specs=[col(rows), col(n), col(low.shape[1]), col(1), col(1), pl.BlockSpec((rows, 128), lambda g: (0, 0))],
        out_shape=[jax.ShapeDtypeStruct((rows, chans), F32), jax.ShapeDtypeStruct((n, chans), F32), jax.ShapeDtypeStruct((low.shape[1], chans), F32),
                   jax.ShapeDtypeStruct((1, chans), F32), jax.ShapeDtypeStruct((1, chans), F32), jax.ShapeDtypeStruct((rows, 128), BF)],
        scratch_shapes=[sq(F32), sq(F32), sq(BF), sq(BF), sq(BF), pltpu.VMEM((rows, wide), F32), pltpu.VMEM((rows, wide), F32),
                        pltpu.VMEM((rows, STEP * n), F32), pltpu.VMEM((rows, STEP * n), F32), pltpu.VMEM((rows, 128), F32)],
        compiler_params=pltpu.CompilerParams(vmem_limit_bytes=VM),
        cost_estimate=pl.CostEstimate(flops=26*rows*chans*n, bytes_accessed=24*rows*chans, transcendentals=rows*chans*n),
        name="back_pass",
    )(dt, dte, dtx, gs, values, pre, skip, rates2, rates, b_wide, c_wide, b_blk, check, nxt, low, wdt)


def conv_back_kernel(halo, gval_ref, proj_ref, xt_ref, values_ref, sum_ref, ext_ref, same_ref, taps_ref, place_ref, slots_ref, first_ref,
                     mixed_ref, gconv_ref, last_ref, rim_ref, gxt_ref, gtaps_ref, pad):
    rows, wide = gval_ref.shape
    taps = taps_ref.shape[0]

    @pl.when(pl.program_id(0) == 0)
    def _():
        mixed_ref[...] = (first_ref[...] + jnp.dot(place_ref[...], slots_ref[...], preferred_element_type=F32)).astype(BF)

    proj = proj_ref[...]
    grad_values = gval_ref[...] + jnp.dot(proj, xt_ref[...], preferred_element_type=F32)
    gxt_ref[...] = lax.dot_general(proj, values_ref[...].astype(BF), TN, preferred_element_type=F32)
    sums = sum_ref[...]
    sig = jax.nn.sigmoid(sums)
    pad[0:rows, :] = grad_values * (sig * (1.0 + sums * (1.0 - sig)))
    pad[rows:, :] = jnp.zeros((pad.shape[0] - rows, wide), F32)
    row = lax.broadcasted_iota(jnp.int32, (8, 128), 0)
    same = [jnp.broadcast_to(same_ref[:, k : k + 1], (rows, 128)) for k in range(taps)]
    rowed = lax.broadcasted_iota(jnp.int32, (rows, 128), 0)
    later = [jnp.where(rowed < rows - (taps - 1 - k), pltpu.roll(same[k], (rows - (taps - 1 - k)) % rows, 0), 0.0) for k in range(taps)]
    for j in range(wide // 128):
        c = slice(j * 128, (j + 1) * 128)
        grads = pad[0:rows, c]
        sums_of = [jnp.sum(grads * same[k] * ext_ref[halo - taps + 1 + k : halo - taps + 1 + k + rows, c], axis=0, keepdims=True) for k in range(taps)]
        sums_of.append(jnp.sum(grads, axis=0, keepdims=True))
        total = jnp.zeros((rows, 128), F32)
        rim = jnp.zeros((8, 128), F32)
        for k in range(taps):
            weight = taps_ref[k : k + 1, c]
            total = total + pad[taps - 1 - k : taps - 1 - k + rows, c] * later[k] * weight
            if k < taps - 1:
                moved = pltpu.roll(grads[0:8] * same[k][0:8], 8 - taps + 1 + k, 0)
                rim = rim + jnp.where(row >= 8 - taps + 1 + k, moved, 0.0) * weight
        gconv_ref[:, c] = total.astype(BF)
        last_ref[:, c] = total[rows - 8 :]
        rim_ref[:, c] = rim
        gtaps_ref[:, c] = jnp.concatenate(sums_of + [jnp.zeros((8 - len(sums_of), 128), F32)], axis=0)


def conv_back(gval, proj, x_t, values, sums, ext, same, conv_taps, place, slots, first, halo, wide):
    rows, chans = gval.shape
    taps = conv_taps.shape[0]
    col = lambda r: pl.BlockSpec((r, wide), lambda g: (0, g))
    fixed = lambda a: pl.BlockSpec(a.shape, lambda g: (0, 0))
    mask = fixed(same)
    f32 = lambda r: jax.ShapeDtypeStruct((r, chans), F32)
    return pl.pallas_call(
        functools.partial(conv_back_kernel, halo),
        grid=(chans // wide,),
        in_specs=[col(rows), pl.BlockSpec(proj.shape, lambda g: (0, 0)), col(x_t.shape[0]), col(rows), col(rows), col(ext.shape[0]), mask, col(taps), fixed(place), fixed(slots), fixed(first)],
        out_specs=[fixed(first), col(rows), col(8), col(8), col(x_t.shape[0]), col(8)],
        out_shape=[jax.ShapeDtypeStruct(first.shape, BF), jax.ShapeDtypeStruct((rows, chans), BF), f32(8), f32(8), f32(x_t.shape[0]), f32(8)],
        scratch_shapes=[pltpu.VMEM((rows + 8, wide), F32)],
        compiler_params=pltpu.CompilerParams(vmem_limit_bytes=VM),
        cost_estimate=pl.CostEstimate(flops=60*rows*chans, bytes_accessed=20*rows*chans, transcendentals=rows*chans),
        name="conv_back",
    )(gval, proj, x_t, values, sums, ext, same, conv_taps, place, slots, first)


def tail_gate_kernel(gz_ref, normed_ref, win_ref, gwin_ref, total_ref):
    @pl.when(pl.program_id(0) == 0)
    def _():
        total_ref[...] = jnp.zeros_like(total_ref)

    grad = gz_ref[...]
    gwin_ref[...] = lax.dot_general(grad, normed_ref[...], TN, preferred_element_type=F32).astype(BF)
    total_ref[...] += jnp.dot(grad, win_ref[...], preferred_element_type=F32)


def tail_gate(grad_z, normed, full_in, wide):
    rows, width = normed.shape
    chans = grad_z.shape[1]
    steps = chans // wide
    whole = pl.BlockSpec((rows, width), lambda g: (0, 0))
    weights = pl.BlockSpec((wide, width), lambda g: (g + steps, 0))
    return pl.pallas_call(
        tail_gate_kernel,
        grid=(steps,),
        in_specs=[pl.BlockSpec((rows, wide), lambda g: (0, g)), whole, weights],
        out_specs=[weights, whole],
        out_shape=[jax.ShapeDtypeStruct((2 * chans, width), BF), jax.ShapeDtypeStruct((rows, width), F32)],
        compiler_params=pltpu.CompilerParams(vmem_limit_bytes=VM),
        cost_estimate=pl.CostEstimate(flops=4*rows*chans*width, bytes_accessed=4*chans*width, transcendentals=0),
        name="tail_gate",
    )(grad_z, normed, full_in)


def tail_kernel(conv_ref, last_ref, rim_ref, normed_ref, win_ref, tok_ref, gain_ref, first_ref, before_ref, _, gwin_ref, gtok_ref, ggain_ref, total, mixed):
    step = pl.program_id(0)
    rows = tok_ref.shape[0]

    @pl.when(step == 0)
    def _():
        total[...] = before_ref[...]

    mixed[0 : rows - 16, :] = conv_ref[0 : rows - 16, :]
    kept = conv_ref[rows - 16 : rows, :].astype(F32)
    mixed[rows - 16 : rows, :] = jnp.concatenate([kept[0:8], last_ref[...] + rim_ref[...]], axis=0).astype(BF)
    grad = mixed[...]
    gwin_ref[...] = lax.dot_general(grad, normed_ref[...], TN, preferred_element_type=F32).astype(BF)
    total[...] += jnp.dot(grad, win_ref[...], preferred_element_type=F32)

    @pl.when(step == pl.num_programs(0) - 1)
    def _():
        tok = tok_ref[...].astype(F32)
        grad_normed = total[...]
        scale = lax.rsqrt(jnp.mean(tok * tok, axis=1, keepdims=True) + EPS)
        scaled = grad_normed * gain_ref[...]
        ggain_ref[...] = jnp.sum(grad_normed * (tok * scale), axis=0, keepdims=True)
        back = scale * scaled - tok * (scale * scale * scale) * jnp.mean(tok * scaled, axis=1, keepdims=True)
        gtok_ref[...] = (first_ref[...] + back).astype(BF)


def tail(grad_conv, last, rim, normed, full_in, tok, gain, grad_first, before, gwin, wide):
    rows, width = tok.shape
    chans = grad_conv.shape[1]
    whole = lambda a: pl.BlockSpec(a.shape, lambda g: (0, 0))
    col = lambda r: pl.BlockSpec((r, wide), lambda g: (0, g))
    weights = pl.BlockSpec((wide, width), lambda g: (g, 0))
    return pl.pallas_call(
        tail_kernel,
        grid=(chans // wide,),
        in_specs=[col(rows), col(8), col(8), whole(normed), weights, whole(tok), whole(gain), whole(grad_first), whole(before), pl.BlockSpec(memory_space=pl.ANY)],
        out_specs=[weights, whole(tok), whole(gain)],
        out_shape=[jax.ShapeDtypeStruct(gwin.shape, BF), jax.ShapeDtypeStruct(tok.shape, BF), jax.ShapeDtypeStruct(gain.shape, F32)],
        input_output_aliases={9: 0},
        scratch_shapes=[pltpu.VMEM((rows, width), F32), pltpu.VMEM((rows, wide), BF)],
        compiler_params=pltpu.CompilerParams(vmem_limit_bytes=VM),
        cost_estimate=pl.CostEstimate(flops=4*rows*chans*width, bytes_accessed=4*chans*width, transcendentals=0),
        name="tail",
    )(grad_conv, last, rim, normed, full_in, tok, gain, grad_first, before, gwin)


def flip(value, bit):
    return value + bit - 2 * bit * (lax.rem(value // bit, 2))


def greet(partners):
    barrier = pltpu.get_barrier_semaphore()
    for partner in partners:
        pl.semaphore_signal(barrier, inc=1, device_id=partner, device_id_type=MESH)
    pl.semaphore_wait(barrier, len(partners))


class ZSwap:
    def __init__(self, pairs, local, send, recv, count):
        self.pairs, self.local, self.send, self.recv, self.count = pairs, local, send, recv, count

    def own(self):
        z = lax.axis_index("seq")
        return [pltpu.make_async_copy(src.at[z], dst.at[z], self.local.at[i]) for i, (src, dst) in enumerate(self.pairs)]

    def out(self):
        dp, z = lax.axis_index("dp"), lax.axis_index("seq")
        made = []
        for j in range(1, self.count):
            peer = lax.rem(z + j, self.count)
            for i, (src, dst) in enumerate(self.pairs):
                made.append(pltpu.make_async_remote_copy(src.at[peer], dst.at[z], self.send.at[i, j - 1], self.recv.at[i, j - 1], device_id=(dp, peer), device_id_type=MESH))
        return made

    def start(self):
        for copy in self.out() + self.own():
            copy.start()

    def wait(self):
        dp, z = lax.axis_index("dp"), lax.axis_index("seq")
        for copy in self.own():
            copy.wait()
        for copy in self.out():
            copy.wait_send()
        for j in range(1, self.count):
            source = lax.rem(z + self.count - j, self.count)
            for i, (src, dst) in enumerate(self.pairs):
                pltpu.make_async_remote_copy(src.at[z], dst.at[source], self.send.at[i, j - 1], self.recv.at[i, j - 1], device_id=(dp, source), device_id_type=MESH).wait_recv()


def gather_kernel(parts, count, in_ref, rest_ref, up_ref, tok_ref, ids_ref, gin_ref, grest_ref, gup_ref, rim_ref, rimids_ref,
                  local_sem, send, recv, share_send, share_recv, pair_send, pair_recv, swap_local, swap_send, swap_recv, rim_send, rim_recv):
    dp, z = lax.axis_index("dp"), lax.axis_index("seq")
    chip, core = dp // 2, lax.rem(dp, 2)
    srcs, dsts = (in_ref, rest_ref), (gin_ref, grest_ref)
    sibling = (flip(dp, 1), z)
    peers = [lax.rem(z + j, count) for j in range(1, count)]
    greet([sibling, (flip(dp, 4), z), (flip(dp, 2), z)] + [(dp, peer) for peer in peers])

    tail = pl.ds(tok_ref.shape[0] - rim_ref.shape[0], rim_ref.shape[0])
    rims = [pltpu.make_async_remote_copy(src, dst, rim_send.at[i], rim_recv.at[i], device_id=(dp, lax.rem(z + 1, count)), device_id_type=MESH)
            for i, (src, dst) in enumerate(((tok_ref.at[tail], rim_ref), (ids_ref, rimids_ref)))]
    for copy in rims:
        copy.start()
    mine = []
    for i, (src, dst) in enumerate(zip(srcs, dsts)):
        local = pltpu.make_async_copy(src, dst.at[chip, core, z], local_sem.at[i])
        pair = pltpu.make_async_remote_copy(src, dst.at[chip, core, z], pair_send.at[i], pair_recv.at[i], device_id=sibling, device_id_type=MESH)
        local.start()
        pair.start()
        mine += [local, pair]
    for copy in mine:
        copy.wait()
    swap = ZSwap(((up_ref, gup_ref),), swap_local, swap_send, swap_recv, count)

    def role(which, first_bit, second_bit):
        subs = parts[which]
        first, second = (flip(dp, first_bit), z), (flip(dp, second_bit), z)
        first_chip, second_chip = flip(chip, first_bit // 2), flip(chip, second_bit // 2)
        both_chip = flip(first_chip, second_bit // 2)

        def copies(sub, at_chip, at_z, slot, to, send_s, recv_s):
            made = []
            for i, (ref, lo, size) in enumerate(subs[sub]):
                view = dsts[ref].at[at_chip, :, at_z, pl.ds(lo, size)]
                made.append(pltpu.make_async_remote_copy(view, view, send_s.at[sub, slot, i], recv_s.at[sub, slot, i], device_id=to, device_id_type=MESH))
            return made

        def start(made):
            for copy in made:
                copy.start()

        def wait_recv(made):
            for copy in made:
                copy.wait_recv()

        def along_first(sub, k):
            return copies(sub, chip, k, 4 + k, first, send, recv)

        def along_second(sub, k, far):
            return copies(sub, first_chip if far else chip, k, 8 + 4 * far + k, second, send, recv)

        def came_first(sub, k):
            return copies(sub, first_chip, k, 4 + k, first, send, recv)

        def came_second(sub, k, far):
            return copies(sub, both_chip if far else second_chip, k, 8 + 4 * far + k, second, send, recv)

        def share(sub, at_chip, k, offset):
            return copies(sub, at_chip, k, 4 * offset + k, sibling, share_send, share_recv)

        def up(sub, k):
            return copies(sub, chip, k, k + count * 5, (dp, z + 1), send, recv)

        def down(sub, k):
            return copies(sub, chip, k, k, (dp, z - 1), send, recv)

        both = range(len(subs))

        def spread(sub, k):
            start(along_first(sub, k))
            start(along_second(sub, k, 0))

        def rest(k):
            for sub in both:
                wait_recv(came_first(sub, k))
                start(along_second(sub, k, 1))
                start(share(sub, first_chip, k, 1))

        def below(hop, work):
            pl.when(z - hop >= 0)(lambda: work(z - hop))

        def above(hop, work):
            pl.when(z + hop <= count - 1)(lambda: work(z + hop))

        def from_below(k):
            for sub in both:
                wait_recv(up(sub, k))
                pl.when(z < count - 1)(lambda: start(up(sub, k)))
                spread(sub, k)
                start(share(sub, chip, k, 0))

        def from_above(k):
            for sub in both:
                wait_recv(down(sub, k))
                pl.when(z > 0)(lambda: start(down(sub, k)))
                spread(sub, k)
                start(share(sub, chip, k, 0))

        for sub in both:
            pl.when(z > 0)(lambda: start(down(sub, z)))
            pl.when(z < count - 1)(lambda: start(up(sub, z)))
            spread(sub, z)
        for hop in range(1, count):
            below(hop, from_below)
            above(hop, from_above)
            if hop == count - 2:
                swap.start()
            if hop == 1:
                rest(z)
            else:
                below(hop - 1, rest)
                above(hop - 1, rest)
        below(count - 1, rest)
        above(count - 1, rest)

        def finish(k, _):
            for far in (0, 1):
                for sub in both:
                    wait_recv(came_second(sub, k, far))
                    start(share(sub, both_chip if far else second_chip, k, 2 + far))
            return 0

        lax.fori_loop(0, count, finish, 0)

        def drain(k, _):
            def wait_send(made):
                for copy in made:
                    copy.wait_send()

            for sub in both:
                wait_send(along_first(sub, k) + along_second(sub, k, 0) + along_second(sub, k, 1))
                for offset, at_chip in ((1, first_chip), (2, second_chip), (3, both_chip)):
                    wait_send(share(sub, at_chip, k, offset))
                pl.when(k != z)(lambda: wait_send(share(sub, chip, k, 0)))
                pl.when((k <= z) & (z < count - 1))(lambda: wait_send(up(sub, k)))
                pl.when((k >= z) & (z > 0))(lambda: wait_send(down(sub, k)))
            return 0

        lax.fori_loop(0, count, drain, 0)

        def shared(k, _):
            for offset, at_chip in enumerate((chip, second_chip, first_chip, both_chip)):
                def wait():
                    for sub, chunks in enumerate(parts[1 - which]):
                        for i, (ref, lo, size) in enumerate(chunks):
                            view = dsts[ref].at[at_chip, :, k, pl.ds(lo, size)]
                            pltpu.make_async_remote_copy(view, view, share_send.at[sub, 4 * offset + k, i], share_recv.at[sub, 4 * offset + k, i], device_id=sibling, device_id_type=MESH).wait_recv()
                if offset:
                    wait()
                else:
                    pl.when(k != z)(wait)
            return 0

        lax.fori_loop(0, count, shared, 0)

    pl.when(core == 0)(lambda: role(0, 4, 2))
    pl.when(core == 1)(lambda: role(1, 2, 4))
    swap.wait()
    for copy in rims:
        copy.wait()


def gather_all(w_in, rest, up, tok, ids, cut, count):
    parts = ((((0, 0, 48),), ((0, 48, cut - 48),)), (((0, cut, 48),), ((0, cut + 48, w_in.shape[0] - cut - 48), (1, 0, rest.shape[0]))))
    shape = lambda a: jax.ShapeDtypeStruct((4, 2, count) + a.shape, a.dtype)
    sems = lambda *s: pltpu.SemaphoreType.DMA(s)
    return pl.pallas_call(
        functools.partial(gather_kernel, parts, count),
        in_specs=[pl.BlockSpec(memory_space=pl.ANY)] * 5,
        out_specs=[pl.BlockSpec(memory_space=pl.ANY)] * 5,
        out_shape=[shape(w_in), shape(rest), jax.ShapeDtypeStruct(up.shape, up.dtype),
                   jax.ShapeDtypeStruct((16, tok.shape[1]), tok.dtype), jax.ShapeDtypeStruct(ids.shape, ids.dtype)],
        scratch_shapes=[sems(2), sems(2, 24, 2), sems(2, 24, 2), sems(2, 16, 2), sems(2, 16, 2), sems(2), sems(2), sems(1), sems(1, count - 1), sems(1, count - 1), sems(2), sems(2)],
        compiler_params=pltpu.CompilerParams(collective_id=1, has_side_effects=True),
        cost_estimate=pl.CostEstimate(flops=0, bytes_accessed=200_000_000, transcendentals=0),
        name="gather_all",
    )(w_in, rest, up, tok, ids)


def scatter_kernel(parts, count, in_ref, rest_ref, proj_ref, down_ref, oin_ref, orest_ref, oproj_ref, odown_ref, mine_a, mine_b, sib_a, sib_b, far_a, far_b, near_a, near_b, zgot_a, zgot_b, final_a, final_b,
                   load_sem, sib_send, sib_recv, two_send, two_recv, one_send, one_recv, z_send, z_recv, end_send, end_recv, end_local,
                   swap_local, swap_send, swap_recv):
    dp, z = lax.axis_index("dp"), lax.axis_index("seq")
    chip, core = dp // 2, lax.rem(dp, 2)
    srcs, outs = (in_ref, rest_ref), (oin_ref, orest_ref)
    mine, sib, far_got, near_got, z_got, final = (mine_a, mine_b), (sib_a, sib_b), (far_a, far_b), (near_a, near_b), (zgot_a, zgot_b), (final_a, final_b)
    sibling = (flip(dp, 1), z)
    peers = [(dp, lax.rem(z + j, count)) for j in range(1, count)]
    greet([sibling, (flip(dp, 4), z), (flip(dp, 2), z)] + peers)

    swap = ZSwap(((proj_ref, oproj_ref), (down_ref, odown_ref)), swap_local, swap_send, swap_recv, count)

    def role(which, first_bit, second_bit):
        chunks, other = parts[which], parts[1 - which]
        first, second = (flip(dp, first_bit), z), (flip(dp, second_bit), z)
        first_chip, second_chip = flip(chip, first_bit // 2), flip(chip, second_bit // 2)
        both_chip = flip(first_chip, second_bit // 2)
        steps = [lax.rem(z + 1 + j, count) for j in range(count)]

        def loads(col, k):
            slot = col * count + k
            return [pltpu.make_async_copy(srcs[ref].at[col, :, k, pl.ds(lo, size)], mine[ref].at[slot, :, pl.ds(0, size)], load_sem.at[slot, ref])
                    for ref, lo, size in chunks]

        def sibling_copies(col, k, pieces):
            slot = col * count + k
            return [pltpu.make_async_remote_copy(srcs[ref].at[col, :, k, pl.ds(lo, size)], sib[ref].at[slot, :, pl.ds(0, size)],
                                                 sib_send.at[slot, ref], sib_recv.at[slot, ref], device_id=sibling, device_id_type=MESH)
                    for ref, lo, size in pieces]

        def send(col, k, dst, slot, send_s, recv_s, to):
            return [pltpu.make_async_remote_copy(mine[ref].at[col * count + k, :, pl.ds(0, size)], dst[ref].at[slot, :, pl.ds(0, size)],
                                                 send_s.at[slot, ref], recv_s.at[slot, ref], device_id=to, device_id_type=MESH)
                    for ref, lo, size in chunks]

        def start(copies):
            for copy in copies:
                copy.start()

        def wait_recv(copies):
            for copy in copies:
                copy.wait_recv()

        def wait_send(copies):
            for copy in copies:
                copy.wait_send()

        def add(col, k, terms, last=False):
            slot = col * count + k
            for copy in loads(col, k):
                copy.wait()
            wait_recv(sibling_copies(col, k, chunks))
            for ref, lo, size in chunks:
                def rows(r, _):
                    at = pl.ds(pl.multiple_of(r * 16, 16), 16)
                    for c in range(2):
                        total = mine[ref][slot, c, at, :].astype(F32) + sib[ref][slot, c, at, :].astype(F32)
                        for buf, place in terms:
                            total = total + buf[ref][place, c, at, :].astype(F32)
                        if last:
                            final[ref][c, at, :] = total
                        else:
                            mine[ref][slot, c, at, :] = total.astype(BF)
                    return 0

                lax.fori_loop(0, size // 16, rows, 0)

        for k in steps:
            for col, sib_col in ((both_chip, both_chip), (second_chip, first_chip), (first_chip, second_chip), (chip, chip)):
                start(sibling_copies(sib_col, k, other) + loads(col, k))

        swap.start()

        def stage_one(k):
            for far, col in ((1, both_chip), (0, second_chip)):
                add(col, k, ())
                start(send(col, k, far_got, far * count + k, two_send, two_recv, second))

        def stage_two(k):
            wait_recv(send(first_chip, k, far_got, count + k, two_send, two_recv, second))
            add(first_chip, k, ((far_got, count + k),))
            start(send(first_chip, k, near_got, k, one_send, one_recv, first))

        def stage_three(j, k):
            wait_recv(send(chip, k, far_got, k, two_send, two_recv, second))
            wait_recv(send(chip, k, near_got, k, one_send, one_recv, first))
            if j < count - 1:
                add(chip, k, ((far_got, k), (near_got, k)))
                start(send(chip, k, z_got, j, z_send, z_recv, (dp, k)))

        for j in range(count + 2):
            if j < count:
                stage_one(steps[j])
            if 1 <= j <= count:
                stage_two(steps[j - 1])
            if j >= 2:
                stage_three(j - 2, steps[j - 2])

        for j in range(count - 1):
            wait_recv(send(chip, z, z_got, j, z_send, z_recv, (dp, z)))
        add(chip, z, ((far_got, z), (near_got, z)) + tuple((z_got, j) for j in range(count - 1)), last=True)
        locals_, remotes = [], []
        for ref, lo, size in chunks:
            locals_.append(pltpu.make_async_copy(final[ref].at[which, pl.ds(0, size)], outs[ref].at[pl.ds(lo, size)], end_local.at[ref]))
            remotes.append(pltpu.make_async_remote_copy(final[ref].at[1 - which, pl.ds(0, size)], outs[ref].at[pl.ds(lo, size)],
                                                        end_send.at[which, ref], end_recv.at[which, ref], device_id=sibling, device_id_type=MESH))
        start(locals_ + remotes)
        for copy in locals_:
            copy.wait()
        wait_send(remotes)
        for ref, lo, size in other:
            pltpu.make_async_remote_copy(final[ref].at[which, pl.ds(0, size)], outs[ref].at[pl.ds(lo, size)],
                                         end_send.at[1 - which, ref], end_recv.at[1 - which, ref], device_id=sibling, device_id_type=MESH).wait_recv()
        for j, k in enumerate(steps):
            for col in (chip, first_chip, second_chip, both_chip):
                wait_send(sibling_copies(col, k, other))
            wait_send(send(both_chip, k, far_got, count + k, two_send, two_recv, second))
            wait_send(send(second_chip, k, far_got, k, two_send, two_recv, second))
            wait_send(send(first_chip, k, near_got, k, one_send, one_recv, first))
            if j < count - 1:
                wait_send(send(chip, k, z_got, j, z_send, z_recv, (dp, k)))

    pl.when(core == 0)(lambda: role(0, 4, 2))
    pl.when(core == 1)(lambda: role(1, 2, 4))
    swap.wait()


def scatter_all(g_in, g_rest, proj, down, cut, collective_id):
    count = g_in.shape[2]
    rows_in, rows_rest = g_in.shape[3], g_rest.shape[3]
    parts = (((0, 0, cut),), ((0, cut, rows_in - cut), (1, 0, rows_rest)))
    sems = lambda *s: pltpu.SemaphoreType.DMA(s)
    places = 4 * count

    def bufs(k, kind=BF):
        lead = (k, 2) if k else (2,)
        return [pltpu.VMEM(lead + (max(cut, rows_in - cut), g_in.shape[4]), kind), pltpu.VMEM(lead + (rows_rest, g_rest.shape[4]), kind)]

    return pl.pallas_call(
        functools.partial(scatter_kernel, parts, count),
        in_specs=[pl.BlockSpec(memory_space=pl.ANY)] * 4,
        out_specs=[pl.BlockSpec(memory_space=pl.ANY)] * 4,
        out_shape=[jax.ShapeDtypeStruct(g_in.shape[3:], F32), jax.ShapeDtypeStruct(g_rest.shape[3:], F32), jax.ShapeDtypeStruct(proj.shape, proj.dtype), jax.ShapeDtypeStruct(down.shape, down.dtype)],
        scratch_shapes=bufs(places) + bufs(places) + bufs(2 * count) + bufs(count) + bufs(count - 1) + bufs(0, F32)
        + [sems(places, 2), sems(places, 2), sems(places, 2), sems(2 * count, 2), sems(2 * count, 2), sems(count, 2), sems(count, 2),
           sems(count - 1, 2), sems(count - 1, 2), sems(2, 2), sems(2, 2), sems(2), sems(2), sems(2, count - 1), sems(2, count - 1)],
        compiler_params=pltpu.CompilerParams(collective_id=collective_id, has_side_effects=True, vmem_limit_bytes=VM),
        cost_estimate=pl.CostEstimate(flops=0, bytes_accessed=200_000_000, transcendentals=0),
        name="scatter_all",
    )(g_in, g_rest, proj, down)


def unpack_kernel(own, cuts, pack_ref, small_ref, *refs):
    outs, tall = refs[:-1], refs[-1]
    for b in range(pack_ref.shape[0]):
        block = pack_ref[b].astype(F32)
        tall[b * own : (b + 1) * own, :] = block[:own]
        small_ref[b : b + 1, :] = block[own : own + 1]
    for j in range(tall.shape[0] // 128):
        c = slice(j * 128, (j + 1) * 128)
        turned = tall[c, :].T
        for ref, (lo, size) in zip(outs, cuts):
            part = turned[lo : lo + size]
            if ref.shape[0] > size:
                part = jnp.concatenate([part, jnp.zeros((ref.shape[0] - size, 128), F32)], axis=0)
            ref[:, c] = part.astype(ref.dtype)


def unpack(pack, own, sizes):
    blocks, _, cols = pack.shape
    chans = blocks * own
    cuts, at = [], 0
    for size in sizes:
        cuts.append((at, size))
        at += size
    rows = [128, 128] + list(sizes[2:])
    kinds = [BF, BF] + [F32] * (len(sizes) - 2)
    if own % 8:
        turned = pack[:, :own].reshape(chans, cols).T
        parts = [jnp.pad(turned[lo : lo + size], ((0, r - size), (0, 0))).astype(kind) for (lo, size), r, kind in zip(cuts, rows, kinds)]
        return [pack[:, own].astype(F32)] + parts
    return pl.pallas_call(
        functools.partial(unpack_kernel, own, tuple(cuts)),
        out_shape=[jax.ShapeDtypeStruct((blocks, cols), F32)] + [jax.ShapeDtypeStruct((r, chans), kind) for r, kind in zip(rows, kinds)],
        scratch_shapes=[pltpu.VMEM((chans, cols), F32)],
        compiler_params=pltpu.CompilerParams(vmem_limit_bytes=VM),
        name="unpack_small",
    )(pack)


def pack_kernel(own, sizes, x_ref, dt_ref, log_ref, taps_ref, dtb_ref, skip_ref, small_ref, part_ref, out_ref, grown_ref, wide, tall):
    at = 0
    for ref, size in zip((x_ref, dt_ref, log_ref, taps_ref, dtb_ref, skip_ref), sizes):
        wide[at : at + size, :] = ref[0:size, :]
        at += size
    wide[at:, :] = jnp.zeros((wide.shape[0] - at, wide.shape[1]), F32)
    for j in range(tall.shape[0] // 128):
        tall[j * 128 : (j + 1) * 128, :] = wide[:, j * 128 : (j + 1) * 128].T
    cols = wide.shape[0]
    first = lax.broadcasted_iota(jnp.int32, (8, cols), 0) == 0
    for b in range(out_ref.shape[0]):
        tail = jnp.where(first, jnp.broadcast_to(small_ref[b : b + 1, :], (8, cols)), 0.0)
        out_ref[b] = jnp.concatenate([tall[b * own : (b + 1) * own, :], tail], axis=0).astype(BF)
    for z in range(part_ref.shape[0]):
        rows = part_ref[z].astype(F32)
        grown_ref[z] = jnp.concatenate([rows, jnp.zeros((grown_ref.shape[1] - own, rows.shape[1]), F32)], axis=0).astype(BF)


def pack_grads(parts, sizes, small, part_out, own):
    blocks, cols = small.shape
    chans = parts[0].shape[1]
    rows = own + -own % 16
    if own % 8:
        turned = jnp.concatenate([part[:size] for part, size in zip(parts, sizes)]).T.reshape(blocks, own, -1)
        turned = jnp.pad(turned, ((0, 0), (0, 0), (0, cols - turned.shape[2])))
        return jnp.concatenate([turned, small[:, None], jnp.zeros((blocks, rows - own - 1, cols), F32)], axis=1).astype(BF), jnp.pad(part_out, ((0, 0), (0, rows - own), (0, 0)))
    return pl.pallas_call(
        functools.partial(pack_kernel, own, sizes),
        out_shape=[jax.ShapeDtypeStruct((blocks, rows, cols), BF), jax.ShapeDtypeStruct((part_out.shape[0], rows, part_out.shape[2]), BF)],
        scratch_shapes=[pltpu.VMEM((cols, chans), F32), pltpu.VMEM((chans, cols), F32)],
        compiler_params=pltpu.CompilerParams(vmem_limit_bytes=VM),
        name="pack_small",
    )(*parts, small, part_out)


def finish_kernel(own, cuts, pack_ref, up_ref, down_ref, proj_ref, up_out, down_out, row_out, proj_out, *small_outs):
    up_out[0] = up_ref[0].astype(F32)
    down_out[0] = down_ref[0].astype(F32)

    @pl.when(pl.program_id(0) == 0)
    def _():
        row_out[...] = pack_ref[own : own + 1, :]
        proj_out[...] = sum(proj_ref[k].astype(F32) for k in range(proj_ref.shape[0]))[:own]
        tall = pack_ref[...]
        turned = jnp.concatenate([tall, jnp.zeros((-tall.shape[0] % 128, tall.shape[1]), F32)], axis=0).T
        for (lo, size, turn), out in zip(cuts, small_outs):
            out[...] = turned[lo : lo + size, :own] if turn else pack_ref[0:own, lo : lo + size]


def finish(pack, up, down, proj, own, cuts):
    experts, piece, width = up.shape
    if own % 8:
        small = [pack[:own, lo : lo + size].T if turn else pack[:own, lo : lo + size] for lo, size, turn in cuts]
        return [up.astype(F32), down.astype(F32), pack[own : own + 1], jnp.sum(proj[:, :own].astype(F32), axis=0)] + small
    whole = lambda shape: pl.BlockSpec(shape, lambda e: (0,) * len(shape))
    part = lambda shape: pl.BlockSpec((1,) + shape[1:], lambda e: (e, 0, 0))
    shapes = [(experts, piece, width)] * 2 + [(1, pack.shape[1]), (own, width)] + [(size, own) if turn else (own, size) for _, size, turn in cuts]
    return pl.pallas_call(
        functools.partial(finish_kernel, own, cuts),
        grid=(experts,),
        in_specs=[whole(pack.shape), part(up.shape), part(up.shape), whole(proj.shape)],
        out_specs=[part(shapes[0]), part(shapes[1])] + [whole(s) for s in shapes[2:]],
        out_shape=[jax.ShapeDtypeStruct(s, F32) for s in shapes],
        compiler_params=pltpu.CompilerParams(vmem_limit_bytes=VM),
        name="finish",
    )(pack, up, down, proj)


def pack_params_kernel(x_ref, dt_ref, log_ref, taps_ref, bias_ref, dtb_ref, skip_ref, small_ref, out_ref, thin, tall):
    own, x_cols = x_ref.shape
    thin[...] = jnp.zeros_like(thin)
    at = 0
    for ref in (log_ref, taps_ref, bias_ref, dtb_ref, skip_ref):
        thin[at : at + ref.shape[0], 0:own] = ref[...].astype(F32)
        at += ref.shape[0]
    tall[...] = jnp.zeros_like(tall)
    at = x_cols + dt_ref.shape[1]
    tall[0:own, 0:x_cols] = x_ref[...].astype(F32)
    tall[0:own, x_cols:at] = dt_ref[...].astype(F32)
    tall[0:own, at : at + thin.shape[0]] = thin[...].T[:own]
    tall[own : own + 1, 0 : small_ref.shape[1]] = small_ref[...].astype(F32)
    out_ref[...] = tall[...].astype(BF)


def pack_params(w_x, w_dt, log_t, taps_t, bias, dtb, skip, small):
    own = w_x.shape[0]
    rows = own + -own % 16
    if own % 8:
        wide = jnp.concatenate([w_x, w_dt, log_t.T, taps_t.T, bias.T, dtb.T, skip.T], axis=1)
        wide = jnp.pad(wide, ((0, -own % 16), (0, 256 - wide.shape[1])))
        return wide + jnp.pad(small, ((own, -own % 16 - 1), (0, 256 - small.shape[1])))
    return pl.pallas_call(
        pack_params_kernel,
        out_shape=jax.ShapeDtypeStruct((rows, 256), BF),
        scratch_shapes=[pltpu.VMEM((32, 128), F32), pltpu.VMEM((rows, 256), F32)],
        name="pack_params",
    )(w_x, w_dt, log_t, taps_t, bias, dtb, skip, small)


def chain_kernel(step, pieces, carry_ref, own_ref, out_ref, inbox, outbox, send, recv):
    dp, z = lax.axis_index("dp"), lax.axis_index("seq")
    last = lax.axis_size("seq") - 1
    has_before = z > 0 if step > 0 else z < last
    has_after = z < last if step > 0 else z > 0
    barrier = pltpu.get_barrier_semaphore()

    def neighbours(act):
        pl.when(has_before)(lambda: act(z - step))
        pl.when(has_after)(lambda: act(z + step))

    neighbours(lambda peer: pl.semaphore_signal(barrier, inc=1, device_id=(dp, peer), device_id_type=MESH))
    count = last + 1
    pl.semaphore_wait(barrier, (z + last) // count + (2 * last - z) // count)
    wide = own_ref.shape[1] // pieces

    def copy(g):
        return pltpu.make_async_remote_copy(outbox.at[g], inbox.at[g], send.at[g], recv.at[g], device_id=(dp, z + step), device_id_type=MESH)

    def back(g):
        return pltpu.make_async_remote_copy(outbox.at[g], inbox.at[g], send.at[g], recv.at[g], device_id=(dp, z - step), device_id_type=MESH)

    for g in range(pieces):
        c = slice(g * wide, (g + 1) * wide)

        @pl.when(has_before)
        def _():
            back(g).wait_recv()
            out_ref[:, c] = inbox[g].astype(F32)

        @pl.when(jnp.logical_not(has_before))
        def _():
            out_ref[:, c] = jnp.zeros((out_ref.shape[0], wide), F32)

        @pl.when(has_after)
        def _():
            outbox[g] = (carry_ref[:, c] * out_ref[:, c] + own_ref[:, c]).astype(BF)
            copy(g).start()

    @pl.when(has_after)
    def _():
        for g in range(pieces):
            copy(g).wait_send()


def chain(carry, own, step, collective_id):
    pieces = 3
    n, chans = own.shape
    return pl.pallas_call(
        functools.partial(chain_kernel, step, pieces),
        in_specs=[pl.BlockSpec(memory_space=pltpu.VMEM)] * 2,
        out_specs=pl.BlockSpec(memory_space=pltpu.VMEM),
        out_shape=jax.ShapeDtypeStruct((n, chans), F32),
        scratch_shapes=[pltpu.VMEM((pieces, n, chans // pieces), BF)] * 2 + [pltpu.SemaphoreType.DMA((pieces,))] * 2,
        compiler_params=pltpu.CompilerParams(collective_id=collective_id, has_side_effects=True),
        name="chain",
    )(carry, own)


def experts_kernel(block, piece, pick_ref, n2_ref, early_ref, go_ref, router_ref, up_hbm, down_hbm, back_ref, late_ref, mixed_ref, grouter_ref, gexp_hbm,
                   up, down, gup, gdown, outbox, inbox, ret, total, disp, load_sem, store_sem, own_sem, out_send, out_recv, back_own, back_send, back_recv):
    dp, z = lax.axis_index("dp"), lax.axis_index("seq")
    count = lax.axis_size("seq")
    peers = [lax.rem(z + j, count) for j in range(1, count)]
    blocks = up.shape[0] // block
    rows, width = total.shape
    each = rows // count

    def loads(b):
        at = pl.ds(pl.multiple_of(b * block, block), block)
        return [pltpu.make_async_copy(up_hbm.at[at], up.at[at], load_sem.at[b, 0]), pltpu.make_async_copy(down_hbm.at[at], down.at[at], load_sem.at[b, 1])]

    def stores(b):
        made = []
        for i in range(block // piece):
            at = pl.ds(pl.multiple_of(b * block + i * piece, 16), piece)
            to = b * (block // piece) + i
            made.append(pltpu.make_async_copy(gup.at[at], gexp_hbm.at[to, 0], store_sem.at[to, 0]))
            made.append(pltpu.make_async_copy(gdown.at[at], gexp_hbm.at[to, 1], store_sem.at[to, 1]))
        return made

    def send(j):
        return pltpu.make_async_remote_copy(outbox.at[peers[j]], inbox.at[z], out_send.at[j], out_recv.at[j], device_id=(dp, peers[j]), device_id_type=MESH)

    def came(j):
        return pltpu.make_async_remote_copy(outbox.at[z], inbox.at[lax.rem(z + count - 1 - j, count)], out_send.at[j], out_recv.at[j], device_id=(dp, z), device_id_type=MESH)

    def kept():
        return pltpu.make_async_copy(outbox.at[z], inbox.at[z], own_sem.at[0])

    def give(half, j):
        return pltpu.make_async_remote_copy(ret.at[half, peers[j]], back_ref.at[z], back_send.at[half, j], back_recv.at[half, j], device_id=(dp, peers[j]), device_id_type=MESH)

    def got(half, j):
        return pltpu.make_async_remote_copy(ret.at[half, z], back_ref.at[lax.rem(z + count - 1 - j, count)], back_send.at[half, j], back_recv.at[half, j], device_id=(dp, z), device_id_type=MESH)

    def give_own(half):
        return pltpu.make_async_copy(ret.at[half, z], back_ref.at[z], back_own.at[half])

    greet([(dp, peer) for peer in peers])
    picked = lax.dot_general(pick_ref[...], n2_ref[...], TN, preferred_element_type=F32)
    outbox[...] = picked.astype(BF).reshape(count, each, width)
    for j in range(count - 1):
        send(j).start()
    kept().start()
    for b in range(blocks):
        for copy in loads(b):
            copy.start()
    lanes = lax.broadcasted_iota(jnp.int32, (rows, router_ref.shape[1]), 1)
    mine = (lanes == z).astype(F32)
    for half in range(2):
        if half:
            kept().wait()
            for j in range(count - 1):
                came(j).wait_recv()
        slots = (inbox if half else early_ref)[...].reshape(rows, width)
        go = go_ref[:, half * each : (half + 1) * each, :].reshape(rows, width).astype(F32)
        logits = jnp.where(lanes < count, jnp.dot(slots, router_ref[...], preferred_element_type=F32), -1e30)
        powers = jnp.exp(logits - jnp.max(logits, axis=1, keepdims=True))
        probs = jnp.where(lanes < count, powers / jnp.sum(powers, axis=1, keepdims=True), 0.0)
        gate = jnp.sum(probs * mine, axis=1, keepdims=True)
        grads = (gate * go).astype(BF)
        total[...] = jnp.zeros_like(total)
        disp[...] = jnp.zeros_like(disp)

        def units(b, _):
            at = pl.ds(pl.multiple_of(b * block, block), block)
            if half == 0:
                for copy in loads(b):
                    copy.wait()
            hidden = lax.dot_general(slots, up[at, :], NT, preferred_element_type=F32)
            phi = 0.5 * (1.0 + lax.erf(hidden * (1.0 / math.sqrt(2.0))))
            act = (hidden * phi).astype(BF)
            slope = phi + hidden * jnp.exp(hidden * hidden * -0.5) * (1.0 / math.sqrt(2.0 * math.pi))
            ghid = (lax.dot_general(grads, down[at, :], NT, preferred_element_type=F32) * slope).astype(BF)
            total[...] += jnp.dot(act, down[at, :], preferred_element_type=F32)
            disp[...] += jnp.dot(ghid, up[at, :], preferred_element_type=F32)
            new_up = lax.dot_general(ghid, slots, TN, preferred_element_type=F32)
            new_down = lax.dot_general(act, grads, TN, preferred_element_type=F32)
            if half == 0:
                gup[at, :] = new_up.astype(BF)
                gdown[at, :] = new_down.astype(BF)
            else:
                gup[at, :] = (gup[at, :].astype(F32) + new_up).astype(BF)
                gdown[at, :] = (gdown[at, :].astype(F32) + new_down).astype(BF)
                for copy in stores(b):
                    copy.start()
            return 0

        lax.fori_loop(0, blocks, units, 0)
        expert_out = total[...]
        mixed_ref[:, half * each : (half + 1) * each, :] = (gate * expert_out).astype(BF).reshape(count, each, width)
        grad_gate = jnp.sum(go * expert_out, axis=1, keepdims=True)
        grad_logits = (grad_gate * gate * (mine - probs)).astype(BF)
        grad_n2 = disp[...] + lax.dot_general(grad_logits, router_ref[...], NT, preferred_element_type=F32)
        if half == 0:
            ret[half] = grad_n2.astype(BF).reshape(count, each, width)
            for j in range(count - 1):
                give(half, j).start()
            give_own(half).start()
        else:
            late_ref[...] = grad_n2.astype(BF).reshape(count, each, width)
        grouter = lax.dot_general(slots, grad_logits, TN, preferred_element_type=F32)
        if half == 0:
            grouter_ref[...] = grouter
        else:
            grouter_ref[...] += grouter
    for b in range(blocks):
        for copy in stores(b):
            copy.wait()
    give_own(0).wait()
    for j in range(count - 1):
        send(j).wait_send()
        give(0, j).wait_send()
        got(0, j).wait_recv()


def experts_pass(pick, n2, early, go, router, up, down, block, piece, collective_id):
    count, slots, width = go.shape
    units = up.shape[0]
    rows = count * slots // 2
    vmem = pl.BlockSpec(memory_space=pltpu.VMEM)
    hbm = pl.BlockSpec(memory_space=pl.ANY)
    sems = lambda *s: pltpu.SemaphoreType.DMA(s)
    blocks = units // block
    return pl.pallas_call(
        functools.partial(experts_kernel, block, piece),
        in_specs=[vmem] * 5 + [hbm] * 2,
        out_specs=[hbm, vmem, vmem, vmem, hbm],
        out_shape=[jax.ShapeDtypeStruct((count, slots // 2, width), BF)] * 2 + [jax.ShapeDtypeStruct((count, slots, width), BF), jax.ShapeDtypeStruct(router.shape, F32),
                   jax.ShapeDtypeStruct((units // piece, 2, piece, width), BF)],
        scratch_shapes=[pltpu.VMEM(up.shape, BF)] * 4
        + [pltpu.VMEM((count, slots // 2, width), BF)] * 2 + [pltpu.VMEM((1, count, slots // 2, width), BF)] + [pltpu.VMEM((rows, width), F32)] * 2
        + [sems(blocks, 2), sems(units // piece, 2), sems(1), sems(count - 1), sems(count - 1), sems(1), sems(1, count - 1), sems(1, count - 1)],
        compiler_params=pltpu.CompilerParams(collective_id=collective_id, has_side_effects=True, vmem_limit_bytes=VM),
        cost_estimate=pl.CostEstimate(flops=24 * rows * units * width, bytes_accessed=100_000_000, transcendentals=4 * rows * units),
        name="experts",
    )(pick, n2, early, go, router, up, down)


def dot(a, b):
    return jnp.dot(a, b, preferred_element_type=F32)


def dot_nt(a, b):
    return lax.dot_general(a, b, NT, preferred_element_type=F32)


def dot_tn(a, b):
    return lax.dot_general(a, b, TN, preferred_element_type=F32)


def shift(value, axis, steps):
    count = lax.axis_size(axis)
    first, last = (max(0, -steps), min(count, count - steps))
    return lax.ppermute(value, axis, [(source, source + steps) for source in range(first, last)])


def rms_scale(value):
    return lax.rsqrt(jnp.mean(value * value, axis=-1, keepdims=True) + EPS)


def rms_back(value, gain, grad):
    scale = rms_scale(value)
    scaled = grad * gain
    grad_gain = jnp.sum(grad * (value * scale), axis=0)
    return scale * scaled - value * (scale * scale * scale) * jnp.mean(value * scaled, axis=-1, keepdims=True), grad_gain


def swap(value):
    return lax.all_to_all(value, "seq", 0, 0)


def shards(tokens, segment_ids, routes, cotangent, small_params, w_in, conv_w, conv_b, w_x, w_dt, dt_bias, a_log, d_skip, w_out, w_up, w_down):
    both = ("dp", "seq")
    devices = lax.axis_size(both)
    width = tokens.shape[2]
    rows = tokens.shape[1]
    experts = w_up.shape[0]
    chans = w_in.shape[0] * devices // 2
    own = w_out.shape[0]
    rank = w_dt.shape[1]
    n = a_log.shape[1]
    taps = conv_w.shape[1]
    slots = rows // 2
    halo = 16
    wide = 768

    tok_b = tokens[0]
    seg_plus = segment_ids[0] + 1

    share = small_params.shape[0]
    packed = pack_params(w_x, w_dt, a_log.T, conv_w.T, conv_b[None], dt_bias[None], d_skip[None], small_params[None])
    direct = lax.axis_size("dp") == 8 and lax.axis_size("seq") == 4
    ring = [[r ^ (r >> 1) for r in range(8)]] if direct else None
    up_t = jnp.swapaxes(w_up, 1, 2)
    full_out = lax.all_gather(w_out, both, axis=0, tiled=True)
    if direct:
        last_ids = jnp.broadcast_to(seg_plus[rows - halo :, None], (halo, 128))
        all_in, all_pack, part_up, rim_tok, rim_ids = gather_all(w_in, packed, up_t, tok_b, last_ids, 80, 4)
        down_late, all_in = lax.optimization_barrier((w_down, all_in))
        part_down = swap(down_late)
        rim_ids = jnp.where(lax.axis_index("seq") > 0, rim_ids[:, 0], 0)
    else:
        all_in, all_pack = lax.all_gather(w_in, both), lax.all_gather(packed, both)
        part_up, part_down = swap(up_t), swap(w_down)
        rim_tok = shift(tok_b[rows - halo :], "seq", 1)
        rim_ids = shift(seg_plus[rows - halo :], "seq", 1)
    full_in = lax.optimization_barrier(all_in.reshape(2 * chans, width))
    small, full_x_t, full_dt_t, alog_t, conv_f, bias_row, dtb_row, skip = unpack(all_pack.reshape(devices, -1, 256), own, (w_x.shape[1], rank, n, taps, 1, 1, 1))
    small, part_up = lax.optimization_barrier((small, part_up))
    full_up = lax.all_gather(part_up, "dp", axis=0, axis_index_groups=ring).reshape(-1, width)
    flat_small = small[:, :share].reshape(-1)
    gain_one = flat_small[:width]
    gain_two = flat_small[width : 2 * width]
    router = flat_small[2 * width :].reshape(width, experts).astype(BF)
    route_ids = routes[0]
    onehot = (route_ids == jnp.arange(experts)[None, :]).astype(BF)
    before = (jnp.arange(rows)[:, None] > jnp.arange(rows)[None, :]).astype(BF)
    place = jnp.sum(dot(before, onehot) * onehot.astype(F32), axis=1).astype(jnp.int32)
    slot_of = route_ids[:, 0] * slots + place
    gather_mat = (slot_of[:, None] == jnp.arange(experts * slots)[None, :]).astype(BF)
    half = slots // 2
    pick_of = place // half * (experts * half) + route_ids[:, 0] * half + place % half
    pick = (pick_of[:, None] == jnp.arange(experts * slots)[None, :]).astype(BF)
    grad_out_b = cotangent[0]
    grad_out = grad_out_b.astype(F32)
    tok_f = tok_b.astype(F32)
    ids_ext = jnp.concatenate([rim_ids, seg_plus])
    same = jnp.stack([ids_ext[halo - taps + 1 + k : halo - taps + 1 + k + rows] == seg_plus for k in range(taps)], axis=1).astype(F32)
    normed, conv_in, conv_sum, values, z, projected = front(rim_tok, tok_b, gain_one[None], full_in, full_x_t, conv_f, bias_row, same, wide)
    low_wide, b_wide, c_wide, b_blk, c_blk, pre_dt, dt, dt_keep, dtx, rates, rates2, own_state, carry = steps(projected, same, values, full_dt_t, dtb_row, alog_t, rank, wide)
    carry, part_down = lax.optimization_barrier((carry, part_down))
    full_down = lax.all_gather(part_down, "dp", axis=0, axis_index_groups=ring).reshape(-1, width)
    start = chain(carry, own_state, 1, 3)
    go_local, start = lax.optimization_barrier((dot_tn(gather_mat, grad_out_b).astype(BF), start))
    go_slots = swap(go_local.reshape(experts, slots, width))
    scanned, checks, gated, first_sum, normed_two, sent = scan_pass(
        dt_keep, dtx, rates2, b_wide, c_blk, start, values, z, skip, full_out, tok_b, gain_two[None], pick[:, : experts * half], wide
    )
    sent, go_slots = lax.optimization_barrier((sent, go_slots))
    early = swap(sent.reshape(experts, half, width))

    piece = w_up.shape[2]
    router_wide = jnp.pad(router, ((0, 0), (0, 128 - experts)))
    back_n2, late_n2, mixed_back, grad_router, grad_exp = experts_pass(pick[:, experts * half :], normed_two, early, go_slots, router_wide, full_up, full_down, 768, piece if piece % 16 == 0 else 768, 5)
    grad_router = grad_router[:, :experts]
    late_n2 = swap(late_n2)
    grad_n2 = dot(pick, jnp.concatenate([back_n2.reshape(-1, width), late_n2.reshape(-1, width)]))
    mixed_slots = swap(mixed_back).reshape(-1, width)
    if piece % 16:
        grad_exp = jnp.swapaxes(jnp.swapaxes(grad_exp, 0, 1).reshape(2, -1, piece, width), 0, 1)
    part_exp = lax.psum_scatter(grad_exp.reshape(-1, width), "dp", scatter_dimension=0, tiled=True, axis_index_groups=ring)

    grad_norm_two, grad_gain_two = rms_back(first_sum, gain_two, grad_n2)
    grad_first = grad_out + grad_norm_two
    grad_mixer = grad_first.astype(BF)
    grad_scanned, grad_z_b, grad_w_out, grad_start = back_front(grad_mixer, full_out, z, scanned, values, skip, gated, dt_keep, rates2, c_wide, chans // 2, ring[0] if direct else None)
    nxt = chain(carry, grad_start, -1, 4)
    grad_vals, g_log, grad_dt_t, grad_dtb, grad_skip, grad_proj = back_pass(
        dt, dt_keep, dtx, grad_scanned, values, pre_dt, skip, rates2, rates, b_wide, c_wide, b_blk, checks, nxt, low_wide, full_dt_t, rank, wide
    )
    grad_vals, mixed_slots, part_exp, grad_w_out = lax.optimization_barrier((grad_vals, mixed_slots, part_exp, grad_w_out))
    part_exp = part_exp.reshape(experts, 2, piece, width)
    part_down = part_exp[:, 1]
    sum_up = swap(part_exp[:, 0])
    mixed_out, grad_conv_b, grad_last, grad_rim, grad_x_t, grad_taps = conv_back(
        grad_vals, grad_proj, full_x_t, values, conv_sum, conv_in, same, conv_f, gather_mat, mixed_slots, first_sum, halo, wide
    )
    grad_z_b, grad_rim = lax.optimization_barrier((grad_z_b, grad_rim))
    grad_w_in, gate_part = tail_gate(grad_z_b, normed, full_in, wide)
    grad_w_in, tokens_grad, grad_gain_one = tail(
        grad_conv_b, grad_last, shift(grad_rim, "seq", -1), normed, full_in, tok_b, gain_one[None], grad_first, gate_part, grad_w_in, wide
    )
    grad_small = jnp.concatenate([grad_gain_one[0], grad_gain_two, grad_router.reshape(-1)])
    part_out = lax.psum_scatter(grad_w_out, "dp", scatter_dimension=0, tiled=True, axis_index_groups=ring).reshape(-1, own, width)
    grad_packed, part_out = pack_grads(
        (grad_x_t, grad_dt_t, g_log, grad_taps, grad_dtb, grad_skip), (w_x.shape[1], rank, n, taps + 1, 1, 1), jnp.pad(grad_small.reshape(devices, -1), ((0, 0), (0, 256 - share))), part_out, own
    )
    if direct:
        grad_packed, sum_up = lax.optimization_barrier((grad_packed, sum_up))
        sum_in, sum_pack, all_out, sum_down = scatter_all(
            grad_w_in.reshape(4, 2, 4, 2 * own, width), grad_packed.reshape((4, 2, 4) + grad_packed.shape[1:]), part_out, part_down, 80, 2
        )
    else:
        sum_in = lax.psum_scatter(grad_w_in, both, scatter_dimension=0, tiled=True).astype(F32)
        sum_pack = lax.psum_scatter(grad_packed, both, scatter_dimension=0, tiled=True)[0].astype(F32)
        all_out, sum_down = swap(part_out), swap(part_down)
    cuts, at = [], 0
    for size, turn in ((w_x.shape[1], False), (rank, False), (n, True), (taps, True), (1, True), (1, True), (1, True)):
        cuts.append((at, size, turn))
        at += size
    up_out, down_out, s_row, sum_out, s_x, s_dt, s_log, s_conv, s_bias, s_dtb, s_skip = finish(sum_pack, sum_up, sum_down, all_out, own, tuple(cuts))
    return (
        mixed_out[None],
        tokens_grad[None],
        s_row[0, :share],
        sum_in,
        s_conv.T,
        s_bias[0],
        s_x,
        s_dt,
        s_dtb[0],
        s_log.T,
        s_skip[0],
        sum_out,
        jnp.swapaxes(up_out, 1, 2),
        down_out,
    )


def solution(mesh):
    split = ("dp", "seq")
    token, row, mat, vec = P("dp", "seq", None), P("dp", "seq"), P(split, None), P(split)
    return jax.shard_map(
        shards,
        mesh=mesh,
        in_specs=(token, row, token, token, vec, mat, mat, vec, mat, mat, vec, mat, vec, mat, P(None, None, split), P(None, split, None)),
        out_specs=(token, token, vec, mat, mat, vec, mat, mat, vec, mat, vec, mat, P(None, None, split), P(None, split, None)),
        check_vma=False,
    )
```
